32 devices in a mesh: bead: 8 (over z, core), space: 4 (over y, x).
Axes of the slice: x: 2, y: 2, z: 4, core: 2. Of those that a mesh axis runs over, the one named last changes fastest.
Arguments:
- positions: float32 [3, 32, 16384], P(None, 'bead', 'space'), may hold values from -0.12 to 2.12
- momenta: float32 [3, 32, 16384], P(None, 'bead', 'space'), may hold values from -6 to 6
- atom_types: int32 [16384], P('space'), may hold values from 0 to 3
- neighbours: int32 [128, 5], P('space'), may hold values from 0 to 127, as said below
- thermal_noise: float32 [2, 3, 32, 16384], P(None, None, 'bead', 'space'), may hold values from -6 to 6
Outputs:
- positions_out: float32 [3, 32, 16384], P(None, 'bead', 'space')
- momenta_out: float32 [3, 32, 16384], P(None, 'bead', 'space')
The draws below stay inside these ranges and needn't reach their ends.
Inputs may be any that keep to these rules, and one draw needn't show every extreme that they name: `neighbours`: the row of block b holds 5 different blocks within 4 blocks of b, b itself and one block exactly 4 away among them.
All inputs are finite; a program needn't handle non-finite values.
Results may differ from the reference program's by a relative error of at most 0.0003.
Values sent between devices are 32-bit elements; how exact they have to be, the bound alone decides.
No kernel may reach another device: no remote copies, remote signals or barrier semaphores. Data moves between devices by JAX's collectives and lax.ppermute only.
A program may use at most 64 MiB of HBM per device.

```python
import math
import jax
import jax.numpy as jnp
from jax import lax

BEADS = 32
BLOCK = 128
HALO = 4
NBR = 5
STEPS = 2
ATOMS = 16384
BLOCKS = 128


def draw_positions(key, part):
    centre_key, spread_key = jax.random.split(jax.random.fold_in(key, 11))
    extent = jnp.array([1.0, 2.0, 2.0], dtype=jnp.float32)[:, None, None]
    centre = jax.random.uniform(centre_key, (3, 1, ATOMS), jnp.float32) * extent
    spread = 0.03 * jnp.clip(jax.random.normal(spread_key, (3, BEADS, ATOMS), jnp.float32), -4.0, 4.0)
    return centre + spread


def draw_neighbours(key, part):
    span_size = 2 * HALO + 1
    candidate = jnp.arange(span_size, dtype=jnp.int32) - HALO
    blocks = jnp.arange(BLOCKS, dtype=jnp.int32)[:, None]
    target = blocks + candidate[None, :]
    in_range = (target >= 0) & (target < BLOCKS)
    random_part = jax.random.randint(jax.random.fold_in(key, 23), (BLOCKS, span_size), 0, 1 << 20, dtype=jnp.int32)
    scores = random_part * span_size + candidate[None, :] + HALO
    top_value = (1 << 20) * span_size
    lower_ok = in_range[:, :1]
    upper_ok = in_range[:, -1:]
    odd_block = blocks % 2 == 1
    pick_upper = odd_block & upper_ok | jnp.logical_not(lower_ok)
    far_pick = jnp.where(pick_upper, candidate[None, :] == HALO, candidate[None, :] == -HALO)
    scores = jnp.where(far_pick, top_value + span_size, scores)
    scores = jnp.where(candidate[None, :] == 0, top_value + 2 * span_size, scores)
    scores = jnp.where(in_range, scores, -1 - candidate[None, :] - HALO)
    chosen = lax.top_k(scores, NBR)[1]
    return jnp.take_along_axis(target, chosen, axis=1).astype(jnp.int32)


def place_ends(values, key, low, largest):
    spot = [jax.random.randint(jax.random.fold_in(key, axis), (), 0, length) for axis, length in enumerate(values.shape)]
    widest = values.shape.index(max(values.shape))
    beside = spot[:widest] + [(spot[widest] + 1) % values.shape[widest]] + spot[widest + 1:]
    return values.at[tuple(spot)].set(low).at[tuple(beside)].set(largest)


def block_scale(rng, dims, shards, smallest, largest):
    def one(axis_at, parts):
        heights = jax.random.uniform(jax.random.fold_in(jax.random.fold_in(rng, 6), axis_at), (parts,), jnp.float32, smallest / len(shards), largest / len(shards))
        return jnp.repeat(jnp.exp(heights), dims[axis_at] // parts).reshape((-1,) + (1,) * (len(dims) - axis_at - 1))

    loudness = one(*shards[0])
    for cut in shards[1:]:
        loudness = loudness * one(*cut)
    return loudness


def gaussian(stream_key, shape, width, reach, shards=(), kind=jnp.bfloat16):
    values = jax.random.normal(stream_key, shape, jnp.float32) * width
    if len(shards) > 0:
        values = block_scale(stream_key, shape, shards, -0.22, 0.18) * values
    return jnp.clip(values, min=-reach, max=reach).astype(kind)


def setup_inputs(seed: int = 0) -> dict:
    keys = jax.random.split(jax.random.key(seed), 6)
    return {
        "positions": draw_positions(jax.random.fold_in(keys[5], 71), 0),
        "momenta": gaussian(keys[1], (3, BEADS, ATOMS), 1.0, 6.0, ((1, 8), (2, 4)), jnp.float32),
        "atom_types": place_ends(jax.random.randint(keys[2], (ATOMS,), 0, 4), jax.random.fold_in(keys[2], 1), 0, 3).astype(jnp.int32),
        "neighbours": draw_neighbours(jax.random.fold_in(keys[5], 71), 0),
        "thermal_noise": gaussian(keys[4], (STEPS, 3, BEADS, ATOMS), 1.0, 6.0, ((2, 8), (3, 4)), jnp.float32),
    }


half_step = 0.025
time_step = 0.05
chain_freq = 12.0
thermal = 0.375
centroid_friction = 1.0
screening = 4.0
softening = 0.09
highest = lax.Precision.HIGHEST

def materials(atom_types):
    onehot = (atom_types[:, None] == jnp.arange(4, dtype=jnp.int32)[None, :]).astype(jnp.float32)
    charge_table = jnp.array([1.0, -1.0, 0.6, -1.4], dtype=jnp.float32)
    mass_table = jnp.array([1.0, 2.0, 3.0, 4.0], dtype=jnp.float32)
    return (lax.optimization_barrier(jnp.sum(onehot * charge_table[None, :], axis=1)), lax.optimization_barrier(jnp.sum(onehot * mass_table[None, :], axis=1)))

def mode_matrix(bead_total):
    bead_ids = jnp.arange(bead_total, dtype=jnp.float32)[:, None]
    mode_ids = jnp.arange(bead_total, dtype=jnp.int32)[None, :]
    phase_grid = 2.0 * jnp.pi * bead_ids * mode_ids.astype(jnp.float32) / bead_total
    half_mode = bead_total // 2
    plain = 1.0 / math.sqrt(bead_total)
    paired = math.sqrt(2.0 / bead_total)
    return jnp.where(mode_ids == 0, plain + 0.0 * phase_grid, jnp.where(mode_ids < half_mode, paired * jnp.cos(phase_grid), jnp.where(mode_ids == half_mode, plain * jnp.cos(phase_grid), paired * jnp.sin(phase_grid))))

def mode_tables(bead_total):
    mode_ids = jnp.arange(bead_total, dtype=jnp.float32)
    frequency = 2.0 * chain_freq * jnp.sin(jnp.pi * mode_ids / bead_total)
    angle_step = frequency * time_step
    cosine = jnp.cos(angle_step)
    sine_ratio = jnp.where(mode_ids == 0, time_step, jnp.sin(angle_step) / jnp.where(mode_ids == 0, 1.0, frequency))
    stiffness = frequency * jnp.sin(angle_step)
    friction = jnp.where(mode_ids == 0, centroid_friction, 2.0 * frequency)
    damping = jnp.exp(-friction * time_step)
    kick_scale = jnp.sqrt(1.0 - damping * damping)
    return (cosine, sine_ratio, stiffness, damping, kick_scale)

def tile_force(own_rows, tile_rows, shift_rows):
    delta_x = own_rows[0][:, None, :, None] - tile_rows[0][:, :, None, :] + shift_rows[:, :, None, None]
    delta_y = own_rows[1][:, None, :, None] - tile_rows[1][:, :, None, :]
    delta_z = own_rows[2][:, None, :, None] - tile_rows[2][:, :, None, :]
    square = delta_x * delta_x + delta_y * delta_y + delta_z * delta_z + softening
    distance = jnp.sqrt(square)
    weight = jnp.exp(-distance / screening) * (1.0 / (screening * distance) + 1.0 / square) / distance
    weight = weight * tile_rows[3][:, :, None, :]
    force_x = own_rows[3] * lax.optimization_barrier(jnp.sum(weight * delta_x, axis=(1, 3)))
    force_y = own_rows[3] * lax.optimization_barrier(jnp.sum(weight * delta_y, axis=(1, 3)))
    force_z = own_rows[3] * lax.optimization_barrier(jnp.sum(weight * delta_z, axis=(1, 3)))
    return jnp.stack([force_x, force_y, force_z])

def bead_forces(extended, first_block, lists, offsets, group_size):
    block_count = lists.shape[0]

    def group_force(group_index):
        begin_row = group_index * group_size
        own_rows = lax.dynamic_slice_in_dim(extended, first_block + begin_row, group_size, 1)
        list_rows = lax.dynamic_slice_in_dim(lists, begin_row, group_size, 0)
        shift_rows = lax.dynamic_slice_in_dim(offsets, begin_row, group_size, 0)
        tile_rows = jnp.take(extended, list_rows, axis=1)
        return tile_force(own_rows, tile_rows, shift_rows)
    result = lax.map(group_force, jnp.arange(block_count // group_size, dtype=jnp.int32))
    return jnp.transpose(result, (1, 0, 2, 3)).reshape(3, block_count * extended.shape[2])

def thermostat_and_drift(mode_coords, mode_moment, noise_now, atom_mass, tables):
    cosine, sine_ratio, stiffness, damping, kick_scale = tuple((entry[None, :, None] for entry in tables))
    mass_row = atom_mass[None, None, :]
    moment_new = damping * mode_moment + kick_scale * jnp.sqrt(thermal * mass_row) * noise_now
    next_coords = cosine * mode_coords + sine_ratio * moment_new / mass_row
    next_moment = cosine * moment_new - stiffness * mass_row * mode_coords
    return (next_coords, next_moment)

def reference(positions, momenta, atom_types, neighbours, thermal_noise):
    charge, atom_mass = materials(atom_types)
    matrix = mode_matrix(BEADS)
    tables = mode_tables(BEADS)
    offsets = (jnp.arange(BLOCKS, dtype=jnp.int32)[:, None] - neighbours).astype(jnp.float32)
    charge_blocks = charge.reshape(1, BLOCKS, BLOCK)

    def all_forces(coords):

        def one_bead(single):
            extended = jnp.concatenate([single.reshape(3, BLOCKS, BLOCK), charge_blocks], axis=0)
            return bead_forces(extended, 0, neighbours, offsets, 2)
        per_bead = lax.map(one_bead, jnp.transpose(coords, (1, 0, 2)))
        return jnp.transpose(per_bead, (1, 0, 2))
    forces_now = all_forces(positions)
    coords, moment = (positions, momenta)
    for turn_index in range(STEPS):
        moment = moment + half_step * forces_now
        mode_coords = jnp.einsum('jk,cja->cka', matrix, coords, precision=highest)
        mode_moment = jnp.einsum('jk,cja->cka', matrix, moment, precision=highest)
        next_coords, next_moment = thermostat_and_drift(mode_coords, mode_moment, thermal_noise[turn_index], atom_mass, tables)
        coords = jnp.einsum('jk,cka->cja', matrix, next_coords, precision=highest)
        moment = jnp.einsum('jk,cka->cja', matrix, next_moment, precision=highest)
        forces_now = all_forces(coords)
        moment = moment + half_step * forces_now
    return (coords, moment)
```

```python
import functools
import math

import jax
import jax.numpy as jnp
import numpy as np
from jax import lax
from jax.experimental import pallas as pl
from jax.experimental.pallas import tpu as pltpu
from jax.sharding import PartitionSpec as P

BLOCK = 128
HALO = 4

half_step = 0.025
time_step = 0.05
chain_freq = 12.0
thermal = 0.375
centroid_friction = 1.0
screening = 4.0
softening = 0.09
CHARGES = (1.0, -1.0, 0.6, -1.4)
MASSES = (1.0, 2.0, 3.0, 4.0)

PAIR_ROWS = 24
SUM_ROWS = 16
f32 = jnp.float32
bf16 = jnp.bfloat16


def mode_constants(bead_total):
    j = np.arange(bead_total)[:, None]
    k = np.arange(bead_total)[None, :]
    half = bead_total // 2
    phase = 2.0 * np.pi * ((j * k) % bead_total) / bead_total
    plain = 1.0 / math.sqrt(bead_total)
    paired = math.sqrt(2.0 / bead_total)
    matrix = np.where(
        k == 0,
        plain,
        np.where(
            k < half,
            paired * np.cos(phase),
            np.where(k == half, plain * np.cos(phase), paired * np.sin(phase)),
        ),
    )
    modes = np.arange(bead_total)
    frequency = 2.0 * chain_freq * np.sin(np.pi * modes / bead_total)
    angle = frequency * time_step
    ratio = np.where(modes == 0, time_step, np.sin(angle) / np.where(modes == 0, 1.0, frequency))
    friction = np.where(modes == 0, centroid_friction, 2.0 * frequency)
    damping = np.exp(-friction * time_step)
    kick = np.sqrt(1.0 - damping * damping)
    tables = np.stack([np.cos(angle), ratio, frequency * np.sin(angle), damping, kick])
    tables = np.broadcast_to(tables[:, :, None], tables.shape + (BLOCK,))
    return matrix.astype(np.float32), np.ascontiguousarray(tables).astype(np.float32)


def split3(v):
    one = v.astype(bf16).astype(f32)
    rest = v - one
    two = rest.astype(bf16).astype(f32)
    three = (rest - two).astype(bf16).astype(f32)
    return one, two, three


def force_kernel(
    hops, beads, blocks, listed, last, kicks,
    index_ref, delta_ref, *refs,
):
    parts = 2 * hops + 1
    x_refs = refs[:parts]
    q_refs = refs[parts:2 * parts]
    rest = refs[2 * parts:]
    if last:
        p_ref, pout_ref = rest[:2]
        scratch = rest[2:]
    else:
        p_ref, noise_ref, mass_ref, matrix_ref, matrix_t_ref, table_ref, xout_ref, pout_ref = rest[:8]
        scratch = rest[8:]
    rows_ref, sums_ref, far_ref, near_ref, weigh_ref, own_ref, total_ref, shift_ref, force_ref = scratch
    own_x = x_refs[hops]
    own_q = q_refs[hops]
    pairs = beads // 2

    for part in range(parts):
        for block in range(blocks):
            lanes = slice(block * BLOCK, (block + 1) * BLOCK)
            coords = [x_refs[part][c, :, lanes] - 1.0 for c in range(3)]
            charge = jnp.broadcast_to(q_refs[part][:, lanes], coords[0].shape)
            norm = coords[0] * coords[0] + coords[1] * coords[1] + coords[2] * coords[2]
            rows = []
            for c in range(3):
                one, two, three = split3(coords[c])
                rows += [one, two, one, two, three, one]
            ones = jnp.ones_like(norm)
            rows += [ones, ones, ones]
            rows += list(split3(norm))
            for k, row in enumerate(rows):
                rows_ref[k * beads:(k + 1) * beads, :] = row
            charged = [split3(v) for v in [charge] + [charge * coords[c] for c in range(3)]]
            for level in range(3):
                for c in range(4):
                    k = level * 4 + c
                    sums_ref[k * beads:(k + 1) * beads, :] = charged[c][level]
            for k in range(12, SUM_ROWS):
                sums_ref[k * beads:(k + 1) * beads, :] = jnp.zeros_like(norm)
            at = part * blocks + block

            def place(pair, carry, at=at):
                both = jnp.concatenate(
                    [rows_ref[pl.ds(2 * pair + i, PAIR_ROWS, stride=beads), :] for i in range(2)], axis=0
                )
                far_ref[at, pair] = jnp.transpose(both).astype(bf16)
                weigh_ref[at, pair] = jnp.concatenate(
                    [sums_ref[pl.ds(2 * pair + i, SUM_ROWS, stride=beads), :] for i in range(2)], axis=0
                ).astype(bf16)
                return carry

            lax.fori_loop(0, pairs, place, 0)

    def one_block(block, carry):
        start = pl.multiple_of(block * BLOCK, BLOCK)
        lanes = pl.ds(start, BLOCK)
        coords = [own_x[c, :, lanes] - 1.0 for c in range(3)]
        side = [split3(v) for v in coords]
        across = coords[1] * coords[1] + coords[2] * coords[2] + softening
        ones = jnp.ones_like(across)
        for m in range(listed):
            moved = coords[0] + delta_ref[block * listed + m]
            rows = []
            for one, two, three in [split3(moved), side[1], side[2]]:
                a, b, c = -2.0 * one, -2.0 * two, -2.0 * three
                rows += [a, a, b, b, a, c]
            rows += list(split3(moved * moved + across))
            rows += [ones, ones, ones]
            for k, row in enumerate(rows):
                own_ref[m, k * beads:(k + 1) * beads, :] = row

        blank = jnp.zeros((PAIR_ROWS, BLOCK), f32)

        def one_pair(pair, inner):
            total = jnp.zeros((2 * SUM_ROWS, 2 * BLOCK), f32)
            shift = jnp.zeros((2 * SUM_ROWS, 2 * BLOCK), f32)
            for m in range(listed):
                at = index_ref[block * listed + m]
                first, second = [
                    own_ref[m, pl.ds(2 * pair + i, PAIR_ROWS, stride=beads), :] for i in range(2)
                ]
                own = jnp.concatenate(
                    [
                        jnp.concatenate([first, blank], axis=0),
                        jnp.concatenate([blank, second], axis=0),
                    ],
                    axis=1,
                ).astype(bf16)
                square = jnp.dot(far_ref[at, pair], own, preferred_element_type=f32)
                inverse = lax.rsqrt(square)
                distance = square * inverse
                decay = jnp.exp2(distance * (-1.0 / (screening * math.log(2.0))))
                weight = decay * ((inverse * inverse) * (inverse + 1.0 / screening))
                high = weight.astype(bf16)
                low = (weight - high.astype(f32)).astype(bf16)
                heavy = weigh_ref[at, pair]
                summed = jnp.dot(
                    jnp.concatenate([heavy, heavy], axis=1),
                    jnp.concatenate([high, low], axis=0),
                    preferred_element_type=f32,
                )
                total = total + summed
                shift = shift + delta_ref[block * listed + m] * summed
            for i in range(2):
                cols = slice(i * BLOCK, (i + 1) * BLOCK)
                low_row = i * SUM_ROWS
                spot = pl.ds(pl.multiple_of((2 * pair + i) * 8, 8), 8)
                total_ref[spot, :] = total[low_row:low_row + 8, cols] + total[low_row + 8:low_row + 16, cols]
                shift_ref[spot, :] = shift[low_row:low_row + 8, cols] + shift[low_row + 8:low_row + 16, cols]
            return inner

        lax.fori_loop(0, pairs, one_pair, 0)

        def gathered(ref, c):
            return ref[pl.ds(c, beads, stride=8), :] + ref[pl.ds(c + 4, beads, stride=8), :]

        charge = jnp.broadcast_to(own_q[:, lanes], across.shape)
        near = gathered(total_ref, 0)
        for c in range(3):
            pull = coords[c] * near - gathered(total_ref, c + 1)
            if c == 0:
                pull = pull + gathered(shift_ref, 0)
            force_ref[c, :, lanes] = charge * pull
        return carry

    lax.fori_loop(0, blocks, one_block, 0)

    scale = kicks * half_step
    if last:
        for c in range(3):
            pout_ref[c] = p_ref[c] + scale * force_ref[c]
        return

    width = blocks * BLOCK
    cosine, ratio, stiffness, damping, kick = [
        jnp.concatenate([table_ref[i]] * blocks, axis=1) for i in range(5)
    ]
    mass = jnp.broadcast_to(mass_ref[...], (beads, width))
    spread = kick * jnp.sqrt(thermal * mass)
    drift = ratio / mass
    stiff = stiffness * mass
    multiply = functools.partial(jnp.dot, precision=lax.Precision.HIGHEST, preferred_element_type=f32)
    for c in range(3):
        moment = p_ref[c] + scale * force_ref[c]
        mode_x = multiply(matrix_t_ref[...], own_x[c])
        mode_p = damping * multiply(matrix_t_ref[...], moment) + spread * noise_ref[c]
        xout_ref[c] = multiply(matrix_ref[...], cosine * mode_x + drift * mode_p)
        pout_ref[c] = multiply(matrix_ref[...], cosine * mode_p - stiff * mode_x)


def run_forces(window_x, window_q, index, delta, moment, last, kicks, extra=()):
    hops = len(window_x) // 2
    _, beads, atoms = window_x[hops].shape
    blocks = atoms // BLOCK
    listed = index.shape[0] // blocks
    parts = 2 * hops + 1
    pairs = beads // 2
    shape = jax.ShapeDtypeStruct((3, beads, atoms), f32)
    vmem = pl.BlockSpec(memory_space=pltpu.VMEM)
    smem = pl.BlockSpec(memory_space=pltpu.SMEM)
    work = beads * blocks * listed * BLOCK * BLOCK
    return pl.pallas_call(
        functools.partial(force_kernel, hops, beads, blocks, listed, last, kicks),
        out_shape=shape if last else (shape, shape),
        in_specs=[smem, smem] + [vmem] * (2 * parts + 1 + len(extra)),
        out_specs=vmem if last else (vmem, vmem),
        scratch_shapes=[
            pltpu.VMEM((PAIR_ROWS * beads, BLOCK), f32),
            pltpu.VMEM((SUM_ROWS * beads, BLOCK), f32),
            pltpu.VMEM((parts * blocks, pairs, BLOCK, 2 * PAIR_ROWS), bf16),
            pltpu.VMEM((8, BLOCK), f32),
            pltpu.VMEM((parts * blocks, pairs, 2 * SUM_ROWS, BLOCK), bf16),
            pltpu.VMEM((listed, PAIR_ROWS * beads, BLOCK), f32),
            pltpu.VMEM((8 * beads, BLOCK), f32),
            pltpu.VMEM((8 * beads, BLOCK), f32),
            pltpu.VMEM((3, beads, atoms), f32),
        ],
        compiler_params=pltpu.CompilerParams(vmem_limit_bytes=40 * 1024 * 1024),
        cost_estimate=pl.CostEstimate(flops=20 * work, bytes_accessed=4 * 1024 * 1024, transcendentals=2 * work),
    )(index, delta, *window_x, *window_q, moment, *extra)


def fold(count):
    return [i // 2 if i % 2 == 0 else count - 1 - i // 2 for i in range(count)]


def to_atoms(values):
    count = lax.axis_size("bead")
    lead, beads, atoms = values.shape
    share = atoms // count
    pieces = jnp.stack([values[:, :, at * share:(at + 1) * share] for at in fold(count)])
    pieces = lax.all_to_all(pieces, "bead", split_axis=0, concat_axis=0)
    return jnp.transpose(pieces, (1, 0, 2, 3)).reshape(lead, count * beads, share)


def to_beads(values):
    count = lax.axis_size("bead")
    lead, beads, share = values.shape
    local = beads // count
    pieces = jnp.transpose(values.reshape(lead, count, local, share), (1, 0, 2, 3))
    pieces = lax.all_to_all(pieces, "bead", split_axis=0, concat_axis=0)
    order = fold(count)
    return jnp.concatenate([pieces[order.index(at)] for at in range(count)], axis=2)


def window(values, hops):
    count = lax.axis_size("bead")
    domains = lax.axis_size("space")
    order = fold(count)
    device = {}
    for bead in range(count):
        for domain in range(domains):
            device[domain * count + order[bead]] = bead * domains + domain
    total = count * domains
    out = []
    for hop in range(-hops, hops + 1):
        if hop == 0:
            out.append(values)
        else:
            route = [(device[at + hop], device[at]) for at in range(total) if 0 <= at + hop < total]
            out.append(lax.ppermute(values, ("bead", "space"), route))
    return out


def body(positions, momenta, atom_types, neighbours, thermal_noise):
    count = lax.axis_size("bead")
    beads = positions.shape[1] * count
    atoms = positions.shape[2]
    share = atoms // count
    blocks = share // BLOCK
    hops = -(-HALO // blocks)
    steps = thermal_noise.shape[0]

    place = jnp.asarray(np.array(fold(count), np.int32))[lax.axis_index("bead")]
    types = lax.dynamic_slice_in_dim(atom_types, place * share, share)[None, :]
    charge = jnp.zeros(types.shape, f32)
    mass = jnp.zeros(types.shape, f32)
    for kind in range(4):
        charge = jnp.where(types == kind, CHARGES[kind], charge)
        mass = jnp.where(types == kind, MASSES[kind], mass)
    first = lax.axis_index("space") * (atoms // BLOCK) + place * blocks
    lists = lax.dynamic_slice_in_dim(neighbours, place * blocks, blocks)
    own = first + jnp.arange(blocks, dtype=jnp.int32)
    delta = (own[:, None] - lists).astype(f32).reshape(-1)
    index = jnp.clip(lists - first + hops * blocks, 0, (2 * hops + 1) * blocks - 1).reshape(-1)

    matrix, tables = mode_constants(beads)
    fixed = (jnp.asarray(matrix), jnp.asarray(np.ascontiguousarray(matrix.T)), jnp.asarray(tables))

    window_q = window(charge, hops)
    coords = to_atoms(positions)
    rest = to_atoms(jnp.concatenate([momenta] + [thermal_noise[t] for t in range(steps)], axis=0))
    moment = rest[:3]
    for step in range(steps):
        noise = rest[3 * step + 3:3 * step + 6]
        coords, moment = run_forces(
            window(coords, hops), window_q, index, delta, moment, False,
            1.0 if step == 0 else 2.0, (noise, mass) + fixed,
        )
    moment = run_forces(window(coords, hops), window_q, index, delta, moment, True, 1.0)
    return to_beads(coords), to_beads(moment)


def solution(mesh):
    placed = (
        P(None, "bead", "space"),
        P(None, "bead", "space"),
        P("space"),
        P("space", None),
        P(None, None, "bead", "space"),
    )
    return jax.shard_map(
        body,
        mesh=mesh,
        in_specs=placed,
        out_specs=(P(None, "bead", "space"), P(None, "bead", "space")),
        check_vma=False,
    )
```

```python
import functools
import math

import jax
import jax.numpy as jnp
import numpy as np
from jax import lax
from jax.experimental import pallas as pl
from jax.experimental.pallas import tpu as pltpu
from jax.sharding import PartitionSpec as P

BLOCK = 128
HALO = 4

half_step = 0.025
time_step = 0.05
chain_freq = 12.0
thermal = 0.375
centroid_friction = 1.0
screening = 4.0
softening = 0.09
CHARGES = (1.0, -1.0, 0.6, -1.4)
MASSES = (1.0, 2.0, 3.0, 4.0)

PAIR_ROWS = 25
PAIR_PAD = 32
QUAD = 4
SUM_ROWS = 16
f32 = jnp.float32
bf16 = jnp.bfloat16


def mode_constants(bead_total):
    j = np.arange(bead_total)[:, None]
    k = np.arange(bead_total)[None, :]
    half = bead_total // 2
    phase = 2.0 * np.pi * ((j * k) % bead_total) / bead_total
    plain = 1.0 / math.sqrt(bead_total)
    paired = math.sqrt(2.0 / bead_total)
    matrix = np.where(
        k == 0,
        plain,
        np.where(
            k < half,
            paired * np.cos(phase),
            np.where(k == half, plain * np.cos(phase), paired * np.sin(phase)),
        ),
    )
    modes = np.arange(bead_total)
    frequency = 2.0 * chain_freq * np.sin(np.pi * modes / bead_total)
    angle = frequency * time_step
    ratio = np.where(modes == 0, time_step, np.sin(angle) / np.where(modes == 0, 1.0, frequency))
    friction = np.where(modes == 0, centroid_friction, 2.0 * frequency)
    damping = np.exp(-friction * time_step)
    kick = np.sqrt(1.0 - damping * damping)
    tables = np.stack([np.cos(angle), ratio, frequency * np.sin(angle), damping, kick])
    tables = np.broadcast_to(tables[:, :, None], tables.shape + (BLOCK,))
    return matrix.astype(np.float32), np.ascontiguousarray(tables).astype(np.float32)


def split3(v):
    one = v.astype(bf16).astype(f32)
    rest = v - one
    two = rest.astype(bf16).astype(f32)
    three = (rest - two).astype(bf16).astype(f32)
    return one, two, three


def force_kernel(
    hops, beads, blocks, listed, last, kicks, moment_base, noise_base,
    index_ref, delta_ref, *refs,
):
    parts = 2 * hops + 1
    x_refs = refs[:parts]
    q_refs = refs[parts:2 * parts]
    rest = refs[2 * parts:]
    if last:
        p_ref, pout_ref = rest[:2]
        scratch = rest[2:]
    else:
        p_ref, noise_ref, mass_ref, matrix_ref, matrix_t_ref, table_ref, xout_ref, pout_ref = rest[:8]
        scratch = rest[8:]
    coord_ref, rows_ref, sums_ref, far_ref, weigh_ref, side_ref, near_ref, total_ref, shift_ref, force_ref = scratch
    groups = x_refs[0].shape[0]
    local = beads // groups
    width = blocks * BLOCK
    quads = beads // QUAD

    def unpack(source, base, target, offset):
        for c in range(3):
            for block in range(blocks):
                row = ((base + c) * blocks + block) * local
                lane = offset + block * BLOCK
                for group in range(groups):
                    target[c, group * local:(group + 1) * local, lane:lane + BLOCK] = source[group, row:row + local, :]

    def pack(value, c, target):
        for block in range(blocks):
            row = (c * blocks + block) * local
            for group in range(groups):
                target[group, row:row + local, :] = value[
                    group * local:(group + 1) * local, block * BLOCK:(block + 1) * BLOCK
                ]

    for part in range(parts):
        unpack(x_refs[part], 0, coord_ref, part * width)

    nothing = jnp.zeros((beads, BLOCK), f32)
    one_row = jnp.ones((beads, BLOCK), f32)
    for k in range(PAIR_ROWS, PAIR_PAD):
        rows_ref[k * beads:(k + 1) * beads, :] = nothing
    for k in range(12, SUM_ROWS):
        sums_ref[k * beads:(k + 1) * beads, :] = nothing
    for k in range(12, 15):
        near_ref[k * beads:(k + 1) * beads, :] = one_row
        rows_ref[(k + 10) * beads:(k + 11) * beads, :] = one_row
    rows_ref[15 * beads:16 * beads, :] = nothing
    near_ref[15 * beads:16 * beads, :] = nothing
    for m in range(listed):
        for k in range(9, 16):
            side_ref[m, k * beads:(k + 1) * beads, :] = nothing

    for part in range(parts):
        def one_table(block, carry, part=part):
            lanes = pl.ds(pl.multiple_of(part * width + block * BLOCK, BLOCK), BLOCK)
            q_lanes = pl.ds(pl.multiple_of(block * BLOCK, BLOCK), BLOCK)
            coords = [coord_ref[c, :, lanes] - 1.0 for c in range(3)]
            charge = jnp.broadcast_to(q_refs[part][:, q_lanes], coords[0].shape)
            norm = coords[0] * coords[0] + coords[1] * coords[1] + coords[2] * coords[2]
            rows = []
            for c in (1, 2):
                one, two, three = split3(coords[c])
                rows += [one, two, one, two, three, one]
            one, two, three = split3(norm)
            rows += [None, None, None, None]
            low = split3(coords[0])
            rows += [low[0], low[1], low[0], low[1], low[2], low[0]]
            for k, row in enumerate(rows):
                if row is not None:
                    rows_ref[k * beads:(k + 1) * beads, :] = row
            for k, row in zip(range(12, 15), (one, two, three)):
                rows_ref[k * beads:(k + 1) * beads, :] = row
            charged = [split3(v) for v in [charge] + [charge * coords[c] for c in range(3)]]
            for level in range(3):
                for c in range(4):
                    k = level * 4 + c
                    sums_ref[k * beads:(k + 1) * beads, :] = charged[c][level]
            at = part * blocks + block
            for quad in range(quads):
                four = jnp.concatenate(
                    [rows_ref[pl.ds(QUAD * quad + i, PAIR_PAD, stride=beads), :] for i in range(QUAD)], axis=0
                )
                far_ref[at, quad] = jnp.transpose(four).astype(bf16)
                weigh_ref[at, quad] = jnp.concatenate(
                    [sums_ref[pl.ds(QUAD * quad + i, SUM_ROWS, stride=beads), :] for i in range(QUAD)], axis=0
                ).astype(bf16)
            return carry

        lax.fori_loop(0, blocks, one_table, 0)

    half = PAIR_PAD // 2
    blank = jnp.zeros((PAIR_PAD, BLOCK), f32)

    def one_block(block, carry):
        start = pl.multiple_of(block * BLOCK, BLOCK)
        lanes = pl.ds(start, BLOCK)
        coords = [coord_ref[c, :, pl.ds(hops * width + start, BLOCK)] - 1.0 for c in range(3)]
        across = coords[1] * coords[1] + coords[2] * coords[2] + softening
        rows = []
        for c in (1, 2):
            a, b, d = [-2.0 * v for v in split3(coords[c])]
            rows += [a, a, b, b, a, d]
        for k, row in enumerate(rows):
            near_ref[k * beads:(k + 1) * beads, :] = row
        for m in range(listed):
            moved = coords[0] + delta_ref[block * listed + m]
            a, b, d = [-2.0 * v for v in split3(moved)]
            rows = [a, a, b, b, a, d] + list(split3(moved * moved + across))
            for k, row in enumerate(rows):
                side_ref[m, k * beads:(k + 1) * beads, :] = row

        def one_quad(quad, inner):
            zero = jnp.zeros((2 * SUM_ROWS, 2 * BLOCK), f32)
            total = [zero] * (QUAD // 2)
            shift = [zero] * (QUAD // 2)
            fixed = [near_ref[pl.ds(QUAD * quad + i, half, stride=beads), :] for i in range(QUAD)]
            for m in range(listed):
                at = index_ref[block * listed + m]
                moved = delta_ref[block * listed + m]
                far = far_ref[at, quad]
                heavy = weigh_ref[at, quad]
                for pair in range(QUAD // 2):
                    columns = []
                    for i in range(2 * pair, 2 * pair + 2):
                        own = jnp.concatenate(
                            [fixed[i], side_ref[m, pl.ds(QUAD * quad + i, half, stride=beads), :]], axis=0
                        )
                        columns.append(
                            jnp.concatenate([own if k == i else blank for k in range(QUAD)], axis=0)
                        )
                    near = jnp.concatenate(columns, axis=1).astype(bf16)
                    square = jnp.dot(far, near, preferred_element_type=f32)
                    inverse = lax.rsqrt(square)
                    decay = jnp.exp2(square * inverse * (-1.0 / (screening * math.log(2.0))))
                    weight = decay * ((inverse * inverse) * (inverse + 1.0 / screening))
                    high = weight.astype(bf16)
                    low = (weight - high.astype(f32)).astype(bf16)
                    load = heavy[2 * pair * SUM_ROWS:2 * (pair + 1) * SUM_ROWS]
                    summed = jnp.dot(
                        jnp.concatenate([load, load], axis=1),
                        jnp.concatenate([high, low], axis=0),
                        preferred_element_type=f32,
                    )
                    total[pair] = total[pair] + summed
                    shift[pair] = shift[pair] + moved * summed
            for i in range(QUAD):
                cols = slice(i % 2 * BLOCK, (i % 2 + 1) * BLOCK)
                row = i % 2 * SUM_ROWS
                spot = pl.ds(pl.multiple_of((QUAD * quad + i) * 8, 8), 8)
                for target, value in ((total_ref, total[i // 2]), (shift_ref, shift[i // 2])):
                    target[spot, :] = value[row:row + 8, cols] + value[row + 8:row + 16, cols]
            return inner

        lax.fori_loop(0, quads, one_quad, 0)

        def gathered(ref, c):
            return ref[pl.ds(c, beads, stride=8), :] + ref[pl.ds(c + 4, beads, stride=8), :]

        charge = jnp.broadcast_to(q_refs[hops][:, lanes], across.shape)
        near = gathered(total_ref, 0)
        for c in range(3):
            pull = coords[c] * near - gathered(total_ref, c + 1)
            if c == 0:
                pull = pull + gathered(shift_ref, 0)
            force_ref[c, :, lanes] = charge * pull
        return carry

    lax.fori_loop(0, blocks, one_block, 0)

    scale = kicks * half_step
    unpack(p_ref, moment_base, coord_ref, 0)
    moments = [coord_ref[c, :, 0:width] + scale * force_ref[c] for c in range(3)]
    if last:
        for c in range(3):
            pack(moments[c], c, pout_ref)
        return

    own_coords = [coord_ref[c, :, hops * width:(hops + 1) * width] for c in range(3)]
    unpack(noise_ref, noise_base, coord_ref, (parts - 1) * width)
    cosine, ratio, stiffness, damping, kick = [
        jnp.concatenate([table_ref[i]] * blocks, axis=1) for i in range(5)
    ]
    mass = jnp.broadcast_to(mass_ref[...], (beads, width))
    spread = kick * jnp.sqrt(thermal * mass)
    drift = ratio / mass
    stiff = stiffness * mass
    multiply = functools.partial(jnp.dot, precision=lax.Precision.HIGHEST, preferred_element_type=f32)
    for c in range(3):
        noise = coord_ref[c, :, (parts - 1) * width:parts * width]
        mode_x = multiply(matrix_t_ref[...], own_coords[c])
        mode_p = damping * multiply(matrix_t_ref[...], moments[c]) + spread * noise
        pack(multiply(matrix_ref[...], cosine * mode_x + drift * mode_p), c, xout_ref)
        pack(multiply(matrix_ref[...], cosine * mode_p - stiff * mode_x), c, pout_ref)


def run_forces(
    window_x, window_q, index, delta, moment, kicks, last=False, moment_base=0, noise_base=0, extra=(),
):
    hops = len(window_x) // 2
    groups = window_x[hops].shape[0]
    blocks = window_q[hops].shape[1] // BLOCK
    beads = groups * window_x[hops].shape[1] // (3 * blocks)
    atoms = blocks * BLOCK
    listed = index.shape[0] // blocks
    parts = 2 * hops + 1
    quads = beads // QUAD
    shape = jax.ShapeDtypeStruct(window_x[hops].shape, f32)
    vmem = pl.BlockSpec(memory_space=pltpu.VMEM)
    smem = pl.BlockSpec(memory_space=pltpu.SMEM)
    work = beads * blocks * listed * BLOCK * BLOCK
    return pl.pallas_call(
        functools.partial(
            force_kernel, hops, beads, blocks, listed, last, kicks, moment_base, noise_base
        ),
        out_shape=shape if last else (shape, shape),
        in_specs=[smem, smem] + [vmem] * (2 * parts + 1 + len(extra)),
        out_specs=vmem if last else (vmem, vmem),
        scratch_shapes=[
            pltpu.VMEM((3, beads, parts * atoms), f32),
            pltpu.VMEM((PAIR_PAD * beads, BLOCK), f32),
            pltpu.VMEM((SUM_ROWS * beads, BLOCK), f32),
            pltpu.VMEM((parts * blocks, quads, BLOCK, QUAD * PAIR_PAD), bf16),
            pltpu.VMEM((parts * blocks, quads, QUAD * SUM_ROWS, BLOCK), bf16),
            pltpu.VMEM((listed, PAIR_PAD // 2 * beads, BLOCK), f32),
            pltpu.VMEM((PAIR_PAD // 2 * beads, BLOCK), f32),
            pltpu.VMEM((8 * beads, BLOCK), f32),
            pltpu.VMEM((8 * beads, BLOCK), f32),
            pltpu.VMEM((3, beads, atoms), f32),
        ],
        compiler_params=pltpu.CompilerParams(vmem_limit_bytes=40 * 1024 * 1024),
        cost_estimate=pl.CostEstimate(flops=20 * work, bytes_accessed=4 * 1024 * 1024, transcendentals=2 * work),
    )(index, delta, *window_x, *window_q, moment, *extra)


def fold(count):
    return [i // 2 if i % 2 == 0 else count - 1 - i // 2 for i in range(count)]


def exchange(pieces):
    order = fold(pieces.shape[0])
    group = [order.index(at) for at in range(len(order))]
    return lax.all_to_all(pieces, "bead", split_axis=0, concat_axis=0, axis_index_groups=[group], tiled=True)


def to_atoms(values):
    count = lax.axis_size("bead")
    lead, local, atoms = values.shape
    blocks = atoms // (count * BLOCK)
    pieces = values.reshape(lead, local, count, blocks, BLOCK).transpose(2, 0, 3, 1, 4)
    return exchange(pieces.reshape(count, lead * blocks * local, BLOCK))


def to_beads(pieces, blocks):
    count, rows, _ = pieces.shape
    local = rows // (3 * blocks)
    pieces = exchange(pieces).reshape(count, 3, blocks, local, BLOCK)
    return pieces.transpose(1, 3, 0, 2, 4).reshape(3, local, count * blocks * BLOCK)


def window(values, hops):
    count = lax.axis_size("bead")
    domains = lax.axis_size("space")
    order = fold(count)
    device = {}
    for bead in range(count):
        for domain in range(domains):
            device[domain * count + order[bead]] = bead * domains + domain
    total = count * domains
    out = []
    for hop in range(-hops, hops + 1):
        if hop == 0:
            out.append(values)
        else:
            route = [(device[at + hop], device[at]) for at in range(total) if 0 <= at + hop < total]
            out.append(lax.ppermute(values, ("bead", "space"), route))
    return out


def body(positions, momenta, atom_types, neighbours, thermal_noise):
    count = lax.axis_size("bead")
    local = positions.shape[1]
    beads = local * count
    atoms = positions.shape[2]
    share = atoms // count
    blocks = share // BLOCK
    hops = -(-HALO // blocks)
    steps = thermal_noise.shape[0]
    order = fold(count)

    place = jnp.asarray(np.array(order, np.int32))[lax.axis_index("bead")]
    types = lax.dynamic_slice_in_dim(atom_types, place * share, share)[None, :]
    charge = jnp.zeros(types.shape, f32)
    mass = jnp.zeros(types.shape, f32)
    for kind in range(4):
        charge = jnp.where(types == kind, CHARGES[kind], charge)
        mass = jnp.where(types == kind, MASSES[kind], mass)
    first = lax.axis_index("space") * (atoms // BLOCK) + place * blocks
    lists = lax.dynamic_slice_in_dim(neighbours, place * blocks, blocks)
    own = first + jnp.arange(blocks, dtype=jnp.int32)
    delta = (own[:, None] - lists).astype(f32).reshape(-1)
    index = jnp.clip(lists - first + hops * blocks, 0, (2 * hops + 1) * blocks - 1).reshape(-1)

    matrix, tables = mode_constants(beads)
    at = np.concatenate([order.index(g) * local + np.arange(local) for g in range(count)])
    matrix = matrix[at][:, at]
    fixed = (jnp.asarray(matrix), jnp.asarray(np.ascontiguousarray(matrix.T)), jnp.asarray(tables[:, at]))

    window_q = window(charge, hops)
    coords = to_atoms(positions)
    moment = rest = to_atoms(jnp.concatenate([momenta, thermal_noise.reshape(3 * steps, local, atoms)], axis=0))
    for step in range(steps):
        coords, moment = run_forces(
            window(coords, hops), window_q, index, delta, moment, 1.0 if step == 0 else 2.0,
            noise_base=3 * step + 3, extra=(rest, mass) + fixed,
        )
    moment = run_forces(window(coords, hops), window_q, index, delta, moment, 1.0, last=True)
    return to_beads(coords, blocks), to_beads(moment, blocks)


def solution(mesh):
    placed = (
        P(None, "bead", "space"),
        P(None, "bead", "space"),
        P("space"),
        P("space", None),
        P(None, None, "bead", "space"),
    )
    return jax.shard_map(
        body,
        mesh=mesh,
        in_specs=placed,
        out_specs=(P(None, "bead", "space"), P(None, "bead", "space")),
        check_vma=False,
    )
```

```python
import functools
import math

import jax
import jax.numpy as jnp
import numpy as np
from jax import lax
from jax.experimental import pallas as pl
from jax.experimental.pallas import tpu as pltpu
from jax.sharding import PartitionSpec as P

BLOCK = 128
HALO = 4

half_step = 0.025
time_step = 0.05
chain_freq = 12.0
thermal = 0.375
centroid_friction = 1.0
screening = 4.0
softening = 0.09
CHARGES = (1.0, -1.0, 0.6, -1.4)
MASSES = (1.0, 2.0, 3.0, 4.0)

PAIR_ROWS = 24
PAIR_PAD = 32
SUM_ROWS = 16
QUAD = 4
FRAME = 8
f32 = jnp.float32
bf16 = jnp.bfloat16


def mode_constants(bead_total):
    j = np.arange(bead_total)[:, None]
    k = np.arange(bead_total)[None, :]
    half = bead_total // 2
    phase = 2.0 * np.pi * ((j * k) % bead_total) / bead_total
    plain = 1.0 / math.sqrt(bead_total)
    paired = math.sqrt(2.0 / bead_total)
    matrix = np.where(
        k == 0,
        plain,
        np.where(
            k < half,
            paired * np.cos(phase),
            np.where(k == half, plain * np.cos(phase), paired * np.sin(phase)),
        ),
    )
    modes = np.arange(bead_total)
    frequency = 2.0 * chain_freq * np.sin(np.pi * modes / bead_total)
    angle = frequency * time_step
    ratio = np.where(modes == 0, time_step, np.sin(angle) / np.where(modes == 0, 1.0, frequency))
    friction = np.where(modes == 0, centroid_friction, 2.0 * frequency)
    damping = np.exp(-friction * time_step)
    kick = np.sqrt(1.0 - damping * damping)
    tables = np.stack([np.cos(angle), ratio, frequency * np.sin(angle), damping, kick])
    tables = np.broadcast_to(tables[:, :, None], tables.shape + (BLOCK,))
    return matrix.astype(np.float32), np.ascontiguousarray(tables).astype(np.float32)


def split3(v):
    one = v.astype(bf16).astype(f32)
    rest = v - one
    two = rest.astype(bf16).astype(f32)
    three = (rest - two).astype(bf16).astype(f32)
    return one, two, three


def pair_rows(coords, norm, own):
    rows = []
    for v in coords:
        one, two, three = split3(v)
        if own:
            one, two, three = -2.0 * one, -2.0 * two, -2.0 * three
            rows += [one, one, two, two, one, three]
        else:
            rows += [one, two, one, two, three, one]
    ones = [jnp.ones_like(norm)] * 3
    norms = list(split3(norm))
    return rows + (norms + ones if own else ones + norms)


def add_forces(beads, blocks, margin, listed, offset_ref, charge_ref, coord_ref, scratch):
    rows_ref, sums_ref, far_ref, weigh_ref, own_ref, total_ref, force_ref = scratch
    frame = min(FRAME, blocks)
    width = frame + 2 * margin
    quad = min(QUAD, beads)
    middle = margin + (frame - 1) / 2.0

    def put(ref, k, value):
        ref[k * beads:(k + 1) * beads, :] = value

    def centred(block, place):
        lanes = pl.ds(pl.multiple_of(block * BLOCK, BLOCK), BLOCK)
        coords = [coord_ref[c, :, lanes] - 1.0 for c in range(3)]
        coords[0] = coords[0] + (place.astype(f32) - middle)
        norm = coords[0] * coords[0] + coords[1] * coords[1] + coords[2] * coords[2]
        return coords, norm, jnp.broadcast_to(charge_ref[:, lanes], norm.shape)

    nothing = jnp.zeros((beads, BLOCK), f32)
    for k in range(PAIR_ROWS, PAIR_PAD):
        put(rows_ref, k, nothing)
    for k in range(12, SUM_ROWS):
        put(sums_ref, k, nothing)

    def one_frame(at_frame, carry):
        first = at_frame * frame

        def one_table(place, inner):
            coords, norm, charge = centred(first + place, place)
            for k, row in enumerate(pair_rows(coords, norm, False)):
                put(rows_ref, k, row)
            for c, v in enumerate([charge] + [charge * x for x in coords]):
                for level, part in enumerate(split3(v)):
                    put(sums_ref, level * 4 + c, part)
            for bead in range(beads):
                far_ref[place, bead] = rows_ref[pl.ds(bead, PAIR_PAD, stride=beads), :].astype(bf16)
                weigh_ref[place, bead] = sums_ref[pl.ds(bead, SUM_ROWS, stride=beads), :].astype(bf16)
            return inner

        lax.fori_loop(0, width, one_table, 0)

        def one_block(block, inner):
            place = block + margin
            coords, norm, charge = centred(first + place, place)
            for k, row in enumerate(pair_rows(coords, norm + softening, True)):
                put(rows_ref, k, row)
            for bead in range(beads):
                own_ref[bead] = jnp.transpose(rows_ref[pl.ds(bead, PAIR_PAD, stride=beads), :]).astype(bf16)
            ats = [place + offset_ref[(first + block) * listed + m] for m in range(listed)]

            def one_quad(at_quad, last):
                for i in range(quad):
                    bead = at_quad * quad + i
                    own = own_ref[bead]
                    total = jnp.zeros((BLOCK, SUM_ROWS), f32)
                    for low in range(0, listed, 2):
                        chosen = ats[low:low + 2]
                        far = jnp.concatenate([far_ref[at, bead] for at in chosen], axis=1)
                        square = jnp.dot(own, far, preferred_element_type=f32)
                        inverse = lax.rsqrt(square)
                        decay = jnp.exp2(square * inverse * (-1.0 / (screening * math.log(2.0))))
                        weight = decay * ((inverse * inverse) * (inverse + 1.0 / screening))
                        high = weight.astype(bf16)
                        rest = (weight - high.astype(f32)).astype(bf16)
                        heavy = jnp.concatenate([weigh_ref[at, bead] for at in chosen] * 2, axis=1)
                        total = total + lax.dot_general(
                            jnp.concatenate([high, rest], axis=1), heavy,
                            (((1,), (1,)), ((), ())), preferred_element_type=f32,
                        )
                    spot = pl.ds(pl.multiple_of(bead * SUM_ROWS, SUM_ROWS), SUM_ROWS)
                    total_ref[spot, :] = jnp.transpose(total)
                return last

            lax.fori_loop(0, beads // quad, one_quad, 0)

            def summed(c):
                return (
                    total_ref[pl.ds(c, beads, stride=SUM_ROWS), :]
                    + total_ref[pl.ds(c + 4, beads, stride=SUM_ROWS), :]
                    + total_ref[pl.ds(c + 8, beads, stride=SUM_ROWS), :]
                )

            near = summed(0)
            lanes = pl.ds(pl.multiple_of((first + block) * BLOCK, BLOCK), BLOCK)
            for c in range(3):
                force_ref[c, :, lanes] = charge * (coords[c] * near - summed(c + 1))
            return inner

        lax.fori_loop(0, frame, one_block, 0)
        return carry

    lax.fori_loop(0, blocks // frame, one_frame, 0)


def force_scratch(beads, blocks, margin):
    frame = min(FRAME, blocks)
    width = frame + 2 * margin
    return [
        pltpu.VMEM((3, beads, (blocks + 2 * margin) * BLOCK), f32),
        pltpu.VMEM((PAIR_PAD * beads, BLOCK), f32),
        pltpu.VMEM((SUM_ROWS * beads, BLOCK), f32),
        pltpu.VMEM((width, beads, PAIR_PAD, BLOCK), bf16),
        pltpu.VMEM((width, beads, SUM_ROWS, BLOCK), bf16),
        pltpu.VMEM((beads, BLOCK, PAIR_PAD), bf16),
        pltpu.VMEM((SUM_ROWS * beads, BLOCK), f32),
        pltpu.VMEM((3, beads, blocks * BLOCK), f32),
    ]


def call(kernel, args, smem_count, shapes, scratch, work):
    vmem = pl.BlockSpec(memory_space=pltpu.VMEM)
    smem = pl.BlockSpec(memory_space=pltpu.SMEM)
    return pl.pallas_call(
        kernel,
        out_shape=[jax.ShapeDtypeStruct(shape, f32) for shape in shapes],
        in_specs=[smem] * smem_count + [vmem] * (len(args) - smem_count),
        out_specs=[vmem] * len(shapes),
        scratch_shapes=scratch,
        compiler_params=pltpu.CompilerParams(vmem_limit_bytes=40 * 1024 * 1024),
        cost_estimate=pl.CostEstimate(
            flops=20 * work + 1024, bytes_accessed=4 * 1024 * 1024, transcendentals=2 * work
        ),
    )(*args)


def row_of(c, block, blocks, local):
    return (c * blocks + block) * local


def unpack_beads(source, base, blocks, local, target, offset):
    for c in range(3):
        for block in range(blocks):
            row = row_of(base + c, block, blocks, local)
            lane = offset + block * BLOCK
            for group in range(source.shape[0]):
                target[c, group * local:(group + 1) * local, lane:lane + BLOCK] = source[group, row:row + local, :]


def pack_beads(value, c, blocks, local, target):
    for block in range(blocks):
        row = row_of(c, block, blocks, local)
        for group in range(target.shape[0]):
            target[group, row:row + local, :] = value[
                group * local:(group + 1) * local, block * BLOCK:(block + 1) * BLOCK
            ]


def first_kernel(
    shares, margin, listed, offset_ref, charge_ref, x_ref, left_ref, right_ref, p_ref, pout_ref, coord_ref, *scratch
):
    _, local, atoms = x_ref.shape
    blocks = atoms // BLOCK
    each = blocks // shares
    edge = margin * BLOCK
    for c in range(3):
        coord_ref[c, :, 0:edge] = left_ref[c]
        coord_ref[c, :, edge:edge + atoms] = x_ref[c]
        coord_ref[c, :, edge + atoms:] = right_ref[c]
    add_forces(local, blocks, margin, listed, offset_ref, charge_ref, coord_ref, scratch)
    force_ref = scratch[-1]
    for c in range(3):
        for block in range(blocks):
            lanes = slice(block * BLOCK, (block + 1) * BLOCK)
            row = row_of(c, block % each, each, local)
            pout_ref[block // each, row:row + local, :] = p_ref[c, :, lanes] + half_step * force_ref[c, :, lanes]


def last_kernel(
    margin, listed, offset_ref, charge_ref, both_ref, left_ref, right_ref, xout_ref, pout_ref, coord_ref, *scratch
):
    shares = both_ref.shape[0]
    _, local, atoms = xout_ref.shape
    blocks = atoms // BLOCK
    each = blocks // shares
    edge = margin * BLOCK
    for c in range(3):
        coord_ref[c, :, 0:edge] = left_ref[c]
        coord_ref[c, :, edge + atoms:] = right_ref[c]
        for block in range(blocks):
            lanes = slice(block * BLOCK, (block + 1) * BLOCK)
            row = row_of(c, block % each, each, local)
            value = both_ref[block // each, row:row + local, :]
            coord_ref[c, :, edge + block * BLOCK:edge + (block + 1) * BLOCK] = value
            xout_ref[c, :, lanes] = value
    add_forces(local, blocks, margin, listed, offset_ref, charge_ref, coord_ref, scratch)
    force_ref = scratch[-1]
    for c in range(3):
        for block in range(blocks):
            lanes = slice(block * BLOCK, (block + 1) * BLOCK)
            row = row_of(3 + c, block % each, each, local)
            pout_ref[c, :, lanes] = both_ref[block // each, row:row + local, :] + half_step * force_ref[c, :, lanes]


def thermostat(coords, moments, noises, mass_ref, matrix_ref, matrix_t_ref, table_ref, store):
    beads, width = moments[0].shape
    cosine, ratio, stiffness, damping, kick = [
        jnp.concatenate([table_ref[i]] * (width // BLOCK), axis=1) for i in range(5)
    ]
    mass = jnp.broadcast_to(mass_ref[...], (beads, width))
    spread = kick * jnp.sqrt(thermal * mass)
    drift = ratio / mass
    stiff = stiffness * mass
    multiply = functools.partial(jnp.dot, precision=lax.Precision.HIGHEST, preferred_element_type=f32)
    for c in range(3):
        mode_x = multiply(matrix_t_ref[...], coords[c])
        mode_p = damping * multiply(matrix_t_ref[...], moments[c]) + spread * noises[c]
        store(
            c,
            multiply(matrix_ref[...], cosine * mode_x + drift * mode_p),
            multiply(matrix_ref[...], cosine * mode_p - stiff * mode_x),
        )


def modes_kernel(
    blocks, noise_base, rest_ref, p_ref, mass_ref, matrix_ref, matrix_t_ref, table_ref,
    xout_ref, pout_ref, coord_ref, moment_ref, noise_ref,
):
    local = p_ref.shape[1] // (3 * blocks)
    unpack_beads(rest_ref, 0, blocks, local, coord_ref, 0)
    unpack_beads(p_ref, 0, blocks, local, moment_ref, 0)
    unpack_beads(rest_ref, noise_base, blocks, local, noise_ref, 0)

    def store(c, x, p):
        pack_beads(x, c, blocks, local, xout_ref)
        pack_beads(p, c, blocks, local, pout_ref)

    thermostat(
        *[[ref[c] for c in range(3)] for ref in (coord_ref, moment_ref, noise_ref)],
        mass_ref, matrix_ref, matrix_t_ref, table_ref, store,
    )


def middle_kernel(hops, blocks, listed, noise_base, joined, offset_ref, charge_ref, *refs):
    parts = 2 * hops + 1
    x_refs = refs[:parts]
    p_ref, noise_ref, mass_ref, matrix_ref, matrix_t_ref, table_ref = refs[parts:parts + 6]
    outs = refs[parts + 6:parts + (7 if joined else 8)]
    coord_ref, *scratch = refs[parts + len(outs) + 6:]
    beads = coord_ref.shape[1]
    local = beads // p_ref.shape[0]
    width = blocks * BLOCK
    for part in range(parts):
        unpack_beads(x_refs[part], 0, blocks, local, coord_ref, part * width)
    add_forces(beads, blocks, hops * blocks, listed, offset_ref, charge_ref, coord_ref, scratch)
    force_ref = scratch[-1]
    unpack_beads(p_ref, 0, blocks, local, coord_ref, 0)
    unpack_beads(noise_ref, noise_base, blocks, local, coord_ref, (parts - 1) * width)

    def share(c, part):
        return coord_ref[c, :, part * width:(part + 1) * width]

    def store(c, x, p):
        pack_beads(x, c, blocks, local, outs[0])
        if joined:
            pack_beads(p, 3 + c, blocks, local, outs[0])
        else:
            pack_beads(p, c, blocks, local, outs[1])

    thermostat(
        [share(c, hops) for c in range(3)],
        [share(c, 0) + 2.0 * half_step * force_ref[c] for c in range(3)],
        [share(c, parts - 1) for c in range(3)],
        mass_ref, matrix_ref, matrix_t_ref, table_ref, store,
    )


def fold(count):
    return [i // 2 if i % 2 == 0 else count - 1 - i // 2 for i in range(count)]


def exchange(pieces):
    order = fold(pieces.shape[0])
    group = [order.index(at) for at in range(len(order))]
    return lax.all_to_all(pieces, "bead", split_axis=0, concat_axis=0, axis_index_groups=[group], tiled=True)


def pack_shares(values):
    count = lax.axis_size("bead")
    lead, local, atoms = values.shape
    blocks = atoms // (count * BLOCK)
    pieces = values.reshape(lead, local, count, blocks, BLOCK).transpose(2, 0, 3, 1, 4)
    return pieces.reshape(count, lead * blocks * local, BLOCK)


def beside(head, tail):
    ends = lax.axis_size("space") - 1
    return (
        lax.ppermute(tail, "space", [(i, i + 1) for i in range(ends)]),
        lax.ppermute(head, "space", [(i + 1, i) for i in range(ends)]),
    )


def window(values, hops):
    count = lax.axis_size("bead")
    domains = lax.axis_size("space")
    order = fold(count)
    device = {}
    for bead in range(count):
        for domain in range(domains):
            device[domain * count + order[bead]] = bead * domains + domain
    total = count * domains
    out = []
    for hop in range(-hops, hops + 1):
        if hop == 0:
            out.append(values)
        else:
            route = [(device[at + hop], device[at]) for at in range(total) if 0 <= at + hop < total]
            out.append(lax.ppermute(values, ("bead", "space"), route))
    return out


def body(positions, momenta, atom_types, neighbours, thermal_noise):
    count = lax.axis_size("bead")
    _, local, atoms = positions.shape
    beads = local * count
    domain = atoms // BLOCK
    blocks = domain // count
    share = blocks * BLOCK
    hops = -(-HALO // blocks)
    margin = hops * blocks
    edge = margin * BLOCK
    steps = thermal_noise.shape[0]
    listed = neighbours.shape[1]
    order = fold(count)

    charge = jnp.zeros(atom_types.shape, f32)
    mass = jnp.zeros(atom_types.shape, f32)
    for kind in range(4):
        charge = jnp.where(atom_types == kind, CHARGES[kind], charge)
        mass = jnp.where(atom_types == kind, MASSES[kind], mass)
    own = lax.axis_index("space") * domain + jnp.arange(domain, dtype=jnp.int32)
    offsets = jnp.clip(neighbours - own[:, None], -margin, margin)
    place = jnp.asarray(np.array(order, np.int32))[lax.axis_index("bead")]
    mass = lax.dynamic_slice_in_dim(mass, place * share, share)[None, :]
    near_offsets = lax.dynamic_slice_in_dim(offsets, place * blocks, blocks).reshape(-1)
    offsets = offsets.reshape(-1)

    matrix, tables = mode_constants(beads)
    at = np.concatenate([order.index(g) * local + np.arange(local) for g in range(count)])
    matrix = matrix[at][:, at]
    fixed = (mass, jnp.asarray(matrix), jnp.asarray(np.ascontiguousarray(matrix.T)), jnp.asarray(tables[:, at]))

    charged = jnp.broadcast_to(charge[None, None, :], (1, local, atoms))
    cells = jnp.concatenate([positions, charged], axis=0)
    left, right = beside(cells[:, :, :edge], cells[:, :, atoms - edge:])
    wide_charge = jnp.concatenate([left[3, :1], charge[None, :], right[3, :1]], axis=1)
    near_charge = lax.dynamic_slice_in_dim(wide_charge, place * share, share + 2 * edge, axis=1)
    rest = exchange(
        pack_shares(jnp.concatenate([positions, thermal_noise.reshape(3 * steps, local, atoms)], axis=0))
    )
    packed = (count, 3 * blocks * local, BLOCK)
    pairs = beads * blocks * listed * BLOCK * BLOCK
    (moment,) = call(
        functools.partial(first_kernel, count, margin, listed),
        (offsets, wide_charge, positions, left, right, momenta), 1, [packed],
        force_scratch(local, domain, margin), pairs,
    )
    coords, moment = call(
        functools.partial(modes_kernel, blocks, 3), (rest, exchange(moment)) + fixed, 0, [packed] * 2,
        [pltpu.VMEM((3, beads, share), f32)] * 3, 0,
    )
    for step in range(1, steps):
        joined = step == steps - 1
        out = call(
            functools.partial(middle_kernel, hops, blocks, listed, 3 * step + 3, joined),
            (near_offsets, near_charge) + tuple(window(coords, hops)) + (moment, rest) + fixed, 1,
            [(count, 6 * blocks * local, BLOCK)] if joined else [packed] * 2,
            force_scratch(beads, blocks, margin), pairs,
        )
        if not joined:
            coords, moment = out
    both = exchange(out[0])
    edges = [
        pieces[:, :packed[1]].reshape(hops, 3, blocks, local, BLOCK).transpose(1, 3, 0, 2, 4).reshape(3, local, edge)
        for pieces in (both[:hops], both[count - hops:])
    ]
    left, right = beside(*edges)
    return tuple(call(
        functools.partial(last_kernel, margin, listed), (offsets, wide_charge, both, left, right), 1,
        [(3, local, atoms)] * 2, force_scratch(local, domain, margin), pairs,
    ))


def solution(mesh):
    placed = (
        P(None, "bead", "space"),
        P(None, "bead", "space"),
        P("space"),
        P("space", None),
        P(None, None, "bead", "space"),
    )
    return jax.shard_map(
        body,
        mesh=mesh,
        in_specs=placed,
        out_specs=(P(None, "bead", "space"), P(None, "bead", "space")),
        check_vma=False,
    )
```

```python
import functools
import math

import jax
import jax.numpy as jnp
import numpy as np
from jax import lax
from jax.experimental import pallas as pl
from jax.experimental.pallas import tpu as pltpu
from jax.sharding import PartitionSpec as P

BLOCK = 128
HALO = 4

half_step = 0.025
time_step = 0.05
chain_freq = 12.0
thermal = 0.375
centroid_friction = 1.0
screening = 4.0
softening = 0.09
CHARGES = (1.0, -1.0, 0.6, -1.4)
MASSES = (1.0, 2.0, 3.0, 4.0)

PAIR_ROWS = 24
PAIR_PAD = 32
SUM_ROWS = 16
QUAD = 4
PASS = 32
FRAME = 8
f32 = jnp.float32
bf16 = jnp.bfloat16


def mode_constants(bead_total):
    j = np.arange(bead_total)[:, None]
    k = np.arange(bead_total)[None, :]
    half = bead_total // 2
    phase = 2.0 * np.pi * ((j * k) % bead_total) / bead_total
    plain = 1.0 / math.sqrt(bead_total)
    paired = math.sqrt(2.0 / bead_total)
    matrix = np.where(
        k == 0,
        plain,
        np.where(
            k < half,
            paired * np.cos(phase),
            np.where(k == half, plain * np.cos(phase), paired * np.sin(phase)),
        ),
    )
    modes = np.arange(bead_total)
    frequency = 2.0 * chain_freq * np.sin(np.pi * modes / bead_total)
    angle = frequency * time_step
    ratio = np.where(modes == 0, time_step, np.sin(angle) / np.where(modes == 0, 1.0, frequency))
    friction = np.where(modes == 0, centroid_friction, 2.0 * frequency)
    damping = np.exp(-friction * time_step)
    kick = np.sqrt(1.0 - damping * damping)
    tables = np.stack([np.cos(angle), ratio, frequency * np.sin(angle), damping, kick])
    tables = np.broadcast_to(tables[:, :, None], tables.shape + (BLOCK,))
    return matrix.astype(np.float32), np.ascontiguousarray(tables).astype(np.float32)


def split3(v):
    one = v.astype(bf16).astype(f32)
    rest = v - one
    two = rest.astype(bf16).astype(f32)
    three = (rest - two).astype(bf16).astype(f32)
    return one, two, three


def pair_rows(coords, norm, own):
    rows = []
    for v in coords:
        one, two, three = split3(v)
        if own:
            one, two, three = -2.0 * one, -2.0 * two, -2.0 * three
            rows += [one, one, two, two, one, three]
        else:
            rows += [one, two, one, two, three, one]
    ones = [jnp.ones_like(norm)] * 3
    norms = list(split3(norm))
    return rows + (norms + ones if own else ones + norms)


def whole_quads(beads):
    return -(-beads // QUAD) * QUAD


def add_forces(blocks, margin, listed, offset_ref, charge_ref, coord_ref, scratch):
    rows_ref, sums_ref, far_ref, heavy_ref, near_ref, total_ref, force_ref, *buffers = scratch
    square_refs, weight_refs = buffers[:2], buffers[2:]
    beads = coord_ref.shape[1]
    pairs = beads // 2
    frame = min(FRAME, blocks)
    width = frame + 2 * margin
    middle = margin + (frame - 1) / 2.0
    at_once = max(1, 8 // beads)
    lines = at_once * beads
    units = blocks * pairs

    def put(ref, k, value):
        ref[k * lines:(k + 1) * lines, :] = value

    def centred(block, place):
        spans = [pl.ds(pl.multiple_of((block + i) * BLOCK, BLOCK), BLOCK) for i in range(at_once)]
        coords = [
            jnp.concatenate([coord_ref[c, :, lanes] for lanes in spans], axis=0) - 1.0 for c in range(3)
        ]
        shift = jnp.concatenate(
            [jnp.full((beads, BLOCK), 1.0, f32) * ((place + i).astype(f32) - middle) for i in range(at_once)], axis=0
        )
        coords[0] = coords[0] + shift
        norm = coords[0] * coords[0] + coords[1] * coords[1] + coords[2] * coords[2]
        charge = jnp.concatenate(
            [jnp.broadcast_to(charge_ref[:, lanes], (beads, BLOCK)) for lanes in spans], axis=0
        )
        return coords, norm, charge

    nothing = jnp.zeros((lines, BLOCK), f32)
    for k in range(PAIR_ROWS, PAIR_PAD):
        put(rows_ref, k, nothing)
    for k in range(12, SUM_ROWS):
        put(sums_ref, k, nothing)
    blank = jnp.zeros((PAIR_PAD, BLOCK), f32)

    def one_frame(at_frame, carry):
        first = at_frame * frame

        def one_table(step, inner):
            place = step * at_once
            coords, norm, charge = centred(first + place, place)
            for k, row in enumerate(pair_rows(coords, norm, False)):
                put(rows_ref, k, row)
            for c, v in enumerate([charge] + [charge * x for x in coords]):
                for level, part in enumerate(split3(v)):
                    put(sums_ref, level * 4 + c, part)
            for i in range(at_once):
                at = at_frame * width + place + i
                for quad in range(beads // QUAD):
                    low = i * beads + quad * QUAD
                    four = jnp.concatenate(
                        [rows_ref[pl.ds(low + j, PAIR_PAD, stride=lines), :] for j in range(QUAD)], axis=0
                    )
                    far_ref[at, quad] = jnp.transpose(four).astype(bf16)
                    for half in range(2):
                        heavy_ref[at, 2 * quad + half] = jnp.concatenate(
                            [
                                sums_ref[pl.ds(low + 2 * half + j, SUM_ROWS, stride=lines), :]
                                for j in range(2)
                            ],
                            axis=0,
                        ).astype(bf16)
            return inner

        lax.fori_loop(0, width // at_once, one_table, 0)

        def one_own(step, inner):
            block = step * at_once
            coords, norm, _ = centred(first + margin + block, block + margin)
            for k, row in enumerate(pair_rows(coords, norm + softening, True)):
                put(rows_ref, k, row)
            for i in range(at_once):
                for pair in range(pairs):
                    columns = []
                    for j in range(2):
                        own = rows_ref[pl.ds(i * beads + 2 * pair + j, PAIR_PAD, stride=lines), :]
                        spot = 2 * pair % QUAD + j
                        columns.append(
                            jnp.concatenate([own if k == spot else blank for k in range(QUAD)], axis=0)
                        )
                    near_ref[(first + block + i) * pairs + pair] = jnp.concatenate(columns, axis=1).astype(bf16)
            return inner

        lax.fori_loop(0, frame // at_once, one_own, 0)
        return carry

    lax.fori_loop(0, blocks // frame, one_frame, 0)

    def places(unit):
        block = unit // pairs
        at_frame = block // frame
        base = at_frame * width + block - at_frame * frame + margin
        return [base + offset_ref[block * listed + m] for m in range(listed)], unit - block * pairs

    def squares(unit, out):
        ats, pair = places(unit)
        far = jnp.concatenate([far_ref[at, pair // (QUAD // 2)] for at in ats], axis=0)
        out[...] = jnp.dot(far, near_ref[unit], preferred_element_type=f32)

    def weights(square_ref, out):
        for m in range(listed):
            for low in range(0, BLOCK, PASS):
                square = square_ref[m * BLOCK + low:m * BLOCK + low + PASS, :]
                inverse = lax.rsqrt(square)
                decay = jnp.exp2(square * inverse * (-1.0 / (screening * math.log(2.0))))
                weight = decay * ((inverse * inverse) * (inverse + 1.0 / screening))
                high = weight.astype(bf16)
                row = 2 * m * BLOCK + low
                out[row:row + PASS, :] = high
                out[row + BLOCK:row + BLOCK + PASS, :] = (weight - high.astype(f32)).astype(bf16)

    def sums(unit, weight_ref, slot):
        ats, pair = places(unit)
        tables = [heavy_ref[at, pair] for at in ats]
        total = jnp.dot(
            jnp.concatenate([t for table in tables for t in (table, table)], axis=1),
            weight_ref[...], preferred_element_type=f32,
        )
        for i in range(2):
            cols = slice(i * BLOCK, (i + 1) * BLOCK)
            row = i * SUM_ROWS
            spot = pl.ds(pl.multiple_of((2 * slot + i) * 8, 8), 8)
            total_ref[spot, :] = total[row:row + 8, cols] + total[row + 8:row + 16, cols]

    squares(0, square_refs[0])

    def two_units(step, carry):
        unit = 2 * step
        squares(unit + 1, square_refs[1])
        weights(square_refs[0], weight_refs[0])
        sums(jnp.maximum(unit - 1, 0), weight_refs[1], jnp.where(unit == 0, units, unit - 1))
        squares(jnp.minimum(unit + 2, units - 1), square_refs[0])
        weights(square_refs[1], weight_refs[1])
        sums(unit, weight_refs[0], unit)
        return carry

    lax.fori_loop(0, units // 2, two_units, 0)
    sums(units - 1, weight_refs[1], units - 1)

    def one_block(block, carry):
        at_frame = block // frame
        place = block - at_frame * frame + margin
        lanes = pl.ds(pl.multiple_of((block + margin) * BLOCK, BLOCK), BLOCK)
        coords = [coord_ref[c, :, lanes] - 1.0 for c in range(3)]
        coords[0] = coords[0] + (place.astype(f32) - middle)
        charge = jnp.broadcast_to(charge_ref[:, lanes], coords[0].shape)

        def summed(c):
            return (
                total_ref[pl.ds(block * beads * 8 + c, beads, stride=8), :]
                + total_ref[pl.ds(block * beads * 8 + c + 4, beads, stride=8), :]
            )

        near = summed(0)
        own = pl.ds(pl.multiple_of(block * BLOCK, BLOCK), BLOCK)
        for c in range(3):
            force_ref[c, :, own] = charge * (coords[c] * near - summed(c + 1))
        return carry

    lax.fori_loop(0, blocks, one_block, 0)


def force_scratch(local, blocks, margin, listed):
    beads = whole_quads(local)
    frame = min(FRAME, blocks)
    tables = (frame + 2 * margin) * (blocks // frame)
    lines = max(8, beads)
    units = blocks * beads // 2
    return [
        pltpu.VMEM((3, beads, (blocks + 2 * margin) * BLOCK), f32),
        pltpu.VMEM((PAIR_PAD * lines, BLOCK), f32),
        pltpu.VMEM((SUM_ROWS * lines, BLOCK), f32),
        pltpu.VMEM((tables, beads // QUAD, BLOCK, QUAD * PAIR_PAD), bf16),
        pltpu.VMEM((tables, beads // 2, 2 * SUM_ROWS, BLOCK), bf16),
        pltpu.VMEM((units, QUAD * PAIR_PAD, 2 * BLOCK), bf16),
        pltpu.VMEM(((units + 1) * 16, BLOCK), f32),
        pltpu.VMEM((3, beads, blocks * BLOCK), f32),
        pltpu.VMEM((listed * BLOCK, 2 * BLOCK), f32),
        pltpu.VMEM((listed * BLOCK, 2 * BLOCK), f32),
        pltpu.VMEM((2 * listed * BLOCK, 2 * BLOCK), bf16),
        pltpu.VMEM((2 * listed * BLOCK, 2 * BLOCK), bf16),
    ]


def call(kernel, args, smem_count, shapes, scratch, work):
    vmem = pl.BlockSpec(memory_space=pltpu.VMEM)
    smem = pl.BlockSpec(memory_space=pltpu.SMEM)
    return pl.pallas_call(
        kernel,
        out_shape=[jax.ShapeDtypeStruct(shape, f32) for shape in shapes],
        in_specs=[smem] * smem_count + [vmem] * (len(args) - smem_count),
        out_specs=[vmem] * len(shapes),
        scratch_shapes=scratch,
        compiler_params=pltpu.CompilerParams(vmem_limit_bytes=40 * 1024 * 1024),
        cost_estimate=pl.CostEstimate(
            flops=20 * work + 1024, bytes_accessed=4 * 1024 * 1024, transcendentals=2 * work
        ),
    )(*args)


def row_of(c, block, blocks, local):
    return (c * blocks + block) * local


def unpack_beads(source, base, blocks, local, target, offset):
    for c in range(3):
        for block in range(blocks):
            row = row_of(base + c, block, blocks, local)
            lane = offset + block * BLOCK
            for group in range(source.shape[0]):
                target[c, group * local:(group + 1) * local, lane:lane + BLOCK] = source[group, row:row + local, :]


def pack_beads(value, c, blocks, local, target):
    for block in range(blocks):
        row = row_of(c, block, blocks, local)
        for group in range(target.shape[0]):
            target[group, row:row + local, :] = value[
                group * local:(group + 1) * local, block * BLOCK:(block + 1) * BLOCK
            ]


FORCE = 6


def clear(coord_ref, local):
    if coord_ref.shape[1] != local:
        coord_ref[...] = jnp.zeros(coord_ref.shape, f32)


def first_kernel(
    shares, margin, listed, offset_ref, charge_ref, x_ref, left_ref, right_ref, p_ref, pout_ref, coord_ref, *scratch
):
    _, local, atoms = x_ref.shape
    blocks = atoms // BLOCK
    each = blocks // shares
    edge = margin * BLOCK
    clear(coord_ref, local)
    for c in range(3):
        coord_ref[c, :local, 0:edge] = left_ref[c]
        coord_ref[c, :local, edge:edge + atoms] = x_ref[c]
        coord_ref[c, :local, edge + atoms:] = right_ref[c]
    add_forces(blocks, margin, listed, offset_ref, charge_ref, coord_ref, scratch)
    force_ref = scratch[FORCE]
    for c in range(3):
        for block in range(blocks):
            lanes = slice(block * BLOCK, (block + 1) * BLOCK)
            row = row_of(c, block % each, each, local)
            pout_ref[block // each, row:row + local, :] = p_ref[c, :, lanes] + half_step * force_ref[c, :local, lanes]


def last_kernel(
    margin, listed, offset_ref, charge_ref, both_ref, left_ref, right_ref, xout_ref, pout_ref, coord_ref, *scratch
):
    shares = both_ref.shape[0]
    _, local, atoms = xout_ref.shape
    blocks = atoms // BLOCK
    each = blocks // shares
    edge = margin * BLOCK
    clear(coord_ref, local)
    for c in range(3):
        coord_ref[c, :local, 0:edge] = left_ref[c]
        coord_ref[c, :local, edge + atoms:] = right_ref[c]
        for block in range(blocks):
            lanes = slice(block * BLOCK, (block + 1) * BLOCK)
            row = row_of(c, block % each, each, local)
            value = both_ref[block // each, row:row + local, :]
            coord_ref[c, :local, edge + block * BLOCK:edge + (block + 1) * BLOCK] = value
            xout_ref[c, :, lanes] = value
    add_forces(blocks, margin, listed, offset_ref, charge_ref, coord_ref, scratch)
    force_ref = scratch[FORCE]
    for c in range(3):
        for block in range(blocks):
            lanes = slice(block * BLOCK, (block + 1) * BLOCK)
            row = row_of(3 + c, block % each, each, local)
            pout_ref[c, :, lanes] = both_ref[block // each, row:row + local, :] + half_step * force_ref[c, :local, lanes]


def thermostat(coords, moments, noises, mass_ref, matrix_ref, matrix_t_ref, table_ref, store):
    beads, width = moments[0].shape
    cosine, ratio, stiffness, damping, kick = [
        jnp.concatenate([table_ref[i]] * (width // BLOCK), axis=1) for i in range(5)
    ]
    mass = jnp.broadcast_to(mass_ref[...], (beads, width))
    spread = kick * jnp.sqrt(thermal * mass)
    drift = ratio / mass
    stiff = stiffness * mass
    multiply = functools.partial(jnp.dot, precision=lax.Precision.HIGHEST, preferred_element_type=f32)
    for c in range(3):
        mode_x = multiply(matrix_t_ref[...], coords[c])
        mode_p = damping * multiply(matrix_t_ref[...], moments[c]) + spread * noises[c]
        store(
            c,
            multiply(matrix_ref[...], cosine * mode_x + drift * mode_p),
            multiply(matrix_ref[...], cosine * mode_p - stiff * mode_x),
        )


def modes_kernel(
    blocks, noise_base, rest_ref, p_ref, mass_ref, matrix_ref, matrix_t_ref, table_ref,
    xout_ref, pout_ref, coord_ref, moment_ref, noise_ref,
):
    local = p_ref.shape[1] // (3 * blocks)
    unpack_beads(rest_ref, 0, blocks, local, coord_ref, 0)
    unpack_beads(p_ref, 0, blocks, local, moment_ref, 0)
    unpack_beads(rest_ref, noise_base, blocks, local, noise_ref, 0)

    def store(c, x, p):
        pack_beads(x, c, blocks, local, xout_ref)
        pack_beads(p, c, blocks, local, pout_ref)

    thermostat(
        *[[ref[c] for c in range(3)] for ref in (coord_ref, moment_ref, noise_ref)],
        mass_ref, matrix_ref, matrix_t_ref, table_ref, store,
    )


def middle_kernel(hops, blocks, listed, noise_base, joined, offset_ref, charge_ref, *refs):
    parts = 2 * hops + 1
    x_refs = refs[:parts]
    p_ref, noise_ref, mass_ref, matrix_ref, matrix_t_ref, table_ref = refs[parts:parts + 6]
    outs = refs[parts + 6:parts + (7 if joined else 8)]
    coord_ref, *scratch = refs[parts + len(outs) + 6:]
    beads = coord_ref.shape[1]
    local = beads // p_ref.shape[0]
    width = blocks * BLOCK
    for part in range(parts):
        unpack_beads(x_refs[part], 0, blocks, local, coord_ref, part * width)
    add_forces(blocks, hops * blocks, listed, offset_ref, charge_ref, coord_ref, scratch)
    force_ref = scratch[FORCE]
    unpack_beads(p_ref, 0, blocks, local, coord_ref, 0)
    unpack_beads(noise_ref, noise_base, blocks, local, coord_ref, (parts - 1) * width)

    def share(c, part):
        return coord_ref[c, :, part * width:(part + 1) * width]

    def store(c, x, p):
        pack_beads(x, c, blocks, local, outs[0])
        if joined:
            pack_beads(p, 3 + c, blocks, local, outs[0])
        else:
            pack_beads(p, c, blocks, local, outs[1])

    thermostat(
        [share(c, hops) for c in range(3)],
        [share(c, 0) + 2.0 * half_step * force_ref[c] for c in range(3)],
        [share(c, parts - 1) for c in range(3)],
        mass_ref, matrix_ref, matrix_t_ref, table_ref, store,
    )


def fold(count):
    return [i // 2 if i % 2 == 0 else count - 1 - i // 2 for i in range(count)]


def exchange(pieces):
    order = fold(pieces.shape[0])
    group = [order.index(at) for at in range(len(order))]
    return lax.all_to_all(pieces, "bead", split_axis=0, concat_axis=0, axis_index_groups=[group], tiled=True)


def pack_shares(values):
    count = lax.axis_size("bead")
    lead, local, atoms = values.shape
    blocks = atoms // (count * BLOCK)
    pieces = values.reshape(lead, local, count, blocks, BLOCK).transpose(2, 0, 3, 1, 4)
    return pieces.reshape(count, lead * blocks * local, BLOCK)


def beside(head, tail):
    ends = lax.axis_size("space") - 1
    return (
        lax.ppermute(tail, "space", [(i, i + 1) for i in range(ends)]),
        lax.ppermute(head, "space", [(i + 1, i) for i in range(ends)]),
    )


def window(values, hops):
    count = lax.axis_size("bead")
    domains = lax.axis_size("space")
    order = fold(count)
    device = {}
    for bead in range(count):
        for domain in range(domains):
            device[domain * count + order[bead]] = bead * domains + domain
    total = count * domains
    out = []
    for hop in range(-hops, hops + 1):
        if hop == 0:
            out.append(values)
        else:
            route = [(device[at + hop], device[at]) for at in range(total) if 0 <= at + hop < total]
            out.append(lax.ppermute(values, ("bead", "space"), route))
    return out


def body(positions, momenta, atom_types, neighbours, thermal_noise):
    count = lax.axis_size("bead")
    _, local, atoms = positions.shape
    beads = local * count
    domain = atoms // BLOCK
    blocks = domain // count
    share = blocks * BLOCK
    hops = -(-HALO // blocks)
    margin = hops * blocks
    edge = margin * BLOCK
    steps = thermal_noise.shape[0]
    listed = neighbours.shape[1]
    order = fold(count)

    charge = jnp.zeros(atom_types.shape, f32)
    mass = jnp.zeros(atom_types.shape, f32)
    for kind in range(4):
        charge = jnp.where(atom_types == kind, CHARGES[kind], charge)
        mass = jnp.where(atom_types == kind, MASSES[kind], mass)
    own = lax.axis_index("space") * domain + jnp.arange(domain, dtype=jnp.int32)
    offsets = jnp.clip(neighbours - own[:, None], -margin, margin)
    place = jnp.asarray(np.array(order, np.int32))[lax.axis_index("bead")]
    mass = lax.dynamic_slice_in_dim(mass, place * share, share)[None, :]
    near_offsets = lax.dynamic_slice_in_dim(offsets, place * blocks, blocks).reshape(-1)
    offsets = offsets.reshape(-1)

    matrix, tables = mode_constants(beads)
    at = np.concatenate([order.index(g) * local + np.arange(local) for g in range(count)])
    matrix = matrix[at][:, at]
    fixed = (mass, jnp.asarray(matrix), jnp.asarray(np.ascontiguousarray(matrix.T)), jnp.asarray(tables[:, at]))

    def cells(low, high):
        charged = jnp.broadcast_to(charge[None, None, low:high], (1, local, high - low))
        return jnp.concatenate([positions[:, :, low:high], charged], axis=0)

    left, right = beside(cells(0, edge), cells(atoms - edge, atoms))
    wide_charge = jnp.concatenate([left[3, :1], charge[None, :], right[3, :1]], axis=1)
    near_charge = lax.dynamic_slice_in_dim(wide_charge, place * share, share + 2 * edge, axis=1)
    rest = exchange(
        pack_shares(jnp.concatenate([positions, thermal_noise.reshape(3 * steps, local, atoms)], axis=0))
    )
    packed = (count, 3 * blocks * local, BLOCK)
    pairs = beads * blocks * listed * BLOCK * BLOCK
    (moment,) = call(
        functools.partial(first_kernel, count, margin, listed),
        (offsets, wide_charge, positions, left, right, momenta), 1, [packed],
        force_scratch(local, domain, margin, listed), pairs,
    )
    moment, rest = lax.optimization_barrier((moment, rest))
    coords, moment = call(
        functools.partial(modes_kernel, blocks, 3), (rest, exchange(moment)) + fixed, 0, [packed] * 2,
        [pltpu.VMEM((3, beads, share), f32)] * 3, 0,
    )
    for step in range(1, steps):
        joined = step == steps - 1
        out = call(
            functools.partial(middle_kernel, hops, blocks, listed, 3 * step + 3, joined),
            (near_offsets, near_charge) + tuple(window(coords, hops)) + (moment, rest) + fixed, 1,
            [(count, 6 * blocks * local, BLOCK)] if joined else [packed] * 2,
            force_scratch(beads, blocks, margin, listed), pairs,
        )
        if not joined:
            coords, moment = out
    both = exchange(out[0])
    edges = [
        pieces[:, :packed[1]].reshape(hops, 3, blocks, local, BLOCK).transpose(1, 3, 0, 2, 4).reshape(3, local, edge)
        for pieces in (both[:hops], both[count - hops:])
    ]
    left, right = beside(*edges)
    return tuple(call(
        functools.partial(last_kernel, margin, listed), (offsets, wide_charge, both, left, right), 1,
        [(3, local, atoms)] * 2, force_scratch(local, domain, margin, listed), pairs,
    ))


def solution(mesh):
    placed = (
        P(None, "bead", "space"),
        P(None, "bead", "space"),
        P("space"),
        P("space", None),
        P(None, None, "bead", "space"),
    )
    return jax.shard_map(
        body,
        mesh=mesh,
        in_specs=placed,
        out_specs=(P(None, "bead", "space"), P(None, "bead", "space")),
        check_vma=False,
    )
```

```python
import functools
import math

import jax
import jax.numpy as jnp
import numpy as np
from jax import lax
from jax.experimental import pallas as pl
from jax.experimental.pallas import tpu as pltpu
from jax.sharding import PartitionSpec as P

BLOCK = 128
HALO = 4

half_step = 0.025
time_step = 0.05
chain_freq = 12.0
thermal = 0.375
centroid_friction = 1.0
screening = 4.0
softening = 0.09
CHARGES = (1.0, -1.0, 0.6, -1.4)
MASSES = (1.0, 2.0, 3.0, 4.0)

PAIR_ROWS = 24
PAIR_PAD = 32
SUM_ROWS = 16
QUAD = 4
PASS = 32
FRAME = 8
f32 = jnp.float32
bf16 = jnp.bfloat16


def mode_constants(bead_total):
    j = np.arange(bead_total)[:, None]
    k = np.arange(bead_total)[None, :]
    half = bead_total // 2
    phase = 2.0 * np.pi * ((j * k) % bead_total) / bead_total
    plain = 1.0 / math.sqrt(bead_total)
    paired = math.sqrt(2.0 / bead_total)
    matrix = np.where(
        k == 0,
        plain,
        np.where(
            k < half,
            paired * np.cos(phase),
            np.where(k == half, plain * np.cos(phase), paired * np.sin(phase)),
        ),
    )
    modes = np.arange(bead_total)
    frequency = 2.0 * chain_freq * np.sin(np.pi * modes / bead_total)
    angle = frequency * time_step
    ratio = np.where(modes == 0, time_step, np.sin(angle) / np.where(modes == 0, 1.0, frequency))
    friction = np.where(modes == 0, centroid_friction, 2.0 * frequency)
    damping = np.exp(-friction * time_step)
    kick = np.sqrt(1.0 - damping * damping)
    tables = np.stack([np.cos(angle), ratio, frequency * np.sin(angle), damping, kick])
    tables = np.broadcast_to(tables[:, :, None], tables.shape + (BLOCK,))
    return matrix.astype(np.float32), np.ascontiguousarray(tables).astype(np.float32)


def split3(v):
    one = v.astype(bf16).astype(f32)
    rest = v - one
    two = rest.astype(bf16).astype(f32)
    three = (rest - two).astype(bf16).astype(f32)
    return one, two, three


def pair_rows(coords, norm, own):
    rows = []
    for v in coords:
        one, two, three = split3(v)
        if own:
            one, two, three = -2.0 * one, -2.0 * two, -2.0 * three
            rows += [one, one, two, two, one, three]
        else:
            rows += [one, two, one, two, three, one]
    ones = [jnp.ones_like(norm)] * 3
    norms = list(split3(norm))
    return rows + (norms + ones if own else ones + norms)


def weigh_plain(square):
    inverse = lax.rsqrt(square)
    decay = jnp.exp2(square * inverse * (-1.0 / (screening * math.log(2.0))))
    return decay * ((inverse * inverse) * (inverse + 1.0 / screening))


def weigh_log(square):
    half = lax.log(square) * (-0.5 / math.log(2.0))
    inverse = jnp.exp2(half)
    decay = jnp.exp2((square * inverse * (-1.0 / (screening * math.log(2.0))) + half) + half)
    return decay * (inverse + 1.0 / screening)


def weigh_newton(square):
    coarse = lax.rsqrt(square.astype(bf16)).astype(f32)
    twice = coarse * (3.0 - square * (coarse * coarse))
    decay = jnp.exp2(square * twice * (-0.5 / (screening * math.log(2.0))))
    return decay * ((twice * twice) * (0.125 * twice + 0.25 / screening))


def whole_quads(beads):
    return -(-beads // QUAD) * QUAD


def add_forces(weigh, blocks, margin, listed, offset_ref, charge_ref, coord_ref, scratch):
    rows_ref, sums_ref, far_ref, heavy_ref, near_ref, total_ref, force_ref, *buffers = scratch
    square_refs, weight_refs = buffers[:2], buffers[2:]
    beads = coord_ref.shape[1]
    pairs = beads // 2
    frame = min(FRAME, blocks)
    width = frame + 2 * margin
    middle = margin + (frame - 1) / 2.0
    at_once = max(1, 8 // beads)
    lines = at_once * beads
    units = blocks * pairs

    def put(ref, k, value):
        ref[k * lines:(k + 1) * lines, :] = value

    def centred(block, place):
        spans = [pl.ds(pl.multiple_of((block + i) * BLOCK, BLOCK), BLOCK) for i in range(at_once)]
        coords = [
            jnp.concatenate([coord_ref[c, :, lanes] for lanes in spans], axis=0) - 1.0 for c in range(3)
        ]
        shift = jnp.concatenate(
            [jnp.full((beads, BLOCK), 1.0, f32) * ((place + i).astype(f32) - middle) for i in range(at_once)], axis=0
        )
        coords[0] = coords[0] + shift
        norm = coords[0] * coords[0] + coords[1] * coords[1] + coords[2] * coords[2]
        charge = jnp.concatenate(
            [jnp.broadcast_to(charge_ref[:, lanes], (beads, BLOCK)) for lanes in spans], axis=0
        )
        return coords, norm, charge

    nothing = jnp.zeros((lines, BLOCK), f32)
    for k in range(PAIR_ROWS, PAIR_PAD):
        put(rows_ref, k, nothing)
    for k in range(12, SUM_ROWS):
        put(sums_ref, k, nothing)
    blank = jnp.zeros((PAIR_PAD, BLOCK), f32)

    def one_frame(at_frame, carry):
        first = at_frame * frame

        def one_table(step, inner):
            place = step * at_once
            coords, norm, charge = centred(first + place, place)
            for k, row in enumerate(pair_rows(coords, norm, False)):
                put(rows_ref, k, row)
            for c, v in enumerate([charge] + [charge * x for x in coords]):
                for level, part in enumerate(split3(v)):
                    put(sums_ref, level * 4 + c, part)
            for i in range(at_once):
                at = at_frame * width + place + i
                for quad in range(beads // QUAD):
                    low = i * beads + quad * QUAD
                    four = jnp.concatenate(
                        [rows_ref[pl.ds(low + j, PAIR_PAD, stride=lines), :] for j in range(QUAD)], axis=0
                    )
                    far_ref[at, quad] = jnp.transpose(four).astype(bf16)
                    for half in range(2):
                        heavy_ref[at, 2 * quad + half] = jnp.concatenate(
                            [
                                sums_ref[pl.ds(low + 2 * half + j, SUM_ROWS, stride=lines), :]
                                for j in range(2)
                            ],
                            axis=0,
                        ).astype(bf16)
            return inner

        lax.fori_loop(0, width // at_once, one_table, 0)

        def one_own(step, inner):
            block = step * at_once
            coords, norm, _ = centred(first + margin + block, block + margin)
            for k, row in enumerate(pair_rows(coords, norm + softening, True)):
                put(rows_ref, k, row)
            for i in range(at_once):
                for pair in range(pairs):
                    columns = []
                    for j in range(2):
                        own = rows_ref[pl.ds(i * beads + 2 * pair + j, PAIR_PAD, stride=lines), :]
                        spot = 2 * pair % QUAD + j
                        columns.append(
                            jnp.concatenate([own if k == spot else blank for k in range(QUAD)], axis=0)
                        )
                    near_ref[(first + block + i) * pairs + pair] = jnp.concatenate(columns, axis=1).astype(bf16)
            return inner

        lax.fori_loop(0, frame // at_once, one_own, 0)
        return carry

    lax.fori_loop(0, blocks // frame, one_frame, 0)

    def places(unit):
        block = unit // pairs
        at_frame = block // frame
        base = at_frame * width + block - at_frame * frame + margin
        return [base + offset_ref[block * listed + m] for m in range(listed)], unit - block * pairs

    def squares(unit, out):
        ats, pair = places(unit)
        far = jnp.concatenate([far_ref[at, pair // (QUAD // 2)] for at in ats], axis=0)
        out[...] = jnp.dot(far, near_ref[unit], preferred_element_type=f32)

    def weights(square_ref, out):
        for m in range(listed):
            for low in range(0, BLOCK, PASS):
                weight = weigh(square_ref[m * BLOCK + low:m * BLOCK + low + PASS, :])
                high = weight.astype(bf16)
                row = 2 * m * BLOCK + low
                out[row:row + PASS, :] = high
                out[row + BLOCK:row + BLOCK + PASS, :] = (weight - high.astype(f32)).astype(bf16)

    def sums(unit, weight_ref, slot):
        ats, pair = places(unit)
        tables = [heavy_ref[at, pair] for at in ats]
        total = jnp.dot(
            jnp.concatenate([t for table in tables for t in (table, table)], axis=1),
            weight_ref[...], preferred_element_type=f32,
        )
        for i in range(2):
            cols = slice(i * BLOCK, (i + 1) * BLOCK)
            row = i * SUM_ROWS
            spot = pl.ds(pl.multiple_of((2 * slot + i) * 8, 8), 8)
            total_ref[spot, :] = total[row:row + 8, cols] + total[row + 8:row + 16, cols]

    squares(0, square_refs[0])

    def two_units(step, carry):
        unit = 2 * step
        squares(unit + 1, square_refs[1])
        weights(square_refs[0], weight_refs[0])
        sums(jnp.maximum(unit - 1, 0), weight_refs[1], jnp.where(unit == 0, units, unit - 1))
        squares(jnp.minimum(unit + 2, units - 1), square_refs[0])
        weights(square_refs[1], weight_refs[1])
        sums(unit, weight_refs[0], unit)
        return carry

    lax.fori_loop(0, units // 2, two_units, 0)
    sums(units - 1, weight_refs[1], units - 1)

    def one_block(block, carry):
        at_frame = block // frame
        place = block - at_frame * frame + margin
        lanes = pl.ds(pl.multiple_of((block + margin) * BLOCK, BLOCK), BLOCK)
        coords = [coord_ref[c, :, lanes] - 1.0 for c in range(3)]
        coords[0] = coords[0] + (place.astype(f32) - middle)
        charge = jnp.broadcast_to(charge_ref[:, lanes], coords[0].shape)

        def summed(c):
            return (
                total_ref[pl.ds(block * beads * 8 + c, beads, stride=8), :]
                + total_ref[pl.ds(block * beads * 8 + c + 4, beads, stride=8), :]
            )

        near = summed(0)
        own = pl.ds(pl.multiple_of(block * BLOCK, BLOCK), BLOCK)
        for c in range(3):
            force_ref[c, :, own] = charge * (coords[c] * near - summed(c + 1))
        return carry

    lax.fori_loop(0, blocks, one_block, 0)


def force_scratch(local, blocks, margin, listed):
    beads = whole_quads(local)
    frame = min(FRAME, blocks)
    tables = (frame + 2 * margin) * (blocks // frame)
    lines = max(8, beads)
    units = blocks * beads // 2
    return [
        pltpu.VMEM((3, beads, (blocks + 2 * margin) * BLOCK), f32),
        pltpu.VMEM((PAIR_PAD * lines, BLOCK), f32),
        pltpu.VMEM((SUM_ROWS * lines, BLOCK), f32),
        pltpu.VMEM((tables, beads // QUAD, BLOCK, QUAD * PAIR_PAD), bf16),
        pltpu.VMEM((tables, beads // 2, 2 * SUM_ROWS, BLOCK), bf16),
        pltpu.VMEM((units, QUAD * PAIR_PAD, 2 * BLOCK), bf16),
        pltpu.VMEM(((units + 1) * 16, BLOCK), f32),
        pltpu.VMEM((3, beads, blocks * BLOCK), f32),
        pltpu.VMEM((listed * BLOCK, 2 * BLOCK), f32),
        pltpu.VMEM((listed * BLOCK, 2 * BLOCK), f32),
        pltpu.VMEM((2 * listed * BLOCK, 2 * BLOCK), bf16),
        pltpu.VMEM((2 * listed * BLOCK, 2 * BLOCK), bf16),
    ]


def call(kernel, args, smem_count, shapes, scratch, work):
    vmem = pl.BlockSpec(memory_space=pltpu.VMEM)
    smem = pl.BlockSpec(memory_space=pltpu.SMEM)
    return pl.pallas_call(
        kernel,
        out_shape=[jax.ShapeDtypeStruct(shape, f32) for shape in shapes],
        in_specs=[smem] * smem_count + [vmem] * (len(args) - smem_count),
        out_specs=[vmem] * len(shapes),
        scratch_shapes=scratch,
        compiler_params=pltpu.CompilerParams(vmem_limit_bytes=40 * 1024 * 1024),
        cost_estimate=pl.CostEstimate(
            flops=20 * work + 1024, bytes_accessed=4 * 1024 * 1024, transcendentals=2 * work
        ),
    )(*args)


def row_of(c, block, blocks, local):
    return (c * blocks + block) * local


def unpack_beads(source, base, blocks, local, target, offset):
    for c in range(3):
        for block in range(blocks):
            row = row_of(base + c, block, blocks, local)
            lane = offset + block * BLOCK
            for group in range(source.shape[0]):
                target[c, group * local:(group + 1) * local, lane:lane + BLOCK] = source[group, row:row + local, :]


def pack_beads(value, c, blocks, local, target):
    for block in range(blocks):
        row = row_of(c, block, blocks, local)
        for group in range(target.shape[0]):
            target[group, row:row + local, :] = value[
                group * local:(group + 1) * local, block * BLOCK:(block + 1) * BLOCK
            ]


FORCE = 6


def clear(coord_ref, local):
    if coord_ref.shape[1] != local:
        coord_ref[...] = jnp.zeros(coord_ref.shape, f32)


def first_kernel(
    shares, margin, listed, offset_ref, charge_ref, x_ref, message_ref, p_ref, pout_ref, coord_ref, *scratch
):
    _, local, atoms = x_ref.shape
    blocks = atoms // BLOCK
    each = blocks // shares
    edge = margin * BLOCK
    clear(coord_ref, local)
    for c in range(3):
        coord_ref[c, :local, 0:atoms] = x_ref[c]
        for part in range(2):
            coord_ref[c, :local, atoms + part * edge:atoms + (part + 1) * edge] = message_ref[3 * part + c]
    add_forces(weigh_log, blocks, margin, listed, offset_ref, charge_ref, coord_ref, scratch)
    force_ref = scratch[FORCE]
    for c in range(3):
        for block in range(blocks):
            lanes = slice(block * BLOCK, (block + 1) * BLOCK)
            at = block * BLOCK + edge
            if at < atoms:
                moment = p_ref[c, :, at:at + BLOCK]
            else:
                moment = message_ref[6 + c, :, at - atoms:at - atoms + BLOCK]
            row = row_of(c, block % each, each, local)
            pout_ref[block // each, row:row + local, :] = moment + half_step * force_ref[c, :local, lanes]


def last_kernel(
    margin, listed, offset_ref, charge_ref, both_ref, message_ref, xout_ref, pout_ref, coord_ref, *scratch
):
    shares = both_ref.shape[0]
    _, local, atoms = xout_ref.shape
    blocks = atoms // BLOCK
    each = blocks // shares
    edge = margin * BLOCK

    def taken(c, block):
        row = row_of(c, block % each, each, local)
        return both_ref[block // each, row:row + local, :]

    clear(coord_ref, local)
    for c in range(3):
        for part in range(2):
            coord_ref[c, :local, part * edge:(part + 1) * edge] = message_ref[3 * part + c]
        for block in range(blocks):
            at = 2 * edge + block * BLOCK
            coord_ref[c, :local, at:at + BLOCK] = taken(c, block)
        xout_ref[c] = coord_ref[c, :local, edge:edge + atoms]
    add_forces(weigh_newton, blocks, margin, listed, offset_ref, charge_ref, coord_ref, scratch)
    force_ref = scratch[FORCE]
    for c in range(3):
        for block in range(blocks):
            lanes = slice(block * BLOCK, (block + 1) * BLOCK)
            moment = message_ref[6 + c, :, lanes] if block < margin else taken(3 + c, block - margin)
            pout_ref[c, :, lanes] = moment + half_step * force_ref[c, :local, lanes]


def thermostat(coords, moments, noises, mass_ref, matrix_ref, matrix_t_ref, table_ref, store):
    beads, width = moments[0].shape
    cosine, ratio, stiffness, damping, kick = [
        jnp.concatenate([table_ref[i]] * (width // BLOCK), axis=1) for i in range(5)
    ]
    mass = jnp.broadcast_to(mass_ref[...], (beads, width))
    spread = kick * jnp.sqrt(thermal * mass)
    drift = ratio / mass
    stiff = stiffness * mass
    multiply = functools.partial(jnp.dot, precision=lax.Precision.HIGHEST, preferred_element_type=f32)
    for c in range(3):
        mode_x = multiply(matrix_t_ref[...], coords[c])
        mode_p = damping * multiply(matrix_t_ref[...], moments[c]) + spread * noises[c]
        store(
            c,
            multiply(matrix_ref[...], cosine * mode_x + drift * mode_p),
            multiply(matrix_ref[...], cosine * mode_p - stiff * mode_x),
        )


def modes_kernel(
    blocks, noise_base, rest_ref, p_ref, mass_ref, matrix_ref, matrix_t_ref, table_ref,
    xout_ref, pout_ref, coord_ref, moment_ref, noise_ref,
):
    local = p_ref.shape[1] // (3 * blocks)
    unpack_beads(rest_ref, 0, blocks, local, coord_ref, 0)
    unpack_beads(p_ref, 0, blocks, local, moment_ref, 0)
    unpack_beads(rest_ref, noise_base, blocks, local, noise_ref, 0)

    def store(c, x, p):
        pack_beads(x, c, blocks, local, xout_ref)
        pack_beads(p, c, blocks, local, pout_ref)

    thermostat(
        *[[ref[c] for c in range(3)] for ref in (coord_ref, moment_ref, noise_ref)],
        mass_ref, matrix_ref, matrix_t_ref, table_ref, store,
    )


def middle_kernel(hops, blocks, listed, noise_base, joined, offset_ref, charge_ref, *refs):
    parts = 2 * hops + 1
    x_refs = refs[:parts]
    p_ref, noise_ref, mass_ref, matrix_ref, matrix_t_ref, table_ref = refs[parts:parts + 6]
    outs = refs[parts + 6:parts + (7 if joined else 8)]
    coord_ref, *scratch = refs[parts + len(outs) + 6:]
    beads = coord_ref.shape[1]
    local = beads // p_ref.shape[0]
    width = blocks * BLOCK
    for part in range(parts):
        unpack_beads(x_refs[part], 0, blocks, local, coord_ref, part * width)
    add_forces(weigh_plain, blocks, hops * blocks, listed, offset_ref, charge_ref, coord_ref, scratch)
    force_ref = scratch[FORCE]
    unpack_beads(p_ref, 0, blocks, local, coord_ref, 0)
    unpack_beads(noise_ref, noise_base, blocks, local, coord_ref, (parts - 1) * width)

    def share(c, part):
        return coord_ref[c, :, part * width:(part + 1) * width]

    def store(c, x, p):
        pack_beads(x, c, blocks, local, outs[0])
        if joined:
            pack_beads(p, 3 + c, blocks, local, outs[0])
        else:
            pack_beads(p, c, blocks, local, outs[1])

    thermostat(
        [share(c, hops) for c in range(3)],
        [share(c, 0) + 2.0 * half_step * force_ref[c] for c in range(3)],
        [share(c, parts - 1) for c in range(3)],
        mass_ref, matrix_ref, matrix_t_ref, table_ref, store,
    )


def fold(count):
    return [i // 2 if i % 2 == 0 else count - 1 - i // 2 for i in range(count)]


def exchange(pieces):
    order = fold(pieces.shape[0])
    group = [order.index(at) for at in range(len(order))]
    return lax.all_to_all(pieces, "bead", split_axis=0, concat_axis=0, axis_index_groups=[group], tiled=True)


def pack_shares(values):
    count = lax.axis_size("bead")
    lead, local, atoms = values.shape
    blocks = atoms // (count * BLOCK)
    pieces = values.reshape(lead, local, count, blocks, BLOCK).transpose(2, 0, 3, 1, 4)
    return pieces.reshape(count, lead * blocks * local, BLOCK)


def passed(values, step):
    count = lax.axis_size("space")
    return lax.ppermute(values, "space", [(i, (i + step) % count) for i in range(count)])


def window(values, hops):
    count = lax.axis_size("bead")
    domains = lax.axis_size("space")
    order = fold(count)
    device = {}
    for bead in range(count):
        for domain in range(domains):
            device[domain * count + order[bead]] = bead * domains + domain
    total = count * domains
    out = []
    for hop in range(-hops, hops + 1):
        if hop == 0:
            out.append(values)
        else:
            route = [(device[(at + hop) % total], device[at]) for at in range(total)]
            out.append(lax.ppermute(values, ("bead", "space"), route))
    return out


def body(positions, momenta, atom_types, neighbours, thermal_noise):
    count = lax.axis_size("bead")
    _, local, atoms = positions.shape
    beads = local * count
    domain = atoms // BLOCK
    blocks = domain // count
    share = blocks * BLOCK
    hops = -(-HALO // blocks)
    margin = hops * blocks
    edge = margin * BLOCK
    steps = thermal_noise.shape[0]
    listed = neighbours.shape[1]
    order = fold(count)

    charge = jnp.zeros(atom_types.shape, f32)
    mass = jnp.zeros(atom_types.shape, f32)
    for kind in range(4):
        charge = jnp.where(atom_types == kind, CHARGES[kind], charge)
        mass = jnp.where(atom_types == kind, MASSES[kind], mass)
    own = lax.axis_index("space") * domain + jnp.arange(domain, dtype=jnp.int32)
    offsets = jnp.clip(neighbours - own[:, None], -margin, margin)
    noises = thermal_noise.reshape(3 * steps, local, atoms)

    wide = jnp.stack([
        charge[:edge], charge[edge:2 * edge], mass[:edge],
        jnp.pad(offsets[:margin].astype(f32).reshape(-1), (0, edge - margin * listed)),
    ])
    message = passed(jnp.concatenate([
        positions[:, :, :edge], positions[:, :, edge:2 * edge], momenta[:, :, :edge], noises[:, :, :edge],
        jnp.broadcast_to(wide[:, None, :], (4, local, edge)),
    ], axis=0), -1)
    side = message[9 + 3 * steps:, 0]
    first_charge = jnp.concatenate([charge, side[0], side[1]])[None, :]
    moved_mass = jnp.concatenate([mass[edge:], side[2]])
    moved_offsets = jnp.concatenate([offsets[margin:].reshape(-1), side[3, :margin * listed].astype(jnp.int32)])
    rest = exchange(pack_shares(jnp.concatenate([
        jnp.concatenate([positions, noises], axis=0)[:, :, edge:],
        jnp.concatenate([message[:3], message[9:9 + 3 * steps]], axis=0),
    ], axis=2)))

    place = jnp.asarray(np.array(order, np.int32))[lax.axis_index("bead")]
    near_charge = lax.dynamic_slice_in_dim(first_charge, place * share, share + 2 * edge, axis=1)
    near_mass = lax.dynamic_slice_in_dim(moved_mass, place * share, share)[None, :]
    near_offsets = lax.dynamic_slice_in_dim(moved_offsets, place * blocks * listed, blocks * listed)

    matrix, tables = mode_constants(beads)
    at = np.concatenate([order.index(g) * local + np.arange(local) for g in range(count)])
    matrix = matrix[at][:, at]
    fixed = (near_mass, jnp.asarray(matrix), jnp.asarray(np.ascontiguousarray(matrix.T)), jnp.asarray(tables[:, at]))

    packed = (count, 3 * blocks * local, BLOCK)
    pairs = beads * blocks * listed * BLOCK * BLOCK
    (moment,) = call(
        functools.partial(first_kernel, count, margin, listed),
        (moved_offsets, first_charge, positions, message, momenta), 1, [packed],
        force_scratch(local, domain, margin, listed), pairs,
    )
    moment, rest = lax.optimization_barrier((moment, rest))
    coords, moment = call(
        functools.partial(modes_kernel, blocks, 3), (rest, exchange(moment)) + fixed, 0, [packed] * 2,
        [pltpu.VMEM((3, beads, share), f32)] * 3, 0,
    )
    for step in range(1, steps):
        joined = step == steps - 1
        out = call(
            functools.partial(middle_kernel, hops, blocks, listed, 3 * step + 3, joined),
            (near_offsets, near_charge) + tuple(window(coords, hops)) + (moment, rest) + fixed, 1,
            [(count, 6 * blocks * local, BLOCK)] if joined else [packed] * 2,
            force_scratch(beads, blocks, margin, listed), pairs,
        )
        if not joined:
            coords, moment = out
    both = exchange(out[0])

    def ends(low, c):
        pieces = both[low:low + hops, c * packed[1]:(c + 1) * packed[1]]
        return pieces.reshape(hops, 3, blocks, local, BLOCK).transpose(1, 3, 0, 2, 4).reshape(3, local, edge)

    message = passed(jnp.concatenate([
        ends(count - 2 * hops, 0), ends(count - hops, 0), ends(count - hops, 1),
        jnp.broadcast_to(charge[None, None, atoms - edge:], (1, local, edge)),
    ], axis=0), 1)
    last_charge = jnp.concatenate([message[9, 0], first_charge[0, :atoms + edge]])[None, :]
    return tuple(call(
        functools.partial(last_kernel, margin, listed), (offsets.reshape(-1), last_charge, both, message), 1,
        [(3, local, atoms)] * 2, force_scratch(local, domain, margin, listed), pairs,
    ))


def solution(mesh):
    placed = (
        P(None, "bead", "space"),
        P(None, "bead", "space"),
        P("space"),
        P("space", None),
        P(None, None, "bead", "space"),
    )
    return jax.shard_map(
        body,
        mesh=mesh,
        in_specs=placed,
        out_specs=(P(None, "bead", "space"), P(None, "bead", "space")),
        check_vma=False,
    )
```

```python
import functools
import math

import jax
import jax.numpy as jnp
import numpy as np
from jax import lax
from jax.experimental import pallas as pl
from jax.experimental.pallas import tpu as pltpu
from jax.sharding import PartitionSpec as P

BLOCK = 128
HALO = 4

half_step = 0.025
time_step = 0.05
chain_freq = 12.0
thermal = 0.375
centroid_friction = 1.0
screening = 4.0
softening = 0.09
CHARGES = (1.0, -1.0, 0.6, -1.4)
MASSES = (1.0, 2.0, 3.0, 4.0)

PAIR_ROWS = 24
PAIR_PAD = 32
SUM_ROWS = 16
QUAD = 4
PASS = 32
FRAME = 8
f32 = jnp.float32
bf16 = jnp.bfloat16


def mode_constants(bead_total):
    j = np.arange(bead_total)[:, None]
    k = np.arange(bead_total)[None, :]
    half = bead_total // 2
    phase = 2.0 * np.pi * ((j * k) % bead_total) / bead_total
    plain = 1.0 / math.sqrt(bead_total)
    paired = math.sqrt(2.0 / bead_total)
    matrix = np.where(
        k == 0,
        plain,
        np.where(
            k < half,
            paired * np.cos(phase),
            np.where(k == half, plain * np.cos(phase), paired * np.sin(phase)),
        ),
    )
    modes = np.arange(bead_total)
    frequency = 2.0 * chain_freq * np.sin(np.pi * modes / bead_total)
    angle = frequency * time_step
    ratio = np.where(modes == 0, time_step, np.sin(angle) / np.where(modes == 0, 1.0, frequency))
    friction = np.where(modes == 0, centroid_friction, 2.0 * frequency)
    damping = np.exp(-friction * time_step)
    kick = np.sqrt(1.0 - damping * damping)
    tables = np.stack([np.cos(angle), ratio, frequency * np.sin(angle), damping, kick])
    tables = np.broadcast_to(tables[:, :, None], tables.shape + (BLOCK,))
    return matrix.astype(np.float32), np.ascontiguousarray(tables).astype(np.float32)


def split3(v):
    one = v.astype(bf16).astype(f32)
    rest = v - one
    two = rest.astype(bf16).astype(f32)
    three = (rest - two).astype(bf16).astype(f32)
    return one, two, three


def pair_rows(coords, norm, own):
    rows = []
    for v in coords:
        one, two, three = split3(v)
        if own:
            one, two, three = -2.0 * one, -2.0 * two, -2.0 * three
            rows += [one, one, two, two, one, three]
        else:
            rows += [one, two, one, two, three, one]
    ones = [jnp.ones_like(norm)] * 3
    norms = list(split3(norm))
    return rows + (norms + ones if own else ones + norms)


def weigh(square):
    inverse = lax.rsqrt(square)
    decay = jnp.exp2(square * inverse * (-1.0 / (screening * math.log(2.0))))
    return decay * ((inverse * inverse) * (inverse + 1.0 / screening))


def whole_quads(beads):
    return -(-beads // QUAD) * QUAD


def add_forces(blocks, margin, listed, offset_ref, charge_ref, coord_ref, scratch):
    rows_ref, sums_ref, far_ref, heavy_ref, near_ref, total_ref, force_ref, *buffers = scratch
    square_refs, weight_refs = buffers[:2], buffers[2:]
    beads = coord_ref.shape[1]
    pairs = beads // 2
    frame = min(FRAME, blocks)
    width = frame + 2 * margin
    middle = margin + (frame - 1) / 2.0
    at_once = max(1, 8 // beads)
    lines = at_once * beads
    units = blocks * pairs

    def put(ref, k, value):
        ref[k * lines:(k + 1) * lines, :] = value

    def centred(block, place):
        spans = [pl.ds(pl.multiple_of((block + i) * BLOCK, BLOCK), BLOCK) for i in range(at_once)]
        coords = [
            jnp.concatenate([coord_ref[c, :, lanes] for lanes in spans], axis=0) - 1.0 for c in range(3)
        ]
        shift = jnp.concatenate(
            [jnp.full((beads, BLOCK), 1.0, f32) * ((place + i).astype(f32) - middle) for i in range(at_once)], axis=0
        )
        coords[0] = coords[0] + shift
        norm = coords[0] * coords[0] + coords[1] * coords[1] + coords[2] * coords[2]
        charge = jnp.concatenate(
            [jnp.broadcast_to(charge_ref[:, lanes], (beads, BLOCK)) for lanes in spans], axis=0
        )
        return coords, norm, charge

    nothing = jnp.zeros((lines, BLOCK), f32)
    for k in range(PAIR_ROWS, PAIR_PAD):
        put(rows_ref, k, nothing)
    for k in range(12, SUM_ROWS):
        put(sums_ref, k, nothing)
    blank = jnp.zeros((PAIR_PAD, BLOCK), f32)

    def one_frame(at_frame, carry):
        first = at_frame * frame

        def one_table(step, inner):
            place = step * at_once
            coords, norm, charge = centred(first + place, place)
            for k, row in enumerate(pair_rows(coords, norm, False)):
                put(rows_ref, k, row)
            for c, v in enumerate([charge] + [charge * x for x in coords]):
                for level, part in enumerate(split3(v)):
                    put(sums_ref, level * 4 + c, part)
            for i in range(at_once):
                at = at_frame * width + place + i
                for quad in range(beads // QUAD):
                    low = i * beads + quad * QUAD
                    four = jnp.concatenate(
                        [rows_ref[pl.ds(low + j, PAIR_PAD, stride=lines), :] for j in range(QUAD)], axis=0
                    )
                    far_ref[at, quad] = jnp.transpose(four).astype(bf16)
                    for half in range(2):
                        heavy_ref[at, 2 * quad + half] = jnp.concatenate(
                            [
                                sums_ref[pl.ds(low + 2 * half + j, SUM_ROWS, stride=lines), :]
                                for j in range(2)
                            ],
                            axis=0,
                        ).astype(bf16)
            return inner

        lax.fori_loop(0, width // at_once, one_table, 0)

        def one_own(step, inner):
            block = step * at_once
            coords, norm, _ = centred(first + margin + block, block + margin)
            for k, row in enumerate(pair_rows(coords, norm + softening, True)):
                put(rows_ref, k, row)
            for i in range(at_once):
                for pair in range(pairs):
                    columns = []
                    for j in range(2):
                        own = rows_ref[pl.ds(i * beads + 2 * pair + j, PAIR_PAD, stride=lines), :]
                        spot = 2 * pair % QUAD + j
                        columns.append(
                            jnp.concatenate([own if k == spot else blank for k in range(QUAD)], axis=0)
                        )
                    near_ref[(first + block + i) * pairs + pair] = jnp.concatenate(columns, axis=1).astype(bf16)
            return inner

        lax.fori_loop(0, frame // at_once, one_own, 0)
        return carry

    lax.fori_loop(0, blocks // frame, one_frame, 0)

    def places(unit):
        block = unit // pairs
        at_frame = block // frame
        base = at_frame * width + block - at_frame * frame + margin
        return [base + offset_ref[block * listed + m] for m in range(listed)], unit - block * pairs

    def square(ats, pair, unit, m, out):
        far = far_ref[ats[m], pair // (QUAD // 2)]
        out[m * BLOCK:(m + 1) * BLOCK, :] = jnp.dot(far, near_ref[unit], preferred_element_type=f32)

    def weights(m, square_ref, out):
        for low in range(0, BLOCK, PASS):
            weight = weigh(square_ref[m * BLOCK + low:m * BLOCK + low + PASS, :])
            high = weight.astype(bf16)
            row = 2 * m * BLOCK + low
            out[row:row + PASS, :] = high
            out[row + BLOCK:row + BLOCK + PASS, :] = (weight - high.astype(f32)).astype(bf16)

    def weighted(ats, pair, m, weight_ref):
        table = heavy_ref[ats[m], pair]
        return jnp.dot(
            jnp.concatenate([table, table], axis=1),
            weight_ref[2 * m * BLOCK:2 * (m + 1) * BLOCK, :], preferred_element_type=f32,
        )

    def keep(total, slot):
        for i in range(2):
            cols = slice(i * BLOCK, (i + 1) * BLOCK)
            row = i * SUM_ROWS
            spot = pl.ds(pl.multiple_of((2 * slot + i) * 8, 8), 8)
            total_ref[spot, :] = total[row:row + 8, cols] + total[row + 8:row + 16, cols]

    def one_unit(unit, now, other):
        after = jnp.minimum(unit + 1, units - 1)
        before = jnp.maximum(unit - 1, 0)
        after_ats, after_pair = places(after)
        before_ats, before_pair = places(before)
        total = jnp.zeros((2 * SUM_ROWS, 2 * BLOCK), f32)
        for m in range(listed):
            square(after_ats, after_pair, after, m, square_refs[other])
            weights(m, square_refs[now], weight_refs[now])
            total = total + weighted(before_ats, before_pair, m, weight_refs[other])
        keep(total, jnp.where(unit == 0, units, unit - 1))

    first_ats, first_pair = places(0)
    for m in range(listed):
        square(first_ats, first_pair, 0, m, square_refs[0])

    def two_units(step, carry):
        one_unit(2 * step, 0, 1)
        one_unit(2 * step + 1, 1, 0)
        return carry

    lax.fori_loop(0, units // 2, two_units, 0)
    last_ats, last_pair = places(units - 1)
    keep(sum(weighted(last_ats, last_pair, m, weight_refs[1]) for m in range(listed)), units - 1)

    def one_block(block, carry):
        at_frame = block // frame
        place = block - at_frame * frame + margin
        lanes = pl.ds(pl.multiple_of((block + margin) * BLOCK, BLOCK), BLOCK)
        coords = [coord_ref[c, :, lanes] - 1.0 for c in range(3)]
        coords[0] = coords[0] + (place.astype(f32) - middle)
        charge = jnp.broadcast_to(charge_ref[:, lanes], coords[0].shape)

        def summed(c):
            return (
                total_ref[pl.ds(block * beads * 8 + c, beads, stride=8), :]
                + total_ref[pl.ds(block * beads * 8 + c + 4, beads, stride=8), :]
            )

        near = summed(0)
        own = pl.ds(pl.multiple_of(block * BLOCK, BLOCK), BLOCK)
        for c in range(3):
            force_ref[c, :, own] = charge * (coords[c] * near - summed(c + 1))
        return carry

    lax.fori_loop(0, blocks, one_block, 0)


def force_scratch(local, blocks, margin, listed):
    beads = whole_quads(local)
    frame = min(FRAME, blocks)
    tables = (frame + 2 * margin) * (blocks // frame)
    lines = max(8, beads)
    units = blocks * beads // 2
    return [
        pltpu.VMEM((3, beads, (blocks + 2 * margin) * BLOCK), f32),
        pltpu.VMEM((PAIR_PAD * lines, BLOCK), f32),
        pltpu.VMEM((SUM_ROWS * lines, BLOCK), f32),
        pltpu.VMEM((tables, beads // QUAD, BLOCK, QUAD * PAIR_PAD), bf16),
        pltpu.VMEM((tables, beads // 2, 2 * SUM_ROWS, BLOCK), bf16),
        pltpu.VMEM((units, QUAD * PAIR_PAD, 2 * BLOCK), bf16),
        pltpu.VMEM(((units + 1) * 16, BLOCK), f32),
        pltpu.VMEM((3, beads, blocks * BLOCK), f32),
        pltpu.VMEM((listed * BLOCK, 2 * BLOCK), f32),
        pltpu.VMEM((listed * BLOCK, 2 * BLOCK), f32),
        pltpu.VMEM((2 * listed * BLOCK, 2 * BLOCK), bf16),
        pltpu.VMEM((2 * listed * BLOCK, 2 * BLOCK), bf16),
    ]


def call(kernel, args, smem_count, shapes, scratch, work):
    vmem = pl.BlockSpec(memory_space=pltpu.VMEM)
    smem = pl.BlockSpec(memory_space=pltpu.SMEM)
    return pl.pallas_call(
        kernel,
        out_shape=[jax.ShapeDtypeStruct(shape, f32) for shape in shapes],
        in_specs=[smem] * smem_count + [vmem] * (len(args) - smem_count),
        out_specs=[vmem] * len(shapes),
        scratch_shapes=scratch,
        compiler_params=pltpu.CompilerParams(vmem_limit_bytes=40 * 1024 * 1024),
        cost_estimate=pl.CostEstimate(
            flops=20 * work + 1024, bytes_accessed=4 * 1024 * 1024, transcendentals=2 * work
        ),
    )(*args)


def row_of(c, block, blocks, local):
    return (c * blocks + block) * local


def unpack_beads(source, base, blocks, local, target, offset):
    for c in range(3):
        for block in range(blocks):
            row = row_of(base + c, block, blocks, local)
            lane = offset + block * BLOCK
            for group in range(source.shape[0]):
                target[c, group * local:(group + 1) * local, lane:lane + BLOCK] = source[group, row:row + local, :]


def pack_beads(value, c, blocks, local, target):
    for block in range(blocks):
        row = row_of(c, block, blocks, local)
        for group in range(target.shape[0]):
            target[group, row:row + local, :] = value[
                group * local:(group + 1) * local, block * BLOCK:(block + 1) * BLOCK
            ]


FORCE = 6


def clear(coord_ref, local):
    if coord_ref.shape[1] != local:
        coord_ref[...] = jnp.zeros(coord_ref.shape, f32)


def message_kernel(x_ref, p_ref, noise_ref, types_ref, offsets_ref, message_ref, charge_ref, mass_ref):
    steps = noise_ref.shape[0]
    _, local, edge = message_ref.shape
    types = types_ref[...]
    charge = jnp.zeros(types.shape, f32)
    mass = jnp.zeros(types.shape, f32)
    for kind in range(4):
        charge = jnp.where(types == kind, CHARGES[kind], charge)
        mass = jnp.where(types == kind, MASSES[kind], mass)
    charge_ref[...] = charge
    mass_ref[...] = mass
    for c in range(3):
        message_ref[c] = x_ref[c, :, :edge]
        message_ref[3 + c] = x_ref[c, :, edge:2 * edge]
        message_ref[6 + c] = p_ref[c, :, :edge]
        for step in range(steps):
            message_ref[9 + 3 * step + c] = noise_ref[step, c, :, :edge]
    at = 9 + 3 * steps
    for i, row in enumerate([charge[:, :edge], charge[:, edge:2 * edge], mass[:, :edge], offsets_ref[...]]):
        message_ref[at + i] = jnp.broadcast_to(row, (local, edge))


def pack_kernel(blocks, x_ref, noise_ref, message_ref, out_ref):
    steps = noise_ref.shape[0]
    _, local, edge = message_ref.shape
    atoms = x_ref.shape[2]
    for c in range(3 + 3 * steps):
        for block in range(atoms // BLOCK):
            at = edge + block * BLOCK
            if at >= atoms:
                value = message_ref[c if c < 3 else 6 + c, :, at - atoms:at - atoms + BLOCK]
            elif c < 3:
                value = x_ref[c, :, at:at + BLOCK]
            else:
                value = noise_ref[c // 3 - 1, c % 3, :, at:at + BLOCK]
            row = row_of(c, block % blocks, blocks, local)
            out_ref[block // blocks, row:row + local, :] = value


def first_kernel(
    shares, margin, listed, offset_ref, charge_ref, x_ref, message_ref, p_ref, pout_ref, coord_ref, *scratch
):
    _, local, atoms = x_ref.shape
    blocks = atoms // BLOCK
    each = blocks // shares
    edge = margin * BLOCK
    clear(coord_ref, local)
    for c in range(3):
        coord_ref[c, :local, 0:atoms] = x_ref[c]
        for part in range(2):
            coord_ref[c, :local, atoms + part * edge:atoms + (part + 1) * edge] = message_ref[3 * part + c]
    add_forces(blocks, margin, listed, offset_ref, charge_ref, coord_ref, scratch)
    force_ref = scratch[FORCE]
    for c in range(3):
        for block in range(blocks):
            lanes = slice(block * BLOCK, (block + 1) * BLOCK)
            at = block * BLOCK + edge
            if at < atoms:
                moment = p_ref[c, :, at:at + BLOCK]
            else:
                moment = message_ref[6 + c, :, at - atoms:at - atoms + BLOCK]
            row = row_of(c, block % each, each, local)
            pout_ref[block // each, row:row + local, :] = moment + half_step * force_ref[c, :local, lanes]


def last_kernel(
    margin, listed, offset_ref, charge_ref, both_ref, message_ref, xout_ref, pout_ref, coord_ref, *scratch
):
    shares = both_ref.shape[0]
    _, local, atoms = xout_ref.shape
    blocks = atoms // BLOCK
    each = blocks // shares
    edge = margin * BLOCK

    def taken(c, block):
        row = row_of(c, block % each, each, local)
        return both_ref[block // each, row:row + local, :]

    clear(coord_ref, local)
    for c in range(3):
        for part in range(2):
            coord_ref[c, :local, part * edge:(part + 1) * edge] = message_ref[3 * part + c]
        for block in range(blocks):
            at = 2 * edge + block * BLOCK
            coord_ref[c, :local, at:at + BLOCK] = taken(c, block)
        xout_ref[c] = coord_ref[c, :local, edge:edge + atoms]
    add_forces(blocks, margin, listed, offset_ref, charge_ref, coord_ref, scratch)
    force_ref = scratch[FORCE]
    for c in range(3):
        for block in range(blocks):
            lanes = slice(block * BLOCK, (block + 1) * BLOCK)
            moment = message_ref[6 + c, :, lanes] if block < margin else taken(3 + c, block - margin)
            pout_ref[c, :, lanes] = moment + half_step * force_ref[c, :local, lanes]


def thermostat(coords, moments, noises, mass_ref, matrix_ref, matrix_t_ref, table_ref, store):
    beads, width = moments[0].shape
    cosine, ratio, stiffness, damping, kick = [
        jnp.concatenate([table_ref[i]] * (width // BLOCK), axis=1) for i in range(5)
    ]
    mass = jnp.broadcast_to(mass_ref[...], (beads, width))
    spread = kick * jnp.sqrt(thermal * mass)
    drift = ratio / mass
    stiff = stiffness * mass
    multiply = functools.partial(jnp.dot, precision=lax.Precision.HIGHEST, preferred_element_type=f32)
    for c in range(3):
        mode_x = multiply(matrix_t_ref[...], coords[c])
        mode_p = damping * multiply(matrix_t_ref[...], moments[c]) + spread * noises[c]
        store(
            c,
            multiply(matrix_ref[...], cosine * mode_x + drift * mode_p),
            multiply(matrix_ref[...], cosine * mode_p - stiff * mode_x),
        )


def modes_kernel(
    blocks, noise_base, rest_ref, p_ref, mass_ref, matrix_ref, matrix_t_ref, table_ref,
    xout_ref, pout_ref, coord_ref, moment_ref, noise_ref,
):
    local = p_ref.shape[1] // (3 * blocks)
    unpack_beads(rest_ref, 0, blocks, local, coord_ref, 0)
    unpack_beads(p_ref, 0, blocks, local, moment_ref, 0)
    unpack_beads(rest_ref, noise_base, blocks, local, noise_ref, 0)

    def store(c, x, p):
        pack_beads(x, c, blocks, local, xout_ref)
        pack_beads(p, c, blocks, local, pout_ref)

    thermostat(
        *[[ref[c] for c in range(3)] for ref in (coord_ref, moment_ref, noise_ref)],
        mass_ref, matrix_ref, matrix_t_ref, table_ref, store,
    )


def middle_kernel(hops, blocks, listed, noise_base, joined, offset_ref, charge_ref, *refs):
    parts = 2 * hops + 1
    x_refs = refs[:parts]
    p_ref, noise_ref, mass_ref, matrix_ref, matrix_t_ref, table_ref = refs[parts:parts + 6]
    outs = refs[parts + 6:parts + (7 if joined else 8)]
    coord_ref, *scratch = refs[parts + len(outs) + 6:]
    beads = coord_ref.shape[1]
    local = beads // p_ref.shape[0]
    width = blocks * BLOCK
    for part in range(parts):
        unpack_beads(x_refs[part], 0, blocks, local, coord_ref, part * width)
    add_forces(blocks, hops * blocks, listed, offset_ref, charge_ref, coord_ref, scratch)
    force_ref = scratch[FORCE]
    unpack_beads(p_ref, 0, blocks, local, coord_ref, 0)
    unpack_beads(noise_ref, noise_base, blocks, local, coord_ref, (parts - 1) * width)

    def share(c, part):
        return coord_ref[c, :, part * width:(part + 1) * width]

    def store(c, x, p):
        pack_beads(x, c, blocks, local, outs[0])
        if joined:
            pack_beads(p, 3 + c, blocks, local, outs[0])
        else:
            pack_beads(p, c, blocks, local, outs[1])

    thermostat(
        [share(c, hops) for c in range(3)],
        [share(c, 0) + 2.0 * half_step * force_ref[c] for c in range(3)],
        [share(c, parts - 1) for c in range(3)],
        mass_ref, matrix_ref, matrix_t_ref, table_ref, store,
    )


def fold(count):
    return [i // 2 if i % 2 == 0 else count - 1 - i // 2 for i in range(count)]


def exchange(pieces):
    order = fold(pieces.shape[0])
    group = [order.index(at) for at in range(len(order))]
    return lax.all_to_all(pieces, "bead", split_axis=0, concat_axis=0, axis_index_groups=[group], tiled=True)


def passed(values, step):
    count = lax.axis_size("space")
    return lax.ppermute(values, "space", [(i, (i + step) % count) for i in range(count)])


def window(values, hops):
    count = lax.axis_size("bead")
    domains = lax.axis_size("space")
    order = fold(count)
    device = {}
    for bead in range(count):
        for domain in range(domains):
            device[domain * count + order[bead]] = bead * domains + domain
    total = count * domains
    out = []
    for hop in range(-hops, hops + 1):
        if hop == 0:
            out.append(values)
        else:
            route = [(device[(at + hop) % total], device[at]) for at in range(total)]
            out.append(lax.ppermute(values, ("bead", "space"), route))
    return out


def body(positions, momenta, atom_types, neighbours, thermal_noise):
    count = lax.axis_size("bead")
    _, local, atoms = positions.shape
    beads = local * count
    domain = atoms // BLOCK
    blocks = domain // count
    share = blocks * BLOCK
    hops = -(-HALO // blocks)
    margin = hops * blocks
    edge = margin * BLOCK
    steps = thermal_noise.shape[0]
    listed = neighbours.shape[1]
    order = fold(count)

    own = lax.axis_index("space") * domain + jnp.arange(domain, dtype=jnp.int32)
    offsets = jnp.clip(neighbours - own[:, None], -margin, margin).reshape(-1)
    sent = jnp.pad(offsets[:margin * listed].astype(f32), (0, edge - margin * listed))[None, :]

    message, charge, mass = call(
        message_kernel, (positions, momenta, thermal_noise, atom_types[None, :], sent), 0,
        [(13 + 3 * steps, local, edge), (1, atoms), (1, atoms)], [], 0,
    )
    message = passed(message, -1)
    side = message[9 + 3 * steps:, 0]
    first_charge = jnp.concatenate([charge, side[:1], side[1:2]], axis=1)
    moved_mass = jnp.concatenate([mass[0, edge:], side[2]])
    moved_offsets = jnp.concatenate([offsets[margin * listed:], side[3, :margin * listed].astype(jnp.int32)])
    (rest,) = call(
        functools.partial(pack_kernel, blocks), (positions, thermal_noise, message), 0,
        [(count, (3 + 3 * steps) * blocks * local, BLOCK)], [], 0,
    )
    rest = exchange(rest)

    place = jnp.asarray(np.array(order, np.int32))[lax.axis_index("bead")]
    near_charge = lax.dynamic_slice_in_dim(first_charge, place * share, share + 2 * edge, axis=1)
    near_mass = lax.dynamic_slice_in_dim(moved_mass, place * share, share)[None, :]
    near_offsets = lax.dynamic_slice_in_dim(moved_offsets, place * blocks * listed, blocks * listed)

    matrix, tables = mode_constants(beads)
    at = np.concatenate([order.index(g) * local + np.arange(local) for g in range(count)])
    matrix = matrix[at][:, at]
    fixed = (near_mass, jnp.asarray(matrix), jnp.asarray(np.ascontiguousarray(matrix.T)), jnp.asarray(tables[:, at]))

    packed = (count, 3 * blocks * local, BLOCK)
    pairs = beads * blocks * listed * BLOCK * BLOCK
    (moment,) = call(
        functools.partial(first_kernel, count, margin, listed),
        (moved_offsets, first_charge, positions, message, momenta), 1, [packed],
        force_scratch(local, domain, margin, listed), pairs,
    )
    moment, rest = lax.optimization_barrier((moment, rest))
    coords, moment = call(
        functools.partial(modes_kernel, blocks, 3), (rest, exchange(moment)) + fixed, 0, [packed] * 2,
        [pltpu.VMEM((3, beads, share), f32)] * 3, 0,
    )
    for step in range(1, steps):
        joined = step == steps - 1
        out = call(
            functools.partial(middle_kernel, hops, blocks, listed, 3 * step + 3, joined),
            (near_offsets, near_charge) + tuple(window(coords, hops)) + (moment, rest) + fixed, 1,
            [(count, 6 * blocks * local, BLOCK)] if joined else [packed] * 2,
            force_scratch(beads, blocks, margin, listed), pairs,
        )
        if not joined:
            coords, moment = out
    both = exchange(out[0])

    def ends(low, c):
        pieces = both[low:low + hops, c * packed[1]:(c + 1) * packed[1]]
        return pieces.reshape(hops, 3, blocks, local, BLOCK).transpose(1, 3, 0, 2, 4).reshape(3, local, edge)

    message = passed(jnp.concatenate([
        ends(count - 2 * hops, 0), ends(count - hops, 0), ends(count - hops, 1),
        jnp.broadcast_to(charge[:, None, atoms - edge:], (1, local, edge)),
    ], axis=0), 1)
    last_charge = jnp.concatenate([message[9, 0], first_charge[0, :atoms + edge]])[None, :]
    return tuple(call(
        functools.partial(last_kernel, margin, listed), (offsets, last_charge, both, message), 1,
        [(3, local, atoms)] * 2, force_scratch(local, domain, margin, listed), pairs,
    ))


def solution(mesh):
    placed = (
        P(None, "bead", "space"),
        P(None, "bead", "space"),
        P("space"),
        P("space", None),
        P(None, None, "bead", "space"),
    )
    return jax.shard_map(
        body,
        mesh=mesh,
        in_specs=placed,
        out_specs=(P(None, "bead", "space"), P(None, "bead", "space")),
        check_vma=False,
    )
```

```python
import functools
import math

import jax
import jax.numpy as jnp
import numpy as np
from jax import lax
from jax.experimental import pallas as pl
from jax.experimental.pallas import tpu as pltpu
from jax.sharding import PartitionSpec as P

BLOCK = 128
HALO = 4

half_step = 0.025
time_step = 0.05
chain_freq = 12.0
thermal = 0.375
centroid_friction = 1.0
screening = 4.0
softening = 0.09
CHARGES = (1.0, -1.0, 0.6, -1.4)
MASSES = (1.0, 2.0, 3.0, 4.0)

PAIR_ROWS = 24
PAIR_PAD = 32
SUM_ROWS = 16
QUAD = 4
PASS = 32
FRAME = 8
f32 = jnp.float32
bf16 = jnp.bfloat16


def mode_constants(bead_total):
    j = np.arange(bead_total)[:, None]
    k = np.arange(bead_total)[None, :]
    half = bead_total // 2
    phase = 2.0 * np.pi * ((j * k) % bead_total) / bead_total
    plain = 1.0 / math.sqrt(bead_total)
    paired = math.sqrt(2.0 / bead_total)
    matrix = np.where(
        k == 0,
        plain,
        np.where(
            k < half,
            paired * np.cos(phase),
            np.where(k == half, plain * np.cos(phase), paired * np.sin(phase)),
        ),
    )
    modes = np.arange(bead_total)
    frequency = 2.0 * chain_freq * np.sin(np.pi * modes / bead_total)
    angle = frequency * time_step
    ratio = np.where(modes == 0, time_step, np.sin(angle) / np.where(modes == 0, 1.0, frequency))
    friction = np.where(modes == 0, centroid_friction, 2.0 * frequency)
    damping = np.exp(-friction * time_step)
    kick = np.sqrt(1.0 - damping * damping)
    tables = np.stack([np.cos(angle), ratio, frequency * np.sin(angle), damping, kick])
    tables = np.broadcast_to(tables[:, :, None], tables.shape + (BLOCK,))
    return matrix.astype(np.float32), np.ascontiguousarray(tables).astype(np.float32)


def split3(v):
    one = v.astype(bf16).astype(f32)
    rest = v - one
    two = rest.astype(bf16).astype(f32)
    three = (rest - two).astype(bf16).astype(f32)
    return one, two, three


def pair_rows(coords, norm, own):
    rows = []
    for v in coords:
        one, two, three = split3(v)
        if own:
            one, two, three = -2.0 * one, -2.0 * two, -2.0 * three
            rows += [one, one, two, two, one, three]
        else:
            rows += [one, two, one, two, three, one]
    ones = [jnp.ones_like(norm)] * 3
    norms = list(split3(norm))
    return rows + (norms + ones if own else ones + norms)


def weigh(square, plain_exp=False):
    inverse = lax.rsqrt(square)
    if plain_exp:
        decay = jnp.exp(square * inverse * (-1.0 / screening))
    else:
        decay = jnp.exp2(square * inverse * (-1.0 / (screening * math.log(2.0))))
    return decay * ((inverse * inverse) * (inverse + 1.0 / screening))


def whole_quads(beads):
    return -(-beads // QUAD) * QUAD


def add_forces(form, blocks, margin, listed, offset_ref, charge_ref, coord_ref, scratch):
    rows_ref, sums_ref, far_ref, heavy_ref, near_ref, total_ref, force_ref, *buffers = scratch
    square_refs, weight_refs = buffers[:2], buffers[2:]
    beads = coord_ref.shape[1]
    pairs = beads // 2
    frame = min(FRAME, blocks)
    width = frame + 2 * margin
    middle = margin + (frame - 1) / 2.0
    at_once = max(1, 8 // beads)
    lines = at_once * beads
    units = blocks * pairs

    def put(ref, k, value):
        ref[k * lines:(k + 1) * lines, :] = value

    def centred(block, place):
        spans = [pl.ds(pl.multiple_of((block + i) * BLOCK, BLOCK), BLOCK) for i in range(at_once)]
        coords = [
            jnp.concatenate([coord_ref[c, :, lanes] for lanes in spans], axis=0) - 1.0 for c in range(3)
        ]
        shift = jnp.concatenate(
            [jnp.full((beads, BLOCK), 1.0, f32) * ((place + i).astype(f32) - middle) for i in range(at_once)], axis=0
        )
        coords[0] = coords[0] + shift
        norm = coords[0] * coords[0] + coords[1] * coords[1] + coords[2] * coords[2]
        charge = jnp.concatenate(
            [jnp.broadcast_to(charge_ref[:, lanes], (beads, BLOCK)) for lanes in spans], axis=0
        )
        return coords, norm, charge

    nothing = jnp.zeros((lines, BLOCK), f32)
    for k in range(PAIR_ROWS, PAIR_PAD):
        put(rows_ref, k, nothing)
    for k in range(12, SUM_ROWS):
        put(sums_ref, k, nothing)
    blank = jnp.zeros((PAIR_PAD, BLOCK), f32)

    def one_frame(at_frame, carry):
        first = at_frame * frame

        def one_table(step, inner):
            place = step * at_once
            coords, norm, charge = centred(first + place, place)
            for k, row in enumerate(pair_rows(coords, norm, False)):
                put(rows_ref, k, row)
            for c, v in enumerate([charge] + [charge * x for x in coords]):
                for level, part in enumerate(split3(v)):
                    put(sums_ref, level * 4 + c, part)
            for i in range(at_once):
                at = at_frame * width + place + i
                for quad in range(beads // QUAD):
                    low = i * beads + quad * QUAD
                    four = jnp.concatenate(
                        [rows_ref[pl.ds(low + j, PAIR_PAD, stride=lines), :] for j in range(QUAD)], axis=0
                    )
                    far_ref[at, quad] = jnp.transpose(four).astype(bf16)
                    for half in range(2):
                        heavy_ref[at, 2 * quad + half] = jnp.concatenate(
                            [
                                sums_ref[pl.ds(low + 2 * half + j, SUM_ROWS, stride=lines), :]
                                for j in range(2)
                            ],
                            axis=0,
                        ).astype(bf16)
            return inner

        lax.fori_loop(0, width // at_once, one_table, 0)

        def one_own(step, inner):
            block = step * at_once
            coords, norm, _ = centred(first + margin + block, block + margin)
            for k, row in enumerate(pair_rows(coords, norm + softening, True)):
                put(rows_ref, k, row)
            for i in range(at_once):
                for pair in range(pairs):
                    columns = []
                    for j in range(2):
                        own = rows_ref[pl.ds(i * beads + 2 * pair + j, PAIR_PAD, stride=lines), :]
                        spot = 2 * pair % QUAD + j
                        columns.append(
                            jnp.concatenate([own if k == spot else blank for k in range(QUAD)], axis=0)
                        )
                    near_ref[(first + block + i) * pairs + pair] = jnp.concatenate(columns, axis=1).astype(bf16)
            return inner

        lax.fori_loop(0, frame // at_once, one_own, 0)
        return carry

    lax.fori_loop(0, blocks // frame, one_frame, 0)

    def places(unit):
        block = unit // pairs
        at_frame = block // frame
        base = at_frame * width + block - at_frame * frame + margin
        return [base + offset_ref[block * listed + m] for m in range(listed)], unit - block * pairs

    def square(ats, pair, unit, m, out):
        far = far_ref[ats[m], pair // (QUAD // 2)]
        out[m * BLOCK:(m + 1) * BLOCK, :] = jnp.dot(far, near_ref[unit], preferred_element_type=f32)

    tall = BLOCK if form == "tall" else PASS

    def weights(m, squared, out):
        for low in range(0, BLOCK, tall):
            weight = weigh(squared[low:low + tall, :], form == "exp")
            high = weight.astype(bf16)
            row = 2 * m * BLOCK + low
            out[row:row + tall, :] = high
            out[row + BLOCK:row + BLOCK + tall, :] = (weight - high.astype(f32)).astype(bf16)

    def weighted(ats, pair, m, weight_ref):
        table = heavy_ref[ats[m], pair]
        return jnp.dot(
            jnp.concatenate([table, table], axis=1),
            weight_ref[2 * m * BLOCK:2 * (m + 1) * BLOCK, :], preferred_element_type=f32,
        )

    def keep(total, slot):
        for i in range(2):
            cols = slice(i * BLOCK, (i + 1) * BLOCK)
            row = i * SUM_ROWS
            spot = pl.ds(pl.multiple_of((2 * slot + i) * 8, 8), 8)
            total_ref[spot, :] = total[row:row + 8, cols] + total[row + 8:row + 16, cols]

    def one_unit(unit, now, other):
        after = jnp.minimum(unit + 1, units - 1)
        before = jnp.maximum(unit - 1, 0)
        if form != "direct":
            after_ats, after_pair = places(after)
        before_ats, before_pair = places(before)
        total = jnp.zeros((2 * SUM_ROWS, 2 * BLOCK), f32)
        if form == "direct":
            ats, pair = places(unit)
        for m in range(listed):
            if form == "direct":
                far = far_ref[ats[m], pair // (QUAD // 2)]
                weights(m, jnp.dot(far, near_ref[unit], preferred_element_type=f32), weight_refs[now])
            else:
                square(after_ats, after_pair, after, m, square_refs[other])
                weights(m, square_refs[now].at[m * BLOCK:(m + 1) * BLOCK], weight_refs[now])
            total = total + weighted(before_ats, before_pair, m, weight_refs[other])
        keep(total, jnp.where(unit == 0, units, unit - 1))

    if form != "direct":
        first_ats, first_pair = places(0)
        for m in range(listed):
            square(first_ats, first_pair, 0, m, square_refs[0])

    def two_units(step, carry):
        one_unit(2 * step, 0, 1)
        one_unit(2 * step + 1, 1, 0)
        return carry

    lax.fori_loop(0, units // 2, two_units, 0)
    last_ats, last_pair = places(units - 1)
    keep(sum(weighted(last_ats, last_pair, m, weight_refs[1]) for m in range(listed)), units - 1)

    def one_block(block, carry):
        at_frame = block // frame
        place = block - at_frame * frame + margin
        lanes = pl.ds(pl.multiple_of((block + margin) * BLOCK, BLOCK), BLOCK)
        coords = [coord_ref[c, :, lanes] - 1.0 for c in range(3)]
        coords[0] = coords[0] + (place.astype(f32) - middle)
        charge = jnp.broadcast_to(charge_ref[:, lanes], coords[0].shape)

        def summed(c):
            return (
                total_ref[pl.ds(block * beads * 8 + c, beads, stride=8), :]
                + total_ref[pl.ds(block * beads * 8 + c + 4, beads, stride=8), :]
            )

        near = summed(0)
        own = pl.ds(pl.multiple_of(block * BLOCK, BLOCK), BLOCK)
        for c in range(3):
            force_ref[c, :, own] = charge * (coords[c] * near - summed(c + 1))
        return carry

    lax.fori_loop(0, blocks, one_block, 0)


def force_scratch(local, blocks, margin, listed):
    beads = whole_quads(local)
    frame = min(FRAME, blocks)
    tables = (frame + 2 * margin) * (blocks // frame)
    lines = max(8, beads)
    units = blocks * beads // 2
    return [
        pltpu.VMEM((3, beads, (blocks + 2 * margin) * BLOCK), f32),
        pltpu.VMEM((PAIR_PAD * lines, BLOCK), f32),
        pltpu.VMEM((SUM_ROWS * lines, BLOCK), f32),
        pltpu.VMEM((tables, beads // QUAD, BLOCK, QUAD * PAIR_PAD), bf16),
        pltpu.VMEM((tables, beads // 2, 2 * SUM_ROWS, BLOCK), bf16),
        pltpu.VMEM((units, QUAD * PAIR_PAD, 2 * BLOCK), bf16),
        pltpu.VMEM(((units + 1) * 16, BLOCK), f32),
        pltpu.VMEM((3, beads, blocks * BLOCK), f32),
        pltpu.VMEM((listed * BLOCK, 2 * BLOCK), f32),
        pltpu.VMEM((listed * BLOCK, 2 * BLOCK), f32),
        pltpu.VMEM((2 * listed * BLOCK, 2 * BLOCK), bf16),
        pltpu.VMEM((2 * listed * BLOCK, 2 * BLOCK), bf16),
    ]


def call(kernel, args, smem_count, shapes, scratch, work, in_specs=None):
    vmem = pl.BlockSpec(memory_space=pltpu.VMEM)
    smem = pl.BlockSpec(memory_space=pltpu.SMEM)
    return pl.pallas_call(
        kernel,
        out_shape=[jax.ShapeDtypeStruct(shape, f32) for shape in shapes],
        grid=() if in_specs is None else (1,),
        in_specs=in_specs or [smem] * smem_count + [vmem] * (len(args) - smem_count),
        out_specs=[vmem] * len(shapes),
        scratch_shapes=scratch,
        compiler_params=pltpu.CompilerParams(vmem_limit_bytes=(40 if in_specs is None else 62) * 1024 * 1024),
        cost_estimate=pl.CostEstimate(
            flops=20 * work + 1024, bytes_accessed=4 * 1024 * 1024, transcendentals=2 * work
        ),
    )(*args)


def row_of(c, block, blocks, local):
    return (c * blocks + block) * local


def unpack_beads(source, base, blocks, local, target, offset):
    for c in range(3):
        for block in range(blocks):
            row = row_of(base + c, block, blocks, local)
            lane = offset + block * BLOCK
            for group in range(source.shape[0]):
                target[c, group * local:(group + 1) * local, lane:lane + BLOCK] = source[group, row:row + local, :]


def pack_beads(value, c, blocks, local, target):
    for block in range(blocks):
        row = row_of(c, block, blocks, local)
        for group in range(target.shape[0]):
            target[group, row:row + local, :] = value[
                group * local:(group + 1) * local, block * BLOCK:(block + 1) * BLOCK
            ]


FORCE = 6


def clear(coord_ref, local):
    if coord_ref.shape[1] != local:
        coord_ref[...] = jnp.zeros(coord_ref.shape, f32)


def message_kernel(x_ref, p_ref, noise_ref, types_ref, offsets_ref, message_ref, charge_ref, mass_ref):
    steps = noise_ref.shape[0]
    _, local, edge = message_ref.shape
    types = types_ref[...]
    charge = jnp.zeros(types.shape, f32)
    mass = jnp.zeros(types.shape, f32)
    for kind in range(4):
        charge = jnp.where(types == kind, CHARGES[kind], charge)
        mass = jnp.where(types == kind, MASSES[kind], mass)
    charge_ref[...] = charge
    mass_ref[...] = mass
    for c in range(3):
        message_ref[c] = x_ref[c, :, :edge]
        message_ref[3 + c] = x_ref[c, :, edge:2 * edge]
        message_ref[6 + c] = p_ref[c, :, :edge]
        for step in range(steps):
            message_ref[9 + 3 * step + c] = noise_ref[step, c, :, :edge]
    at = 9 + 3 * steps
    for i, row in enumerate([charge[:, :edge], charge[:, edge:2 * edge], mass[:, :edge], offsets_ref[...]]):
        message_ref[at + i] = jnp.broadcast_to(row, (local, edge))


def pack_kernel(blocks, x_ref, noise_ref, message_ref, out_ref):
    steps = noise_ref.shape[0]
    _, local, edge = message_ref.shape
    atoms = x_ref.shape[2]
    for c in range(3 + 3 * steps):
        for block in range(atoms // BLOCK):
            at = edge + block * BLOCK
            if at >= atoms:
                value = message_ref[c if c < 3 else 6 + c, :, at - atoms:at - atoms + BLOCK]
            elif c < 3:
                value = x_ref[c, :, at:at + BLOCK]
            else:
                value = noise_ref[c // 3 - 1, c % 3, :, at:at + BLOCK]
            row = row_of(c, block % blocks, blocks, local)
            out_ref[block // blocks, row:row + local, :] = value


def first_kernel(
    shares, margin, listed, offset_ref, charge_ref, x_ref, message_ref, p_ref, pout_ref, coord_ref, *scratch
):
    _, local, atoms = x_ref.shape
    blocks = atoms // BLOCK
    each = blocks // shares
    edge = margin * BLOCK
    clear(coord_ref, local)
    for c in range(3):
        coord_ref[c, :local, 0:atoms] = x_ref[c]
        for part in range(2):
            coord_ref[c, :local, atoms + part * edge:atoms + (part + 1) * edge] = message_ref[3 * part + c]
    add_forces("exp", blocks, margin, listed, offset_ref, charge_ref, coord_ref, scratch)
    force_ref = scratch[FORCE]
    for c in range(3):
        for block in range(blocks):
            lanes = slice(block * BLOCK, (block + 1) * BLOCK)
            at = block * BLOCK + edge
            if at < atoms:
                moment = p_ref[c, :, at:at + BLOCK]
            else:
                moment = message_ref[6 + c, :, at - atoms:at - atoms + BLOCK]
            row = row_of(c, block % each, each, local)
            pout_ref[block // each, row:row + local, :] = moment + half_step * force_ref[c, :local, lanes]


def last_kernel(
    margin, listed, offset_ref, charge_ref, both_ref, message_ref, xout_ref, pout_ref, coord_ref, *scratch
):
    shares = both_ref.shape[0]
    _, local, atoms = xout_ref.shape
    blocks = atoms // BLOCK
    each = blocks // shares
    edge = margin * BLOCK

    def taken(c, block):
        row = row_of(c, block % each, each, local)
        return both_ref[block // each, row:row + local, :]

    clear(coord_ref, local)
    for c in range(3):
        for part in range(2):
            coord_ref[c, :local, part * edge:(part + 1) * edge] = message_ref[3 * part + c]
        for block in range(blocks):
            at = 2 * edge + block * BLOCK
            coord_ref[c, :local, at:at + BLOCK] = taken(c, block)
        xout_ref[c] = coord_ref[c, :local, edge:edge + atoms]
    add_forces("direct", blocks, margin, listed, offset_ref, charge_ref, coord_ref, scratch)
    force_ref = scratch[FORCE]
    for c in range(3):
        for block in range(blocks):
            lanes = slice(block * BLOCK, (block + 1) * BLOCK)
            moment = message_ref[6 + c, :, lanes] if block < margin else taken(3 + c, block - margin)
            pout_ref[c, :, lanes] = moment + half_step * force_ref[c, :local, lanes]


def thermostat(coords, moments, noises, mass_ref, matrix_ref, matrix_t_ref, table_ref, store):
    beads, width = moments[0].shape
    cosine, ratio, stiffness, damping, kick = [
        jnp.concatenate([table_ref[i]] * (width // BLOCK), axis=1) for i in range(5)
    ]
    mass = jnp.broadcast_to(mass_ref[...], (beads, width))
    spread = kick * jnp.sqrt(thermal * mass)
    drift = ratio / mass
    stiff = stiffness * mass
    multiply = functools.partial(jnp.dot, precision=lax.Precision.HIGHEST, preferred_element_type=f32)
    for c in range(3):
        mode_x = multiply(matrix_t_ref[...], coords[c])
        mode_p = damping * multiply(matrix_t_ref[...], moments[c]) + spread * noises[c]
        store(
            c,
            multiply(matrix_ref[...], cosine * mode_x + drift * mode_p),
            multiply(matrix_ref[...], cosine * mode_p - stiff * mode_x),
        )


def modes_kernel(
    blocks, noise_base, rest_ref, p_ref, mass_ref, matrix_ref, matrix_t_ref, table_ref,
    xout_ref, pout_ref, coord_ref, moment_ref, noise_ref,
):
    local = p_ref.shape[1] // (3 * blocks)
    unpack_beads(rest_ref, 0, blocks, local, coord_ref, 0)
    unpack_beads(p_ref, 0, blocks, local, moment_ref, 0)
    unpack_beads(rest_ref, noise_base, blocks, local, noise_ref, 0)

    def store(c, x, p):
        pack_beads(x, c, blocks, local, xout_ref)
        pack_beads(p, c, blocks, local, pout_ref)

    thermostat(
        *[[ref[c] for c in range(3)] for ref in (coord_ref, moment_ref, noise_ref)],
        mass_ref, matrix_ref, matrix_t_ref, table_ref, store,
    )


def middle_kernel(hops, blocks, listed, noise_base, joined, offset_ref, charge_ref, *refs):
    parts = 2 * hops + 1
    x_refs = refs[:parts]
    p_ref, noise_ref, mass_ref, matrix_ref, matrix_t_ref, table_ref = refs[parts:parts + 6]
    outs = refs[parts + 6:parts + (7 if joined else 8)]
    coord_ref, *scratch = refs[parts + len(outs) + 6:]
    beads = coord_ref.shape[1]
    local = beads // p_ref.shape[0]
    width = blocks * BLOCK
    for part in range(parts):
        unpack_beads(x_refs[part], 0, blocks, local, coord_ref, part * width)
    add_forces("tall", blocks, hops * blocks, listed, offset_ref, charge_ref, coord_ref, scratch)
    force_ref = scratch[FORCE]
    unpack_beads(p_ref, 0, blocks, local, coord_ref, 0)
    unpack_beads(noise_ref, noise_base, blocks, local, coord_ref, (parts - 1) * width)

    def share(c, part):
        return coord_ref[c, :, part * width:(part + 1) * width]

    def store(c, x, p):
        pack_beads(x, c, blocks, local, outs[0])
        if joined:
            pack_beads(p, 3 + c, blocks, local, outs[0])
        else:
            pack_beads(p, c, blocks, local, outs[1])

    thermostat(
        [share(c, hops) for c in range(3)],
        [share(c, 0) + 2.0 * half_step * force_ref[c] for c in range(3)],
        [share(c, parts - 1) for c in range(3)],
        mass_ref, matrix_ref, matrix_t_ref, table_ref, store,
    )


def fold(count):
    return [i // 2 if i % 2 == 0 else count - 1 - i // 2 for i in range(count)]


def exchange(pieces):
    order = fold(pieces.shape[0])
    group = [order.index(at) for at in range(len(order))]
    return lax.all_to_all(pieces, "bead", split_axis=0, concat_axis=0, axis_index_groups=[group], tiled=True)


def passed(values, step):
    count = lax.axis_size("space")
    return lax.ppermute(values, "space", [(i, (i + step) % count) for i in range(count)])


def window(values, hops):
    count = lax.axis_size("bead")
    domains = lax.axis_size("space")
    order = fold(count)
    device = {}
    for bead in range(count):
        for domain in range(domains):
            device[domain * count + order[bead]] = bead * domains + domain
    total = count * domains
    out = []
    for hop in range(-hops, hops + 1):
        if hop == 0:
            out.append(values)
        else:
            route = [(device[(at + hop) % total], device[at]) for at in range(total)]
            out.append(lax.ppermute(values, ("bead", "space"), route))
    return out


def body(positions, momenta, atom_types, neighbours, thermal_noise):
    count = lax.axis_size("bead")
    _, local, atoms = positions.shape
    beads = local * count
    domain = atoms // BLOCK
    blocks = domain // count
    share = blocks * BLOCK
    hops = -(-HALO // blocks)
    margin = hops * blocks
    edge = margin * BLOCK
    steps = thermal_noise.shape[0]
    listed = neighbours.shape[1]
    order = fold(count)

    own = lax.axis_index("space") * domain + jnp.arange(domain, dtype=jnp.int32)
    offsets = jnp.clip(neighbours - own[:, None], -margin, margin).reshape(-1)
    sent = jnp.pad(offsets[:margin * listed].astype(f32), (0, edge - margin * listed))[None, :]

    message, charge, mass = call(
        message_kernel, (positions, momenta, thermal_noise, atom_types[None, :], sent), 0,
        [(13 + 3 * steps, local, edge), (1, atoms), (1, atoms)], [], 0,
        [
            pl.BlockSpec(shape, lambda i, rank=len(shape): (0,) * rank)
            for shape in (
                (3, local, 2 * edge), (3, local, edge), (steps, 3, local, edge), (1, atoms), (1, edge)
            )
        ],
    )
    message = passed(message, -1)
    side = message[9 + 3 * steps:, 0]
    first_charge = jnp.concatenate([charge, side[:1], side[1:2]], axis=1)
    moved_mass = jnp.concatenate([mass[0, edge:], side[2]])
    moved_offsets = jnp.concatenate([offsets[margin * listed:], side[3, :margin * listed].astype(jnp.int32)])
    (rest,) = call(
        functools.partial(pack_kernel, blocks), (positions, thermal_noise, message), 0,
        [(count, (3 + 3 * steps) * blocks * local, BLOCK)], [], 0,
    )
    rest = exchange(rest)

    place = jnp.asarray(np.array(order, np.int32))[lax.axis_index("bead")]
    near_charge = lax.dynamic_slice_in_dim(first_charge, place * share, share + 2 * edge, axis=1)
    near_mass = lax.dynamic_slice_in_dim(moved_mass, place * share, share)[None, :]
    near_offsets = lax.dynamic_slice_in_dim(moved_offsets, place * blocks * listed, blocks * listed)

    matrix, tables = mode_constants(beads)
    at = np.concatenate([order.index(g) * local + np.arange(local) for g in range(count)])
    matrix = matrix[at][:, at]
    fixed = (near_mass, jnp.asarray(matrix), jnp.asarray(np.ascontiguousarray(matrix.T)), jnp.asarray(tables[:, at]))

    packed = (count, 3 * blocks * local, BLOCK)
    pairs = beads * blocks * listed * BLOCK * BLOCK
    (moment,) = call(
        functools.partial(first_kernel, count, margin, listed),
        (moved_offsets, first_charge, positions, message, momenta), 1, [packed],
        force_scratch(local, domain, margin, listed), pairs,
    )
    moment, rest = lax.optimization_barrier((moment, rest))
    coords, moment = call(
        functools.partial(modes_kernel, blocks, 3), (rest, exchange(moment)) + fixed, 0, [packed] * 2,
        [pltpu.VMEM((3, beads, share), f32)] * 3, 0,
    )
    for step in range(1, steps):
        joined = step == steps - 1
        out = call(
            functools.partial(middle_kernel, hops, blocks, listed, 3 * step + 3, joined),
            (near_offsets, near_charge) + tuple(window(coords, hops)) + (moment, rest) + fixed, 1,
            [(count, 6 * blocks * local, BLOCK)] if joined else [packed] * 2,
            force_scratch(beads, blocks, margin, listed), pairs,
        )
        if not joined:
            coords, moment = out
    both = exchange(out[0])

    def ends(low, c):
        pieces = both[low:low + hops, c * packed[1]:(c + 1) * packed[1]]
        return pieces.reshape(hops, 3, blocks, local, BLOCK).transpose(1, 3, 0, 2, 4).reshape(3, local, edge)

    message = passed(jnp.concatenate([
        ends(count - 2 * hops, 0), ends(count - hops, 0), ends(count - hops, 1),
        jnp.broadcast_to(charge[:, None, atoms - edge:], (1, local, edge)),
    ], axis=0), 1)
    last_charge = jnp.concatenate([message[9, 0], first_charge[0, :atoms + edge]])[None, :]
    return tuple(call(
        functools.partial(last_kernel, margin, listed), (offsets, last_charge, both, message), 1,
        [(3, local, atoms)] * 2, force_scratch(local, domain, margin, listed), pairs,
    ))


def solution(mesh):
    placed = (
        P(None, "bead", "space"),
        P(None, "bead", "space"),
        P("space"),
        P("space", None),
        P(None, None, "bead", "space"),
    )
    return jax.shard_map(
        body,
        mesh=mesh,
        in_specs=placed,
        out_specs=(P(None, "bead", "space"), P(None, "bead", "space")),
        check_vma=False,
    )
```

```python
import functools
import math

import jax
import jax.numpy as jnp
import numpy as np
from jax import lax
from jax.experimental import pallas as pl
from jax.experimental.pallas import tpu as pltpu
from jax.sharding import PartitionSpec as P

BLOCK = 128
HALO = 4

half_step = 0.025
time_step = 0.05
chain_freq = 12.0
thermal = 0.375
centroid_friction = 1.0
screening = 4.0
softening = 0.09
CHARGES = (1.0, -1.0, 0.6, -1.4)
MASSES = (1.0, 2.0, 3.0, 4.0)

PAIR_ROWS = 24
PAIR_PAD = 32
SUM_ROWS = 16
QUAD = 4
FRAME = 8
f32 = jnp.float32
bf16 = jnp.bfloat16


def mode_constants(bead_total):
    j = np.arange(bead_total)[:, None]
    k = np.arange(bead_total)[None, :]
    half = bead_total // 2
    phase = 2.0 * np.pi * ((j * k) % bead_total) / bead_total
    plain = 1.0 / math.sqrt(bead_total)
    paired = math.sqrt(2.0 / bead_total)
    matrix = np.where(
        k == 0,
        plain,
        np.where(
            k < half,
            paired * np.cos(phase),
            np.where(k == half, plain * np.cos(phase), paired * np.sin(phase)),
        ),
    )
    modes = np.arange(bead_total)
    frequency = 2.0 * chain_freq * np.sin(np.pi * modes / bead_total)
    angle = frequency * time_step
    ratio = np.where(modes == 0, time_step, np.sin(angle) / np.where(modes == 0, 1.0, frequency))
    friction = np.where(modes == 0, centroid_friction, 2.0 * frequency)
    damping = np.exp(-friction * time_step)
    kick = np.sqrt(1.0 - damping * damping)
    tables = np.stack([np.cos(angle), ratio, frequency * np.sin(angle), damping, kick])
    tables = np.broadcast_to(tables[:, :, None], tables.shape + (BLOCK,))
    return matrix.astype(np.float32), np.ascontiguousarray(tables).astype(np.float32)


def split3(v):
    one = v.astype(bf16).astype(f32)
    rest = v - one
    two = rest.astype(bf16).astype(f32)
    three = (rest - two).astype(bf16).astype(f32)
    return one, two, three


def pair_rows(coords, norm, own):
    rows = []
    for v in coords:
        one, two, three = split3(v)
        if own:
            one, two, three = -2.0 * one, -2.0 * two, -2.0 * three
            rows += [one, one, two, two, one, three]
        else:
            rows += [one, two, one, two, three, one]
    ones = [jnp.ones_like(norm)] * 3
    norms = list(split3(norm))
    return rows + (norms + ones if own else ones + norms)


SCALE = 1.0 / (screening * math.log(2.0))


def weigh(square):
    inverse = lax.rsqrt(square)
    decay = jnp.exp2(-(square * inverse))
    return decay * ((inverse * inverse) * (inverse + math.log(2.0)))


def whole_quads(beads):
    return -(-beads // QUAD) * QUAD


def add_forces(form, blocks, margin, listed, offset_ref, charge_ref, coord_ref, scratch):
    rows_ref, sums_ref, far_ref, heavy_ref, near_ref, total_ref, force_ref, *buffers = scratch
    weight_refs = buffers
    beads = coord_ref.shape[1]
    pairs = beads // 2
    frame = min(FRAME, blocks)
    width = frame + 2 * margin
    middle = margin + (frame - 1) / 2.0
    at_once = max(1, 8 // beads)
    lines = at_once * beads
    units = blocks * pairs

    def put(ref, k, value):
        ref[k * lines:(k + 1) * lines, :] = value

    def centred(block, place):
        spans = [pl.ds(pl.multiple_of((block + i) * BLOCK, BLOCK), BLOCK) for i in range(at_once)]
        coords = [
            (jnp.concatenate([coord_ref[c, :, lanes] for lanes in spans], axis=0) - 1.0) * SCALE for c in range(3)
        ]
        shift = jnp.concatenate(
            [jnp.full((beads, BLOCK), SCALE, f32) * ((place + i).astype(f32) - middle) for i in range(at_once)], axis=0
        )
        coords[0] = coords[0] + shift
        norm = coords[0] * coords[0] + coords[1] * coords[1] + coords[2] * coords[2]
        charge = jnp.concatenate(
            [jnp.broadcast_to(charge_ref[:, lanes], (beads, BLOCK)) for lanes in spans], axis=0
        )
        return coords, norm, charge

    nothing = jnp.zeros((lines, BLOCK), f32)
    for k in range(PAIR_ROWS, PAIR_PAD):
        put(rows_ref, k, nothing)
    for k in range(12, SUM_ROWS):
        put(sums_ref, k, nothing)
    blank = jnp.zeros((PAIR_PAD, BLOCK), f32)

    def one_frame(at_frame, carry):
        first = at_frame * frame

        def one_table(step, inner):
            place = step * at_once
            coords, norm, charge = centred(first + place, place)
            for k, row in enumerate(pair_rows(coords, norm, False)):
                put(rows_ref, k, row)
            for c, v in enumerate([charge] + [charge * x for x in coords]):
                for level, part in enumerate(split3(v)):
                    put(sums_ref, level * 4 + c, part)
            for i in range(at_once):
                at = at_frame * width + place + i
                for quad in range(beads // QUAD):
                    low = i * beads + quad * QUAD
                    four = jnp.concatenate(
                        [rows_ref[pl.ds(low + j, PAIR_PAD, stride=lines), :] for j in range(QUAD)], axis=0
                    )
                    far_ref[at, quad] = jnp.transpose(four).astype(bf16)
                    for half in range(2):
                        heavy_ref[at, 2 * quad + half] = jnp.concatenate(
                            [
                                sums_ref[pl.ds(low + 2 * half + j, SUM_ROWS, stride=lines), :]
                                for j in range(2)
                            ],
                            axis=0,
                        ).astype(bf16)
            return inner

        lax.fori_loop(0, width // at_once, one_table, 0)

        def one_own(step, inner):
            block = step * at_once
            coords, norm, _ = centred(first + margin + block, block + margin)
            for k, row in enumerate(pair_rows(coords, norm + softening * SCALE * SCALE, True)):
                put(rows_ref, k, row)
            for i in range(at_once):
                for pair in range(pairs):
                    columns = []
                    for j in range(2):
                        own = rows_ref[pl.ds(i * beads + 2 * pair + j, PAIR_PAD, stride=lines), :]
                        spot = 2 * pair % QUAD + j
                        columns.append(
                            jnp.concatenate([own if k == spot else blank for k in range(QUAD)], axis=0)
                        )
                    near_ref[(first + block + i) * pairs + pair] = jnp.concatenate(columns, axis=1).astype(bf16)
            return inner

        lax.fori_loop(0, frame // at_once, one_own, 0)
        return carry

    lax.fori_loop(0, blocks // frame, one_frame, 0)

    def places(unit):
        block = unit // pairs
        at_frame = block // frame
        base = at_frame * width + block - at_frame * frame + margin
        return [base + offset_ref[block * listed + m] for m in range(listed)], unit - block * pairs

    def weights(ats, pair, unit, m):
        far = far_ref[ats[m], pair // (QUAD // 2)]
        weight = weigh(jnp.dot(far, near_ref[unit], preferred_element_type=f32))
        high = weight.astype(bf16)
        return high, (weight - high.astype(f32)).astype(bf16)

    def weighted(ats, pair, m, both):
        table = heavy_ref[ats[m], pair]
        return jnp.dot(jnp.concatenate([table, table], axis=1), both, preferred_element_type=f32)

    def keep(total, slot):
        for i in range(2):
            cols = slice(i * BLOCK, (i + 1) * BLOCK)
            row = i * SUM_ROWS
            spot = pl.ds(pl.multiple_of((2 * slot + i) * 8, 8), 8)
            total_ref[spot, :] = total[row:row + 8, cols] + total[row + 8:row + 16, cols]

    def whole_unit(unit):
        ats, pair = places(unit)
        keep(
            sum(weighted(ats, pair, m, jnp.concatenate(weights(ats, pair, unit, m), axis=0)) for m in range(listed)),
            unit,
        )

    def one_unit(unit, now, other):
        before = jnp.maximum(unit - 1, 0)
        ats, pair = places(unit)
        before_ats, before_pair = places(before)
        total = jnp.zeros((2 * SUM_ROWS, 2 * BLOCK), f32)
        for m in range(listed):
            spot = slice(2 * m * BLOCK, 2 * (m + 1) * BLOCK)
            weight_refs[now][spot, :] = jnp.concatenate(weights(ats, pair, unit, m), axis=0)
            total = total + weighted(before_ats, before_pair, m, weight_refs[other][spot, :])
        keep(total, jnp.where(unit == 0, units, unit - 1))

    def two_units(step, carry):
        if form == "whole":
            whole_unit(2 * step)
            whole_unit(2 * step + 1)
        else:
            one_unit(2 * step, 0, 1)
            one_unit(2 * step + 1, 1, 0)
        return carry

    lax.fori_loop(0, units // 2, two_units, 0)
    if form != "whole":
        last_ats, last_pair = places(units - 1)
        keep(
            sum(
                weighted(last_ats, last_pair, m, weight_refs[1][2 * m * BLOCK:2 * (m + 1) * BLOCK, :])
                for m in range(listed)
            ),
            units - 1,
        )

    def one_block(block, carry):
        at_frame = block // frame
        place = block - at_frame * frame + margin
        lanes = pl.ds(pl.multiple_of((block + margin) * BLOCK, BLOCK), BLOCK)
        coords = [(coord_ref[c, :, lanes] - 1.0) * SCALE for c in range(3)]
        coords[0] = coords[0] + SCALE * (place.astype(f32) - middle)
        charge = jnp.broadcast_to(SCALE * SCALE * charge_ref[:, lanes], coords[0].shape)

        def summed(c):
            return (
                total_ref[pl.ds(block * beads * 8 + c, beads, stride=8), :]
                + total_ref[pl.ds(block * beads * 8 + c + 4, beads, stride=8), :]
            )

        near = summed(0)
        own = pl.ds(pl.multiple_of(block * BLOCK, BLOCK), BLOCK)
        for c in range(3):
            force_ref[c, :, own] = charge * (coords[c] * near - summed(c + 1))
        return carry

    lax.fori_loop(0, blocks, one_block, 0)


def force_scratch(local, blocks, margin, listed):
    beads = whole_quads(local)
    frame = min(FRAME, blocks)
    tables = (frame + 2 * margin) * (blocks // frame)
    lines = max(8, beads)
    units = blocks * beads // 2
    return [
        pltpu.VMEM((3, beads, (blocks + 2 * margin) * BLOCK), f32),
        pltpu.VMEM((PAIR_PAD * lines, BLOCK), f32),
        pltpu.VMEM((SUM_ROWS * lines, BLOCK), f32),
        pltpu.VMEM((tables, beads // QUAD, BLOCK, QUAD * PAIR_PAD), bf16),
        pltpu.VMEM((tables, beads // 2, 2 * SUM_ROWS, BLOCK), bf16),
        pltpu.VMEM((units, QUAD * PAIR_PAD, 2 * BLOCK), bf16),
        pltpu.VMEM(((units + 1) * 16, BLOCK), f32),
        pltpu.VMEM((3, beads, blocks * BLOCK), f32),
        pltpu.VMEM((2 * listed * BLOCK, 2 * BLOCK), bf16),
        pltpu.VMEM((2 * listed * BLOCK, 2 * BLOCK), bf16),
    ]


def call(kernel, args, smem_count, shapes, scratch, work, in_specs=None):
    vmem = pl.BlockSpec(memory_space=pltpu.VMEM)
    smem = pl.BlockSpec(memory_space=pltpu.SMEM)
    return pl.pallas_call(
        kernel,
        out_shape=[jax.ShapeDtypeStruct(shape, f32) for shape in shapes],
        grid=() if in_specs is None else (1,),
        in_specs=in_specs or [smem] * smem_count + [vmem] * (len(args) - smem_count),
        out_specs=[vmem] * len(shapes),
        scratch_shapes=scratch,
        compiler_params=pltpu.CompilerParams(vmem_limit_bytes=(40 if in_specs is None else 62) * 1024 * 1024),
        cost_estimate=pl.CostEstimate(
            flops=20 * work + 1024, bytes_accessed=4 * 1024 * 1024, transcendentals=2 * work
        ),
    )(*args)


def row_of(c, block, blocks, local):
    return (c * blocks + block) * local


def unpack_beads(source, base, blocks, local, target, offset):
    for c in range(3):
        for block in range(blocks):
            row = row_of(base + c, block, blocks, local)
            lane = offset + block * BLOCK
            for group in range(source.shape[0]):
                target[c, group * local:(group + 1) * local, lane:lane + BLOCK] = source[group, row:row + local, :]


def pack_beads(value, c, blocks, local, target):
    for block in range(blocks):
        row = row_of(c, block, blocks, local)
        for group in range(target.shape[0]):
            target[group, row:row + local, :] = value[
                group * local:(group + 1) * local, block * BLOCK:(block + 1) * BLOCK
            ]


FORCE = 6


def clear(coord_ref, local):
    if coord_ref.shape[1] != local:
        coord_ref[...] = jnp.zeros(coord_ref.shape, f32)


def message_kernel(x_ref, p_ref, noise_ref, types_ref, offsets_ref, message_ref, charge_ref, mass_ref):
    steps = noise_ref.shape[0]
    _, local, edge = message_ref.shape
    types = types_ref[...]
    charge = jnp.zeros(types.shape, f32)
    mass = jnp.zeros(types.shape, f32)
    for kind in range(4):
        charge = jnp.where(types == kind, CHARGES[kind], charge)
        mass = jnp.where(types == kind, MASSES[kind], mass)
    charge_ref[...] = charge
    mass_ref[...] = mass
    for c in range(3):
        message_ref[c] = x_ref[c, :, :edge]
        message_ref[3 + c] = x_ref[c, :, edge:2 * edge]
        message_ref[6 + c] = p_ref[c, :, :edge]
        for step in range(steps):
            message_ref[9 + 3 * step + c] = noise_ref[step, c, :, :edge]
    at = 9 + 3 * steps
    for i, row in enumerate([charge[:, :edge], charge[:, edge:2 * edge], mass[:, :edge], offsets_ref[...]]):
        message_ref[at + i] = jnp.broadcast_to(row, (local, edge))


def pack_kernel(blocks, x_ref, noise_ref, message_ref, out_ref):
    steps = noise_ref.shape[0]
    _, local, edge = message_ref.shape
    atoms = x_ref.shape[2]
    for c in range(3 + 3 * steps):
        for block in range(atoms // BLOCK):
            at = edge + block * BLOCK
            if at >= atoms:
                value = message_ref[c if c < 3 else 6 + c, :, at - atoms:at - atoms + BLOCK]
            elif c < 3:
                value = x_ref[c, :, at:at + BLOCK]
            else:
                value = noise_ref[c // 3 - 1, c % 3, :, at:at + BLOCK]
            row = row_of(c, block % blocks, blocks, local)
            out_ref[block // blocks, row:row + local, :] = value


def first_kernel(
    shares, margin, listed, offset_ref, charge_ref, x_ref, message_ref, p_ref, pout_ref, coord_ref, *scratch
):
    _, local, atoms = x_ref.shape
    blocks = atoms // BLOCK
    each = blocks // shares
    edge = margin * BLOCK
    clear(coord_ref, local)
    for c in range(3):
        coord_ref[c, :local, 0:atoms] = x_ref[c]
        for part in range(2):
            coord_ref[c, :local, atoms + part * edge:atoms + (part + 1) * edge] = message_ref[3 * part + c]
    add_forces("whole", blocks, margin, listed, offset_ref, charge_ref, coord_ref, scratch)
    force_ref = scratch[FORCE]
    for c in range(3):
        for block in range(blocks):
            lanes = slice(block * BLOCK, (block + 1) * BLOCK)
            at = block * BLOCK + edge
            if at < atoms:
                moment = p_ref[c, :, at:at + BLOCK]
            else:
                moment = message_ref[6 + c, :, at - atoms:at - atoms + BLOCK]
            row = row_of(c, block % each, each, local)
            pout_ref[block // each, row:row + local, :] = moment + half_step * force_ref[c, :local, lanes]


def last_kernel(
    margin, listed, offset_ref, charge_ref, both_ref, message_ref, xout_ref, pout_ref, coord_ref, *scratch
):
    shares = both_ref.shape[0]
    _, local, atoms = xout_ref.shape
    blocks = atoms // BLOCK
    each = blocks // shares
    edge = margin * BLOCK

    def taken(c, block):
        row = row_of(c, block % each, each, local)
        return both_ref[block // each, row:row + local, :]

    clear(coord_ref, local)
    for c in range(3):
        for part in range(2):
            coord_ref[c, :local, part * edge:(part + 1) * edge] = message_ref[3 * part + c]
        for block in range(blocks):
            at = 2 * edge + block * BLOCK
            coord_ref[c, :local, at:at + BLOCK] = taken(c, block)
        xout_ref[c] = coord_ref[c, :local, edge:edge + atoms]
    add_forces("late", blocks, margin, listed, offset_ref, charge_ref, coord_ref, scratch)
    force_ref = scratch[FORCE]
    for c in range(3):
        for block in range(blocks):
            lanes = slice(block * BLOCK, (block + 1) * BLOCK)
            moment = message_ref[6 + c, :, lanes] if block < margin else taken(3 + c, block - margin)
            pout_ref[c, :, lanes] = moment + half_step * force_ref[c, :local, lanes]


def thermostat(coords, moments, noises, mass_ref, matrix_ref, matrix_t_ref, table_ref, store):
    beads, width = moments[0].shape
    cosine, ratio, stiffness, damping, kick = [
        jnp.concatenate([table_ref[i]] * (width // BLOCK), axis=1) for i in range(5)
    ]
    mass = jnp.broadcast_to(mass_ref[...], (beads, width))
    spread = kick * jnp.sqrt(thermal * mass)
    drift = ratio / mass
    stiff = stiffness * mass
    multiply = functools.partial(jnp.dot, precision=lax.Precision.HIGHEST, preferred_element_type=f32)
    for c in range(3):
        mode_x = multiply(matrix_t_ref[...], coords[c])
        mode_p = damping * multiply(matrix_t_ref[...], moments[c]) + spread * noises[c]
        store(
            c,
            multiply(matrix_ref[...], cosine * mode_x + drift * mode_p),
            multiply(matrix_ref[...], cosine * mode_p - stiff * mode_x),
        )


def modes_kernel(
    blocks, noise_base, rest_ref, p_ref, mass_ref, matrix_ref, matrix_t_ref, table_ref,
    xout_ref, pout_ref, coord_ref, moment_ref, noise_ref,
):
    local = p_ref.shape[1] // (3 * blocks)
    unpack_beads(rest_ref, 0, blocks, local, coord_ref, 0)
    unpack_beads(p_ref, 0, blocks, local, moment_ref, 0)
    unpack_beads(rest_ref, noise_base, blocks, local, noise_ref, 0)

    def store(c, x, p):
        pack_beads(x, c, blocks, local, xout_ref)
        pack_beads(p, c, blocks, local, pout_ref)

    thermostat(
        *[[ref[c] for c in range(3)] for ref in (coord_ref, moment_ref, noise_ref)],
        mass_ref, matrix_ref, matrix_t_ref, table_ref, store,
    )


def middle_kernel(hops, blocks, listed, noise_base, joined, offset_ref, charge_ref, *refs):
    parts = 2 * hops + 1
    x_refs = refs[:parts]
    p_ref, noise_ref, mass_ref, matrix_ref, matrix_t_ref, table_ref = refs[parts:parts + 6]
    outs = refs[parts + 6:parts + (7 if joined else 8)]
    coord_ref, *scratch = refs[parts + len(outs) + 6:]
    beads = coord_ref.shape[1]
    local = beads // p_ref.shape[0]
    width = blocks * BLOCK
    for part in range(parts):
        unpack_beads(x_refs[part], 0, blocks, local, coord_ref, part * width)
    add_forces("late", blocks, hops * blocks, listed, offset_ref, charge_ref, coord_ref, scratch)
    force_ref = scratch[FORCE]
    unpack_beads(p_ref, 0, blocks, local, coord_ref, 0)
    unpack_beads(noise_ref, noise_base, blocks, local, coord_ref, (parts - 1) * width)

    def share(c, part):
        return coord_ref[c, :, part * width:(part + 1) * width]

    def store(c, x, p):
        pack_beads(x, c, blocks, local, outs[0])
        if joined:
            pack_beads(p, 3 + c, blocks, local, outs[0])
        else:
            pack_beads(p, c, blocks, local, outs[1])

    thermostat(
        [share(c, hops) for c in range(3)],
        [share(c, 0) + 2.0 * half_step * force_ref[c] for c in range(3)],
        [share(c, parts - 1) for c in range(3)],
        mass_ref, matrix_ref, matrix_t_ref, table_ref, store,
    )


def fold(count):
    return [i // 2 if i % 2 == 0 else count - 1 - i // 2 for i in range(count)]


def exchange(pieces):
    order = fold(pieces.shape[0])
    group = [order.index(at) for at in range(len(order))]
    return lax.all_to_all(pieces, "bead", split_axis=0, concat_axis=0, axis_index_groups=[group], tiled=True)


def passed(values, step):
    count = lax.axis_size("space")
    return lax.ppermute(values, "space", [(i, (i + step) % count) for i in range(count)])


def window(values, hops):
    count = lax.axis_size("bead")
    domains = lax.axis_size("space")
    order = fold(count)
    device = {}
    for bead in range(count):
        for domain in range(domains):
            device[domain * count + order[bead]] = bead * domains + domain
    total = count * domains
    out = []
    for hop in range(-hops, hops + 1):
        if hop == 0:
            out.append(values)
        else:
            route = [(device[(at + hop) % total], device[at]) for at in range(total)]
            out.append(lax.ppermute(values, ("bead", "space"), route))
    return out


def body(positions, momenta, atom_types, neighbours, thermal_noise):
    count = lax.axis_size("bead")
    _, local, atoms = positions.shape
    beads = local * count
    domain = atoms // BLOCK
    blocks = domain // count
    share = blocks * BLOCK
    hops = -(-HALO // blocks)
    margin = hops * blocks
    edge = margin * BLOCK
    steps = thermal_noise.shape[0]
    listed = neighbours.shape[1]
    order = fold(count)

    own = lax.axis_index("space") * domain + jnp.arange(domain, dtype=jnp.int32)
    offsets = jnp.clip(neighbours - own[:, None], -margin, margin).reshape(-1)
    sent = jnp.pad(offsets[:margin * listed].astype(f32), (0, edge - margin * listed))[None, :]

    message, charge, mass = call(
        message_kernel, (positions, momenta, thermal_noise, atom_types[None, :], sent), 0,
        [(13 + 3 * steps, local, edge), (1, atoms), (1, atoms)], [], 0,
        [
            pl.BlockSpec(shape, lambda i, rank=len(shape): (0,) * rank)
            for shape in (
                (3, local, 2 * edge), (3, local, edge), (steps, 3, local, edge), (1, atoms), (1, edge)
            )
        ],
    )
    message = passed(message, -1)
    side = message[9 + 3 * steps:, 0]
    first_charge = jnp.concatenate([charge, side[:1], side[1:2]], axis=1)
    moved_mass = jnp.concatenate([mass[0, edge:], side[2]])
    moved_offsets = jnp.concatenate([offsets[margin * listed:], side[3, :margin * listed].astype(jnp.int32)])
    (rest,) = call(
        functools.partial(pack_kernel, blocks), (positions, thermal_noise, message), 0,
        [(count, (3 + 3 * steps) * blocks * local, BLOCK)], [], 0,
    )
    rest = exchange(rest)

    place = jnp.asarray(np.array(order, np.int32))[lax.axis_index("bead")]
    near_charge = lax.dynamic_slice_in_dim(first_charge, place * share, share + 2 * edge, axis=1)
    near_mass = lax.dynamic_slice_in_dim(moved_mass, place * share, share)[None, :]
    near_offsets = lax.dynamic_slice_in_dim(moved_offsets, place * blocks * listed, blocks * listed)

    matrix, tables = mode_constants(beads)
    at = np.concatenate([order.index(g) * local + np.arange(local) for g in range(count)])
    matrix = matrix[at][:, at]
    fixed = (near_mass, jnp.asarray(matrix), jnp.asarray(np.ascontiguousarray(matrix.T)), jnp.asarray(tables[:, at]))

    packed = (count, 3 * blocks * local, BLOCK)
    pairs = beads * blocks * listed * BLOCK * BLOCK
    (moment,) = call(
        functools.partial(first_kernel, count, margin, listed),
        (moved_offsets, first_charge, positions, message, momenta), 1, [packed],
        force_scratch(local, domain, margin, listed), pairs,
    )
    moment, rest = lax.optimization_barrier((moment, rest))
    coords, moment = call(
        functools.partial(modes_kernel, blocks, 3), (rest, exchange(moment)) + fixed, 0, [packed] * 2,
        [pltpu.VMEM((3, beads, share), f32)] * 3, 0,
    )
    for step in range(1, steps):
        joined = step == steps - 1
        out = call(
            functools.partial(middle_kernel, hops, blocks, listed, 3 * step + 3, joined),
            (near_offsets, near_charge) + tuple(window(coords, hops)) + (moment, rest) + fixed, 1,
            [(count, 6 * blocks * local, BLOCK)] if joined else [packed] * 2,
            force_scratch(beads, blocks, margin, listed), pairs,
        )
        if not joined:
            coords, moment = out
    both = exchange(out[0])

    def ends(low, c):
        pieces = both[low:low + hops, c * packed[1]:(c + 1) * packed[1]]
        return pieces.reshape(hops, 3, blocks, local, BLOCK).transpose(1, 3, 0, 2, 4).reshape(3, local, edge)

    message = passed(jnp.concatenate([
        ends(count - 2 * hops, 0), ends(count - hops, 0), ends(count - hops, 1),
        jnp.broadcast_to(charge[:, None, atoms - edge:], (1, local, edge)),
    ], axis=0), 1)
    last_charge = jnp.concatenate([message[9, 0], first_charge[0, :atoms + edge]])[None, :]
    return tuple(call(
        functools.partial(last_kernel, margin, listed), (offsets, last_charge, both, message), 1,
        [(3, local, atoms)] * 2, force_scratch(local, domain, margin, listed), pairs,
    ))


def solution(mesh):
    placed = (
        P(None, "bead", "space"),
        P(None, "bead", "space"),
        P("space"),
        P("space", None),
        P(None, None, "bead", "space"),
    )
    return jax.shard_map(
        body,
        mesh=mesh,
        in_specs=placed,
        out_specs=(P(None, "bead", "space"), P(None, "bead", "space")),
        check_vma=False,
    )
```

```python
import functools
import math

import jax
import jax.numpy as jnp
import numpy as np
from jax import lax
from jax.experimental import pallas as pl
from jax.experimental.pallas import tpu as pltpu
from jax.sharding import PartitionSpec as P

BLOCK = 128
HALO = 4

half_step = 0.025
time_step = 0.05
chain_freq = 12.0
thermal = 0.375
centroid_friction = 1.0
screening = 4.0
softening = 0.09
CHARGES = (1.0, -1.0, 0.6, -1.4)
MASSES = (1.0, 2.0, 3.0, 4.0)

PAIR_ROWS = 24
PAIR_PAD = 32
SUM_ROWS = 16
QUAD = 4
PASS = 32
FRAME = 8
f32 = jnp.float32
bf16 = jnp.bfloat16


def mode_constants(bead_total):
    j = np.arange(bead_total)[:, None]
    k = np.arange(bead_total)[None, :]
    half = bead_total // 2
    phase = 2.0 * np.pi * ((j * k) % bead_total) / bead_total
    plain = 1.0 / math.sqrt(bead_total)
    paired = math.sqrt(2.0 / bead_total)
    matrix = np.where(
        k == 0,
        plain,
        np.where(
            k < half,
            paired * np.cos(phase),
            np.where(k == half, plain * np.cos(phase), paired * np.sin(phase)),
        ),
    )
    modes = np.arange(bead_total)
    frequency = 2.0 * chain_freq * np.sin(np.pi * modes / bead_total)
    angle = frequency * time_step
    ratio = np.where(modes == 0, time_step, np.sin(angle) / np.where(modes == 0, 1.0, frequency))
    friction = np.where(modes == 0, centroid_friction, 2.0 * frequency)
    damping = np.exp(-friction * time_step)
    kick = np.sqrt(1.0 - damping * damping)
    tables = np.stack([np.cos(angle), ratio, frequency * np.sin(angle), damping, kick])
    tables = np.broadcast_to(tables[:, :, None], tables.shape + (BLOCK,))
    return matrix.astype(np.float32), np.ascontiguousarray(tables).astype(np.float32)


def split3(v):
    one = v.astype(bf16).astype(f32)
    rest = v - one
    two = rest.astype(bf16).astype(f32)
    three = (rest - two).astype(bf16).astype(f32)
    return one, two, three


def pair_rows(coords, norm, own):
    rows = []
    for v in coords:
        one, two, three = split3(v)
        if own:
            one, two, three = -2.0 * one, -2.0 * two, -2.0 * three
            rows += [one, one, two, two, one, three]
        else:
            rows += [one, two, one, two, three, one]
    ones = [jnp.ones_like(norm)] * 3
    norms = list(split3(norm))
    return rows + (norms + ones if own else ones + norms)


SCALE = 1.0 / (screening * math.log(2.0))


def weigh(square):
    inverse = lax.rsqrt(square)
    decay = jnp.exp2(-(square * inverse))
    return decay * ((inverse * inverse) * (inverse + math.log(2.0)))


def whole_quads(beads):
    return -(-beads // QUAD) * QUAD


def add_forces(form, blocks, margin, listed, offset_ref, charge_ref, coord_ref, scratch):
    rows_ref, sums_ref, far_ref, heavy_ref, near_ref, total_ref, force_ref, *buffers = scratch
    square_refs, weight_refs = buffers[:2], buffers[2:]
    beads = coord_ref.shape[1]
    pairs = beads // 2
    frame = min(FRAME, blocks)
    width = frame + 2 * margin
    middle = margin + (frame - 1) / 2.0
    at_once = max(1, 8 // beads)
    lines = at_once * beads
    units = blocks * pairs

    def put(ref, k, value):
        ref[k * lines:(k + 1) * lines, :] = value

    def centred(block, place):
        spans = [pl.ds(pl.multiple_of((block + i) * BLOCK, BLOCK), BLOCK) for i in range(at_once)]
        coords = [
            (jnp.concatenate([coord_ref[c, :, lanes] for lanes in spans], axis=0) - 1.0) * SCALE for c in range(3)
        ]
        shift = jnp.concatenate(
            [jnp.full((beads, BLOCK), SCALE, f32) * ((place + i).astype(f32) - middle) for i in range(at_once)], axis=0
        )
        coords[0] = coords[0] + shift
        norm = coords[0] * coords[0] + coords[1] * coords[1] + coords[2] * coords[2]
        charge = jnp.concatenate(
            [jnp.broadcast_to(charge_ref[:, lanes], (beads, BLOCK)) for lanes in spans], axis=0
        )
        return coords, norm, charge

    nothing = jnp.zeros((lines, BLOCK), f32)
    for k in range(PAIR_ROWS, PAIR_PAD):
        put(rows_ref, k, nothing)
    for k in range(12, SUM_ROWS):
        put(sums_ref, k, nothing)
    blank = jnp.zeros((PAIR_PAD, BLOCK), f32)

    def one_frame(at_frame, carry):
        first = at_frame * frame

        def one_table(step, inner):
            place = step * at_once
            coords, norm, charge = centred(first + place, place)
            for k, row in enumerate(pair_rows(coords, norm, False)):
                put(rows_ref, k, row)
            for c, v in enumerate([charge] + [charge * x for x in coords]):
                for level, part in enumerate(split3(v)):
                    put(sums_ref, level * 4 + c, part)
            for i in range(at_once):
                at = at_frame * width + place + i
                for quad in range(beads // QUAD):
                    low = i * beads + quad * QUAD
                    four = jnp.concatenate(
                        [rows_ref[pl.ds(low + j, PAIR_PAD, stride=lines), :] for j in range(QUAD)], axis=0
                    )
                    far_ref[at, quad] = jnp.transpose(four).astype(bf16)
                    for half in range(2):
                        heavy_ref[at, 2 * quad + half] = jnp.concatenate(
                            [
                                sums_ref[pl.ds(low + 2 * half + j, SUM_ROWS, stride=lines), :]
                                for j in range(2)
                            ],
                            axis=0,
                        ).astype(bf16)
            return inner

        lax.fori_loop(0, width // at_once, one_table, 0)

        def one_own(step, inner):
            block = step * at_once
            coords, norm, _ = centred(first + margin + block, block + margin)
            for k, row in enumerate(pair_rows(coords, norm + softening * SCALE * SCALE, True)):
                put(rows_ref, k, row)
            for i in range(at_once):
                for pair in range(pairs):
                    columns = []
                    for j in range(2):
                        own = rows_ref[pl.ds(i * beads + 2 * pair + j, PAIR_PAD, stride=lines), :]
                        spot = 2 * pair % QUAD + j
                        columns.append(
                            jnp.concatenate([own if k == spot else blank for k in range(QUAD)], axis=0)
                        )
                    near_ref[(first + block + i) * pairs + pair] = jnp.concatenate(columns, axis=1).astype(bf16)
            return inner

        lax.fori_loop(0, frame // at_once, one_own, 0)
        return carry

    lax.fori_loop(0, blocks // frame, one_frame, 0)

    def places(unit):
        block = unit // pairs
        at_frame = block // frame
        base = at_frame * width + block - at_frame * frame + margin
        return [base + offset_ref[block * listed + m] for m in range(listed)], unit - block * pairs

    def parts(square):
        weight = weigh(square)
        high = weight.astype(bf16)
        return high, (weight - high.astype(f32)).astype(bf16)

    def squares(ats, pair, unit, m):
        return jnp.dot(far_ref[ats[m], pair // (QUAD // 2)], near_ref[unit], preferred_element_type=f32)

    def weighted(at, pair, both):
        table = heavy_ref[at, pair]
        return jnp.dot(jnp.concatenate([table, table], axis=1), both, preferred_element_type=f32)

    def keep(total, slot):
        for i in range(2):
            cols = slice(i * BLOCK, (i + 1) * BLOCK)
            row = i * SUM_ROWS
            spot = pl.ds(pl.multiple_of((2 * slot + i) * 8, 8), 8)
            total_ref[spot, :] = total[row:row + 8, cols] + total[row + 8:row + 16, cols]

    def one_unit(unit, now, other):
        before = jnp.maximum(unit - 1, 0)
        ats, pair = places(unit)
        before_ats, before_pair = places(before)
        total = jnp.zeros((2 * SUM_ROWS, 2 * BLOCK), f32)
        for m in range(listed):
            spot = slice(2 * m * BLOCK, 2 * (m + 1) * BLOCK)
            weight_refs[now][spot, :] = jnp.concatenate(parts(squares(ats, pair, unit, m)), axis=0)
            total = total + weighted(before_ats[m], before_pair, weight_refs[other][spot, :])
        keep(total, jnp.where(unit == 0, units, unit - 1))

    def two_units(step, carry):
        one_unit(2 * step, 0, 1)
        one_unit(2 * step + 1, 1, 0)
        return carry

    tiles = units * listed

    def tile_place(tile):
        unit = tile // listed
        block = unit // pairs
        at_frame = block // frame
        base = at_frame * width + block - at_frame * frame + margin
        at = base + offset_ref[block * listed + tile - unit * listed]
        return at, unit - block * pairs, unit

    def tile_squares(tile, out):
        at, pair, unit = tile_place(tile)
        out[0:BLOCK, :] = jnp.dot(far_ref[at, pair // (QUAD // 2)], near_ref[unit], preferred_element_type=f32)

    def tile_sums(tile, weight_ref, slot):
        at, pair, _ = tile_place(tile)
        keep(weighted(at, pair, weight_ref[0:2 * BLOCK, :]), slot)

    def one_tile(tile, now, other):
        if form == "staged":
            tile_squares(jnp.minimum(tile + 1, tiles - 1), square_refs[other])
            for low in range(0, BLOCK, PASS):
                high, rest = parts(square_refs[now][low:low + PASS, :])
                weight_refs[now][low:low + PASS, :] = high
                weight_refs[now][BLOCK + low:BLOCK + low + PASS, :] = rest
        else:
            at, pair, unit = tile_place(tile)
            square = jnp.dot(far_ref[at, pair // (QUAD // 2)], near_ref[unit], preferred_element_type=f32)
            weight_refs[now][0:2 * BLOCK, :] = jnp.concatenate(parts(square), axis=0)
        tile_sums(jnp.maximum(tile - 1, 0), weight_refs[other], jnp.where(tile == 0, tiles, tile - 1))

    def two_tiles(step, carry):
        one_tile(2 * step, 0, 1)
        one_tile(2 * step + 1, 1, 0)
        return carry

    if form == "late":
        lax.fori_loop(0, units // 2, two_units, 0)
        last_ats, last_pair = places(units - 1)
        keep(
            sum(
                weighted(last_ats[m], last_pair, weight_refs[1][2 * m * BLOCK:2 * (m + 1) * BLOCK, :])
                for m in range(listed)
            ),
            units - 1,
        )
    else:
        if form == "staged":
            tile_squares(0, square_refs[0])
        lax.fori_loop(0, tiles // 2, two_tiles, 0)
        tile_sums(tiles - 1, weight_refs[1], tiles - 1)

    def one_block(block, carry):
        at_frame = block // frame
        place = block - at_frame * frame + margin
        lanes = pl.ds(pl.multiple_of((block + margin) * BLOCK, BLOCK), BLOCK)
        coords = [(coord_ref[c, :, lanes] - 1.0) * SCALE for c in range(3)]
        coords[0] = coords[0] + SCALE * (place.astype(f32) - middle)
        charge = jnp.broadcast_to(SCALE * SCALE * charge_ref[:, lanes], coords[0].shape)

        def summed(c):
            if form == "late":
                return sum(total_ref[pl.ds(block * beads * 8 + c + i, beads, stride=8), :] for i in (0, 4))
            low = block * pairs * listed * 16
            halves = [
                sum(
                    total_ref[pl.ds(low + m * 16 + bead * 8 + c + i, pairs, stride=listed * 16), :]
                    for m in range(listed) for i in (0, 4)
                )
                for bead in range(2)
            ]
            return jnp.stack(halves, axis=1).reshape(beads, BLOCK)

        near = summed(0)
        own = pl.ds(pl.multiple_of(block * BLOCK, BLOCK), BLOCK)
        for c in range(3):
            force_ref[c, :, own] = charge * (coords[c] * near - summed(c + 1))
        return carry

    lax.fori_loop(0, blocks, one_block, 0)


def force_scratch(local, blocks, margin, listed):
    beads = whole_quads(local)
    frame = min(FRAME, blocks)
    tables = (frame + 2 * margin) * (blocks // frame)
    lines = max(8, beads)
    units = blocks * beads // 2
    return [
        pltpu.VMEM((3, beads, (blocks + 2 * margin) * BLOCK), f32),
        pltpu.VMEM((PAIR_PAD * lines, BLOCK), f32),
        pltpu.VMEM((SUM_ROWS * lines, BLOCK), f32),
        pltpu.VMEM((tables, beads // QUAD, BLOCK, QUAD * PAIR_PAD), bf16),
        pltpu.VMEM((tables, beads // 2, 2 * SUM_ROWS, BLOCK), bf16),
        pltpu.VMEM((units, QUAD * PAIR_PAD, 2 * BLOCK), bf16),
        pltpu.VMEM(((units * listed + 1) * 16, BLOCK), f32),
        pltpu.VMEM((3, beads, blocks * BLOCK), f32),
        pltpu.VMEM((BLOCK, 2 * BLOCK), f32),
        pltpu.VMEM((BLOCK, 2 * BLOCK), f32),
        pltpu.VMEM((2 * listed * BLOCK, 2 * BLOCK), bf16),
        pltpu.VMEM((2 * listed * BLOCK, 2 * BLOCK), bf16),
    ]


def call(kernel, args, smem_count, shapes, scratch, work, in_specs=None):
    vmem = pl.BlockSpec(memory_space=pltpu.VMEM)
    smem = pl.BlockSpec(memory_space=pltpu.SMEM)
    return pl.pallas_call(
        kernel,
        out_shape=[jax.ShapeDtypeStruct(shape, f32) for shape in shapes],
        grid=() if in_specs is None else (1,),
        in_specs=in_specs or [smem] * smem_count + [vmem] * (len(args) - smem_count),
        out_specs=[vmem] * len(shapes),
        scratch_shapes=scratch,
        compiler_params=pltpu.CompilerParams(vmem_limit_bytes=(40 if in_specs is None else 62) * 1024 * 1024),
        cost_estimate=pl.CostEstimate(
            flops=20 * work + 1024, bytes_accessed=4 * 1024 * 1024, transcendentals=2 * work
        ),
    )(*args)


def row_of(c, block, blocks, local):
    return (c * blocks + block) * local


def unpack_beads(source, base, blocks, local, target, offset):
    for c in range(3):
        for block in range(blocks):
            row = row_of(base + c, block, blocks, local)
            lane = offset + block * BLOCK
            for group in range(source.shape[0]):
                target[c, group * local:(group + 1) * local, lane:lane + BLOCK] = source[group, row:row + local, :]


def pack_beads(value, c, blocks, local, target):
    for block in range(blocks):
        row = row_of(c, block, blocks, local)
        for group in range(target.shape[0]):
            target[group, row:row + local, :] = value[
                group * local:(group + 1) * local, block * BLOCK:(block + 1) * BLOCK
            ]


FORCE = 6


def clear(coord_ref, local):
    if coord_ref.shape[1] != local:
        coord_ref[...] = jnp.zeros(coord_ref.shape, f32)


def message_kernel(x_ref, p_ref, noise_ref, types_ref, offsets_ref, message_ref, charge_ref, mass_ref):
    steps = noise_ref.shape[0]
    _, local, edge = message_ref.shape
    types = types_ref[...]
    charge = jnp.zeros(types.shape, f32)
    mass = jnp.zeros(types.shape, f32)
    for kind in range(4):
        charge = jnp.where(types == kind, CHARGES[kind], charge)
        mass = jnp.where(types == kind, MASSES[kind], mass)
    charge_ref[...] = charge
    mass_ref[...] = mass
    for c in range(3):
        message_ref[c] = x_ref[c, :, :edge]
        message_ref[3 + c] = x_ref[c, :, edge:2 * edge]
        message_ref[6 + c] = p_ref[c, :, :edge]
        for step in range(steps):
            message_ref[9 + 3 * step + c] = noise_ref[step, c, :, :edge]
    at = 9 + 3 * steps
    for i, row in enumerate([charge[:, :edge], charge[:, edge:2 * edge], mass[:, :edge], offsets_ref[...]]):
        message_ref[at + i] = jnp.broadcast_to(row, (local, edge))


def pack_kernel(blocks, x_ref, noise_ref, message_ref, out_ref):
    steps = noise_ref.shape[0]
    _, local, edge = message_ref.shape
    atoms = x_ref.shape[2]
    for c in range(3 + 3 * steps):
        for block in range(atoms // BLOCK):
            at = edge + block * BLOCK
            if at >= atoms:
                value = message_ref[c if c < 3 else 6 + c, :, at - atoms:at - atoms + BLOCK]
            elif c < 3:
                value = x_ref[c, :, at:at + BLOCK]
            else:
                value = noise_ref[c // 3 - 1, c % 3, :, at:at + BLOCK]
            row = row_of(c, block % blocks, blocks, local)
            out_ref[block // blocks, row:row + local, :] = value


def first_kernel(
    shares, margin, listed, offset_ref, charge_ref, x_ref, message_ref, p_ref, pout_ref, coord_ref, *scratch
):
    _, local, atoms = x_ref.shape
    blocks = atoms // BLOCK
    each = blocks // shares
    edge = margin * BLOCK
    clear(coord_ref, local)
    for c in range(3):
        coord_ref[c, :local, 0:atoms] = x_ref[c]
        for part in range(2):
            coord_ref[c, :local, atoms + part * edge:atoms + (part + 1) * edge] = message_ref[3 * part + c]
    add_forces("staged", blocks, margin, listed, offset_ref, charge_ref, coord_ref, scratch)
    force_ref = scratch[FORCE]
    for c in range(3):
        for block in range(blocks):
            lanes = slice(block * BLOCK, (block + 1) * BLOCK)
            at = block * BLOCK + edge
            if at < atoms:
                moment = p_ref[c, :, at:at + BLOCK]
            else:
                moment = message_ref[6 + c, :, at - atoms:at - atoms + BLOCK]
            row = row_of(c, block % each, each, local)
            pout_ref[block // each, row:row + local, :] = moment + half_step * force_ref[c, :local, lanes]


def last_kernel(
    margin, listed, offset_ref, charge_ref, both_ref, message_ref, xout_ref, pout_ref, coord_ref, *scratch
):
    shares = both_ref.shape[0]
    _, local, atoms = xout_ref.shape
    blocks = atoms // BLOCK
    each = blocks // shares
    edge = margin * BLOCK

    def taken(c, block):
        row = row_of(c, block % each, each, local)
        return both_ref[block // each, row:row + local, :]

    clear(coord_ref, local)
    for c in range(3):
        for part in range(2):
            coord_ref[c, :local, part * edge:(part + 1) * edge] = message_ref[3 * part + c]
        for block in range(blocks):
            at = 2 * edge + block * BLOCK
            coord_ref[c, :local, at:at + BLOCK] = taken(c, block)
        xout_ref[c] = coord_ref[c, :local, edge:edge + atoms]
    add_forces("straight", blocks, margin, listed, offset_ref, charge_ref, coord_ref, scratch)
    force_ref = scratch[FORCE]
    for c in range(3):
        for block in range(blocks):
            lanes = slice(block * BLOCK, (block + 1) * BLOCK)
            moment = message_ref[6 + c, :, lanes] if block < margin else taken(3 + c, block - margin)
            pout_ref[c, :, lanes] = moment + half_step * force_ref[c, :local, lanes]


def thermostat(coords, moments, noises, mass_ref, matrix_ref, matrix_t_ref, table_ref, store):
    beads, width = moments[0].shape
    cosine, ratio, stiffness, damping, kick = [
        jnp.concatenate([table_ref[i]] * (width // BLOCK), axis=1) for i in range(5)
    ]
    mass = jnp.broadcast_to(mass_ref[...], (beads, width))
    spread = kick * jnp.sqrt(thermal * mass)
    drift = ratio / mass
    stiff = stiffness * mass
    multiply = functools.partial(jnp.dot, precision=lax.Precision.HIGHEST, preferred_element_type=f32)
    for c in range(3):
        mode_x = multiply(matrix_t_ref[...], coords[c])
        mode_p = damping * multiply(matrix_t_ref[...], moments[c]) + spread * noises[c]
        store(
            c,
            multiply(matrix_ref[...], cosine * mode_x + drift * mode_p),
            multiply(matrix_ref[...], cosine * mode_p - stiff * mode_x),
        )


def modes_kernel(
    blocks, noise_base, rest_ref, p_ref, mass_ref, matrix_ref, matrix_t_ref, table_ref,
    xout_ref, pout_ref, coord_ref, moment_ref, noise_ref,
):
    local = p_ref.shape[1] // (3 * blocks)
    unpack_beads(rest_ref, 0, blocks, local, coord_ref, 0)
    unpack_beads(p_ref, 0, blocks, local, moment_ref, 0)
    unpack_beads(rest_ref, noise_base, blocks, local, noise_ref, 0)

    def store(c, x, p):
        pack_beads(x, c, blocks, local, xout_ref)
        pack_beads(p, c, blocks, local, pout_ref)

    thermostat(
        *[[ref[c] for c in range(3)] for ref in (coord_ref, moment_ref, noise_ref)],
        mass_ref, matrix_ref, matrix_t_ref, table_ref, store,
    )


def middle_kernel(hops, blocks, listed, noise_base, joined, offset_ref, charge_ref, *refs):
    parts = 2 * hops + 1
    x_refs = refs[:parts]
    p_ref, noise_ref, mass_ref, matrix_ref, matrix_t_ref, table_ref = refs[parts:parts + 6]
    outs = refs[parts + 6:parts + (7 if joined else 8)]
    coord_ref, *scratch = refs[parts + len(outs) + 6:]
    beads = coord_ref.shape[1]
    local = beads // p_ref.shape[0]
    width = blocks * BLOCK
    for part in range(parts):
        unpack_beads(x_refs[part], 0, blocks, local, coord_ref, part * width)
    add_forces("late", blocks, hops * blocks, listed, offset_ref, charge_ref, coord_ref, scratch)
    force_ref = scratch[FORCE]
    unpack_beads(p_ref, 0, blocks, local, coord_ref, 0)
    unpack_beads(noise_ref, noise_base, blocks, local, coord_ref, (parts - 1) * width)

    def share(c, part):
        return coord_ref[c, :, part * width:(part + 1) * width]

    def store(c, x, p):
        pack_beads(x, c, blocks, local, outs[0])
        if joined:
            pack_beads(p, 3 + c, blocks, local, outs[0])
        else:
            pack_beads(p, c, blocks, local, outs[1])

    thermostat(
        [share(c, hops) for c in range(3)],
        [share(c, 0) + 2.0 * half_step * force_ref[c] for c in range(3)],
        [share(c, parts - 1) for c in range(3)],
        mass_ref, matrix_ref, matrix_t_ref, table_ref, store,
    )


def fold(count):
    return [i // 2 if i % 2 == 0 else count - 1 - i // 2 for i in range(count)]


def exchange(pieces):
    order = fold(pieces.shape[0])
    group = [order.index(at) for at in range(len(order))]
    return lax.all_to_all(pieces, "bead", split_axis=0, concat_axis=0, axis_index_groups=[group], tiled=True)


def passed(values, step):
    count = lax.axis_size("space")
    return lax.ppermute(values, "space", [(i, (i + step) % count) for i in range(count)])


def window(values, hops):
    count = lax.axis_size("bead")
    domains = lax.axis_size("space")
    order = fold(count)
    device = {}
    for bead in range(count):
        for domain in range(domains):
            device[domain * count + order[bead]] = bead * domains + domain
    total = count * domains
    out = []
    for hop in range(-hops, hops + 1):
        if hop == 0:
            out.append(values)
        else:
            route = [(device[(at + hop) % total], device[at]) for at in range(total)]
            out.append(lax.ppermute(values, ("bead", "space"), route))
    return out


def body(positions, momenta, atom_types, neighbours, thermal_noise):
    count = lax.axis_size("bead")
    _, local, atoms = positions.shape
    beads = local * count
    domain = atoms // BLOCK
    blocks = domain // count
    share = blocks * BLOCK
    hops = -(-HALO // blocks)
    margin = hops * blocks
    edge = margin * BLOCK
    steps = thermal_noise.shape[0]
    listed = neighbours.shape[1]
    order = fold(count)

    own = lax.axis_index("space") * domain + jnp.arange(domain, dtype=jnp.int32)
    offsets = jnp.clip(neighbours - own[:, None], -margin, margin).reshape(-1)
    sent = jnp.pad(offsets[:margin * listed].astype(f32), (0, edge - margin * listed))[None, :]

    message, charge, mass = call(
        message_kernel, (positions, momenta, thermal_noise, atom_types[None, :], sent), 0,
        [(13 + 3 * steps, local, edge), (1, atoms), (1, atoms)], [], 0,
        [
            pl.BlockSpec(shape, lambda i, rank=len(shape): (0,) * rank)
            for shape in (
                (3, local, 2 * edge), (3, local, edge), (steps, 3, local, edge), (1, atoms), (1, edge)
            )
        ],
    )
    message = passed(message, -1)
    side = message[9 + 3 * steps:, 0]
    first_charge = jnp.concatenate([charge, side[:1], side[1:2]], axis=1)
    moved_mass = jnp.concatenate([mass[0, edge:], side[2]])
    moved_offsets = jnp.concatenate([offsets[margin * listed:], side[3, :margin * listed].astype(jnp.int32)])
    (rest,) = call(
        functools.partial(pack_kernel, blocks), (positions, thermal_noise, message), 0,
        [(count, (3 + 3 * steps) * blocks * local, BLOCK)], [], 0,
    )
    rest = exchange(rest)

    place = jnp.asarray(np.array(order, np.int32))[lax.axis_index("bead")]
    near_charge = lax.dynamic_slice_in_dim(first_charge, place * share, share + 2 * edge, axis=1)
    near_mass = lax.dynamic_slice_in_dim(moved_mass, place * share, share)[None, :]
    near_offsets = lax.dynamic_slice_in_dim(moved_offsets, place * blocks * listed, blocks * listed)

    matrix, tables = mode_constants(beads)
    at = np.concatenate([order.index(g) * local + np.arange(local) for g in range(count)])
    matrix = matrix[at][:, at]
    fixed = (near_mass, jnp.asarray(matrix), jnp.asarray(np.ascontiguousarray(matrix.T)), jnp.asarray(tables[:, at]))

    packed = (count, 3 * blocks * local, BLOCK)
    pairs = beads * blocks * listed * BLOCK * BLOCK
    (moment,) = call(
        functools.partial(first_kernel, count, margin, listed),
        (moved_offsets, first_charge, positions, message, momenta), 1, [packed],
        force_scratch(local, domain, margin, listed), pairs,
    )
    moment, rest = lax.optimization_barrier((moment, rest))
    coords, moment = call(
        functools.partial(modes_kernel, blocks, 3), (rest, exchange(moment)) + fixed, 0, [packed] * 2,
        [pltpu.VMEM((3, beads, share), f32)] * 3, 0,
    )
    for step in range(1, steps):
        joined = step == steps - 1
        out = call(
            functools.partial(middle_kernel, hops, blocks, listed, 3 * step + 3, joined),
            (near_offsets, near_charge) + tuple(window(coords, hops)) + (moment, rest) + fixed, 1,
            [(count, 6 * blocks * local, BLOCK)] if joined else [packed] * 2,
            force_scratch(beads, blocks, margin, listed), pairs,
        )
        if not joined:
            coords, moment = out
    both = exchange(out[0])

    def ends(low, c):
        pieces = both[low:low + hops, c * packed[1]:(c + 1) * packed[1]]
        return pieces.reshape(hops, 3, blocks, local, BLOCK).transpose(1, 3, 0, 2, 4).reshape(3, local, edge)

    message = passed(jnp.concatenate([
        ends(count - 2 * hops, 0), ends(count - hops, 0), ends(count - hops, 1),
        jnp.broadcast_to(charge[:, None, atoms - edge:], (1, local, edge)),
    ], axis=0), 1)
    last_charge = jnp.concatenate([message[9, 0], first_charge[0, :atoms + edge]])[None, :]
    return tuple(call(
        functools.partial(last_kernel, margin, listed), (offsets, last_charge, both, message), 1,
        [(3, local, atoms)] * 2, force_scratch(local, domain, margin, listed), pairs,
    ))


def solution(mesh):
    placed = (
        P(None, "bead", "space"),
        P(None, "bead", "space"),
        P("space"),
        P("space", None),
        P(None, None, "bead", "space"),
    )
    return jax.shard_map(
        body,
        mesh=mesh,
        in_specs=placed,
        out_specs=(P(None, "bead", "space"), P(None, "bead", "space")),
        check_vma=False,
    )
```

```python
import functools
import math

import jax
import jax.numpy as jnp
import numpy as np
from jax import lax
from jax.experimental import pallas as pl
from jax.experimental.pallas import tpu as pltpu
from jax.sharding import PartitionSpec as P

BLOCK = 128
HALO = 4

half_step = 0.025
time_step = 0.05
chain_freq = 12.0
thermal = 0.375
centroid_friction = 1.0
screening = 4.0
softening = 0.09
CHARGES = (1.0, -1.0, 0.6, -1.4)
MASSES = (1.0, 2.0, 3.0, 4.0)

PAIR_ROWS = 24
PAIR_PAD = 32
SUM_ROWS = 16
QUAD = 4
FRAME = 8
f32 = jnp.float32
bf16 = jnp.bfloat16


def mode_constants(bead_total):
    j = np.arange(bead_total)[:, None]
    k = np.arange(bead_total)[None, :]
    half = bead_total // 2
    phase = 2.0 * np.pi * ((j * k) % bead_total) / bead_total
    plain = 1.0 / math.sqrt(bead_total)
    paired = math.sqrt(2.0 / bead_total)
    matrix = np.where(
        k == 0,
        plain,
        np.where(
            k < half,
            paired * np.cos(phase),
            np.where(k == half, plain * np.cos(phase), paired * np.sin(phase)),
        ),
    )
    modes = np.arange(bead_total)
    frequency = 2.0 * chain_freq * np.sin(np.pi * modes / bead_total)
    angle = frequency * time_step
    ratio = np.where(modes == 0, time_step, np.sin(angle) / np.where(modes == 0, 1.0, frequency))
    friction = np.where(modes == 0, centroid_friction, 2.0 * frequency)
    damping = np.exp(-friction * time_step)
    kick = np.sqrt(1.0 - damping * damping)
    tables = np.stack([np.cos(angle), ratio, frequency * np.sin(angle), damping, kick])
    tables = np.broadcast_to(tables[:, :, None], tables.shape + (BLOCK,))
    return matrix.astype(np.float32), np.ascontiguousarray(tables).astype(np.float32)


def split3(v):
    one = v.astype(bf16).astype(f32)
    rest = v - one
    two = rest.astype(bf16).astype(f32)
    three = (rest - two).astype(bf16).astype(f32)
    return one, two, three


def pair_rows(coords, norm, own):
    rows = []
    for v in coords:
        one, two, three = split3(v)
        if own:
            one, two, three = -2.0 * one, -2.0 * two, -2.0 * three
            rows += [one, one, two, two, one, three]
        else:
            rows += [one, two, one, two, three, one]
    ones = [jnp.ones_like(norm)] * 3
    norms = list(split3(norm))
    return rows + (norms + ones if own else ones + norms)


SCALE = 1.0 / (screening * math.log(2.0))


def weigh(square):
    inverse = lax.rsqrt(square)
    decay = jnp.exp2(-(square * inverse))
    return decay * ((inverse * inverse) * (inverse + math.log(2.0)))


def whole_quads(beads):
    return -(-beads // QUAD) * QUAD


def add_forces(group, ahead, blocks, margin, listed, offset_ref, charge_ref, coord_ref, scratch):
    rows_ref, sums_ref, far_ref, heavy_ref, near_ref, total_ref, force_ref, *buffers = scratch
    ahead_ref, *weight_refs = buffers
    beads = coord_ref.shape[1]
    pairs = beads // 2
    frame = min(FRAME, blocks)
    width = frame + 2 * margin
    middle = margin + (frame - 1) / 2.0
    at_once = max(1, 8 // beads)
    lines = at_once * beads
    units = blocks * pairs

    def put(ref, k, value):
        ref[k * lines:(k + 1) * lines, :] = value

    def centred(block, place):
        spans = [pl.ds(pl.multiple_of((block + i) * BLOCK, BLOCK), BLOCK) for i in range(at_once)]
        coords = [
            (jnp.concatenate([coord_ref[c, :, lanes] for lanes in spans], axis=0) - 1.0) * SCALE for c in range(3)
        ]
        shift = jnp.concatenate(
            [jnp.full((beads, BLOCK), SCALE, f32) * ((place + i).astype(f32) - middle) for i in range(at_once)], axis=0
        )
        coords[0] = coords[0] + shift
        norm = coords[0] * coords[0] + coords[1] * coords[1] + coords[2] * coords[2]
        charge = jnp.concatenate(
            [jnp.broadcast_to(charge_ref[:, lanes], (beads, BLOCK)) for lanes in spans], axis=0
        )
        return coords, norm, charge

    nothing = jnp.zeros((lines, BLOCK), f32)
    for k in range(PAIR_ROWS, PAIR_PAD):
        put(rows_ref, k, nothing)
    for k in range(12, SUM_ROWS):
        put(sums_ref, k, nothing)
    blank = jnp.zeros((PAIR_PAD, BLOCK), f32)

    def one_frame(at_frame, carry):
        first = at_frame * frame

        def one_table(step, inner):
            place = step * at_once
            coords, norm, charge = centred(first + place, place)
            for k, row in enumerate(pair_rows(coords, norm, False)):
                put(rows_ref, k, row)
            for c, v in enumerate([charge] + [charge * x for x in coords]):
                for level, part in enumerate(split3(v)):
                    put(sums_ref, level * 4 + c, part)
            for i in range(at_once):
                at = at_frame * width + place + i
                for quad in range(beads // QUAD):
                    low = i * beads + quad * QUAD
                    four = jnp.concatenate(
                        [rows_ref[pl.ds(low + j, PAIR_PAD, stride=lines), :] for j in range(QUAD)], axis=0
                    )
                    far_ref[at, quad] = jnp.transpose(four).astype(bf16)
                    for half in range(2):
                        heavy_ref[at, 2 * quad + half] = jnp.concatenate(
                            [
                                sums_ref[pl.ds(low + 2 * half + j, SUM_ROWS, stride=lines), :]
                                for j in range(2)
                            ],
                            axis=0,
                        ).astype(bf16)
            return inner

        lax.fori_loop(0, width // at_once, one_table, 0)

        def one_own(step, inner):
            block = step * at_once
            coords, norm, _ = centred(first + margin + block, block + margin)
            for k, row in enumerate(pair_rows(coords, norm + softening * SCALE * SCALE, True)):
                put(rows_ref, k, row)
            for i in range(at_once):
                for pair in range(pairs):
                    columns = []
                    for j in range(2):
                        own = rows_ref[pl.ds(i * beads + 2 * pair + j, PAIR_PAD, stride=lines), :]
                        spot = 2 * pair % QUAD + j
                        columns.append(
                            jnp.concatenate([own if k == spot else blank for k in range(QUAD)], axis=0)
                        )
                    near_ref[(first + block + i) * pairs + pair] = jnp.concatenate(columns, axis=1).astype(bf16)
            return inner

        lax.fori_loop(0, frame // at_once, one_own, 0)
        return carry

    lax.fori_loop(0, blocks // frame, one_frame, 0)

    def places(unit):
        block = unit // pairs
        at_frame = block // frame
        base = at_frame * width + block - at_frame * frame + margin
        return [base + offset_ref[block * listed + m] for m in range(listed)], unit - block * pairs

    def parts(square):
        weight = weigh(square)
        high = weight.astype(bf16)
        return high, (weight - high.astype(f32)).astype(bf16)

    def squares(ats, pair, unit, m):
        return jnp.dot(far_ref[ats[m], pair // (QUAD // 2)], near_ref[unit], preferred_element_type=f32)

    def weighted(at, pair, both):
        table = heavy_ref[at, pair]
        return jnp.dot(jnp.concatenate([table, table], axis=1), both, preferred_element_type=f32)

    def keep(total, slot):
        for i in range(2):
            cols = slice(i * BLOCK, (i + 1) * BLOCK)
            row = i * SUM_ROWS
            spot = pl.ds(pl.multiple_of((2 * slot + i) * 8, 8), 8)
            total_ref[spot, :] = total[row:row + 8, cols] + total[row + 8:row + 16, cols]

    def body(step, carry):
        before_ats, before_pair = places(jnp.maximum(step * group - 1, 0))
        for turn in range(group):
            unit = step * group + turn
            now, other = turn % 2, (turn + 1) % 2
            ats, pair = places(unit)
            total = jnp.zeros((2 * SUM_ROWS, 2 * BLOCK), f32)
            for m in range(listed):
                spot = slice(2 * m * BLOCK, 2 * (m + 1) * BLOCK)
                square = ahead_ref[...] if ahead and turn == m == 0 else squares(ats, pair, unit, m)
                weight_refs[now][spot, :] = jnp.concatenate(parts(square), axis=0)
                total = total + weighted(before_ats[m], before_pair, weight_refs[other][spot, :])
            keep(total, jnp.where(unit == 0, units, unit - 1))
            before_ats, before_pair = ats, pair
        if ahead:
            look(jnp.minimum((step + 1) * group, units - 1))
        return carry

    def look(unit):
        ats, pair = places(unit)
        ahead_ref[...] = squares(ats, pair, unit, 0)

    group = math.gcd(units, group)
    if ahead:
        look(0)
    lax.fori_loop(0, units // group, body, 0)
    last_ats, last_pair = places(units - 1)
    keep(
        sum(
            weighted(last_ats[m], last_pair, weight_refs[(group - 1) % 2][2 * m * BLOCK:2 * (m + 1) * BLOCK, :])
            for m in range(listed)
        ),
        units - 1,
    )

    def one_block(block, carry):
        at_frame = block // frame
        place = block - at_frame * frame + margin
        lanes = pl.ds(pl.multiple_of((block + margin) * BLOCK, BLOCK), BLOCK)
        coords = [(coord_ref[c, :, lanes] - 1.0) * SCALE for c in range(3)]
        coords[0] = coords[0] + SCALE * (place.astype(f32) - middle)
        charge = jnp.broadcast_to(SCALE * SCALE * charge_ref[:, lanes], coords[0].shape)

        def summed(c):
            return sum(total_ref[pl.ds(block * beads * 8 + c + i, beads, stride=8), :] for i in (0, 4))

        near = summed(0)
        own = pl.ds(pl.multiple_of(block * BLOCK, BLOCK), BLOCK)
        for c in range(3):
            force_ref[c, :, own] = charge * (coords[c] * near - summed(c + 1))
        return carry

    lax.fori_loop(0, blocks, one_block, 0)


def force_scratch(local, blocks, margin, listed):
    beads = whole_quads(local)
    frame = min(FRAME, blocks)
    tables = (frame + 2 * margin) * (blocks // frame)
    lines = max(8, beads)
    units = blocks * beads // 2
    return [
        pltpu.VMEM((3, beads, (blocks + 2 * margin) * BLOCK), f32),
        pltpu.VMEM((PAIR_PAD * lines, BLOCK), f32),
        pltpu.VMEM((SUM_ROWS * lines, BLOCK), f32),
        pltpu.VMEM((tables, beads // QUAD, BLOCK, QUAD * PAIR_PAD), bf16),
        pltpu.VMEM((tables, beads // 2, 2 * SUM_ROWS, BLOCK), bf16),
        pltpu.VMEM((units, QUAD * PAIR_PAD, 2 * BLOCK), bf16),
        pltpu.VMEM(((units + 1) * 16, BLOCK), f32),
        pltpu.VMEM((3, beads, blocks * BLOCK), f32),
        pltpu.VMEM((BLOCK, 2 * BLOCK), f32),
        pltpu.VMEM((2 * listed * BLOCK, 2 * BLOCK), bf16),
        pltpu.VMEM((2 * listed * BLOCK, 2 * BLOCK), bf16),
    ]


def call(kernel, args, smem_count, shapes, scratch, work, in_specs=None):
    vmem = pl.BlockSpec(memory_space=pltpu.VMEM)
    smem = pl.BlockSpec(memory_space=pltpu.SMEM)
    return pl.pallas_call(
        kernel,
        out_shape=[jax.ShapeDtypeStruct(shape, f32) for shape in shapes],
        grid=() if in_specs is None else (1,),
        in_specs=in_specs or [smem] * smem_count + [vmem] * (len(args) - smem_count),
        out_specs=[vmem] * len(shapes),
        scratch_shapes=scratch,
        compiler_params=pltpu.CompilerParams(vmem_limit_bytes=(40 if in_specs is None else 62) * 1024 * 1024),
        cost_estimate=pl.CostEstimate(
            flops=20 * work + 1024, bytes_accessed=4 * 1024 * 1024, transcendentals=2 * work
        ),
    )(*args)


def row_of(c, block, blocks, local):
    return (c * blocks + block) * local


def unpack_beads(source, base, blocks, local, target, offset):
    for c in range(3):
        for block in range(blocks):
            row = row_of(base + c, block, blocks, local)
            lane = offset + block * BLOCK
            for group in range(source.shape[0]):
                target[c, group * local:(group + 1) * local, lane:lane + BLOCK] = source[group, row:row + local, :]


def pack_beads(value, c, blocks, local, target):
    for block in range(blocks):
        row = row_of(c, block, blocks, local)
        for group in range(target.shape[0]):
            target[group, row:row + local, :] = value[
                group * local:(group + 1) * local, block * BLOCK:(block + 1) * BLOCK
            ]


FORCE = 6


def clear(coord_ref, local):
    if coord_ref.shape[1] != local:
        coord_ref[...] = jnp.zeros(coord_ref.shape, f32)


def message_kernel(x_ref, p_ref, noise_ref, types_ref, offsets_ref, message_ref, charge_ref, mass_ref):
    steps = noise_ref.shape[0]
    _, local, edge = message_ref.shape
    types = types_ref[...]
    charge = jnp.zeros(types.shape, f32)
    mass = jnp.zeros(types.shape, f32)
    for kind in range(4):
        charge = jnp.where(types == kind, CHARGES[kind], charge)
        mass = jnp.where(types == kind, MASSES[kind], mass)
    charge_ref[...] = charge
    mass_ref[...] = mass
    for c in range(3):
        message_ref[c] = x_ref[c, :, :edge]
        message_ref[3 + c] = x_ref[c, :, edge:2 * edge]
        message_ref[6 + c] = p_ref[c, :, :edge]
        for step in range(steps):
            message_ref[9 + 3 * step + c] = noise_ref[step, c, :, :edge]
    at = 9 + 3 * steps
    for i, row in enumerate([charge[:, :edge], charge[:, edge:2 * edge], mass[:, :edge], offsets_ref[...]]):
        message_ref[at + i] = jnp.broadcast_to(row, (local, edge))


def pack_kernel(blocks, x_ref, noise_ref, message_ref, out_ref):
    steps = noise_ref.shape[0]
    _, local, edge = message_ref.shape
    atoms = x_ref.shape[2]
    for c in range(3 + 3 * steps):
        for block in range(atoms // BLOCK):
            at = edge + block * BLOCK
            if at >= atoms:
                value = message_ref[c if c < 3 else 6 + c, :, at - atoms:at - atoms + BLOCK]
            elif c < 3:
                value = x_ref[c, :, at:at + BLOCK]
            else:
                value = noise_ref[c // 3 - 1, c % 3, :, at:at + BLOCK]
            row = row_of(c, block % blocks, blocks, local)
            out_ref[block // blocks, row:row + local, :] = value


def first_kernel(
    shares, margin, listed, offset_ref, charge_ref, x_ref, message_ref, p_ref, pout_ref, coord_ref, *scratch
):
    _, local, atoms = x_ref.shape
    blocks = atoms // BLOCK
    each = blocks // shares
    edge = margin * BLOCK
    clear(coord_ref, local)
    for c in range(3):
        coord_ref[c, :local, 0:atoms] = x_ref[c]
        for part in range(2):
            coord_ref[c, :local, atoms + part * edge:atoms + (part + 1) * edge] = message_ref[3 * part + c]
    add_forces(4, False, blocks, margin, listed, offset_ref, charge_ref, coord_ref, scratch)
    force_ref = scratch[FORCE]
    for c in range(3):
        for block in range(blocks):
            lanes = slice(block * BLOCK, (block + 1) * BLOCK)
            at = block * BLOCK + edge
            if at < atoms:
                moment = p_ref[c, :, at:at + BLOCK]
            else:
                moment = message_ref[6 + c, :, at - atoms:at - atoms + BLOCK]
            row = row_of(c, block % each, each, local)
            pout_ref[block // each, row:row + local, :] = moment + half_step * force_ref[c, :local, lanes]


def last_kernel(
    margin, listed, offset_ref, charge_ref, both_ref, message_ref, xout_ref, pout_ref, coord_ref, *scratch
):
    shares = both_ref.shape[0]
    _, local, atoms = xout_ref.shape
    blocks = atoms // BLOCK
    each = blocks // shares
    edge = margin * BLOCK

    def taken(c, block):
        row = row_of(c, block % each, each, local)
        return both_ref[block // each, row:row + local, :]

    clear(coord_ref, local)
    for c in range(3):
        for part in range(2):
            coord_ref[c, :local, part * edge:(part + 1) * edge] = message_ref[3 * part + c]
        for block in range(blocks):
            at = 2 * edge + block * BLOCK
            coord_ref[c, :local, at:at + BLOCK] = taken(c, block)
        xout_ref[c] = coord_ref[c, :local, edge:edge + atoms]
    add_forces(8, False, blocks, margin, listed, offset_ref, charge_ref, coord_ref, scratch)
    force_ref = scratch[FORCE]
    for c in range(3):
        for block in range(blocks):
            lanes = slice(block * BLOCK, (block + 1) * BLOCK)
            moment = message_ref[6 + c, :, lanes] if block < margin else taken(3 + c, block - margin)
            pout_ref[c, :, lanes] = moment + half_step * force_ref[c, :local, lanes]


def thermostat(coords, moments, noises, mass_ref, matrix_ref, matrix_t_ref, table_ref, store):
    beads, width = moments[0].shape
    cosine, ratio, stiffness, damping, kick = [
        jnp.concatenate([table_ref[i]] * (width // BLOCK), axis=1) for i in range(5)
    ]
    mass = jnp.broadcast_to(mass_ref[...], (beads, width))
    spread = kick * jnp.sqrt(thermal * mass)
    drift = ratio / mass
    stiff = stiffness * mass
    multiply = functools.partial(jnp.dot, precision=lax.Precision.HIGHEST, preferred_element_type=f32)
    for c in range(3):
        mode_x = multiply(matrix_t_ref[...], coords[c])
        mode_p = damping * multiply(matrix_t_ref[...], moments[c]) + spread * noises[c]
        store(
            c,
            multiply(matrix_ref[...], cosine * mode_x + drift * mode_p),
            multiply(matrix_ref[...], cosine * mode_p - stiff * mode_x),
        )


def modes_kernel(
    blocks, noise_base, rest_ref, p_ref, mass_ref, matrix_ref, matrix_t_ref, table_ref,
    xout_ref, pout_ref, coord_ref, moment_ref, noise_ref,
):
    local = p_ref.shape[1] // (3 * blocks)
    unpack_beads(rest_ref, 0, blocks, local, coord_ref, 0)
    unpack_beads(p_ref, 0, blocks, local, moment_ref, 0)
    unpack_beads(rest_ref, noise_base, blocks, local, noise_ref, 0)

    def store(c, x, p):
        pack_beads(x, c, blocks, local, xout_ref)
        pack_beads(p, c, blocks, local, pout_ref)

    thermostat(
        *[[ref[c] for c in range(3)] for ref in (coord_ref, moment_ref, noise_ref)],
        mass_ref, matrix_ref, matrix_t_ref, table_ref, store,
    )


def middle_kernel(hops, blocks, listed, noise_base, joined, offset_ref, charge_ref, *refs):
    parts = 2 * hops + 1
    x_refs = refs[:parts]
    p_ref, noise_ref, mass_ref, matrix_ref, matrix_t_ref, table_ref = refs[parts:parts + 6]
    outs = refs[parts + 6:parts + (7 if joined else 8)]
    coord_ref, *scratch = refs[parts + len(outs) + 6:]
    beads = coord_ref.shape[1]
    local = beads // p_ref.shape[0]
    width = blocks * BLOCK
    for part in range(parts):
        unpack_beads(x_refs[part], 0, blocks, local, coord_ref, part * width)
    add_forces(4, True, blocks, hops * blocks, listed, offset_ref, charge_ref, coord_ref, scratch)
    force_ref = scratch[FORCE]
    unpack_beads(p_ref, 0, blocks, local, coord_ref, 0)
    unpack_beads(noise_ref, noise_base, blocks, local, coord_ref, (parts - 1) * width)

    def share(c, part):
        return coord_ref[c, :, part * width:(part + 1) * width]

    def store(c, x, p):
        pack_beads(x, c, blocks, local, outs[0])
        if joined:
            pack_beads(p, 3 + c, blocks, local, outs[0])
        else:
            pack_beads(p, c, blocks, local, outs[1])

    thermostat(
        [share(c, hops) for c in range(3)],
        [share(c, 0) + 2.0 * half_step * force_ref[c] for c in range(3)],
        [share(c, parts - 1) for c in range(3)],
        mass_ref, matrix_ref, matrix_t_ref, table_ref, store,
    )


def fold(count):
    return [i // 2 if i % 2 == 0 else count - 1 - i // 2 for i in range(count)]


def exchange(pieces):
    order = fold(pieces.shape[0])
    group = [order.index(at) for at in range(len(order))]
    return lax.all_to_all(pieces, "bead", split_axis=0, concat_axis=0, axis_index_groups=[group], tiled=True)


def passed(values, step):
    count = lax.axis_size("space")
    return lax.ppermute(values, "space", [(i, (i + step) % count) for i in range(count)])


def window(values, hops):
    count = lax.axis_size("bead")
    domains = lax.axis_size("space")
    order = fold(count)
    device = {}
    for bead in range(count):
        for domain in range(domains):
            device[domain * count + order[bead]] = bead * domains + domain
    total = count * domains
    out = []
    for hop in range(-hops, hops + 1):
        if hop == 0:
            out.append(values)
        else:
            route = [(device[(at + hop) % total], device[at]) for at in range(total)]
            out.append(lax.ppermute(values, ("bead", "space"), route))
    return out


def body(positions, momenta, atom_types, neighbours, thermal_noise):
    count = lax.axis_size("bead")
    _, local, atoms = positions.shape
    beads = local * count
    domain = atoms // BLOCK
    blocks = domain // count
    share = blocks * BLOCK
    hops = -(-HALO // blocks)
    margin = hops * blocks
    edge = margin * BLOCK
    steps = thermal_noise.shape[0]
    listed = neighbours.shape[1]
    order = fold(count)

    own = lax.axis_index("space") * domain + jnp.arange(domain, dtype=jnp.int32)
    offsets = jnp.clip(neighbours - own[:, None], -margin, margin).reshape(-1)
    sent = jnp.pad(offsets[:margin * listed].astype(f32), (0, edge - margin * listed))[None, :]

    message, charge, mass = call(
        message_kernel, (positions, momenta, thermal_noise, atom_types[None, :], sent), 0,
        [(13 + 3 * steps, local, edge), (1, atoms), (1, atoms)], [], 0,
        [
            pl.BlockSpec(shape, lambda i, rank=len(shape): (0,) * rank)
            for shape in (
                (3, local, 2 * edge), (3, local, edge), (steps, 3, local, edge), (1, atoms), (1, edge)
            )
        ],
    )
    message = passed(message, -1)
    side = message[9 + 3 * steps:, 0]
    first_charge = jnp.concatenate([charge, side[:1], side[1:2]], axis=1)
    moved_mass = jnp.concatenate([mass[0, edge:], side[2]])
    moved_offsets = jnp.concatenate([offsets[margin * listed:], side[3, :margin * listed].astype(jnp.int32)])
    (rest,) = call(
        functools.partial(pack_kernel, blocks), (positions, thermal_noise, message), 0,
        [(count, (3 + 3 * steps) * blocks * local, BLOCK)], [], 0,
    )
    rest = exchange(rest)

    place = jnp.asarray(np.array(order, np.int32))[lax.axis_index("bead")]
    near_charge = lax.dynamic_slice_in_dim(first_charge, place * share, share + 2 * edge, axis=1)
    near_mass = lax.dynamic_slice_in_dim(moved_mass, place * share, share)[None, :]
    near_offsets = lax.dynamic_slice_in_dim(moved_offsets, place * blocks * listed, blocks * listed)

    matrix, tables = mode_constants(beads)
    at = np.concatenate([order.index(g) * local + np.arange(local) for g in range(count)])
    matrix = matrix[at][:, at]
    fixed = (near_mass, jnp.asarray(matrix), jnp.asarray(np.ascontiguousarray(matrix.T)), jnp.asarray(tables[:, at]))

    packed = (count, 3 * blocks * local, BLOCK)
    pairs = beads * blocks * listed * BLOCK * BLOCK
    (moment,) = call(
        functools.partial(first_kernel, count, margin, listed),
        (moved_offsets, first_charge, positions, message, momenta), 1, [packed],
        force_scratch(local, domain, margin, listed), pairs,
    )
    moment, rest = lax.optimization_barrier((moment, rest))
    coords, moment = call(
        functools.partial(modes_kernel, blocks, 3), (rest, exchange(moment)) + fixed, 0, [packed] * 2,
        [pltpu.VMEM((3, beads, share), f32)] * 3, 0,
    )
    for step in range(1, steps):
        joined = step == steps - 1
        out = call(
            functools.partial(middle_kernel, hops, blocks, listed, 3 * step + 3, joined),
            (near_offsets, near_charge) + tuple(window(coords, hops)) + (moment, rest) + fixed, 1,
            [(count, 6 * blocks * local, BLOCK)] if joined else [packed] * 2,
            force_scratch(beads, blocks, margin, listed), pairs,
        )
        if not joined:
            coords, moment = out
    both = exchange(out[0])

    def ends(low, c):
        pieces = both[low:low + hops, c * packed[1]:(c + 1) * packed[1]]
        return pieces.reshape(hops, 3, blocks, local, BLOCK).transpose(1, 3, 0, 2, 4).reshape(3, local, edge)

    message = passed(jnp.concatenate([
        ends(count - 2 * hops, 0), ends(count - hops, 0), ends(count - hops, 1),
        jnp.broadcast_to(charge[:, None, atoms - edge:], (1, local, edge)),
    ], axis=0), 1)
    last_charge = jnp.concatenate([message[9, 0], first_charge[0, :atoms + edge]])[None, :]
    return tuple(call(
        functools.partial(last_kernel, margin, listed), (offsets, last_charge, both, message), 1,
        [(3, local, atoms)] * 2, force_scratch(local, domain, margin, listed), pairs,
    ))


def solution(mesh):
    placed = (
        P(None, "bead", "space"),
        P(None, "bead", "space"),
        P("space"),
        P("space", None),
        P(None, None, "bead", "space"),
    )
    return jax.shard_map(
        body,
        mesh=mesh,
        in_specs=placed,
        out_specs=(P(None, "bead", "space"), P(None, "bead", "space")),
        check_vma=False,
    )
```

```python
import functools
import math

import jax
import jax.numpy as jnp
import numpy as np
from jax import lax
from jax.experimental import pallas as pl
from jax.experimental.pallas import tpu as pltpu
from jax.sharding import PartitionSpec as P

BLOCK = 128
HALO = 4

half_step = 0.025
time_step = 0.05
chain_freq = 12.0
thermal = 0.375
centroid_friction = 1.0
screening = 4.0
softening = 0.09
CHARGES = (1.0, -1.0, 0.6, -1.4)
MASSES = (1.0, 2.0, 3.0, 4.0)

PAIR_ROWS = 24
PAIR_PAD = 32
SUM_ROWS = 16
QUAD = 4
SLOTS = 4
FRAME = 8
f32 = jnp.float32
bf16 = jnp.bfloat16


def mode_constants(bead_total):
    j = np.arange(bead_total)[:, None]
    k = np.arange(bead_total)[None, :]
    half = bead_total // 2
    phase = 2.0 * np.pi * ((j * k) % bead_total) / bead_total
    plain = 1.0 / math.sqrt(bead_total)
    paired = math.sqrt(2.0 / bead_total)
    matrix = np.where(
        k == 0,
        plain,
        np.where(
            k < half,
            paired * np.cos(phase),
            np.where(k == half, plain * np.cos(phase), paired * np.sin(phase)),
        ),
    )
    modes = np.arange(bead_total)
    frequency = 2.0 * chain_freq * np.sin(np.pi * modes / bead_total)
    angle = frequency * time_step
    ratio = np.where(modes == 0, time_step, np.sin(angle) / np.where(modes == 0, 1.0, frequency))
    friction = np.where(modes == 0, centroid_friction, 2.0 * frequency)
    damping = np.exp(-friction * time_step)
    kick = np.sqrt(1.0 - damping * damping)
    tables = np.stack([np.cos(angle), ratio, frequency * np.sin(angle), damping, kick])
    tables = np.broadcast_to(tables[:, :, None], tables.shape + (BLOCK,))
    return matrix.astype(np.float32), np.ascontiguousarray(tables).astype(np.float32)


def split3(v):
    one = v.astype(bf16).astype(f32)
    rest = v - one
    two = rest.astype(bf16).astype(f32)
    three = (rest - two).astype(bf16).astype(f32)
    return one, two, three


def pair_rows(coords, norm, own):
    rows = []
    for v in coords:
        one, two, three = split3(v)
        if own:
            one, two, three = -2.0 * one, -2.0 * two, -2.0 * three
            rows += [one, one, two, two, one, three]
        else:
            rows += [one, two, one, two, three, one]
    ones = [jnp.ones_like(norm)] * 3
    norms = list(split3(norm))
    return rows + (norms + ones if own else ones + norms)


SCALE = 1.0 / (screening * math.log(2.0))


def weigh(square):
    inverse = lax.rsqrt(square)
    decay = jnp.exp2(-(square * inverse))
    return decay * ((inverse * inverse) * (inverse + math.log(2.0)))


def whole_quads(beads):
    return -(-beads // QUAD) * QUAD


def add_forces(group, blocks, margin, listed, offset_ref, charge_ref, coord_ref, scratch):
    rows_ref, sums_ref, far_ref, heavy_ref, near_ref, total_ref, force_ref, *buffers = scratch
    weight_refs = buffers
    beads = coord_ref.shape[1]
    pairs = beads // 2
    frame = min(FRAME, blocks)
    width = frame + 2 * margin
    middle = margin + (frame - 1) / 2.0
    at_once = max(1, 8 // beads)
    lines = at_once * beads
    units = blocks * pairs

    def put(ref, slot, k, value):
        ref[slot, k * lines:(k + 1) * lines, :] = value

    def centred(block, place):
        spans = [pl.ds(pl.multiple_of((block + i) * BLOCK, BLOCK), BLOCK) for i in range(at_once)]
        coords = [
            (jnp.concatenate([coord_ref[c, :, lanes] for lanes in spans], axis=0) - 1.0) * SCALE for c in range(3)
        ]
        shift = jnp.concatenate(
            [jnp.full((beads, BLOCK), SCALE, f32) * ((place + i).astype(f32) - middle) for i in range(at_once)], axis=0
        )
        coords[0] = coords[0] + shift
        norm = coords[0] * coords[0] + coords[1] * coords[1] + coords[2] * coords[2]
        charge = jnp.concatenate(
            [jnp.broadcast_to(charge_ref[:, lanes], (beads, BLOCK)) for lanes in spans], axis=0
        )
        return coords, norm, charge

    def steps(count, one):
        slots = math.gcd(count, SLOTS)

        def some(turn, carry):
            for slot in range(slots):
                one(turn * slots + slot, slot)
            return carry

        lax.fori_loop(0, count // slots, some, 0)

    nothing = jnp.zeros((lines, BLOCK), f32)
    for slot in range(SLOTS):
        for k in range(PAIR_ROWS, PAIR_PAD):
            put(rows_ref, slot, k, nothing)
        for k in range(12, SUM_ROWS):
            put(sums_ref, slot, k, nothing)
    blank = jnp.zeros((PAIR_PAD, BLOCK), f32)
    passes = width // at_once

    def one_table(step, slot):
        at_frame = step // passes
        place = (step - at_frame * passes) * at_once
        coords, norm, charge = centred(at_frame * frame + place, place)
        for k, row in enumerate(pair_rows(coords, norm, False)):
            put(rows_ref, slot, k, row)
        for c, v in enumerate([charge] + [charge * x for x in coords]):
            for level, part in enumerate(split3(v)):
                put(sums_ref, slot, level * 4 + c, part)
        for i in range(at_once):
            at = at_frame * width + place + i
            for quad in range(beads // QUAD):
                low = i * beads + quad * QUAD
                four = jnp.concatenate(
                    [rows_ref[slot, pl.ds(low + j, PAIR_PAD, stride=lines), :] for j in range(QUAD)], axis=0
                )
                far_ref[at, quad] = jnp.transpose(four).astype(bf16)
                for half in range(2):
                    heavy_ref[at, 2 * quad + half] = jnp.concatenate(
                        [
                            sums_ref[slot, pl.ds(low + 2 * half + j, SUM_ROWS, stride=lines), :]
                            for j in range(2)
                        ],
                        axis=0,
                    ).astype(bf16)

    def one_own(step, slot):
        block = step * at_once
        place = block - block // frame * frame + margin
        coords, norm, _ = centred(block + margin, place)
        for k, row in enumerate(pair_rows(coords, norm + softening * SCALE * SCALE, True)):
            put(rows_ref, slot, k, row)
        for i in range(at_once):
            for pair in range(pairs):
                columns = []
                for j in range(2):
                    own = rows_ref[slot, pl.ds(i * beads + 2 * pair + j, PAIR_PAD, stride=lines), :]
                    spot = 2 * pair % QUAD + j
                    columns.append(
                        jnp.concatenate([own if k == spot else blank for k in range(QUAD)], axis=0)
                    )
                near_ref[(block + i) * pairs + pair] = jnp.concatenate(columns, axis=1).astype(bf16)

    steps(blocks // frame * passes, one_table)
    steps(blocks // at_once, one_own)

    def places(unit):
        block = unit // pairs
        at_frame = block // frame
        base = at_frame * width + block - at_frame * frame + margin
        return [base + offset_ref[block * listed + m] for m in range(listed)], unit - block * pairs

    def parts(square):
        weight = weigh(square)
        high = weight.astype(bf16)
        return high, (weight - high.astype(f32)).astype(bf16)

    def squares(ats, pair, unit, m):
        return jnp.dot(far_ref[ats[m], pair // (QUAD // 2)], near_ref[unit], preferred_element_type=f32)

    def weighted(at, pair, both):
        table = heavy_ref[at, pair]
        return jnp.dot(jnp.concatenate([table, table], axis=1), both, preferred_element_type=f32)

    def keep(total, slot):
        for i in range(2):
            cols = slice(i * BLOCK, (i + 1) * BLOCK)
            row = i * SUM_ROWS
            spot = pl.ds(pl.multiple_of((2 * slot + i) * 8, 8), 8)
            total_ref[spot, :] = total[row:row + 8, cols] + total[row + 8:row + 16, cols]

    def body(step, carry):
        before_ats, before_pair = places(jnp.maximum(step * group - 1, 0))
        for turn in range(group):
            unit = step * group + turn
            now, other = turn % 2, (turn + 1) % 2
            ats, pair = places(unit)
            total = jnp.zeros((2 * SUM_ROWS, 2 * BLOCK), f32)
            for m in range(listed):
                spot = slice(2 * m * BLOCK, 2 * (m + 1) * BLOCK)
                weight_refs[now][spot, :] = jnp.concatenate(parts(squares(ats, pair, unit, m)), axis=0)
                total = total + weighted(before_ats[m], before_pair, weight_refs[other][spot, :])
            keep(total, jnp.where(unit == 0, units, unit - 1))
            before_ats, before_pair = ats, pair
        return carry

    group = math.gcd(units, group)
    lax.fori_loop(0, units // group, body, 0)
    last_ats, last_pair = places(units - 1)
    keep(
        sum(
            weighted(last_ats[m], last_pair, weight_refs[(group - 1) % 2][2 * m * BLOCK:2 * (m + 1) * BLOCK, :])
            for m in range(listed)
        ),
        units - 1,
    )

    def one_block(block, slot):
        at_frame = block // frame
        place = block - at_frame * frame + margin
        lanes = pl.ds(pl.multiple_of((block + margin) * BLOCK, BLOCK), BLOCK)
        coords = [(coord_ref[c, :, lanes] - 1.0) * SCALE for c in range(3)]
        coords[0] = coords[0] + SCALE * (place.astype(f32) - middle)
        charge = jnp.broadcast_to(SCALE * SCALE * charge_ref[:, lanes], coords[0].shape)

        def summed(c):
            return sum(total_ref[pl.ds(block * beads * 8 + c + i, beads, stride=8), :] for i in (0, 4))

        near = summed(0)
        own = pl.ds(pl.multiple_of(block * BLOCK, BLOCK), BLOCK)
        for c in range(3):
            force_ref[c, :, own] = charge * (coords[c] * near - summed(c + 1))

    steps(blocks, one_block)


def force_scratch(local, blocks, margin, listed):
    beads = whole_quads(local)
    frame = min(FRAME, blocks)
    tables = (frame + 2 * margin) * (blocks // frame)
    lines = max(8, beads)
    units = blocks * beads // 2
    return [
        pltpu.VMEM((3, beads, (blocks + 2 * margin) * BLOCK), f32),
        pltpu.VMEM((SLOTS, PAIR_PAD * lines, BLOCK), f32),
        pltpu.VMEM((SLOTS, SUM_ROWS * lines, BLOCK), f32),
        pltpu.VMEM((tables, beads // QUAD, BLOCK, QUAD * PAIR_PAD), bf16),
        pltpu.VMEM((tables, beads // 2, 2 * SUM_ROWS, BLOCK), bf16),
        pltpu.VMEM((units, QUAD * PAIR_PAD, 2 * BLOCK), bf16),
        pltpu.VMEM(((units + 1) * 16, BLOCK), f32),
        pltpu.VMEM((3, beads, blocks * BLOCK), f32),
        pltpu.VMEM((2 * listed * BLOCK, 2 * BLOCK), bf16),
        pltpu.VMEM((2 * listed * BLOCK, 2 * BLOCK), bf16),
    ]


def call(kernel, args, smem_count, shapes, scratch, work, in_specs=None):
    vmem = pl.BlockSpec(memory_space=pltpu.VMEM)
    smem = pl.BlockSpec(memory_space=pltpu.SMEM)
    return pl.pallas_call(
        kernel,
        out_shape=[jax.ShapeDtypeStruct(shape, f32) for shape in shapes],
        grid=() if in_specs is None else (1,),
        in_specs=in_specs or [smem] * smem_count + [vmem] * (len(args) - smem_count),
        out_specs=[vmem] * len(shapes),
        scratch_shapes=scratch,
        compiler_params=pltpu.CompilerParams(vmem_limit_bytes=(40 if in_specs is None else 62) * 1024 * 1024),
        cost_estimate=pl.CostEstimate(
            flops=20 * work + 1024, bytes_accessed=4 * 1024 * 1024, transcendentals=2 * work
        ),
    )(*args)


def row_of(c, block, blocks, local):
    return (c * blocks + block) * local


def unpack_beads(source, base, blocks, local, target, offset):
    for c in range(3):
        for block in range(blocks):
            row = row_of(base + c, block, blocks, local)
            lane = offset + block * BLOCK
            for group in range(source.shape[0]):
                target[c, group * local:(group + 1) * local, lane:lane + BLOCK] = source[group, row:row + local, :]


def pack_beads(value, c, blocks, local, target):
    for block in range(blocks):
        row = row_of(c, block, blocks, local)
        for group in range(target.shape[0]):
            target[group, row:row + local, :] = value[
                group * local:(group + 1) * local, block * BLOCK:(block + 1) * BLOCK
            ]


FORCE = 6


def clear(coord_ref, local):
    if coord_ref.shape[1] != local:
        coord_ref[...] = jnp.zeros(coord_ref.shape, f32)


def message_kernel(x_ref, p_ref, noise_ref, types_ref, offsets_ref, message_ref, charge_ref, mass_ref):
    steps = noise_ref.shape[0]
    _, local, edge = message_ref.shape
    types = types_ref[...]
    charge = jnp.zeros(types.shape, f32)
    mass = jnp.zeros(types.shape, f32)
    for kind in range(4):
        charge = jnp.where(types == kind, CHARGES[kind], charge)
        mass = jnp.where(types == kind, MASSES[kind], mass)
    charge_ref[...] = charge
    mass_ref[...] = mass
    for c in range(3):
        message_ref[c] = x_ref[c, :, :edge]
        message_ref[3 + c] = x_ref[c, :, edge:2 * edge]
        message_ref[6 + c] = p_ref[c, :, :edge]
        for step in range(steps):
            message_ref[9 + 3 * step + c] = noise_ref[step, c, :, :edge]
    at = 9 + 3 * steps
    for i, row in enumerate([charge[:, :edge], charge[:, edge:2 * edge], mass[:, :edge], offsets_ref[...]]):
        message_ref[at + i] = jnp.broadcast_to(row, (local, edge))


def pack_kernel(blocks, x_ref, noise_ref, message_ref, out_ref):
    steps = noise_ref.shape[0]
    _, local, edge = message_ref.shape
    atoms = x_ref.shape[2]
    for c in range(3 + 3 * steps):
        for block in range(atoms // BLOCK):
            at = edge + block * BLOCK
            if at >= atoms:
                value = message_ref[c if c < 3 else 6 + c, :, at - atoms:at - atoms + BLOCK]
            elif c < 3:
                value = x_ref[c, :, at:at + BLOCK]
            else:
                value = noise_ref[c // 3 - 1, c % 3, :, at:at + BLOCK]
            row = row_of(c, block % blocks, blocks, local)
            out_ref[block // blocks, row:row + local, :] = value


def first_kernel(
    shares, margin, listed, offset_ref, charge_ref, x_ref, message_ref, p_ref, pout_ref, coord_ref, *scratch
):
    _, local, atoms = x_ref.shape
    blocks = atoms // BLOCK
    each = blocks // shares
    edge = margin * BLOCK
    clear(coord_ref, local)
    for c in range(3):
        coord_ref[c, :local, 0:atoms] = x_ref[c]
        for part in range(2):
            coord_ref[c, :local, atoms + part * edge:atoms + (part + 1) * edge] = message_ref[3 * part + c]
    add_forces(16, blocks, margin, listed, offset_ref, charge_ref, coord_ref, scratch)
    force_ref = scratch[FORCE]
    for c in range(3):
        for block in range(blocks):
            lanes = slice(block * BLOCK, (block + 1) * BLOCK)
            at = block * BLOCK + edge
            if at < atoms:
                moment = p_ref[c, :, at:at + BLOCK]
            else:
                moment = message_ref[6 + c, :, at - atoms:at - atoms + BLOCK]
            row = row_of(c, block % each, each, local)
            pout_ref[block // each, row:row + local, :] = moment + half_step * force_ref[c, :local, lanes]


def last_kernel(
    margin, listed, offset_ref, charge_ref, both_ref, message_ref, xout_ref, pout_ref, coord_ref, *scratch
):
    shares = both_ref.shape[0]
    _, local, atoms = xout_ref.shape
    blocks = atoms // BLOCK
    each = blocks // shares
    edge = margin * BLOCK

    def taken(c, block):
        row = row_of(c, block % each, each, local)
        return both_ref[block // each, row:row + local, :]

    clear(coord_ref, local)
    for c in range(3):
        for part in range(2):
            coord_ref[c, :local, part * edge:(part + 1) * edge] = message_ref[3 * part + c]
        for block in range(blocks):
            at = 2 * edge + block * BLOCK
            coord_ref[c, :local, at:at + BLOCK] = taken(c, block)
        xout_ref[c] = coord_ref[c, :local, edge:edge + atoms]
    add_forces(8, blocks, margin, listed, offset_ref, charge_ref, coord_ref, scratch)
    force_ref = scratch[FORCE]
    for c in range(3):
        for block in range(blocks):
            lanes = slice(block * BLOCK, (block + 1) * BLOCK)
            moment = message_ref[6 + c, :, lanes] if block < margin else taken(3 + c, block - margin)
            pout_ref[c, :, lanes] = moment + half_step * force_ref[c, :local, lanes]


def thermostat(coords, moments, noises, mass_ref, matrix_ref, matrix_t_ref, table_ref, store):
    beads, width = moments[0].shape
    cosine, ratio, stiffness, damping, kick = [
        jnp.concatenate([table_ref[i]] * (width // BLOCK), axis=1) for i in range(5)
    ]
    mass = jnp.broadcast_to(mass_ref[...], (beads, width))
    spread = kick * jnp.sqrt(thermal * mass)
    drift = ratio / mass
    stiff = stiffness * mass
    multiply = functools.partial(jnp.dot, precision=lax.Precision.HIGHEST, preferred_element_type=f32)
    for c in range(3):
        mode_x = multiply(matrix_t_ref[...], coords[c])
        mode_p = damping * multiply(matrix_t_ref[...], moments[c]) + spread * noises[c]
        store(
            c,
            multiply(matrix_ref[...], cosine * mode_x + drift * mode_p),
            multiply(matrix_ref[...], cosine * mode_p - stiff * mode_x),
        )


def modes_kernel(
    blocks, noise_base, rest_ref, p_ref, mass_ref, matrix_ref, matrix_t_ref, table_ref,
    xout_ref, pout_ref, coord_ref, moment_ref, noise_ref,
):
    local = p_ref.shape[1] // (3 * blocks)
    unpack_beads(rest_ref, 0, blocks, local, coord_ref, 0)
    unpack_beads(p_ref, 0, blocks, local, moment_ref, 0)
    unpack_beads(rest_ref, noise_base, blocks, local, noise_ref, 0)

    def store(c, x, p):
        pack_beads(x, c, blocks, local, xout_ref)
        pack_beads(p, c, blocks, local, pout_ref)

    thermostat(
        *[[ref[c] for c in range(3)] for ref in (coord_ref, moment_ref, noise_ref)],
        mass_ref, matrix_ref, matrix_t_ref, table_ref, store,
    )


def middle_kernel(hops, blocks, listed, noise_base, joined, offset_ref, charge_ref, *refs):
    parts = 2 * hops + 1
    x_refs = refs[:parts]
    p_ref, noise_ref, mass_ref, matrix_ref, matrix_t_ref, table_ref = refs[parts:parts + 6]
    outs = refs[parts + 6:parts + (7 if joined else 8)]
    coord_ref, *scratch = refs[parts + len(outs) + 6:]
    beads = coord_ref.shape[1]
    local = beads // p_ref.shape[0]
    width = blocks * BLOCK
    for part in range(parts):
        unpack_beads(x_refs[part], 0, blocks, local, coord_ref, part * width)
    add_forces(8, blocks, hops * blocks, listed, offset_ref, charge_ref, coord_ref, scratch)
    force_ref = scratch[FORCE]
    unpack_beads(p_ref, 0, blocks, local, coord_ref, 0)
    unpack_beads(noise_ref, noise_base, blocks, local, coord_ref, (parts - 1) * width)

    def share(c, part):
        return coord_ref[c, :, part * width:(part + 1) * width]

    def store(c, x, p):
        pack_beads(x, c, blocks, local, outs[0])
        if joined:
            pack_beads(p, 3 + c, blocks, local, outs[0])
        else:
            pack_beads(p, c, blocks, local, outs[1])

    thermostat(
        [share(c, hops) for c in range(3)],
        [share(c, 0) + 2.0 * half_step * force_ref[c] for c in range(3)],
        [share(c, parts - 1) for c in range(3)],
        mass_ref, matrix_ref, matrix_t_ref, table_ref, store,
    )


def fold(count):
    return [i // 2 if i % 2 == 0 else count - 1 - i // 2 for i in range(count)]


def exchange(pieces):
    order = fold(pieces.shape[0])
    group = [order.index(at) for at in range(len(order))]
    return lax.all_to_all(pieces, "bead", split_axis=0, concat_axis=0, axis_index_groups=[group], tiled=True)


def passed(values, step):
    count = lax.axis_size("space")
    return lax.ppermute(values, "space", [(i, (i + step) % count) for i in range(count)])


def window(values, hops):
    count = lax.axis_size("bead")
    domains = lax.axis_size("space")
    order = fold(count)
    device = {}
    for bead in range(count):
        for domain in range(domains):
            device[domain * count + order[bead]] = bead * domains + domain
    total = count * domains
    out = []
    for hop in range(-hops, hops + 1):
        if hop == 0:
            out.append(values)
        else:
            route = [(device[(at + hop) % total], device[at]) for at in range(total)]
            out.append(lax.ppermute(values, ("bead", "space"), route))
    return out


def body(positions, momenta, atom_types, neighbours, thermal_noise):
    count = lax.axis_size("bead")
    _, local, atoms = positions.shape
    beads = local * count
    domain = atoms // BLOCK
    blocks = domain // count
    share = blocks * BLOCK
    hops = -(-HALO // blocks)
    margin = hops * blocks
    edge = margin * BLOCK
    steps = thermal_noise.shape[0]
    listed = neighbours.shape[1]
    order = fold(count)

    own = lax.axis_index("space") * domain + jnp.arange(domain, dtype=jnp.int32)
    offsets = jnp.clip(neighbours - own[:, None], -margin, margin).reshape(-1)
    sent = jnp.pad(offsets[:margin * listed].astype(f32), (0, edge - margin * listed))[None, :]

    message, charge, mass = call(
        message_kernel, (positions, momenta, thermal_noise, atom_types[None, :], sent), 0,
        [(13 + 3 * steps, local, edge), (1, atoms), (1, atoms)], [], 0,
        [
            pl.BlockSpec(shape, lambda i, rank=len(shape): (0,) * rank)
            for shape in (
                (3, local, 2 * edge), (3, local, edge), (steps, 3, local, edge), (1, atoms), (1, edge)
            )
        ],
    )
    message = passed(message, -1)
    side = message[9 + 3 * steps:, 0]
    first_charge = jnp.concatenate([charge, side[:1], side[1:2]], axis=1)
    moved_mass = jnp.concatenate([mass[0, edge:], side[2]])
    moved_offsets = jnp.concatenate([offsets[margin * listed:], side[3, :margin * listed].astype(jnp.int32)])
    (rest,) = call(
        functools.partial(pack_kernel, blocks), (positions, thermal_noise, message), 0,
        [(count, (3 + 3 * steps) * blocks * local, BLOCK)], [], 0,
    )
    rest = exchange(rest)

    place = jnp.asarray(np.array(order, np.int32))[lax.axis_index("bead")]
    near_charge = lax.dynamic_slice_in_dim(first_charge, place * share, share + 2 * edge, axis=1)
    near_mass = lax.dynamic_slice_in_dim(moved_mass, place * share, share)[None, :]
    near_offsets = lax.dynamic_slice_in_dim(moved_offsets, place * blocks * listed, blocks * listed)

    matrix, tables = mode_constants(beads)
    at = np.concatenate([order.index(g) * local + np.arange(local) for g in range(count)])
    matrix = matrix[at][:, at]
    fixed = (near_mass, jnp.asarray(matrix), jnp.asarray(np.ascontiguousarray(matrix.T)), jnp.asarray(tables[:, at]))

    packed = (count, 3 * blocks * local, BLOCK)
    pairs = beads * blocks * listed * BLOCK * BLOCK
    (moment,) = call(
        functools.partial(first_kernel, count, margin, listed),
        (moved_offsets, first_charge, positions, message, momenta), 1, [packed],
        force_scratch(local, domain, margin, listed), pairs,
    )
    moment, rest = lax.optimization_barrier((moment, rest))
    coords, moment = call(
        functools.partial(modes_kernel, blocks, 3), (rest, exchange(moment)) + fixed, 0, [packed] * 2,
        [pltpu.VMEM((3, beads, share), f32)] * 3, 0,
    )
    for step in range(1, steps):
        joined = step == steps - 1
        out = call(
            functools.partial(middle_kernel, hops, blocks, listed, 3 * step + 3, joined),
            (near_offsets, near_charge) + tuple(window(coords, hops)) + (moment, rest) + fixed, 1,
            [(count, 6 * blocks * local, BLOCK)] if joined else [packed] * 2,
            force_scratch(beads, blocks, margin, listed), pairs,
        )
        if not joined:
            coords, moment = out
    both = exchange(out[0])

    def ends(low, c):
        pieces = both[low:low + hops, c * packed[1]:(c + 1) * packed[1]]
        return pieces.reshape(hops, 3, blocks, local, BLOCK).transpose(1, 3, 0, 2, 4).reshape(3, local, edge)

    message = passed(jnp.concatenate([
        ends(count - 2 * hops, 0), ends(count - hops, 0), ends(count - hops, 1),
        jnp.broadcast_to(charge[:, None, atoms - edge:], (1, local, edge)),
    ], axis=0), 1)
    last_charge = jnp.concatenate([message[9, 0], first_charge[0, :atoms + edge]])[None, :]
    return tuple(call(
        functools.partial(last_kernel, margin, listed), (offsets, last_charge, both, message), 1,
        [(3, local, atoms)] * 2, force_scratch(local, domain, margin, listed), pairs,
    ))


def solution(mesh):
    placed = (
        P(None, "bead", "space"),
        P(None, "bead", "space"),
        P("space"),
        P("space", None),
        P(None, None, "bead", "space"),
    )
    return jax.shard_map(
        body,
        mesh=mesh,
        in_specs=placed,
        out_specs=(P(None, "bead", "space"), P(None, "bead", "space")),
        check_vma=False,
    )
```

```python
import functools
import math

import jax
import jax.numpy as jnp
import numpy as np
from jax import lax
from jax.experimental import pallas as pl
from jax.experimental.pallas import tpu as pltpu
from jax.sharding import PartitionSpec as P

BLOCK = 128
HALO = 4

half_step = 0.025
time_step = 0.05
chain_freq = 12.0
thermal = 0.375
centroid_friction = 1.0
screening = 4.0
softening = 0.09
CHARGES = (1.0, -1.0, 0.6, -1.4)
MASSES = (1.0, 2.0, 3.0, 4.0)

PAIR_ROWS = 24
PAIR_PAD = 32
SUM_ROWS = 16
QUAD = 4
SLOTS = 4
FRAME = 8
f32 = jnp.float32
bf16 = jnp.bfloat16


def mode_constants(bead_total):
    j = np.arange(bead_total)[:, None]
    k = np.arange(bead_total)[None, :]
    half = bead_total // 2
    phase = 2.0 * np.pi * ((j * k) % bead_total) / bead_total
    plain = 1.0 / math.sqrt(bead_total)
    paired = math.sqrt(2.0 / bead_total)
    matrix = np.where(
        k == 0,
        plain,
        np.where(
            k < half,
            paired * np.cos(phase),
            np.where(k == half, plain * np.cos(phase), paired * np.sin(phase)),
        ),
    )
    modes = np.arange(bead_total)
    frequency = 2.0 * chain_freq * np.sin(np.pi * modes / bead_total)
    angle = frequency * time_step
    ratio = np.where(modes == 0, time_step, np.sin(angle) / np.where(modes == 0, 1.0, frequency))
    friction = np.where(modes == 0, centroid_friction, 2.0 * frequency)
    damping = np.exp(-friction * time_step)
    kick = np.sqrt(1.0 - damping * damping)
    tables = np.stack([np.cos(angle), ratio, frequency * np.sin(angle), damping, kick])
    tables = np.broadcast_to(tables[:, :, None], tables.shape + (BLOCK,))
    return matrix.astype(np.float32), np.ascontiguousarray(tables).astype(np.float32)


def split3(v):
    one = v.astype(bf16).astype(f32)
    rest = v - one
    two = rest.astype(bf16).astype(f32)
    three = (rest - two).astype(bf16).astype(f32)
    return one, two, three


def pair_rows(coords, norm, own):
    rows = []
    for v in coords:
        one, two, three = split3(v)
        if own:
            one, two, three = -2.0 * one, -2.0 * two, -2.0 * three
            rows += [one, one, two, two, one, three]
        else:
            rows += [one, two, one, two, three, one]
    ones = [jnp.ones_like(norm)] * 3
    norms = list(split3(norm))
    return rows + (norms + ones if own else ones + norms)


SCALE = 1.0 / (screening * math.log(2.0))


def weigh(square):
    inverse = lax.rsqrt(square)
    decay = jnp.exp2(-(square * inverse))
    return decay * ((inverse * inverse) * (inverse + math.log(2.0)))


def whole_quads(beads):
    return -(-beads // QUAD) * QUAD


def add_forces(group, blocks, margin, listed, offset_ref, charge_ref, coord_ref, scratch):
    rows_ref, sums_ref, far_ref, heavy_ref, near_ref, total_ref, force_ref, *buffers = scratch
    weight_refs = buffers
    beads = coord_ref.shape[1]
    pairs = beads // 2
    frame = min(FRAME, blocks)
    width = frame + 2 * margin
    middle = margin + (frame - 1) / 2.0
    at_once = max(1, 8 // beads)
    lines = at_once * beads
    units = blocks * pairs

    def put(ref, slot, k, value):
        ref[slot, k * lines:(k + 1) * lines, :] = value

    def centred(block, place):
        spans = [pl.ds(pl.multiple_of((block + i) * BLOCK, BLOCK), BLOCK) for i in range(at_once)]
        coords = [
            (jnp.concatenate([coord_ref[c, :, lanes] for lanes in spans], axis=0) - 1.0) * SCALE for c in range(3)
        ]
        shift = jnp.concatenate(
            [jnp.full((beads, BLOCK), SCALE, f32) * ((place + i).astype(f32) - middle) for i in range(at_once)], axis=0
        )
        coords[0] = coords[0] + shift
        norm = coords[0] * coords[0] + coords[1] * coords[1] + coords[2] * coords[2]
        charge = jnp.concatenate(
            [jnp.broadcast_to(charge_ref[:, lanes], (beads, BLOCK)) for lanes in spans], axis=0
        )
        return coords, norm, charge

    def steps(count, one):
        slots = math.gcd(count, SLOTS)

        def some(turn, carry):
            for slot in range(slots):
                one(turn * slots + slot, slot)
            return carry

        lax.fori_loop(0, count // slots, some, 0)

    nothing = jnp.zeros((lines, BLOCK), f32)
    for slot in range(SLOTS):
        for k in range(PAIR_ROWS, PAIR_PAD):
            put(rows_ref, slot, k, nothing)
        for k in range(12, SUM_ROWS):
            put(sums_ref, slot, k, nothing)
    blank = jnp.zeros((PAIR_PAD, BLOCK), f32)
    passes = width // at_once

    def one_table(step, slot):
        at_frame = step // passes
        place = (step - at_frame * passes) * at_once
        coords, norm, charge = centred(at_frame * frame + place, place)
        for k, row in enumerate(pair_rows(coords, norm, False)):
            put(rows_ref, slot, k, row)
        for c, v in enumerate([charge] + [charge * x for x in coords]):
            for level, part in enumerate(split3(v)):
                put(sums_ref, slot, level * 4 + c, part)
        for i in range(at_once):
            at = at_frame * width + place + i
            for quad in range(beads // QUAD):
                low = i * beads + quad * QUAD
                four = jnp.concatenate(
                    [rows_ref[slot, pl.ds(low + j, PAIR_PAD, stride=lines), :] for j in range(QUAD)], axis=0
                )
                far_ref[at, quad] = jnp.transpose(four.astype(bf16))
                for half in range(2):
                    heavy_ref[at, 2 * quad + half] = jnp.concatenate(
                        [
                            sums_ref[slot, pl.ds(low + 2 * half + j, SUM_ROWS, stride=lines), :]
                            for j in range(2)
                        ],
                        axis=0,
                    ).astype(bf16)

    def one_own(step, slot):
        block = step * at_once
        place = block - block // frame * frame + margin
        coords, norm, _ = centred(block + margin, place)
        for k, row in enumerate(pair_rows(coords, norm + softening * SCALE * SCALE, True)):
            put(rows_ref, slot, k, row)
        for i in range(at_once):
            for pair in range(pairs):
                columns = []
                for j in range(2):
                    own = rows_ref[slot, pl.ds(i * beads + 2 * pair + j, PAIR_PAD, stride=lines), :]
                    spot = 2 * pair % QUAD + j
                    columns.append(
                        jnp.concatenate([own if k == spot else blank for k in range(QUAD)], axis=0)
                    )
                near_ref[(block + i) * pairs + pair] = jnp.concatenate(columns, axis=1).astype(bf16)

    steps(blocks // frame * passes, one_table)
    steps(blocks // at_once, one_own)

    def places(unit):
        block = unit // pairs
        at_frame = block // frame
        base = at_frame * width + block - at_frame * frame + margin
        return [base + offset_ref[block * listed + m] for m in range(listed)], unit - block * pairs

    def parts(square):
        weight = weigh(square)
        high = weight.astype(bf16)
        return high, (weight - high.astype(f32)).astype(bf16)

    def squares(ats, pair, unit, m):
        return jnp.dot(far_ref[ats[m], pair // (QUAD // 2)], near_ref[unit], preferred_element_type=f32)

    def weighted(at, pair, both):
        table = heavy_ref[at, pair]
        return jnp.dot(jnp.concatenate([table, table], axis=1), both, preferred_element_type=f32)

    def keep(total, slot):
        for i in range(2):
            cols = slice(i * BLOCK, (i + 1) * BLOCK)
            row = i * SUM_ROWS
            spot = pl.ds(pl.multiple_of((2 * slot + i) * 8, 8), 8)
            total_ref[spot, :] = total[row:row + 8, cols] + total[row + 8:row + 16, cols]

    def body(step, carry):
        before_ats, before_pair = places(jnp.maximum(step * group - 1, 0))
        for turn in range(group):
            unit = step * group + turn
            now, other = turn % 2, (turn + 1) % 2
            ats, pair = places(unit)
            total = jnp.zeros((2 * SUM_ROWS, 2 * BLOCK), f32)
            for m in range(listed):
                spot = slice(2 * m * BLOCK, 2 * (m + 1) * BLOCK)
                weight_refs[now][spot, :] = jnp.concatenate(parts(squares(ats, pair, unit, m)), axis=0)
                total = total + weighted(before_ats[m], before_pair, weight_refs[other][spot, :])
            keep(total, jnp.where(unit == 0, units, unit - 1))
            before_ats, before_pair = ats, pair
        return carry

    group = math.gcd(units, group)
    lax.fori_loop(0, units // group, body, 0)
    last_ats, last_pair = places(units - 1)
    keep(
        sum(
            weighted(last_ats[m], last_pair, weight_refs[(group - 1) % 2][2 * m * BLOCK:2 * (m + 1) * BLOCK, :])
            for m in range(listed)
        ),
        units - 1,
    )

    def one_block(block, slot):
        at_frame = block // frame
        place = block - at_frame * frame + margin
        lanes = pl.ds(pl.multiple_of((block + margin) * BLOCK, BLOCK), BLOCK)
        coords = [(coord_ref[c, :, lanes] - 1.0) * SCALE for c in range(3)]
        coords[0] = coords[0] + SCALE * (place.astype(f32) - middle)
        charge = jnp.broadcast_to(SCALE * SCALE * charge_ref[:, lanes], coords[0].shape)

        def summed(c):
            return sum(total_ref[pl.ds(block * beads * 8 + c + i, beads, stride=8), :] for i in (0, 4))

        near = summed(0)
        own = pl.ds(pl.multiple_of(block * BLOCK, BLOCK), BLOCK)
        for c in range(3):
            force_ref[c, :, own] = charge * (coords[c] * near - summed(c + 1))

    steps(blocks, one_block)


def force_scratch(local, blocks, margin, listed):
    beads = whole_quads(local)
    frame = min(FRAME, blocks)
    tables = (frame + 2 * margin) * (blocks // frame)
    lines = max(8, beads)
    units = blocks * beads // 2
    return [
        pltpu.VMEM((3, beads, (blocks + 2 * margin) * BLOCK), f32),
        pltpu.VMEM((SLOTS, PAIR_PAD * lines, BLOCK), f32),
        pltpu.VMEM((SLOTS, SUM_ROWS * lines, BLOCK), f32),
        pltpu.VMEM((tables, beads // QUAD, BLOCK, QUAD * PAIR_PAD), bf16),
        pltpu.VMEM((tables, beads // 2, 2 * SUM_ROWS, BLOCK), bf16),
        pltpu.VMEM((units, QUAD * PAIR_PAD, 2 * BLOCK), bf16),
        pltpu.VMEM(((units + 1) * 16, BLOCK), f32),
        pltpu.VMEM((3, beads, blocks * BLOCK), f32),
        pltpu.VMEM((2 * listed * BLOCK, 2 * BLOCK), bf16),
        pltpu.VMEM((2 * listed * BLOCK, 2 * BLOCK), bf16),
    ]


def call(kernel, args, smem_count, shapes, scratch, work, in_specs=None):
    vmem = pl.BlockSpec(memory_space=pltpu.VMEM)
    smem = pl.BlockSpec(memory_space=pltpu.SMEM)
    return pl.pallas_call(
        kernel,
        out_shape=[jax.ShapeDtypeStruct(shape, f32) for shape in shapes],
        grid=() if in_specs is None else (1,),
        in_specs=in_specs or [smem] * smem_count + [vmem] * (len(args) - smem_count),
        out_specs=[vmem] * len(shapes),
        scratch_shapes=scratch,
        compiler_params=pltpu.CompilerParams(vmem_limit_bytes=(40 if in_specs is None else 62) * 1024 * 1024),
        cost_estimate=pl.CostEstimate(
            flops=20 * work + 1024, bytes_accessed=4 * 1024 * 1024, transcendentals=2 * work
        ),
    )(*args)


def row_of(c, block, blocks, local):
    return (c * blocks + block) * local


def unpack_beads(source, base, blocks, local, target, offset):
    for c in range(3):
        for block in range(blocks):
            row = row_of(base + c, block, blocks, local)
            lane = offset + block * BLOCK
            for group in range(source.shape[0]):
                target[c, group * local:(group + 1) * local, lane:lane + BLOCK] = source[group, row:row + local, :]


def pack_beads(value, c, blocks, local, target):
    for block in range(blocks):
        row = row_of(c, block, blocks, local)
        for group in range(target.shape[0]):
            target[group, row:row + local, :] = value[
                group * local:(group + 1) * local, block * BLOCK:(block + 1) * BLOCK
            ]


FORCE = 6


def clear(coord_ref, local):
    if coord_ref.shape[1] != local:
        coord_ref[...] = jnp.zeros(coord_ref.shape, f32)


def message_kernel(x_ref, p_ref, types_ref, offsets_ref, message_ref, charge_ref, mass_ref):
    _, local, edge = message_ref.shape
    types = types_ref[...]
    charge = jnp.zeros(types.shape, f32)
    mass = jnp.zeros(types.shape, f32)
    for kind in range(4):
        charge = jnp.where(types == kind, CHARGES[kind], charge)
        mass = jnp.where(types == kind, MASSES[kind], mass)
    charge_ref[...] = charge
    mass_ref[...] = mass
    for c in range(3):
        message_ref[c] = x_ref[c, :, :edge]
        message_ref[3 + c] = x_ref[c, :, edge:2 * edge]
        message_ref[6 + c] = p_ref[c, :, :edge]
    for i, row in enumerate([charge[:, :edge], charge[:, edge:2 * edge], mass[:, :edge], offsets_ref[...]]):
        message_ref[9 + i] = jnp.broadcast_to(row, (local, edge))


def pack_kernel(blocks, x_ref, noise_ref, out_ref):
    steps, _, local, atoms = noise_ref.shape
    for c in range(3 + 3 * steps):
        for block in range(atoms // BLOCK):
            lanes = slice(block * BLOCK, (block + 1) * BLOCK)
            value = x_ref[c, :, lanes] if c < 3 else noise_ref[c // 3 - 1, c % 3, :, lanes]
            row = row_of(c, block % blocks, blocks, local)
            out_ref[block // blocks, row:row + local, :] = value


def front_kernel(each, margin, listed, offset_ref, charge_ref, x_ref, p_ref, pout_ref, coord_ref, *scratch):
    _, local, _ = x_ref.shape
    blocks = pout_ref.shape[0] * each
    clear(coord_ref, local)
    for c in range(3):
        coord_ref[c, :local, :] = x_ref[c, :, :(blocks + 2 * margin) * BLOCK]
    add_forces(16, blocks, margin, listed, offset_ref, charge_ref, coord_ref, scratch)
    force_ref = scratch[FORCE]
    for c in range(3):
        for block in range(blocks):
            lanes = slice(block * BLOCK, (block + 1) * BLOCK)
            moment = p_ref[c, :, (block + margin) * BLOCK:(block + margin + 1) * BLOCK]
            row = row_of(c, block % each, each, local)
            pout_ref[block // each, row:row + local, :] = moment + half_step * force_ref[c, :local, lanes]


def back_kernel(
    each, margin, listed, offset_ref, charge_ref, x_ref, message_ref, p_ref, front_ref, pout_ref, coord_ref, *scratch
):
    _, local, atoms = x_ref.shape
    edge = margin * BLOCK
    done = front_ref.shape[0]
    first = done * each
    blocks = (pout_ref.shape[0] - done) * each
    own = atoms - first * BLOCK
    clear(coord_ref, local)
    for c in range(3):
        coord_ref[c, :local, :own] = x_ref[c, :, first * BLOCK:]
        for part in range(2):
            coord_ref[c, :local, own + part * edge:own + (part + 1) * edge] = message_ref[3 * part + c]
    add_forces(8, blocks, margin, listed, offset_ref, charge_ref, coord_ref, scratch)
    force_ref = scratch[FORCE]
    pout_ref[:done] = front_ref[...]
    for c in range(3):
        for block in range(blocks):
            lanes = slice(block * BLOCK, (block + 1) * BLOCK)
            at = (first + block) * BLOCK + edge
            if at < atoms:
                moment = p_ref[c, :, at:at + BLOCK]
            else:
                moment = message_ref[6 + c, :, at - atoms:at - atoms + BLOCK]
            row = row_of(c, block % each, each, local)
            pout_ref[done + block // each, row:row + local, :] = moment + half_step * force_ref[c, :local, lanes]


def from_packed(ref, c, block, each, local):
    row = row_of(c, block % each, each, local)
    return ref[block // each, row:row + local, :]


def upper_kernel(each, margin, listed, offset_ref, charge_ref, both_ref, pout_ref, coord_ref, *scratch):
    _, local, atoms = pout_ref.shape
    blocks = atoms // BLOCK
    domain = both_ref.shape[0] * each
    skipped = domain - blocks - 2 * margin
    clear(coord_ref, local)
    for c in range(3):
        for block in range(skipped, domain):
            at = (block - skipped) * BLOCK
            coord_ref[c, :local, at:at + BLOCK] = from_packed(both_ref, c, block, each, local)
    add_forces(16, blocks, margin, listed, offset_ref, charge_ref, coord_ref, scratch)
    force_ref = scratch[FORCE]
    for c in range(3):
        for block in range(blocks):
            lanes = slice(block * BLOCK, (block + 1) * BLOCK)
            moment = from_packed(both_ref, 3 + c, domain - blocks + block - margin, each, local)
            pout_ref[c, :, lanes] = moment + half_step * force_ref[c, :local, lanes]


def lower_kernel(
    each, margin, listed, offset_ref, charge_ref, both_ref, message_ref, upper_ref, xout_ref, pout_ref, coord_ref, *scratch
):
    _, local, atoms = xout_ref.shape
    edge = margin * BLOCK
    lower = atoms - upper_ref.shape[2]
    blocks = lower // BLOCK
    clear(coord_ref, local)
    for c in range(3):
        for part in range(2):
            coord_ref[c, :local, part * edge:(part + 1) * edge] = message_ref[3 * part + c]
        for block in range(blocks):
            at = 2 * edge + block * BLOCK
            coord_ref[c, :local, at:at + BLOCK] = from_packed(both_ref, c, block, each, local)
        xout_ref[c, :, :edge] = message_ref[3 + c]
        for block in range(margin, atoms // BLOCK):
            lanes = slice(block * BLOCK, (block + 1) * BLOCK)
            xout_ref[c, :, lanes] = from_packed(both_ref, c, block - margin, each, local)
        pout_ref[c, :, lower:] = upper_ref[c]
    add_forces(8, blocks, margin, listed, offset_ref, charge_ref, coord_ref, scratch)
    force_ref = scratch[FORCE]
    for c in range(3):
        for block in range(blocks):
            lanes = slice(block * BLOCK, (block + 1) * BLOCK)
            if block < margin:
                moment = message_ref[6 + c, :, lanes]
            else:
                moment = from_packed(both_ref, 3 + c, block - margin, each, local)
            pout_ref[c, :, lanes] = moment + half_step * force_ref[c, :local, lanes]


def thermostat(coords, moments, noises, mass_ref, matrix_ref, matrix_t_ref, table_ref, store):
    beads, width = moments[0].shape
    cosine, ratio, stiffness, damping, kick = [
        jnp.concatenate([table_ref[i]] * (width // BLOCK), axis=1) for i in range(5)
    ]
    mass = jnp.broadcast_to(mass_ref[...], (beads, width))
    spread = kick * jnp.sqrt(thermal * mass)
    drift = ratio / mass
    stiff = stiffness * mass
    multiply = functools.partial(jnp.dot, precision=lax.Precision.HIGHEST, preferred_element_type=f32)
    for c in range(3):
        mode_x = multiply(matrix_t_ref[...], coords[c])
        mode_p = damping * multiply(matrix_t_ref[...], moments[c]) + spread * noises[c]
        store(
            c,
            multiply(matrix_ref[...], cosine * mode_x + drift * mode_p),
            multiply(matrix_ref[...], cosine * mode_p - stiff * mode_x),
        )


def modes_kernel(
    blocks, noise_base, rest_ref, p_ref, mass_ref, matrix_ref, matrix_t_ref, table_ref,
    xout_ref, pout_ref, coord_ref, moment_ref, noise_ref,
):
    local = p_ref.shape[1] // (3 * blocks)
    unpack_beads(rest_ref, 0, blocks, local, coord_ref, 0)
    unpack_beads(p_ref, 0, blocks, local, moment_ref, 0)
    unpack_beads(rest_ref, noise_base, blocks, local, noise_ref, 0)

    def store(c, x, p):
        pack_beads(x, c, blocks, local, xout_ref)
        pack_beads(p, c, blocks, local, pout_ref)

    thermostat(
        *[[ref[c] for c in range(3)] for ref in (coord_ref, moment_ref, noise_ref)],
        mass_ref, matrix_ref, matrix_t_ref, table_ref, store,
    )


def middle_kernel(hops, blocks, listed, noise_base, joined, offset_ref, charge_ref, *refs):
    parts = 2 * hops + 1
    x_refs = refs[:parts]
    p_ref, noise_ref, mass_ref, matrix_ref, matrix_t_ref, table_ref = refs[parts:parts + 6]
    outs = refs[parts + 6:parts + (7 if joined else 8)]
    coord_ref, *scratch = refs[parts + len(outs) + 6:]
    beads = coord_ref.shape[1]
    local = beads // p_ref.shape[0]
    width = blocks * BLOCK
    for part in range(parts):
        unpack_beads(x_refs[part], 0, blocks, local, coord_ref, part * width)
    add_forces(16, blocks, hops * blocks, listed, offset_ref, charge_ref, coord_ref, scratch)
    force_ref = scratch[FORCE]
    unpack_beads(p_ref, 0, blocks, local, coord_ref, 0)
    unpack_beads(noise_ref, noise_base, blocks, local, coord_ref, (parts - 1) * width)

    def share(c, part):
        return coord_ref[c, :, part * width:(part + 1) * width]

    def store(c, x, p):
        pack_beads(x, c, blocks, local, outs[0])
        if joined:
            pack_beads(p, 3 + c, blocks, local, outs[0])
        else:
            pack_beads(p, c, blocks, local, outs[1])

    thermostat(
        [share(c, hops) for c in range(3)],
        [share(c, 0) + 2.0 * half_step * force_ref[c] for c in range(3)],
        [share(c, parts - 1) for c in range(3)],
        mass_ref, matrix_ref, matrix_t_ref, table_ref, store,
    )


def fold(count):
    return [i // 2 if i % 2 == 0 else count - 1 - i // 2 for i in range(count)]


def exchange(pieces):
    order = fold(pieces.shape[0])
    group = [order.index(at) for at in range(len(order))]
    return lax.all_to_all(pieces, "bead", split_axis=0, concat_axis=0, axis_index_groups=[group], tiled=True)


def passed(values, step):
    count = lax.axis_size("space")
    return lax.ppermute(values, "space", [(i, (i + step) % count) for i in range(count)])


def round_ring(values, hop):
    count = lax.axis_size("bead")
    domains = lax.axis_size("space")
    order = fold(count)
    device = {}
    for bead in range(count):
        for domain in range(domains):
            device[domain * count + order[bead]] = bead * domains + domain
    total = count * domains
    return lax.ppermute(values, ("bead", "space"), [(device[(at + hop) % total], device[at]) for at in range(total)])


def window(values, hops):
    return [round_ring(values, hop) if hop else values for hop in range(-hops, hops + 1)]


def body(positions, momenta, atom_types, neighbours, thermal_noise):
    count = lax.axis_size("bead")
    _, local, atoms = positions.shape
    beads = local * count
    domain = atoms // BLOCK
    blocks = domain // count
    share = blocks * BLOCK
    hops = -(-HALO // blocks)
    margin = hops * blocks
    edge = margin * BLOCK
    steps = thermal_noise.shape[0]
    listed = neighbours.shape[1]
    order = fold(count)

    own = lax.axis_index("space") * domain + jnp.arange(domain, dtype=jnp.int32)
    offsets = jnp.clip(neighbours - own[:, None], -margin, margin).reshape(-1)
    sent = jnp.pad(offsets[:margin * listed].astype(f32), (0, edge - margin * listed))[None, :]

    (rest,) = call(
        functools.partial(pack_kernel, blocks), (positions, thermal_noise), 0,
        [(count, (3 + 3 * steps) * blocks * local, BLOCK)], [], 0,
    )
    rest = exchange(rest)

    message, charge, mass = call(
        message_kernel, (positions, momenta, atom_types[None, :], sent), 0,
        [(13, local, edge), (1, atoms), (1, atoms)], [], 0,
        [
            pl.BlockSpec(shape, lambda i, rank=len(shape): (0,) * rank)
            for shape in ((3, local, 2 * edge), (3, local, edge), (1, atoms), (1, edge))
        ],
    )
    message = passed(message, -1)
    side = message[9:, 0]
    first_charge = jnp.concatenate([charge, side[:1], side[1:2]], axis=1)
    moved_mass = jnp.concatenate([mass[0, edge:], side[2]])
    moved_offsets = jnp.concatenate([offsets[margin * listed:], side[3, :margin * listed].astype(jnp.int32)])

    place = jnp.asarray(np.array(order, np.int32))[lax.axis_index("bead")]
    near_charge = lax.dynamic_slice_in_dim(first_charge, place * share, share + 2 * edge, axis=1)
    near_mass = lax.dynamic_slice_in_dim(moved_mass, place * share, share)[None, :]
    near_offsets = lax.dynamic_slice_in_dim(moved_offsets, place * blocks * listed, blocks * listed)

    matrix, tables = mode_constants(beads)
    at = np.concatenate([order.index(g) * local + np.arange(local) for g in range(count)])
    matrix = matrix[at][:, at]
    fixed = (near_mass, jnp.asarray(matrix), jnp.asarray(np.ascontiguousarray(matrix.T)), jnp.asarray(tables[:, at]))

    packed = (count, 3 * blocks * local, BLOCK)
    pairs = beads * blocks * listed * BLOCK * BLOCK
    frame = min(FRAME, domain)
    most = domain - frame
    window_atoms = (most + 2 * margin) * BLOCK
    (moment,) = call(
        functools.partial(front_kernel, blocks, margin, listed),
        (offsets[margin * listed:(margin + most) * listed], charge[:, :window_atoms], positions, momenta), 1,
        [(most // blocks,) + packed[1:]], force_scratch(local, most, margin, listed), pairs * most // domain,
    )
    moment, rest = lax.optimization_barrier((moment, rest))
    rest = round_ring(rest, hops)
    (moment,) = call(
        functools.partial(back_kernel, blocks, margin, listed),
        (moved_offsets[most * listed:], first_charge[:, most * BLOCK:], positions, message, momenta, moment), 1,
        [packed], force_scratch(local, frame, margin, listed), pairs * frame // domain,
    )
    moment, rest = lax.optimization_barrier((moment, rest))
    coords, moment = call(
        functools.partial(modes_kernel, blocks, 3), (rest, exchange(moment)) + fixed, 0, [packed] * 2,
        [pltpu.VMEM((3, beads, share), f32)] * 3, 0,
    )
    for step in range(1, steps):
        joined = step == steps - 1
        out = call(
            functools.partial(middle_kernel, hops, blocks, listed, 3 * step + 3, joined),
            (near_offsets, near_charge) + tuple(window(coords, hops)) + (moment, rest) + fixed, 1,
            [(count, 6 * blocks * local, BLOCK)] if joined else [packed] * 2,
            force_scratch(beads, blocks, margin, listed), pairs,
        )
        if not joined:
            coords, moment = out
    both = exchange(out[0])

    def ends(low, c):
        pieces = both[low:low + hops, c * packed[1]:(c + 1) * packed[1]]
        return pieces.reshape(hops, 3, blocks, local, BLOCK).transpose(1, 3, 0, 2, 4).reshape(3, local, edge)

    message = passed(jnp.concatenate([
        ends(count - 2 * hops, 0), ends(count - hops, 0), ends(count - hops, 1),
        jnp.broadcast_to(charge[:, None, atoms - edge:], (1, local, edge)),
    ], axis=0), 1)
    (upper,) = call(
        functools.partial(upper_kernel, blocks, margin, listed),
        (offsets[frame * listed:], first_charge[:, frame * BLOCK - edge:atoms + edge], both), 1,
        [(3, local, most * BLOCK)], force_scratch(local, most, margin, listed), pairs * most // domain,
    )
    last_charge = jnp.concatenate([message[9, :1], first_charge[:, :frame * BLOCK + edge]], axis=1)
    return tuple(call(
        functools.partial(lower_kernel, blocks, margin, listed),
        (offsets[:frame * listed], last_charge, both, message, upper), 1,
        [(3, local, atoms)] * 2, force_scratch(local, frame, margin, listed), pairs * frame // domain,
    ))


def solution(mesh):
    placed = (
        P(None, "bead", "space"),
        P(None, "bead", "space"),
        P("space"),
        P("space", None),
        P(None, None, "bead", "space"),
    )
    return jax.shard_map(
        body,
        mesh=mesh,
        in_specs=placed,
        out_specs=(P(None, "bead", "space"), P(None, "bead", "space")),
        check_vma=False,
    )
```

```python
import functools
import math

import jax
import jax.numpy as jnp
import numpy as np
from jax import lax
from jax.experimental import pallas as pl
from jax.experimental.pallas import tpu as pltpu
from jax.sharding import PartitionSpec as P

BLOCK = 128
HALO = 4

half_step = 0.025
time_step = 0.05
chain_freq = 12.0
thermal = 0.375
centroid_friction = 1.0
screening = 4.0
softening = 0.09
CHARGES = (1.0, -1.0, 0.6, -1.4)
MASSES = (1.0, 2.0, 3.0, 4.0)

PAIR_ROWS = 24
PAIR_PAD = 32
SUM_ROWS = 16
QUAD = 4
SLOTS = 4
FRAME = 8
f32 = jnp.float32
bf16 = jnp.bfloat16


def mode_constants(bead_total):
    j = np.arange(bead_total)[:, None]
    k = np.arange(bead_total)[None, :]
    half = bead_total // 2
    phase = 2.0 * np.pi * ((j * k) % bead_total) / bead_total
    plain = 1.0 / math.sqrt(bead_total)
    paired = math.sqrt(2.0 / bead_total)
    matrix = np.where(
        k == 0,
        plain,
        np.where(
            k < half,
            paired * np.cos(phase),
            np.where(k == half, plain * np.cos(phase), paired * np.sin(phase)),
        ),
    )
    modes = np.arange(bead_total)
    frequency = 2.0 * chain_freq * np.sin(np.pi * modes / bead_total)
    angle = frequency * time_step
    ratio = np.where(modes == 0, time_step, np.sin(angle) / np.where(modes == 0, 1.0, frequency))
    friction = np.where(modes == 0, centroid_friction, 2.0 * frequency)
    damping = np.exp(-friction * time_step)
    kick = np.sqrt(1.0 - damping * damping)
    tables = np.stack([np.cos(angle), ratio, frequency * np.sin(angle), damping, kick])
    tables = np.broadcast_to(tables[:, :, None], tables.shape + (BLOCK,))
    return matrix.astype(np.float32), np.ascontiguousarray(tables).astype(np.float32)


def split3(v):
    one = v.astype(bf16).astype(f32)
    rest = v - one
    two = rest.astype(bf16).astype(f32)
    three = (rest - two).astype(bf16).astype(f32)
    return one, two, three


def pair_rows(coords, norm, own):
    rows = []
    for v in coords:
        one, two, three = split3(v)
        if own:
            one, two, three = -2.0 * one, -2.0 * two, -2.0 * three
            rows += [one, one, two, two, one, three]
        else:
            rows += [one, two, one, two, three, one]
    ones = [jnp.ones_like(norm)] * 3
    norms = list(split3(norm))
    return rows + (norms + ones if own else ones + norms)


SCALE = 1.0 / (screening * math.log(2.0))


def weigh(square):
    inverse = lax.rsqrt(square)
    decay = jnp.exp2(-(square * inverse))
    return decay * ((inverse * inverse) * (inverse + math.log(2.0)))


def offsets_of(where_ref, lists_ref, skip, origin, margin):
    first = where_ref[0] + origin

    def offset_at(block, m):
        return jnp.clip(lists_ref[skip + block, m] - (first + block), -margin, margin)

    return offset_at


def whole_quads(beads):
    return -(-beads // QUAD) * QUAD


def add_forces(group, blocks, margin, listed, offset_at, charge_ref, coord_ref, scratch):
    rows_ref, sums_ref, far_ref, heavy_ref, near_ref, total_ref, force_ref, *buffers = scratch
    weight_refs = buffers
    beads = coord_ref.shape[1]
    pairs = beads // 2
    frame = min(FRAME, blocks)
    width = frame + 2 * margin
    middle = margin + (frame - 1) / 2.0
    at_once = max(1, 8 // beads)
    lines = at_once * beads
    units = blocks * pairs

    def put(ref, slot, k, value):
        ref[slot, k * lines:(k + 1) * lines, :] = value

    def centred(block, place):
        spans = [pl.ds(pl.multiple_of((block + i) * BLOCK, BLOCK), BLOCK) for i in range(at_once)]
        coords = [
            (jnp.concatenate([coord_ref[c, :, lanes] for lanes in spans], axis=0) - 1.0) * SCALE for c in range(3)
        ]
        shift = jnp.concatenate(
            [jnp.full((beads, BLOCK), SCALE, f32) * ((place + i).astype(f32) - middle) for i in range(at_once)], axis=0
        )
        coords[0] = coords[0] + shift
        norm = coords[0] * coords[0] + coords[1] * coords[1] + coords[2] * coords[2]
        charge = jnp.concatenate(
            [jnp.broadcast_to(charge_ref[:, lanes], (beads, BLOCK)) for lanes in spans], axis=0
        )
        return coords, norm, charge

    def steps(count, one):
        slots = math.gcd(count, SLOTS)

        def some(turn, carry):
            for slot in range(slots):
                one(turn * slots + slot, slot)
            return carry

        lax.fori_loop(0, count // slots, some, 0)

    nothing = jnp.zeros((lines, BLOCK), f32)
    for slot in range(SLOTS):
        for k in range(PAIR_ROWS, PAIR_PAD):
            put(rows_ref, slot, k, nothing)
        for k in range(12, SUM_ROWS):
            put(sums_ref, slot, k, nothing)
    blank = jnp.zeros((PAIR_PAD, BLOCK), f32)
    passes = width // at_once

    def one_table(step, slot):
        at_frame = step // passes
        place = (step - at_frame * passes) * at_once
        coords, norm, charge = centred(at_frame * frame + place, place)
        for k, row in enumerate(pair_rows(coords, norm, False)):
            put(rows_ref, slot, k, row)
        for c, v in enumerate([charge] + [charge * x for x in coords]):
            for level, part in enumerate(split3(v)):
                put(sums_ref, slot, level * 4 + c, part)
        for i in range(at_once):
            at = at_frame * width + place + i
            for quad in range(beads // QUAD):
                low = i * beads + quad * QUAD
                four = jnp.concatenate(
                    [rows_ref[slot, pl.ds(low + j, PAIR_PAD, stride=lines), :] for j in range(QUAD)], axis=0
                )
                far_ref[at, quad] = jnp.transpose(four.astype(bf16))
                for half in range(2):
                    heavy_ref[at, 2 * quad + half] = jnp.concatenate(
                        [
                            sums_ref[slot, pl.ds(low + 2 * half + j, SUM_ROWS, stride=lines), :]
                            for j in range(2)
                        ],
                        axis=0,
                    ).astype(bf16)

    def one_own(step, slot):
        block = step * at_once
        place = block - block // frame * frame + margin
        coords, norm, _ = centred(block + margin, place)
        for k, row in enumerate(pair_rows(coords, norm + softening * SCALE * SCALE, True)):
            put(rows_ref, slot, k, row)
        for i in range(at_once):
            for pair in range(pairs):
                columns = []
                for j in range(2):
                    own = rows_ref[slot, pl.ds(i * beads + 2 * pair + j, PAIR_PAD, stride=lines), :]
                    spot = 2 * pair % QUAD + j
                    columns.append(
                        jnp.concatenate([own if k == spot else blank for k in range(QUAD)], axis=0)
                    )
                near_ref[(block + i) * pairs + pair] = jnp.concatenate(columns, axis=1).astype(bf16)

    steps(blocks // frame * passes, one_table)
    steps(blocks // at_once, one_own)

    def places(unit):
        block = unit // pairs
        at_frame = block // frame
        base = at_frame * width + block - at_frame * frame + margin
        return [base + offset_at(block, m) for m in range(listed)], unit - block * pairs

    def parts(square):
        weight = weigh(square)
        high = weight.astype(bf16)
        return high, (weight - high.astype(f32)).astype(bf16)

    def squares(ats, pair, unit, m):
        return jnp.dot(far_ref[ats[m], pair // (QUAD // 2)], near_ref[unit], preferred_element_type=f32)

    def weighted(at, pair, both):
        table = heavy_ref[at, pair]
        return jnp.dot(jnp.concatenate([table, table], axis=1), both, preferred_element_type=f32)

    def keep(total, slot):
        for i in range(2):
            cols = slice(i * BLOCK, (i + 1) * BLOCK)
            row = i * SUM_ROWS
            spot = pl.ds(pl.multiple_of((2 * slot + i) * 8, 8), 8)
            total_ref[spot, :] = total[row:row + 8, cols] + total[row + 8:row + 16, cols]

    def body(step, carry):
        before_ats, before_pair = places(jnp.maximum(step * group - 1, 0))
        for turn in range(group):
            unit = step * group + turn
            now, other = turn % 2, (turn + 1) % 2
            ats, pair = places(unit)
            total = jnp.zeros((2 * SUM_ROWS, 2 * BLOCK), f32)
            for m in range(listed):
                spot = slice(2 * m * BLOCK, 2 * (m + 1) * BLOCK)
                weight_refs[now][spot, :] = jnp.concatenate(parts(squares(ats, pair, unit, m)), axis=0)
                total = total + weighted(before_ats[m], before_pair, weight_refs[other][spot, :])
            keep(total, jnp.where(unit == 0, units, unit - 1))
            before_ats, before_pair = ats, pair
        return carry

    group = math.gcd(units, group)
    lax.fori_loop(0, units // group, body, 0)
    last_ats, last_pair = places(units - 1)
    keep(
        sum(
            weighted(last_ats[m], last_pair, weight_refs[(group - 1) % 2][2 * m * BLOCK:2 * (m + 1) * BLOCK, :])
            for m in range(listed)
        ),
        units - 1,
    )

    def one_block(block, slot):
        at_frame = block // frame
        place = block - at_frame * frame + margin
        lanes = pl.ds(pl.multiple_of((block + margin) * BLOCK, BLOCK), BLOCK)
        coords = [(coord_ref[c, :, lanes] - 1.0) * SCALE for c in range(3)]
        coords[0] = coords[0] + SCALE * (place.astype(f32) - middle)
        charge = jnp.broadcast_to(SCALE * SCALE * charge_ref[:, lanes], coords[0].shape)

        def summed(c):
            return sum(total_ref[pl.ds(block * beads * 8 + c + i, beads, stride=8), :] for i in (0, 4))

        near = summed(0)
        own = pl.ds(pl.multiple_of(block * BLOCK, BLOCK), BLOCK)
        for c in range(3):
            force_ref[c, :, own] = charge * (coords[c] * near - summed(c + 1))

    steps(blocks, one_block)


def force_scratch(local, blocks, margin, listed):
    beads = whole_quads(local)
    frame = min(FRAME, blocks)
    tables = (frame + 2 * margin) * (blocks // frame)
    lines = max(8, beads)
    units = blocks * beads // 2
    return [
        pltpu.VMEM((3, beads, (blocks + 2 * margin) * BLOCK), f32),
        pltpu.VMEM((SLOTS, PAIR_PAD * lines, BLOCK), f32),
        pltpu.VMEM((SLOTS, SUM_ROWS * lines, BLOCK), f32),
        pltpu.VMEM((tables, beads // QUAD, BLOCK, QUAD * PAIR_PAD), bf16),
        pltpu.VMEM((tables, beads // 2, 2 * SUM_ROWS, BLOCK), bf16),
        pltpu.VMEM((units, QUAD * PAIR_PAD, 2 * BLOCK), bf16),
        pltpu.VMEM(((units + 1) * 16, BLOCK), f32),
        pltpu.VMEM((3, beads, blocks * BLOCK), f32),
        pltpu.VMEM((2 * listed * BLOCK, 2 * BLOCK), bf16),
        pltpu.VMEM((2 * listed * BLOCK, 2 * BLOCK), bf16),
    ]


def call(kernel, args, smem_count, shapes, scratch, work, in_specs=None):
    vmem = pl.BlockSpec(memory_space=pltpu.VMEM)
    smem = pl.BlockSpec(memory_space=pltpu.SMEM)
    return pl.pallas_call(
        kernel,
        out_shape=[jax.ShapeDtypeStruct(shape, f32) for shape in shapes],
        grid=() if in_specs is None else (1,),
        in_specs=in_specs or [smem] * smem_count + [vmem] * (len(args) - smem_count),
        out_specs=[vmem] * len(shapes),
        scratch_shapes=scratch,
        compiler_params=pltpu.CompilerParams(vmem_limit_bytes=(40 if in_specs is None else 62) * 1024 * 1024),
        cost_estimate=pl.CostEstimate(
            flops=20 * work + 1024, bytes_accessed=4 * 1024 * 1024, transcendentals=2 * work
        ),
    )(*args)


def row_of(c, block, blocks, local):
    return (c * blocks + block) * local


def unpack_beads(source, base, blocks, local, target, offset):
    for c in range(3):
        for block in range(blocks):
            row = row_of(base + c, block, blocks, local)
            lane = offset + block * BLOCK
            for group in range(source.shape[0]):
                target[c, group * local:(group + 1) * local, lane:lane + BLOCK] = source[group, row:row + local, :]


def pack_beads(value, c, blocks, local, target):
    for block in range(blocks):
        row = row_of(c, block, blocks, local)
        for group in range(target.shape[0]):
            target[group, row:row + local, :] = value[
                group * local:(group + 1) * local, block * BLOCK:(block + 1) * BLOCK
            ]


FORCE = 6


def clear(coord_ref, local):
    if coord_ref.shape[1] != local:
        coord_ref[...] = jnp.zeros(coord_ref.shape, f32)


def prepare_kernel(
    blocks, x_ref, edge_ref, noise_ref, types_ref, lists_ref, rest_ref, message_ref, charge_ref, mass_ref
):
    steps, _, local, atoms = noise_ref.shape
    edge = message_ref.shape[2]
    types = types_ref[...]
    charge = jnp.zeros(types.shape, f32)
    mass = jnp.zeros(types.shape, f32)
    for kind in range(4):
        charge = jnp.where(types == kind, CHARGES[kind], charge)
        mass = jnp.where(types == kind, MASSES[kind], mass)
    charge_ref[...] = charge
    mass_ref[...] = mass
    for c in range(3):
        message_ref[c] = x_ref[c, :, :edge]
        message_ref[3 + c] = x_ref[c, :, edge:2 * edge]
        message_ref[6 + c] = edge_ref[c]
    for i, row in enumerate([charge[:, :edge], charge[:, edge:2 * edge], mass[:, :edge]]):
        message_ref[9 + i] = jnp.broadcast_to(row, (local, edge))
    message_ref[12] = jnp.zeros((local, edge), f32)
    for block in range(edge // BLOCK):
        at = block * BLOCK
        message_ref[12, 0:1, at:at + lists_ref.shape[1]] = lists_ref[block:block + 1, :].astype(f32)
    for c in range(3 + 3 * steps):
        for block in range(atoms // BLOCK):
            lanes = slice(block * BLOCK, (block + 1) * BLOCK)
            value = x_ref[c, :, lanes] if c < 3 else noise_ref[c // 3 - 1, c % 3, :, lanes]
            row = row_of(c, block % blocks, blocks, local)
            rest_ref[block // blocks, row:row + local, :] = value


def front_kernel(
    each, margin, listed, where_ref, lists_ref, charge_ref, x_ref, p_ref, pout_ref, coord_ref, *scratch
):
    _, local, _ = x_ref.shape
    blocks = pout_ref.shape[0] * each
    clear(coord_ref, local)
    for c in range(3):
        coord_ref[c, :local, :] = x_ref[c, :, :(blocks + 2 * margin) * BLOCK]
    offset_at = offsets_of(where_ref, lists_ref, margin, margin, margin)
    add_forces(16, blocks, margin, listed, offset_at, charge_ref, coord_ref, scratch)
    force_ref = scratch[FORCE]
    for c in range(3):
        for block in range(blocks):
            lanes = slice(block * BLOCK, (block + 1) * BLOCK)
            moment = p_ref[c, :, (block + margin) * BLOCK:(block + margin + 1) * BLOCK]
            row = row_of(c, block % each, each, local)
            pout_ref[block // each, row:row + local, :] = moment + half_step * force_ref[c, :local, lanes]


def back_kernel(
    each, margin, listed, where_ref, lists_ref, charge_ref, x_ref, message_ref, p_ref, front_ref, *refs
):
    count = lists_ref.shape[0] // each
    pout_refs, (stage_ref, coord_ref, *scratch) = refs[:count], refs[count:]
    _, local, atoms = x_ref.shape
    edge = margin * BLOCK
    done = front_ref.shape[0]
    first = done * each
    blocks = (count - done) * each
    own = atoms - first * BLOCK
    clear(coord_ref, local)
    for c in range(3):
        coord_ref[c, :local, :own] = x_ref[c, :, first * BLOCK:]
        for part in range(2):
            coord_ref[c, :local, own + part * edge:own + (part + 1) * edge] = message_ref[3 * part + c]
    offset_at = offsets_of(where_ref, lists_ref, first, first + margin, margin)
    add_forces(16, blocks, margin, listed, offset_at, charge_ref, coord_ref, scratch)
    force_ref = scratch[FORCE]
    stage_ref[:done] = front_ref[...]
    for c in range(3):
        for block in range(blocks):
            lanes = slice(block * BLOCK, (block + 1) * BLOCK)
            at = (first + block) * BLOCK + edge
            if at < atoms:
                moment = p_ref[c, :, at:at + BLOCK]
            else:
                moment = message_ref[6 + c, :, at - atoms:at - atoms + BLOCK]
            row = row_of(c, block % each, each, local)
            stage_ref[done + block // each, row:row + local, :] = moment + half_step * force_ref[c, :local, lanes]
    hand_out(stage_ref, pout_refs, where_ref[1])


def hand_out(stage_ref, out_refs, place):
    count = len(out_refs)
    for away in range(count):
        out_refs[away][...] = stage_ref[lax.rem(place + away, count)]


def take_in(refs, stage_ref, place):
    count = len(refs)
    for away in range(count):
        stage_ref[lax.rem(place - away + count, count)] = refs[away][...]


def from_packed(ref, c, block, each, local):
    row = row_of(c, block % each, each, local)
    return ref[block // each, row:row + local, :]


def upper_kernel(each, margin, listed, where_ref, lists_ref, charge_ref, both_ref, pout_ref, coord_ref, *scratch):
    _, local, atoms = pout_ref.shape
    blocks = atoms // BLOCK
    domain = both_ref.shape[0] * each
    skipped = domain - blocks - 2 * margin
    clear(coord_ref, local)
    for c in range(3):
        for block in range(skipped, domain):
            at = (block - skipped) * BLOCK
            coord_ref[c, :local, at:at + BLOCK] = from_packed(both_ref, c, block, each, local)
    offset_at = offsets_of(where_ref, lists_ref, domain - blocks, domain - blocks, margin)
    add_forces(16, blocks, margin, listed, offset_at, charge_ref, coord_ref, scratch)
    force_ref = scratch[FORCE]
    for c in range(3):
        for block in range(blocks):
            lanes = slice(block * BLOCK, (block + 1) * BLOCK)
            moment = from_packed(both_ref, 3 + c, domain - blocks + block - margin, each, local)
            pout_ref[c, :, lanes] = moment + half_step * force_ref[c, :local, lanes]


def lower_kernel(
    each, margin, listed, where_ref, lists_ref, charge_ref, both_ref, message_ref, upper_ref, xout_ref, pout_ref, coord_ref,
    *scratch,
):
    _, local, atoms = xout_ref.shape
    edge = margin * BLOCK
    lower = atoms - upper_ref.shape[2]
    blocks = lower // BLOCK
    clear(coord_ref, local)
    for c in range(3):
        for part in range(2):
            coord_ref[c, :local, part * edge:(part + 1) * edge] = message_ref[3 * part + c]
        for block in range(blocks):
            at = 2 * edge + block * BLOCK
            coord_ref[c, :local, at:at + BLOCK] = from_packed(both_ref, c, block, each, local)
        xout_ref[c, :, :edge] = message_ref[3 + c]
        for block in range(margin, atoms // BLOCK):
            lanes = slice(block * BLOCK, (block + 1) * BLOCK)
            xout_ref[c, :, lanes] = from_packed(both_ref, c, block - margin, each, local)
        pout_ref[c, :, lower:] = upper_ref[c]
    offset_at = offsets_of(where_ref, lists_ref, 0, 0, margin)
    add_forces(16, blocks, margin, listed, offset_at, charge_ref, coord_ref, scratch)
    force_ref = scratch[FORCE]
    for c in range(3):
        for block in range(blocks):
            lanes = slice(block * BLOCK, (block + 1) * BLOCK)
            if block < margin:
                moment = message_ref[6 + c, :, lanes]
            else:
                moment = from_packed(both_ref, 3 + c, block - margin, each, local)
            pout_ref[c, :, lanes] = moment + half_step * force_ref[c, :local, lanes]


def thermostat(coords, moments, noises, mass_ref, matrix_ref, matrix_t_ref, table_ref, store):
    beads, width = moments[0].shape
    cosine, ratio, stiffness, damping, kick = [
        jnp.concatenate([table_ref[i]] * (width // BLOCK), axis=1) for i in range(5)
    ]
    mass = jnp.broadcast_to(mass_ref[...], (beads, width))
    spread = kick * jnp.sqrt(thermal * mass)
    drift = ratio / mass
    stiff = stiffness * mass
    multiply = functools.partial(jnp.dot, precision=lax.Precision.HIGHEST, preferred_element_type=f32)
    for c in range(3):
        mode_x = multiply(matrix_t_ref[...], coords[c])
        mode_p = damping * multiply(matrix_t_ref[...], moments[c]) + spread * noises[c]
        store(
            c,
            multiply(matrix_ref[...], cosine * mode_x + drift * mode_p),
            multiply(matrix_ref[...], cosine * mode_p - stiff * mode_x),
        )


def modes_kernel(blocks, noise_base, count, where_ref, rest_ref, *refs):
    p_refs, refs = refs[:count], refs[count:]
    mass_ref, matrix_ref, matrix_t_ref, table_ref, xout_ref, pout_ref, stage_ref, coord_ref, moment_ref, noise_ref = refs
    local = stage_ref.shape[1] // (3 * blocks)
    take_in(p_refs, stage_ref, where_ref[1])
    unpack_beads(rest_ref, 0, blocks, local, coord_ref, 0)
    unpack_beads(stage_ref, 0, blocks, local, moment_ref, 0)
    unpack_beads(rest_ref, noise_base, blocks, local, noise_ref, 0)

    def store(c, x, p):
        pack_beads(x, c, blocks, local, xout_ref)
        pack_beads(p, c, blocks, local, pout_ref)

    thermostat(
        *[[ref[c] for c in range(3)] for ref in (coord_ref, moment_ref, noise_ref)],
        mass_ref, matrix_ref, matrix_t_ref, table_ref, store,
    )


def middle_kernel(hops, blocks, listed, noise_base, joined, where_ref, lists_ref, charge_ref, *refs):
    parts = 2 * hops + 1
    x_refs = refs[:parts]
    p_ref, noise_ref, mass_ref, matrix_ref, matrix_t_ref, table_ref = refs[parts:parts + 6]
    outs = refs[parts + 6:parts + (7 if joined else 8)]
    coord_ref, *scratch = refs[parts + len(outs) + 6:]
    beads = coord_ref.shape[1]
    local = beads // p_ref.shape[0]
    width = blocks * BLOCK
    for part in range(parts):
        unpack_beads(x_refs[part], 0, blocks, local, coord_ref, part * width)
    offset_at = offsets_of(where_ref, lists_ref, 0, 0, hops * blocks)
    add_forces(16, blocks, hops * blocks, listed, offset_at, charge_ref, coord_ref, scratch)
    force_ref = scratch[FORCE]
    unpack_beads(p_ref, 0, blocks, local, coord_ref, 0)
    unpack_beads(noise_ref, noise_base, blocks, local, coord_ref, (parts - 1) * width)

    def share(c, part):
        return coord_ref[c, :, part * width:(part + 1) * width]

    def store(c, x, p):
        pack_beads(x, c, blocks, local, outs[0])
        if joined:
            pack_beads(p, 3 + c, blocks, local, outs[0])
        else:
            pack_beads(p, c, blocks, local, outs[1])

    thermostat(
        [share(c, hops) for c in range(3)],
        [share(c, 0) + 2.0 * half_step * force_ref[c] for c in range(3)],
        [share(c, parts - 1) for c in range(3)],
        mass_ref, matrix_ref, matrix_t_ref, table_ref, store,
    )


def fold(count):
    return [i // 2 if i % 2 == 0 else count - 1 - i // 2 for i in range(count)]


def exchange(pieces):
    order = fold(pieces.shape[0])
    group = [order.index(at) for at in range(len(order))]
    return lax.all_to_all(pieces, "bead", split_axis=0, concat_axis=0, axis_index_groups=[group], tiled=True)


def exchange_steps(pieces):
    count = len(pieces)
    order = fold(count)
    return [
        lax.ppermute(piece, "bead", [(order.index(i), order.index((i + away) % count)) for i in range(count)])
        if away else piece
        for away, piece in enumerate(pieces)
    ]


def passed(values, step):
    count = lax.axis_size("space")
    return lax.ppermute(values, "space", [(i, (i + step) % count) for i in range(count)])


def round_ring(values, hop):
    count = lax.axis_size("bead")
    domains = lax.axis_size("space")
    order = fold(count)
    device = {}
    for bead in range(count):
        for domain in range(domains):
            device[domain * count + order[bead]] = bead * domains + domain
    total = count * domains
    return lax.ppermute(values, ("bead", "space"), [(device[(at + hop) % total], device[at]) for at in range(total)])


def window(values, hops):
    return [round_ring(values, hop) if hop else values for hop in range(-hops, hops + 1)]


def body(positions, momenta, atom_types, neighbours, thermal_noise):
    count = lax.axis_size("bead")
    _, local, atoms = positions.shape
    beads = local * count
    domain = atoms // BLOCK
    blocks = domain // count
    share = blocks * BLOCK
    hops = -(-HALO // blocks)
    margin = hops * blocks
    edge = margin * BLOCK
    steps = thermal_noise.shape[0]
    listed = neighbours.shape[1]
    order = fold(count)

    packed = (count, 3 * blocks * local, BLOCK)
    whole = [positions.shape, (3, local, edge), thermal_noise.shape, (1, atoms), neighbours.shape]
    rest, message, charge, mass = call(
        functools.partial(prepare_kernel, blocks),
        (positions, momenta, thermal_noise, atom_types[None, :], neighbours), 0,
        [(count, (1 + steps) * packed[1], BLOCK), (13, local, edge), (1, atoms), (1, atoms)], [], 0,
        [pl.BlockSpec(shape, lambda i, rank=len(shape): (0,) * rank) for shape in whole],
    )
    message = passed(message, -1)
    rest = exchange(rest)
    side = message[9:, 0]
    first_charge = jnp.concatenate([charge, side[:1], side[1:2]], axis=1)
    moved_mass = jnp.concatenate([mass[0, edge:], side[2]])
    domains = lax.axis_size("space")
    at_space = lax.axis_index("space")
    foreign = side[3].reshape(margin, BLOCK)[:, :listed].astype(jnp.int32)
    foreign = foreign + jnp.where(at_space == domains - 1, domains * domain, 0)
    moved_lists = jnp.concatenate([neighbours[margin:], foreign], axis=0)

    place = jnp.asarray(np.array(order, np.int32))[lax.axis_index("bead")]
    near_charge = lax.dynamic_slice_in_dim(first_charge, place * share, share + 2 * edge, axis=1)
    near_mass = lax.dynamic_slice_in_dim(moved_mass, place * share, share)[None, :]
    near_lists = lax.dynamic_slice_in_dim(moved_lists, place * blocks, blocks)
    first_block = at_space * domain
    where = jnp.stack([first_block, place]).astype(jnp.int32)
    near_where = jnp.stack([first_block + margin + place * blocks, place]).astype(jnp.int32)

    matrix, tables = mode_constants(beads)
    at = np.concatenate([order.index(g) * local + np.arange(local) for g in range(count)])
    matrix = matrix[at][:, at]
    fixed = (near_mass, jnp.asarray(matrix), jnp.asarray(np.ascontiguousarray(matrix.T)), jnp.asarray(tables[:, at]))

    pairs = beads * blocks * listed * BLOCK * BLOCK
    frame = min(FRAME, domain // 2)
    most = domain - 2 * frame
    window_atoms = (most + 2 * margin) * BLOCK
    (moment,) = call(
        functools.partial(front_kernel, blocks, margin, listed),
        (where, neighbours, charge[:, :window_atoms], positions, momenta), 2,
        [(most // blocks,) + packed[1:]], force_scratch(local, most, margin, listed), pairs * most // domain,
    )
    moment, rest = lax.optimization_barrier((moment, rest))
    rest = round_ring(rest, hops)
    moments = call(
        functools.partial(back_kernel, blocks, margin, listed),
        (where, moved_lists, first_charge[:, most * BLOCK:], positions, message, momenta, moment), 2,
        [packed[1:]] * count, [pltpu.VMEM(packed, f32)] + force_scratch(local, domain - most, margin, listed),
        pairs * (domain - most) // domain,
    )
    coords, moment = call(
        functools.partial(modes_kernel, blocks, 3, count),
        (where, rest) + tuple(exchange_steps(moments)) + fixed, 1, [packed] * 2,
        [pltpu.VMEM(packed, f32)] + [pltpu.VMEM((3, beads, share), f32)] * 3, 0,
    )
    for step in range(1, steps):
        joined = step == steps - 1
        out = call(
            functools.partial(middle_kernel, hops, blocks, listed, 3 * step + 3, joined),
            (near_where, near_lists, near_charge) + tuple(window(coords, hops)) + (moment, rest) + fixed, 2,
            [(count, 6 * blocks * local, BLOCK)] if joined else [packed] * 2,
            force_scratch(beads, blocks, margin, listed), pairs,
        )
        if not joined:
            coords, moment = out
    both = exchange(out[0])

    def ends(low, c):
        pieces = both[low:low + hops, c * packed[1]:(c + 1) * packed[1]]
        return pieces.reshape(hops, 3, blocks, local, BLOCK).transpose(1, 3, 0, 2, 4).reshape(3, local, edge)

    message = passed(jnp.concatenate([
        ends(count - 2 * hops, 0), ends(count - hops, 0), ends(count - hops, 1),
        jnp.broadcast_to(charge[:, None, atoms - edge:], (1, local, edge)),
    ], axis=0), 1)
    (upper,) = call(
        functools.partial(upper_kernel, blocks, margin, listed),
        (where, neighbours, first_charge[:, 2 * frame * BLOCK - edge:atoms + edge], both), 2,
        [(3, local, most * BLOCK)], force_scratch(local, most, margin, listed), pairs * most // domain,
    )
    last_charge = jnp.concatenate([message[9, :1], first_charge[:, :2 * frame * BLOCK + edge]], axis=1)
    return tuple(call(
        functools.partial(lower_kernel, blocks, margin, listed),
        (where, neighbours, last_charge, both, message, upper), 2,
        [(3, local, atoms)] * 2, force_scratch(local, domain - most, margin, listed), pairs * (domain - most) // domain,
    ))


def solution(mesh):
    placed = (
        P(None, "bead", "space"),
        P(None, "bead", "space"),
        P("space"),
        P("space", None),
        P(None, None, "bead", "space"),
    )
    return jax.shard_map(
        body,
        mesh=mesh,
        in_specs=placed,
        out_specs=(P(None, "bead", "space"), P(None, "bead", "space")),
        check_vma=False,
    )
```

```python
import functools
import math

import jax
import jax.numpy as jnp
import numpy as np
from jax import lax
from jax.experimental import pallas as pl
from jax.experimental.pallas import tpu as pltpu
from jax.sharding import PartitionSpec as P

BLOCK = 128
HALO = 4

half_step = 0.025
time_step = 0.05
chain_freq = 12.0
thermal = 0.375
centroid_friction = 1.0
screening = 4.0
softening = 0.09
CHARGES = (1.0, -1.0, 0.6, -1.4)
MASSES = (1.0, 2.0, 3.0, 4.0)

PAIR_ROWS = 24
PAIR_PAD = 32
SUM_ROWS = 16
QUAD = 4
SLOTS = 4
FRAME = 8
f32 = jnp.float32
bf16 = jnp.bfloat16


def mode_constants(bead_total):
    j = np.arange(bead_total)[:, None]
    k = np.arange(bead_total)[None, :]
    half = bead_total // 2
    phase = 2.0 * np.pi * ((j * k) % bead_total) / bead_total
    plain = 1.0 / math.sqrt(bead_total)
    paired = math.sqrt(2.0 / bead_total)
    matrix = np.where(
        k == 0,
        plain,
        np.where(
            k < half,
            paired * np.cos(phase),
            np.where(k == half, plain * np.cos(phase), paired * np.sin(phase)),
        ),
    )
    modes = np.arange(bead_total)
    frequency = 2.0 * chain_freq * np.sin(np.pi * modes / bead_total)
    angle = frequency * time_step
    ratio = np.where(modes == 0, time_step, np.sin(angle) / np.where(modes == 0, 1.0, frequency))
    friction = np.where(modes == 0, centroid_friction, 2.0 * frequency)
    damping = np.exp(-friction * time_step)
    kick = np.sqrt(1.0 - damping * damping)
    tables = np.stack([np.cos(angle), ratio, frequency * np.sin(angle), damping, kick])
    tables = np.broadcast_to(tables[:, :, None], tables.shape + (BLOCK,))
    return matrix.astype(np.float32), np.ascontiguousarray(tables).astype(np.float32)


def split3(v):
    one = v.astype(bf16).astype(f32)
    rest = v - one
    two = rest.astype(bf16).astype(f32)
    three = (rest - two).astype(bf16).astype(f32)
    return one, two, three


def pair_rows(coords, norm, own):
    rows = []
    for v in coords:
        one, two, three = split3(v)
        if own:
            one, two, three = -2.0 * one, -2.0 * two, -2.0 * three
            rows += [one, one, two, two, one, three]
        else:
            rows += [one, two, one, two, three, one]
    ones = [jnp.ones_like(norm)] * 3
    norms = list(split3(norm))
    return rows + (norms + ones if own else ones + norms)


SCALE = 1.0 / (screening * math.log(2.0))


def weigh(square):
    inverse = lax.rsqrt(square)
    decay = jnp.exp2(-(square * inverse))
    return decay * ((inverse * inverse) * (inverse + math.log(2.0)))


def own_place(count):
    bead = lax.axis_index("bead")
    half = lax.div(bead, 2)
    return jnp.where(lax.rem(bead, 2) == 0, half, count - 1 - half)


def offsets_of(lists_ref, skip, origin, margin):
    first = lax.axis_index("space") * lists_ref.shape[1] + origin

    def offset_at(block, m):
        return jnp.clip(lists_ref[m, skip + block] - (first + block), -margin, margin)

    return offset_at


def charges(types):
    charge = jnp.zeros(types.shape, f32)
    for kind in range(4):
        charge = jnp.where(types == kind, CHARGES[kind], charge)
    return charge


def odd_tiles(lines):
    return lines + 8 * (1 - lines // 8 % 2)


def whole_quads(beads):
    return -(-beads // QUAD) * QUAD


def add_forces(group, blocks, margin, listed, offset_at, charge_ref, coord_ref, scratch, charge_from=0):
    rows_ref, sums_ref, far_ref, heavy_ref, near_ref, total_ref, force_ref, *buffers = scratch
    weight_refs = buffers
    beads = coord_ref.shape[1]
    pairs = beads // 2
    frame = min(FRAME, blocks)
    width = frame + 2 * margin
    middle = margin + (frame - 1) / 2.0
    at_once = max(1, 8 // beads)
    lines = at_once * beads
    apart = odd_tiles(lines)
    units = blocks * pairs

    def charge_at(block):
        return charge_ref[:, pl.ds(pl.multiple_of((charge_from + block) * BLOCK, BLOCK), BLOCK)]

    def put(ref, slot, k, value):
        ref[slot, k * apart:k * apart + lines, :] = value

    def centred(block, place):
        spans = [pl.ds(pl.multiple_of((block + i) * BLOCK, BLOCK), BLOCK) for i in range(at_once)]
        coords = [
            (jnp.concatenate([coord_ref[c, :, lanes] for lanes in spans], axis=0) - 1.0) * SCALE for c in range(3)
        ]
        shift = jnp.concatenate(
            [jnp.full((beads, BLOCK), SCALE, f32) * ((place + i).astype(f32) - middle) for i in range(at_once)], axis=0
        )
        coords[0] = coords[0] + shift
        norm = coords[0] * coords[0] + coords[1] * coords[1] + coords[2] * coords[2]
        charge = jnp.concatenate(
            [jnp.broadcast_to(charge_at(block + i), (beads, BLOCK)) for i in range(at_once)], axis=0
        )
        return coords, norm, charge

    def steps(count, one):
        slots = math.gcd(count, SLOTS)

        def some(turn, carry):
            for slot in range(slots):
                one(turn * slots + slot, slot)
            return carry

        lax.fori_loop(0, count // slots, some, 0)

    nothing = jnp.zeros((lines, BLOCK), f32)
    for slot in range(SLOTS):
        for k in range(PAIR_ROWS, PAIR_PAD):
            put(rows_ref, slot, k, nothing)
        for k in range(12, SUM_ROWS):
            put(sums_ref, slot, k, nothing)
    blank = jnp.zeros((PAIR_PAD, BLOCK), f32)
    passes = width // at_once

    def one_table(step, slot):
        at_frame = step // passes
        place = (step - at_frame * passes) * at_once
        coords, norm, charge = centred(at_frame * frame + place, place)
        for k, row in enumerate(pair_rows(coords, norm, False)):
            put(rows_ref, slot, k, row)
        for c, v in enumerate([charge] + [charge * x for x in coords]):
            for level, part in enumerate(split3(v)):
                put(sums_ref, slot, level * 4 + c, part)
        for i in range(at_once):
            at = at_frame * width + place + i
            for quad in range(beads // QUAD):
                low = i * beads + quad * QUAD
                four = jnp.concatenate(
                    [rows_ref[slot, pl.ds(low + j, PAIR_PAD, stride=apart), :] for j in range(QUAD)], axis=0
                )
                far_ref[at, quad] = jnp.transpose(four.astype(bf16))
                for half in range(2):
                    heavy_ref[at, 2 * quad + half] = jnp.concatenate(
                        [
                            sums_ref[slot, pl.ds(low + 2 * half + j, SUM_ROWS, stride=apart), :]
                            for j in range(2)
                        ],
                        axis=0,
                    ).astype(bf16)

    def one_own(step, slot):
        block = step * at_once
        place = block - block // frame * frame + margin
        coords, norm, _ = centred(block + margin, place)
        for k, row in enumerate(pair_rows(coords, norm + softening * SCALE * SCALE, True)):
            put(rows_ref, slot, k, row)
        for i in range(at_once):
            for pair in range(pairs):
                columns = []
                for j in range(2):
                    own = rows_ref[slot, pl.ds(i * beads + 2 * pair + j, PAIR_PAD, stride=apart), :]
                    spot = 2 * pair % QUAD + j
                    columns.append(
                        jnp.concatenate([own if k == spot else blank for k in range(QUAD)], axis=0)
                    )
                near_ref[(block + i) * pairs + pair] = jnp.concatenate(columns, axis=1).astype(bf16)

    steps(blocks // frame * passes, one_table)
    steps(blocks // at_once, one_own)

    def places(unit):
        block = unit // pairs
        at_frame = block // frame
        base = at_frame * width + block - at_frame * frame + margin
        return [base + offset_at(block, m) for m in range(listed)], unit - block * pairs

    def parts(square):
        weight = weigh(square)
        high = weight.astype(bf16)
        return high, (weight - high.astype(f32)).astype(bf16)

    def squares(ats, pair, unit, m):
        return jnp.dot(far_ref[ats[m], pair // (QUAD // 2)], near_ref[unit], preferred_element_type=f32)

    def weighted(at, pair, both):
        table = heavy_ref[at, pair]
        return jnp.dot(jnp.concatenate([table, table], axis=1), both, preferred_element_type=f32)

    def keep(total, slot):
        for i in range(2):
            cols = slice(i * BLOCK, (i + 1) * BLOCK)
            row = i * SUM_ROWS
            spot = pl.ds(pl.multiple_of((2 * slot + i) * 8, 8), 8)
            total_ref[spot, :] = total[row:row + 8, cols] + total[row + 8:row + 16, cols]

    def body(step, carry):
        before_ats, before_pair = places(jnp.maximum(step * group - 1, 0))
        for turn in range(group):
            unit = step * group + turn
            now, other = turn % 2, (turn + 1) % 2
            ats, pair = places(unit)
            total = jnp.zeros((2 * SUM_ROWS, 2 * BLOCK), f32)
            for m in range(listed):
                spot = slice(2 * m * BLOCK, 2 * (m + 1) * BLOCK)
                weight_refs[now][spot, :] = jnp.concatenate(parts(squares(ats, pair, unit, m)), axis=0)
                total = total + weighted(before_ats[m], before_pair, weight_refs[other][spot, :])
            keep(total, jnp.where(unit == 0, units, unit - 1))
            before_ats, before_pair = ats, pair
        return carry

    group = math.gcd(units, group)
    lax.fori_loop(0, units // group, body, 0)
    last_ats, last_pair = places(units - 1)
    keep(
        sum(
            weighted(last_ats[m], last_pair, weight_refs[(group - 1) % 2][2 * m * BLOCK:2 * (m + 1) * BLOCK, :])
            for m in range(listed)
        ),
        units - 1,
    )

    def one_block(block, slot):
        at_frame = block // frame
        place = block - at_frame * frame + margin
        lanes = pl.ds(pl.multiple_of((block + margin) * BLOCK, BLOCK), BLOCK)
        coords = [(coord_ref[c, :, lanes] - 1.0) * SCALE for c in range(3)]
        coords[0] = coords[0] + SCALE * (place.astype(f32) - middle)
        charge = jnp.broadcast_to(SCALE * SCALE * charge_at(block + margin), coords[0].shape)

        def summed(c):
            return sum(total_ref[pl.ds(block * beads * 8 + c + i, beads, stride=8), :] for i in (0, 4))

        near = summed(0)
        own = pl.ds(pl.multiple_of(block * BLOCK, BLOCK), BLOCK)
        for c in range(3):
            force_ref[c, :, own] = charge * (coords[c] * near - summed(c + 1))

    steps(blocks, one_block)


def force_scratch(local, blocks, margin, listed):
    beads = whole_quads(local)
    frame = min(FRAME, blocks)
    tables = (frame + 2 * margin) * (blocks // frame)
    lines = max(8, beads)
    units = blocks * beads // 2
    return [
        pltpu.VMEM((3, beads, (blocks + 2 * margin) * BLOCK), f32),
        pltpu.VMEM((SLOTS, PAIR_PAD * odd_tiles(lines), BLOCK), f32),
        pltpu.VMEM((SLOTS, SUM_ROWS * odd_tiles(lines), BLOCK), f32),
        pltpu.VMEM((tables, beads // QUAD, BLOCK, QUAD * PAIR_PAD), bf16),
        pltpu.VMEM((tables, beads // 2, 2 * SUM_ROWS, BLOCK), bf16),
        pltpu.VMEM((units, QUAD * PAIR_PAD, 2 * BLOCK), bf16),
        pltpu.VMEM(((units + 1) * 16, BLOCK), f32),
        pltpu.VMEM((3, beads, blocks * BLOCK), f32),
        pltpu.VMEM((2 * listed * BLOCK, 2 * BLOCK), bf16),
        pltpu.VMEM((2 * listed * BLOCK, 2 * BLOCK), bf16),
    ]


def call(kernel, args, smem_count, shapes, scratch, work, in_specs=None):
    vmem = pl.BlockSpec(memory_space=pltpu.VMEM)
    smem = pl.BlockSpec(memory_space=pltpu.SMEM)
    return pl.pallas_call(
        kernel,
        out_shape=[jax.ShapeDtypeStruct(shape, f32) for shape in shapes],
        grid=() if in_specs is None else (1,),
        in_specs=in_specs or [smem] * smem_count + [vmem] * (len(args) - smem_count),
        out_specs=[vmem] * len(shapes),
        scratch_shapes=scratch,
        compiler_params=pltpu.CompilerParams(vmem_limit_bytes=(40 if in_specs is None else 62) * 1024 * 1024),
        cost_estimate=pl.CostEstimate(
            flops=20 * work + 1024, bytes_accessed=4 * 1024 * 1024, transcendentals=2 * work
        ),
    )(*args)


def row_of(c, block, blocks, local):
    return (c * blocks + block) * local


def unpack_beads(source, base, blocks, local, target, offset):
    for c in range(3):
        for block in range(blocks):
            row = row_of(base + c, block, blocks, local)
            lane = offset + block * BLOCK
            for group in range(source.shape[0]):
                target[c, group * local:(group + 1) * local, lane:lane + BLOCK] = source[group, row:row + local, :]


def pack_beads(value, c, blocks, local, target):
    for block in range(blocks):
        row = row_of(c, block, blocks, local)
        for group in range(target.shape[0]):
            target[group, row:row + local, :] = value[
                group * local:(group + 1) * local, block * BLOCK:(block + 1) * BLOCK
            ]


FORCE = 6


def clear(coord_ref, local):
    if coord_ref.shape[1] != local:
        coord_ref[...] = jnp.zeros(coord_ref.shape, f32)


def prepare_kernel(
    blocks, x_ref, edge_ref, noise_ref, types_ref, lists_ref, rest_ref, message_ref, charge_ref, mass_ref
):
    steps, _, local, atoms = noise_ref.shape
    edge = message_ref.shape[2]
    types = types_ref[...]
    charge = charges(types)
    mass = jnp.zeros(types.shape, f32)
    for kind in range(4):
        mass = jnp.where(types == kind, MASSES[kind], mass)
    charge_ref[...] = charge
    mass_ref[...] = mass
    for c in range(3):
        message_ref[c] = x_ref[c, :, :edge]
        message_ref[3 + c] = x_ref[c, :, edge:2 * edge]
        message_ref[6 + c] = edge_ref[c]
    for i, row in enumerate([charge[:, :edge], charge[:, edge:2 * edge], mass[:, :edge]]):
        message_ref[9 + i] = jnp.broadcast_to(row, (local, edge))
    message_ref[12] = jnp.zeros((local, edge), f32)
    for m in range(lists_ref.shape[0]):
        at = m * (edge // 8)
        message_ref[12, 0:1, at:at + edge // BLOCK] = lists_ref[m:m + 1, :edge // BLOCK].astype(f32)
    for c in range(3 + 3 * steps):
        for block in range(atoms // BLOCK):
            lanes = slice(block * BLOCK, (block + 1) * BLOCK)
            value = x_ref[c, :, lanes] if c < 3 else noise_ref[c // 3 - 1, c % 3, :, lanes]
            row = row_of(c, block % blocks, blocks, local)
            rest_ref[block // blocks, row:row + local, :] = value


def front_kernel(
    each, margin, listed, lists_ref, types_ref, x_ref, p_ref, pout_ref, charge_ref, coord_ref, *scratch
):
    _, local, _ = x_ref.shape
    blocks = pout_ref.shape[0] * each
    charge_ref[...] = charges(types_ref[...])
    clear(coord_ref, local)
    for c in range(3):
        coord_ref[c, :local, :] = x_ref[c, :, :(blocks + 2 * margin) * BLOCK]
    offset_at = offsets_of(lists_ref, margin, margin, margin)
    add_forces(16, blocks, margin, listed, offset_at, charge_ref, coord_ref, scratch)
    force_ref = scratch[FORCE]
    for c in range(3):
        for block in range(blocks):
            lanes = slice(block * BLOCK, (block + 1) * BLOCK)
            moment = p_ref[c, :, (block + margin) * BLOCK:(block + margin + 1) * BLOCK]
            row = row_of(c, block % each, each, local)
            pout_ref[block // each, row:row + local, :] = moment + half_step * force_ref[c, :local, lanes]


def back_kernel(
    each, margin, listed, lists_ref, charge_ref, x_ref, message_ref, p_ref, front_ref, pout_ref, coord_ref, *scratch
):
    _, local, atoms = x_ref.shape
    edge = margin * BLOCK
    done = front_ref.shape[0]
    first = done * each
    blocks = (pout_ref.shape[0] - done) * each
    own = atoms - first * BLOCK
    clear(coord_ref, local)
    for c in range(3):
        coord_ref[c, :local, :own] = x_ref[c, :, first * BLOCK:]
        for part in range(2):
            coord_ref[c, :local, own + part * edge:own + (part + 1) * edge] = message_ref[3 * part + c]
    offset_at = offsets_of(lists_ref, first, first + margin, margin)
    add_forces(16, blocks, margin, listed, offset_at, charge_ref, coord_ref, scratch, first)
    force_ref = scratch[FORCE]
    pout_ref[:done] = front_ref[...]
    for c in range(3):
        for block in range(blocks):
            lanes = slice(block * BLOCK, (block + 1) * BLOCK)
            at = (first + block) * BLOCK + edge
            if at < atoms:
                moment = p_ref[c, :, at:at + BLOCK]
            else:
                moment = message_ref[6 + c, :, at - atoms:at - atoms + BLOCK]
            row = row_of(c, block % each, each, local)
            pout_ref[done + block // each, row:row + local, :] = moment + half_step * force_ref[c, :local, lanes]


def from_packed(ref, c, block, each, local):
    row = row_of(c, block % each, each, local)
    return ref[block // each, row:row + local, :]


def upper_kernel(each, margin, listed, lists_ref, charge_ref, both_ref, pout_ref, coord_ref, *scratch):
    _, local, atoms = pout_ref.shape
    blocks = atoms // BLOCK
    domain = both_ref.shape[0] * each
    skipped = domain - blocks - 2 * margin
    clear(coord_ref, local)
    for c in range(3):
        for block in range(skipped, domain):
            at = (block - skipped) * BLOCK
            coord_ref[c, :local, at:at + BLOCK] = from_packed(both_ref, c, block, each, local)
    offset_at = offsets_of(lists_ref, domain - blocks, domain - blocks, margin)
    add_forces(16, blocks, margin, listed, offset_at, charge_ref, coord_ref, scratch, skipped + margin)
    force_ref = scratch[FORCE]
    for c in range(3):
        for block in range(blocks):
            lanes = slice(block * BLOCK, (block + 1) * BLOCK)
            moment = from_packed(both_ref, 3 + c, domain - blocks + block - margin, each, local)
            pout_ref[c, :, lanes] = moment + half_step * force_ref[c, :local, lanes]


def lower_kernel(
    each, margin, listed, lists_ref, charge_ref, both_ref, message_ref, upper_ref, xout_ref, pout_ref, coord_ref,
    *scratch,
):
    _, local, atoms = xout_ref.shape
    edge = margin * BLOCK
    lower = atoms - upper_ref.shape[2]
    blocks = lower // BLOCK
    clear(coord_ref, local)
    for c in range(3):
        for part in range(2):
            coord_ref[c, :local, part * edge:(part + 1) * edge] = message_ref[3 * part + c]
        for block in range(blocks):
            at = 2 * edge + block * BLOCK
            coord_ref[c, :local, at:at + BLOCK] = from_packed(both_ref, c, block, each, local)
        xout_ref[c, :, :edge] = message_ref[3 + c]
        for block in range(margin, atoms // BLOCK):
            lanes = slice(block * BLOCK, (block + 1) * BLOCK)
            xout_ref[c, :, lanes] = from_packed(both_ref, c, block - margin, each, local)
        pout_ref[c, :, lower:] = upper_ref[c]
    offset_at = offsets_of(lists_ref, 0, 0, margin)
    add_forces(16, blocks, margin, listed, offset_at, charge_ref, coord_ref, scratch)
    force_ref = scratch[FORCE]
    for c in range(3):
        for block in range(blocks):
            lanes = slice(block * BLOCK, (block + 1) * BLOCK)
            if block < margin:
                moment = message_ref[6 + c, :, lanes]
            else:
                moment = from_packed(both_ref, 3 + c, block - margin, each, local)
            pout_ref[c, :, lanes] = moment + half_step * force_ref[c, :local, lanes]


def thermostat(coords, moments, noises, mass_ref, matrix_ref, matrix_t_ref, table_ref, store):
    beads, width = moments[0].shape
    cosine, ratio, stiffness, damping, kick = [
        jnp.concatenate([table_ref[i]] * (width // BLOCK), axis=1) for i in range(5)
    ]
    first = pl.multiple_of(own_place(mass_ref.shape[1] // width) * width, BLOCK)
    mass = jnp.broadcast_to(mass_ref[:, pl.ds(first, width)], (beads, width))
    spread = kick * jnp.sqrt(thermal * mass)
    drift = ratio / mass
    stiff = stiffness * mass
    multiply = functools.partial(jnp.dot, precision=lax.Precision.HIGHEST, preferred_element_type=f32)
    for c in range(3):
        mode_x = multiply(matrix_t_ref[...], coords[c])
        mode_p = damping * multiply(matrix_t_ref[...], moments[c]) + spread * noises[c]
        store(
            c,
            multiply(matrix_ref[...], cosine * mode_x + drift * mode_p),
            multiply(matrix_ref[...], cosine * mode_p - stiff * mode_x),
        )


def modes_kernel(
    blocks, noise_base, rest_ref, p_ref, mass_ref, matrix_ref, matrix_t_ref, table_ref,
    xout_ref, pout_ref, coord_ref, moment_ref, noise_ref,
):
    local = p_ref.shape[1] // (3 * blocks)
    unpack_beads(rest_ref, 0, blocks, local, coord_ref, 0)
    unpack_beads(p_ref, 0, blocks, local, moment_ref, 0)
    unpack_beads(rest_ref, noise_base, blocks, local, noise_ref, 0)

    def store(c, x, p):
        pack_beads(x, c, blocks, local, xout_ref)
        pack_beads(p, c, blocks, local, pout_ref)

    thermostat(
        *[[ref[c] for c in range(3)] for ref in (coord_ref, moment_ref, noise_ref)],
        mass_ref, matrix_ref, matrix_t_ref, table_ref, store,
    )


def middle_kernel(hops, blocks, listed, noise_base, joined, lists_ref, charge_ref, *refs):
    parts = 2 * hops + 1
    x_refs = refs[:parts]
    p_ref, noise_ref, mass_ref, matrix_ref, matrix_t_ref, table_ref = refs[parts:parts + 6]
    outs = refs[parts + 6:parts + (7 if joined else 8)]
    coord_ref, *scratch = refs[parts + len(outs) + 6:]
    beads = coord_ref.shape[1]
    local = beads // p_ref.shape[0]
    width = blocks * BLOCK
    for part in range(parts):
        unpack_beads(x_refs[part], 0, blocks, local, coord_ref, part * width)
    margin = hops * blocks
    first = own_place(p_ref.shape[0]) * blocks
    offset_at = offsets_of(lists_ref, first, first + margin, margin)
    add_forces(16, blocks, margin, listed, offset_at, charge_ref, coord_ref, scratch, first)
    force_ref = scratch[FORCE]
    unpack_beads(p_ref, 0, blocks, local, coord_ref, 0)
    unpack_beads(noise_ref, noise_base, blocks, local, coord_ref, (parts - 1) * width)

    def share(c, part):
        return coord_ref[c, :, part * width:(part + 1) * width]

    def store(c, x, p):
        pack_beads(x, c, blocks, local, outs[0])
        if joined:
            pack_beads(p, 3 + c, blocks, local, outs[0])
        else:
            pack_beads(p, c, blocks, local, outs[1])

    thermostat(
        [share(c, hops) for c in range(3)],
        [share(c, 0) + 2.0 * half_step * force_ref[c] for c in range(3)],
        [share(c, parts - 1) for c in range(3)],
        mass_ref, matrix_ref, matrix_t_ref, table_ref, store,
    )


def fold(count):
    return [i // 2 if i % 2 == 0 else count - 1 - i // 2 for i in range(count)]


def exchange(pieces):
    order = fold(pieces.shape[0])
    group = [order.index(at) for at in range(len(order))]
    return lax.all_to_all(pieces, "bead", split_axis=0, concat_axis=0, axis_index_groups=[group], tiled=True)


def passed(values, step):
    count = lax.axis_size("space")
    return lax.ppermute(values, "space", [(i, (i + step) % count) for i in range(count)])


def round_ring(values, hop):
    count = lax.axis_size("bead")
    domains = lax.axis_size("space")
    order = fold(count)
    device = {}
    for bead in range(count):
        for domain in range(domains):
            device[domain * count + order[bead]] = bead * domains + domain
    total = count * domains
    return lax.ppermute(values, ("bead", "space"), [(device[(at + hop) % total], device[at]) for at in range(total)])


def window(values, hops):
    return [round_ring(values, hop) if hop else values for hop in range(-hops, hops + 1)]


def body(positions, momenta, atom_types, neighbours, thermal_noise):
    count = lax.axis_size("bead")
    _, local, atoms = positions.shape
    beads = local * count
    domain = atoms // BLOCK
    blocks = domain // count
    share = blocks * BLOCK
    hops = -(-HALO // blocks)
    margin = hops * blocks
    edge = margin * BLOCK
    steps = thermal_noise.shape[0]
    listed = neighbours.shape[1]
    order = fold(count)
    lists = neighbours.T
    types = atom_types[None, :]

    packed = (count, 3 * blocks * local, BLOCK)
    whole = [positions.shape, (3, local, edge), thermal_noise.shape, types.shape, lists.shape]
    rest, message, charge, mass = call(
        functools.partial(prepare_kernel, blocks),
        (positions, momenta, thermal_noise, types, lists), 0,
        [(count, (1 + steps) * packed[1], BLOCK), (13, local, edge), (1, atoms), (1, atoms)], [], 0,
        [pl.BlockSpec(shape, lambda i, rank=len(shape): (0,) * rank) for shape in whole],
    )
    message = passed(message, -1)
    rest = exchange(rest)
    side = message[9:, 0]
    first_charge = jnp.concatenate([charge, side[:1], side[1:2]], axis=1)
    moved_mass = jnp.concatenate([mass[:, edge:], side[2:3]], axis=1)
    domains = lax.axis_size("space")
    foreign = side[3].reshape(8, edge // 8)[:listed, :margin].astype(jnp.int32)
    foreign = foreign + jnp.where(lax.axis_index("space") == domains - 1, domains * domain, 0)
    moved_lists = jnp.concatenate([lists[:, margin:], foreign], axis=1)

    matrix, tables = mode_constants(beads)
    at = np.concatenate([order.index(g) * local + np.arange(local) for g in range(count)])
    matrix = matrix[at][:, at]
    fixed = (moved_mass, jnp.asarray(matrix), jnp.asarray(np.ascontiguousarray(matrix.T)), jnp.asarray(tables[:, at]))

    pairs = beads * blocks * listed * BLOCK * BLOCK
    frame = min(FRAME, domain // 2)
    most = domain - 2 * frame
    (moment,) = call(
        functools.partial(front_kernel, blocks, margin, listed), (lists, types, positions, momenta), 1,
        [(most // blocks,) + packed[1:]],
        [pltpu.VMEM(types.shape, f32)] + force_scratch(local, most, margin, listed), pairs * most // domain,
    )
    moment, rest = lax.optimization_barrier((moment, rest))
    rest = round_ring(rest, hops)
    (moment,) = call(
        functools.partial(back_kernel, blocks, margin, listed),
        (moved_lists, first_charge, positions, message, momenta, moment), 1,
        [packed], force_scratch(local, domain - most, margin, listed), pairs * (domain - most) // domain,
    )
    moment, rest = lax.optimization_barrier((moment, rest))
    coords, moment = call(
        functools.partial(modes_kernel, blocks, 3), (rest, exchange(moment)) + fixed, 0, [packed] * 2,
        [pltpu.VMEM((3, beads, share), f32)] * 3, 0,
    )
    for step in range(1, steps):
        joined = step == steps - 1
        out = call(
            functools.partial(middle_kernel, hops, blocks, listed, 3 * step + 3, joined),
            (moved_lists, first_charge) + tuple(window(coords, hops)) + (moment, rest) + fixed, 1,
            [(count, 6 * blocks * local, BLOCK)] if joined else [packed] * 2,
            force_scratch(beads, blocks, margin, listed), pairs,
        )
        if not joined:
            coords, moment = out
    both = exchange(out[0])

    def ends(low, c):
        pieces = both[low:low + hops, c * packed[1]:(c + 1) * packed[1]]
        return pieces.reshape(hops, 3, blocks, local, BLOCK).transpose(1, 3, 0, 2, 4).reshape(3, local, edge)

    message = passed(jnp.concatenate([
        ends(count - 2 * hops, 0), ends(count - hops, 0), ends(count - hops, 1),
        jnp.broadcast_to(charge[:, None, atoms - edge:], (1, local, edge)),
    ], axis=0), 1)
    (upper,) = call(
        functools.partial(upper_kernel, blocks, margin, listed),
        (lists, first_charge, both), 1,
        [(3, local, most * BLOCK)], force_scratch(local, most, margin, listed), pairs * most // domain,
    )
    last_charge = jnp.concatenate([message[9, :1], first_charge[:, :2 * frame * BLOCK + edge]], axis=1)
    return tuple(call(
        functools.partial(lower_kernel, blocks, margin, listed),
        (lists, last_charge, both, message, upper), 1,
        [(3, local, atoms)] * 2, force_scratch(local, domain - most, margin, listed), pairs * (domain - most) // domain,
    ))


def solution(mesh):
    placed = (
        P(None, "bead", "space"),
        P(None, "bead", "space"),
        P("space"),
        P("space", None),
        P(None, None, "bead", "space"),
    )
    return jax.shard_map(
        body,
        mesh=mesh,
        in_specs=placed,
        out_specs=(P(None, "bead", "space"), P(None, "bead", "space")),
        check_vma=False,
    )
```

```python
import functools
import math

import jax
import jax.numpy as jnp
import numpy as np
from jax import lax
from jax.experimental import pallas as pl
from jax.experimental.pallas import tpu as pltpu
from jax.sharding import PartitionSpec as P

BLOCK = 128
HALO = 4

half_step = 0.025
time_step = 0.05
chain_freq = 12.0
thermal = 0.375
centroid_friction = 1.0
screening = 4.0
softening = 0.09
CHARGES = (1.0, -1.0, 0.6, -1.4)
MASSES = (1.0, 2.0, 3.0, 4.0)

PAIR_ROWS = 24
PAIR_PAD = 32
SUM_ROWS = 16
QUAD = 4
SLOTS = 8
FRAME = 16
f32 = jnp.float32
bf16 = jnp.bfloat16


def mode_constants(bead_total):
    j = np.arange(bead_total)[:, None]
    k = np.arange(bead_total)[None, :]
    half = bead_total // 2
    phase = 2.0 * np.pi * ((j * k) % bead_total) / bead_total
    plain = 1.0 / math.sqrt(bead_total)
    paired = math.sqrt(2.0 / bead_total)
    matrix = np.where(
        k == 0,
        plain,
        np.where(
            k < half,
            paired * np.cos(phase),
            np.where(k == half, plain * np.cos(phase), paired * np.sin(phase)),
        ),
    )
    modes = np.arange(bead_total)
    frequency = 2.0 * chain_freq * np.sin(np.pi * modes / bead_total)
    angle = frequency * time_step
    ratio = np.where(modes == 0, time_step, np.sin(angle) / np.where(modes == 0, 1.0, frequency))
    friction = np.where(modes == 0, centroid_friction, 2.0 * frequency)
    damping = np.exp(-friction * time_step)
    kick = np.sqrt(1.0 - damping * damping)
    tables = np.stack([np.cos(angle), ratio, frequency * np.sin(angle), damping, kick])
    tables = np.broadcast_to(tables[:, :, None], tables.shape + (BLOCK,))
    return matrix.astype(np.float32), np.ascontiguousarray(tables).astype(np.float32)


def split3(v):
    one = v.astype(bf16).astype(f32)
    rest = v - one
    two = rest.astype(bf16).astype(f32)
    three = (rest - two).astype(bf16).astype(f32)
    return one, two, three


def pair_rows(coords, norm, own):
    rows = []
    for v in coords:
        one, two, three = split3(v)
        if own:
            one, two, three = -2.0 * one, -2.0 * two, -2.0 * three
            rows += [one, one, two, two, one, three]
        else:
            rows += [one, two, one, two, three, one]
    ones = [jnp.ones_like(norm)] * 3
    norms = list(split3(norm))
    return rows + (norms + ones if own else ones + norms)


SCALE = 1.0 / (screening * math.log(2.0))


def weigh(square):
    inverse = lax.rsqrt(square)
    decay = jnp.exp2(-(square * inverse))
    return decay * ((inverse * inverse) * (inverse + math.log(2.0)))


def own_place(count):
    bead = lax.axis_index("bead")
    half = lax.div(bead, 2)
    return jnp.where(lax.rem(bead, 2) == 0, half, count - 1 - half)


def offsets_of(lists_ref, skip, origin, margin):
    first = lax.axis_index("space") * lists_ref.shape[1] + origin

    def offset_at(block, m):
        return jnp.clip(lists_ref[m, skip + block] - (first + block), -margin, margin)

    return offset_at


def charges(types):
    charge = jnp.zeros(types.shape, f32)
    for kind in range(4):
        charge = jnp.where(types == kind, CHARGES[kind], charge)
    return charge


def odd_tiles(lines):
    return lines + 8 * (1 - lines // 8 % 2)


def whole_quads(beads):
    return -(-beads // QUAD) * QUAD


def add_forces(group, blocks, margin, listed, offset_at, charge_ref, coord_ref, scratch, charge_from=0):
    rows_ref, sums_ref, far_ref, heavy_ref, near_ref, total_ref, force_ref, *buffers = scratch
    weight_refs = buffers
    beads = coord_ref.shape[1]
    pairs = beads // 2
    frame = min(FRAME, blocks)
    width = frame + 2 * margin
    middle = margin + (frame - 1) / 2.0
    at_once = max(1, 8 // beads)
    lines = at_once * beads
    apart = odd_tiles(lines)
    units = blocks * pairs

    def charge_at(block):
        return charge_ref[:, pl.ds(pl.multiple_of((charge_from + block) * BLOCK, BLOCK), BLOCK)]

    def put(ref, slot, k, value):
        ref[slot, k * apart:k * apart + lines, :] = value

    def centred(block, place):
        spans = [pl.ds(pl.multiple_of((block + i) * BLOCK, BLOCK), BLOCK) for i in range(at_once)]
        coords = [
            (jnp.concatenate([coord_ref[c, :, lanes] for lanes in spans], axis=0) - 1.0) * SCALE for c in range(3)
        ]
        shift = jnp.concatenate(
            [jnp.full((beads, BLOCK), SCALE, f32) * ((place + i).astype(f32) - middle) for i in range(at_once)], axis=0
        )
        coords[0] = coords[0] + shift
        norm = coords[0] * coords[0] + coords[1] * coords[1] + coords[2] * coords[2]
        charge = jnp.concatenate(
            [jnp.broadcast_to(charge_at(block + i), (beads, BLOCK)) for i in range(at_once)], axis=0
        )
        return coords, norm, charge

    def steps(count, one):
        slots = max(n for n in range(1, SLOTS + 1) if count % n == 0)

        def some(turn, carry):
            for slot in range(slots):
                one(turn * slots + slot, slot)
            return carry

        lax.fori_loop(0, count // slots, some, 0)

    nothing = jnp.zeros((lines, BLOCK), f32)
    for slot in range(SLOTS):
        for k in range(PAIR_ROWS, PAIR_PAD):
            put(rows_ref, slot, k, nothing)
        for k in range(12, SUM_ROWS):
            put(sums_ref, slot, k, nothing)
    blank = jnp.zeros((PAIR_PAD, BLOCK), bf16)
    passes = width // at_once

    def one_table(step, slot):
        at_frame = step // passes
        place = (step - at_frame * passes) * at_once
        coords, norm, charge = centred(at_frame * frame + place, place)
        for k, row in enumerate(pair_rows(coords, norm, False)):
            put(rows_ref, slot, k, row)
        for c, v in enumerate([charge] + [charge * x for x in coords]):
            for level, part in enumerate(split3(v)):
                put(sums_ref, slot, level * 4 + c, part)
        for i in range(at_once):
            at = at_frame * width + place + i
            for quad in range(beads // QUAD):
                low = i * beads + quad * QUAD
                four = jnp.concatenate(
                    [rows_ref[slot, pl.ds(low + j, PAIR_PAD, stride=apart), :] for j in range(QUAD)], axis=0
                )
                far_ref[at, quad] = jnp.transpose(four.astype(bf16))
                for half in range(2):
                    heavy_ref[at, 2 * quad + half] = jnp.concatenate(
                        [
                            sums_ref[slot, pl.ds(low + 2 * half + j, SUM_ROWS, stride=apart), :]
                            for j in range(2)
                        ],
                        axis=0,
                    ).astype(bf16)

    def one_own(step, slot):
        block = step * at_once
        place = block - block // frame * frame + margin
        coords, norm, _ = centred(block + margin, place)
        for k, row in enumerate(pair_rows(coords, norm + softening * SCALE * SCALE, True)):
            put(rows_ref, slot, k, row)
        for i in range(at_once):
            for bead in range(beads):
                near_ref[(block + i) * beads + bead] = rows_ref[
                    slot, pl.ds(i * beads + bead, PAIR_PAD, stride=apart), :
                ].astype(bf16)

    steps(blocks // frame * passes, one_table)
    steps(blocks // at_once, one_own)

    def places(unit):
        block = unit // pairs
        at_frame = block // frame
        base = at_frame * width + block - at_frame * frame + margin
        return [base + offset_at(block, m) for m in range(listed)], unit - block * pairs

    def parts(square):
        weight = weigh(square)
        high = weight.astype(bf16)
        return high, (weight - high.astype(f32)).astype(bf16)

    def squares(ats, pair, near, m):
        return jnp.dot(far_ref[ats[m], pair // (QUAD // 2)], near, preferred_element_type=f32)

    def own_columns(unit, half):
        columns = [
            jnp.concatenate([near_ref[2 * unit + j] if k == 2 * half + j else blank for k in range(QUAD)], axis=0)
            for j in range(2)
        ]
        return jnp.concatenate(columns, axis=1)

    def weighted(at, pair, both):
        table = heavy_ref[at, pair]
        return jnp.dot(jnp.concatenate([table, table], axis=1), both, preferred_element_type=f32)

    def keep(total, slot):
        for i in range(2):
            cols = slice(i * BLOCK, (i + 1) * BLOCK)
            row = i * SUM_ROWS
            spot = pl.ds(pl.multiple_of((2 * slot + i) * 8, 8), 8)
            total_ref[spot, :] = total[row:row + 8, cols] + total[row + 8:row + 16, cols]

    def body(step, carry):
        before_ats, before_pair = places(jnp.maximum(step * group - 1, 0))
        for turn in range(group):
            unit = step * group + turn
            now, other = turn % 2, (turn + 1) % 2
            ats, pair = places(unit)
            near = own_columns(unit, turn % 2)
            total = jnp.zeros((2 * SUM_ROWS, 2 * BLOCK), f32)
            for m in range(listed):
                spot = slice(2 * m * BLOCK, 2 * (m + 1) * BLOCK)
                weight_refs[now][spot, :] = jnp.concatenate(parts(squares(ats, pair, near, m)), axis=0)
                total = total + weighted(before_ats[m], before_pair, weight_refs[other][spot, :])
            keep(total, jnp.where(unit == 0, units, unit - 1))
            before_ats, before_pair = ats, pair
        return carry

    group = math.gcd(units, group)
    lax.fori_loop(0, units // group, body, 0)
    last_ats, last_pair = places(units - 1)
    keep(
        sum(
            weighted(last_ats[m], last_pair, weight_refs[(group - 1) % 2][2 * m * BLOCK:2 * (m + 1) * BLOCK, :])
            for m in range(listed)
        ),
        units - 1,
    )

    def one_block(block, slot):
        at_frame = block // frame
        place = block - at_frame * frame + margin
        lanes = pl.ds(pl.multiple_of((block + margin) * BLOCK, BLOCK), BLOCK)
        coords = [(coord_ref[c, :, lanes] - 1.0) * SCALE for c in range(3)]
        coords[0] = coords[0] + SCALE * (place.astype(f32) - middle)
        charge = jnp.broadcast_to(SCALE * SCALE * charge_at(block + margin), coords[0].shape)

        def summed(c):
            return sum(total_ref[pl.ds(block * beads * 8 + c + i, beads, stride=8), :] for i in (0, 4))

        near = summed(0)
        own = pl.ds(pl.multiple_of(block * BLOCK, BLOCK), BLOCK)
        for c in range(3):
            force_ref[c, :, own] = charge * (coords[c] * near - summed(c + 1))

    steps(blocks, one_block)


def force_scratch(local, blocks, margin, listed):
    beads = whole_quads(local)
    frame = min(FRAME, blocks)
    tables = (frame + 2 * margin) * (blocks // frame)
    lines = max(8, beads)
    units = blocks * beads // 2
    return [
        pltpu.VMEM((3, beads, (blocks + 2 * margin) * BLOCK), f32),
        pltpu.VMEM((SLOTS, PAIR_PAD * odd_tiles(lines), BLOCK), f32),
        pltpu.VMEM((SLOTS, SUM_ROWS * odd_tiles(lines), BLOCK), f32),
        pltpu.VMEM((tables, beads // QUAD, BLOCK, QUAD * PAIR_PAD), bf16),
        pltpu.VMEM((tables, beads // 2, 2 * SUM_ROWS, BLOCK), bf16),
        pltpu.VMEM((2 * units, PAIR_PAD, BLOCK), bf16),
        pltpu.VMEM(((units + 1) * 16, BLOCK), f32),
        pltpu.VMEM((3, beads, blocks * BLOCK), f32),
        pltpu.VMEM((2 * listed * BLOCK, 2 * BLOCK), bf16),
        pltpu.VMEM((2 * listed * BLOCK, 2 * BLOCK), bf16),
    ]


def call(kernel, args, smem_count, shapes, scratch, work, in_specs=None):
    vmem = pl.BlockSpec(memory_space=pltpu.VMEM)
    smem = pl.BlockSpec(memory_space=pltpu.SMEM)
    return pl.pallas_call(
        kernel,
        out_shape=[jax.ShapeDtypeStruct(shape, f32) for shape in shapes],
        grid=() if in_specs is None else (1,),
        in_specs=in_specs or [smem] * smem_count + [vmem] * (len(args) - smem_count),
        out_specs=[vmem] * len(shapes),
        scratch_shapes=scratch,
        compiler_params=pltpu.CompilerParams(vmem_limit_bytes=(40 if in_specs is None else 62) * 1024 * 1024),
        cost_estimate=pl.CostEstimate(
            flops=20 * work + 1024, bytes_accessed=4 * 1024 * 1024, transcendentals=2 * work
        ),
    )(*args)


def row_of(c, block, blocks, local):
    return (c * blocks + block) * local


def unpack_beads(source, base, blocks, local, target, offset):
    for c in range(3):
        for block in range(blocks):
            row = row_of(base + c, block, blocks, local)
            lane = offset + block * BLOCK
            for group in range(source.shape[0]):
                target[c, group * local:(group + 1) * local, lane:lane + BLOCK] = source[group, row:row + local, :]


def pack_beads(value, c, blocks, local, target):
    for block in range(blocks):
        row = row_of(c, block, blocks, local)
        for group in range(target.shape[0]):
            target[group, row:row + local, :] = value[
                group * local:(group + 1) * local, block * BLOCK:(block + 1) * BLOCK
            ]


FORCE = 6


def clear(coord_ref, local):
    if coord_ref.shape[1] != local:
        coord_ref[...] = jnp.zeros(coord_ref.shape, f32)


def prepare_kernel(
    blocks, x_ref, edge_ref, noise_ref, types_ref, lists_ref, rest_ref, message_ref, charge_ref, mass_ref
):
    steps, _, local, atoms = noise_ref.shape
    edge = message_ref.shape[2]
    types = types_ref[...]
    charge = charges(types)
    mass = jnp.zeros(types.shape, f32)
    for kind in range(4):
        mass = jnp.where(types == kind, MASSES[kind], mass)
    charge_ref[...] = charge
    mass_ref[...] = mass
    for c in range(3):
        message_ref[c] = x_ref[c, :, :edge]
        message_ref[3 + c] = x_ref[c, :, edge:2 * edge]
        message_ref[6 + c] = edge_ref[c]
    for i, row in enumerate([charge[:, :edge], charge[:, edge:2 * edge], mass[:, :edge]]):
        message_ref[9 + i] = jnp.broadcast_to(row, (local, edge))
    message_ref[12] = jnp.zeros((local, edge), f32)
    for m in range(lists_ref.shape[0]):
        at = m * (edge // 8)
        message_ref[12, 0:1, at:at + edge // BLOCK] = lists_ref[m:m + 1, :edge // BLOCK].astype(f32)
    for c in range(3 + 3 * steps):
        for block in range(atoms // BLOCK):
            lanes = slice(block * BLOCK, (block + 1) * BLOCK)
            value = x_ref[c, :, lanes] if c < 3 else noise_ref[c // 3 - 1, c % 3, :, lanes]
            row = row_of(c, block % blocks, blocks, local)
            rest_ref[block // blocks, row:row + local, :] = value


def front_kernel(
    each, margin, listed, lists_ref, types_ref, x_ref, p_ref, pout_ref, charge_ref, coord_ref, *scratch
):
    _, local, _ = x_ref.shape
    blocks = pout_ref.shape[0] * each
    charge_ref[...] = charges(types_ref[...])
    clear(coord_ref, local)
    for c in range(3):
        coord_ref[c, :local, :] = x_ref[c, :, :(blocks + 2 * margin) * BLOCK]
    offset_at = offsets_of(lists_ref, margin, margin, margin)
    add_forces(16, blocks, margin, listed, offset_at, charge_ref, coord_ref, scratch)
    force_ref = scratch[FORCE]
    for c in range(3):
        for block in range(blocks):
            lanes = slice(block * BLOCK, (block + 1) * BLOCK)
            moment = p_ref[c, :, (block + margin) * BLOCK:(block + margin + 1) * BLOCK]
            row = row_of(c, block % each, each, local)
            pout_ref[block // each, row:row + local, :] = moment + half_step * force_ref[c, :local, lanes]


def back_kernel(
    each, margin, listed, lists_ref, charge_ref, x_ref, message_ref, p_ref, front_ref, pout_ref, coord_ref, *scratch
):
    _, local, atoms = x_ref.shape
    edge = margin * BLOCK
    done = front_ref.shape[0]
    first = done * each
    blocks = (pout_ref.shape[0] - done) * each
    own = atoms - first * BLOCK
    clear(coord_ref, local)
    for c in range(3):
        coord_ref[c, :local, :own] = x_ref[c, :, first * BLOCK:]
        for part in range(2):
            coord_ref[c, :local, own + part * edge:own + (part + 1) * edge] = message_ref[3 * part + c]
    offset_at = offsets_of(lists_ref, first, first + margin, margin)
    add_forces(16, blocks, margin, listed, offset_at, charge_ref, coord_ref, scratch, first)
    force_ref = scratch[FORCE]
    pout_ref[:done] = front_ref[...]
    for c in range(3):
        for block in range(blocks):
            lanes = slice(block * BLOCK, (block + 1) * BLOCK)
            at = (first + block) * BLOCK + edge
            if at < atoms:
                moment = p_ref[c, :, at:at + BLOCK]
            else:
                moment = message_ref[6 + c, :, at - atoms:at - atoms + BLOCK]
            row = row_of(c, block % each, each, local)
            pout_ref[done + block // each, row:row + local, :] = moment + half_step * force_ref[c, :local, lanes]


def from_packed(ref, c, block, each, local):
    row = row_of(c, block % each, each, local)
    return ref[block // each, row:row + local, :]


def upper_kernel(each, margin, listed, lists_ref, charge_ref, both_ref, pout_ref, coord_ref, *scratch):
    _, local, atoms = pout_ref.shape
    blocks = atoms // BLOCK
    domain = both_ref.shape[0] * each
    skipped = domain - blocks - 2 * margin
    clear(coord_ref, local)
    for c in range(3):
        for block in range(skipped, domain):
            at = (block - skipped) * BLOCK
            coord_ref[c, :local, at:at + BLOCK] = from_packed(both_ref, c, block, each, local)
    offset_at = offsets_of(lists_ref, domain - blocks, domain - blocks, margin)
    add_forces(16, blocks, margin, listed, offset_at, charge_ref, coord_ref, scratch, skipped + margin)
    force_ref = scratch[FORCE]
    for c in range(3):
        for block in range(blocks):
            lanes = slice(block * BLOCK, (block + 1) * BLOCK)
            moment = from_packed(both_ref, 3 + c, domain - blocks + block - margin, each, local)
            pout_ref[c, :, lanes] = moment + half_step * force_ref[c, :local, lanes]


def lower_kernel(
    each, margin, listed, lists_ref, charge_ref, both_ref, message_ref, upper_ref, xout_ref, pout_ref, coord_ref,
    *scratch,
):
    _, local, atoms = xout_ref.shape
    edge = margin * BLOCK
    lower = atoms - upper_ref.shape[2]
    blocks = lower // BLOCK
    clear(coord_ref, local)
    for c in range(3):
        for part in range(2):
            coord_ref[c, :local, part * edge:(part + 1) * edge] = message_ref[3 * part + c]
        for block in range(blocks):
            at = 2 * edge + block * BLOCK
            coord_ref[c, :local, at:at + BLOCK] = from_packed(both_ref, c, block, each, local)
        xout_ref[c, :, :edge] = message_ref[3 + c]
        for block in range(margin, atoms // BLOCK):
            lanes = slice(block * BLOCK, (block + 1) * BLOCK)
            xout_ref[c, :, lanes] = from_packed(both_ref, c, block - margin, each, local)
        pout_ref[c, :, lower:] = upper_ref[c]
    offset_at = offsets_of(lists_ref, 0, 0, margin)
    add_forces(16, blocks, margin, listed, offset_at, charge_ref, coord_ref, scratch)
    force_ref = scratch[FORCE]
    for c in range(3):
        for block in range(blocks):
            lanes = slice(block * BLOCK, (block + 1) * BLOCK)
            if block < margin:
                moment = message_ref[6 + c, :, lanes]
            else:
                moment = from_packed(both_ref, 3 + c, block - margin, each, local)
            pout_ref[c, :, lanes] = moment + half_step * force_ref[c, :local, lanes]


def thermostat(coords, moments, noises, mass_ref, matrix_ref, matrix_t_ref, table_ref, store):
    beads, width = moments[0].shape
    cosine, ratio, stiffness, damping, kick = [
        jnp.concatenate([table_ref[i]] * (width // BLOCK), axis=1) for i in range(5)
    ]
    first = pl.multiple_of(own_place(mass_ref.shape[1] // width) * width, BLOCK)
    mass = jnp.broadcast_to(mass_ref[:, pl.ds(first, width)], (beads, width))
    spread = kick * jnp.sqrt(thermal * mass)
    drift = ratio / mass
    stiff = stiffness * mass
    multiply = functools.partial(jnp.dot, precision=lax.Precision.HIGHEST, preferred_element_type=f32)
    for c in range(3):
        mode_x = multiply(matrix_t_ref[...], coords[c])
        mode_p = damping * multiply(matrix_t_ref[...], moments[c]) + spread * noises[c]
        store(
            c,
            multiply(matrix_ref[...], cosine * mode_x + drift * mode_p),
            multiply(matrix_ref[...], cosine * mode_p - stiff * mode_x),
        )


def modes_kernel(
    blocks, noise_base, rest_ref, p_ref, mass_ref, matrix_ref, matrix_t_ref, table_ref,
    xout_ref, pout_ref, coord_ref, moment_ref, noise_ref,
):
    local = p_ref.shape[1] // (3 * blocks)
    unpack_beads(rest_ref, 0, blocks, local, coord_ref, 0)
    unpack_beads(p_ref, 0, blocks, local, moment_ref, 0)
    unpack_beads(rest_ref, noise_base, blocks, local, noise_ref, 0)

    def store(c, x, p):
        pack_beads(x, c, blocks, local, xout_ref)
        pack_beads(p, c, blocks, local, pout_ref)

    thermostat(
        *[[ref[c] for c in range(3)] for ref in (coord_ref, moment_ref, noise_ref)],
        mass_ref, matrix_ref, matrix_t_ref, table_ref, store,
    )


def middle_kernel(hops, blocks, listed, noise_base, joined, lists_ref, charge_ref, *refs):
    parts = 2 * hops + 1
    x_refs = refs[:parts]
    p_ref, noise_ref, mass_ref, matrix_ref, matrix_t_ref, table_ref = refs[parts:parts + 6]
    outs = refs[parts + 6:parts + (7 if joined else 8)]
    coord_ref, *scratch = refs[parts + len(outs) + 6:]
    beads = coord_ref.shape[1]
    local = beads // p_ref.shape[0]
    width = blocks * BLOCK
    for part in range(parts):
        unpack_beads(x_refs[part], 0, blocks, local, coord_ref, part * width)
    margin = hops * blocks
    first = own_place(p_ref.shape[0]) * blocks
    offset_at = offsets_of(lists_ref, first, first + margin, margin)
    add_forces(16, blocks, margin, listed, offset_at, charge_ref, coord_ref, scratch, first)
    force_ref = scratch[FORCE]
    unpack_beads(p_ref, 0, blocks, local, coord_ref, 0)
    unpack_beads(noise_ref, noise_base, blocks, local, coord_ref, (parts - 1) * width)

    def share(c, part):
        return coord_ref[c, :, part * width:(part + 1) * width]

    def store(c, x, p):
        pack_beads(x, c, blocks, local, outs[0])
        if joined:
            pack_beads(p, 3 + c, blocks, local, outs[0])
        else:
            pack_beads(p, c, blocks, local, outs[1])

    thermostat(
        [share(c, hops) for c in range(3)],
        [share(c, 0) + 2.0 * half_step * force_ref[c] for c in range(3)],
        [share(c, parts - 1) for c in range(3)],
        mass_ref, matrix_ref, matrix_t_ref, table_ref, store,
    )


def fold(count):
    return [i // 2 if i % 2 == 0 else count - 1 - i // 2 for i in range(count)]


def exchange(pieces):
    order = fold(pieces.shape[0])
    group = [order.index(at) for at in range(len(order))]
    return lax.all_to_all(pieces, "bead", split_axis=0, concat_axis=0, axis_index_groups=[group], tiled=True)


def passed(values, step):
    count = lax.axis_size("space")
    return lax.ppermute(values, "space", [(i, (i + step) % count) for i in range(count)])


def round_ring(values, hop):
    count = lax.axis_size("bead")
    domains = lax.axis_size("space")
    order = fold(count)
    device = {}
    for bead in range(count):
        for domain in range(domains):
            device[domain * count + order[bead]] = bead * domains + domain
    total = count * domains
    return lax.ppermute(values, ("bead", "space"), [(device[(at + hop) % total], device[at]) for at in range(total)])


def window(values, hops):
    return [round_ring(values, hop) if hop else values for hop in range(-hops, hops + 1)]


def body(positions, momenta, atom_types, neighbours, thermal_noise):
    count = lax.axis_size("bead")
    _, local, atoms = positions.shape
    beads = local * count
    domain = atoms // BLOCK
    blocks = domain // count
    share = blocks * BLOCK
    hops = -(-HALO // blocks)
    margin = hops * blocks
    edge = margin * BLOCK
    steps = thermal_noise.shape[0]
    listed = neighbours.shape[1]
    order = fold(count)
    lists = neighbours.T
    types = atom_types[None, :]

    packed = (count, 3 * blocks * local, BLOCK)
    whole = [positions.shape, (3, local, edge), thermal_noise.shape, types.shape, lists.shape]
    rest, message, charge, mass = call(
        functools.partial(prepare_kernel, blocks),
        (positions, momenta, thermal_noise, types, lists), 0,
        [(count, (1 + steps) * packed[1], BLOCK), (13, local, edge), (1, atoms), (1, atoms)], [], 0,
        [pl.BlockSpec(shape, lambda i, rank=len(shape): (0,) * rank) for shape in whole],
    )
    message = passed(message, -1)
    rest = exchange(rest)
    side = message[9:, 0]
    first_charge = jnp.concatenate([charge, side[:1], side[1:2]], axis=1)
    moved_mass = jnp.concatenate([mass[:, edge:], side[2:3]], axis=1)
    domains = lax.axis_size("space")
    foreign = side[3].reshape(8, edge // 8)[:listed, :margin].astype(jnp.int32)
    foreign = foreign + jnp.where(lax.axis_index("space") == domains - 1, domains * domain, 0)
    moved_lists = jnp.concatenate([lists[:, margin:], foreign], axis=1)

    matrix, tables = mode_constants(beads)
    at = np.concatenate([order.index(g) * local + np.arange(local) for g in range(count)])
    matrix = matrix[at][:, at]
    fixed = (moved_mass, jnp.asarray(matrix), jnp.asarray(np.ascontiguousarray(matrix.T)), jnp.asarray(tables[:, at]))

    pairs = beads * blocks * listed * BLOCK * BLOCK
    half = domain // 2
    most = domain - half
    (moment,) = call(
        functools.partial(front_kernel, blocks, margin, listed), (lists, types, positions, momenta), 1,
        [(most // blocks,) + packed[1:]],
        [pltpu.VMEM(types.shape, f32)] + force_scratch(local, most, margin, listed), pairs * most // domain,
    )
    moment, rest = lax.optimization_barrier((moment, rest))
    rest = round_ring(rest, hops)
    (moment,) = call(
        functools.partial(back_kernel, blocks, margin, listed),
        (moved_lists, first_charge, positions, message, momenta, moment), 1,
        [packed], force_scratch(local, domain - most, margin, listed), pairs * (domain - most) // domain,
    )
    moment, rest = lax.optimization_barrier((moment, rest))
    coords, moment = call(
        functools.partial(modes_kernel, blocks, 3), (rest, exchange(moment)) + fixed, 0, [packed] * 2,
        [pltpu.VMEM((3, beads, share), f32)] * 3, 0,
    )
    for step in range(1, steps):
        joined = step == steps - 1
        out = call(
            functools.partial(middle_kernel, hops, blocks, listed, 3 * step + 3, joined),
            (moved_lists, first_charge) + tuple(window(coords, hops)) + (moment, rest) + fixed, 1,
            [(count, 6 * blocks * local, BLOCK)] if joined else [packed] * 2,
            force_scratch(beads, blocks, margin, listed), pairs,
        )
        if not joined:
            coords, moment = out
    both = exchange(out[0])

    def ends(low, c):
        pieces = both[low:low + hops, c * packed[1]:(c + 1) * packed[1]]
        return pieces.reshape(hops, 3, blocks, local, BLOCK).transpose(1, 3, 0, 2, 4).reshape(3, local, edge)

    message = passed(jnp.concatenate([
        ends(count - 2 * hops, 0), ends(count - hops, 0), ends(count - hops, 1),
        jnp.broadcast_to(charge[:, None, atoms - edge:], (1, local, edge)),
    ], axis=0), 1)
    (upper,) = call(
        functools.partial(upper_kernel, blocks, margin, listed),
        (lists, first_charge, both), 1,
        [(3, local, most * BLOCK)], force_scratch(local, most, margin, listed), pairs * most // domain,
    )
    last_charge = jnp.concatenate([message[9, :1], first_charge[:, :half * BLOCK + edge]], axis=1)
    return tuple(call(
        functools.partial(lower_kernel, blocks, margin, listed),
        (lists, last_charge, both, message, upper), 1,
        [(3, local, atoms)] * 2, force_scratch(local, domain - most, margin, listed), pairs * (domain - most) // domain,
    ))


def solution(mesh):
    placed = (
        P(None, "bead", "space"),
        P(None, "bead", "space"),
        P("space"),
        P("space", None),
        P(None, None, "bead", "space"),
    )
    return jax.shard_map(
        body,
        mesh=mesh,
        in_specs=placed,
        out_specs=(P(None, "bead", "space"), P(None, "bead", "space")),
        check_vma=False,
    )
```

```python
import functools
import math

import jax
import jax.numpy as jnp
import numpy as np
from jax import lax
from jax.experimental import pallas as pl
from jax.experimental.pallas import tpu as pltpu
from jax.sharding import PartitionSpec as P

BLOCK = 128
HALO = 4

half_step = 0.025
time_step = 0.05
chain_freq = 12.0
thermal = 0.375
centroid_friction = 1.0
screening = 4.0
softening = 0.09
CHARGES = (1.0, -1.0, 0.6, -1.4)
MASSES = (1.0, 2.0, 3.0, 4.0)

PAIR_ROWS = 24
PAIR_PAD = 32
SUM_ROWS = 16
QUAD = 4
SLOTS = 8
FRAME = 16
f32 = jnp.float32
bf16 = jnp.bfloat16


def mode_constants(bead_total):
    j = np.arange(bead_total)[:, None]
    k = np.arange(bead_total)[None, :]
    half = bead_total // 2
    phase = 2.0 * np.pi * ((j * k) % bead_total) / bead_total
    plain = 1.0 / math.sqrt(bead_total)
    paired = math.sqrt(2.0 / bead_total)
    matrix = np.where(
        k == 0,
        plain,
        np.where(
            k < half,
            paired * np.cos(phase),
            np.where(k == half, plain * np.cos(phase), paired * np.sin(phase)),
        ),
    )
    modes = np.arange(bead_total)
    frequency = 2.0 * chain_freq * np.sin(np.pi * modes / bead_total)
    angle = frequency * time_step
    ratio = np.where(modes == 0, time_step, np.sin(angle) / np.where(modes == 0, 1.0, frequency))
    friction = np.where(modes == 0, centroid_friction, 2.0 * frequency)
    damping = np.exp(-friction * time_step)
    kick = np.sqrt(1.0 - damping * damping)
    tables = np.stack([np.cos(angle), ratio, frequency * np.sin(angle), damping, kick])
    tables = np.broadcast_to(tables[:, :, None], tables.shape + (BLOCK,))
    return matrix.astype(np.float32), np.ascontiguousarray(tables).astype(np.float32)


def split_rows(matrix):
    parts = []
    for _ in range(3):
        parts.append(matrix.astype(jnp.bfloat16))
        matrix = matrix - parts[-1].astype(np.float32)
    one, two, three = parts
    return jnp.asarray(np.concatenate([one, one, two, two, one, three], axis=1))


def split3(v):
    one = v.astype(bf16).astype(f32)
    rest = v - one
    two = rest.astype(bf16).astype(f32)
    three = (rest - two).astype(bf16).astype(f32)
    return one, two, three


def pair_rows(coords, norm, own):
    rows = []
    for v in coords:
        one, two, three = split3(v)
        if own:
            one, two, three = -2.0 * one, -2.0 * two, -2.0 * three
            rows += [one, one, two, two, one, three]
        else:
            rows += [one, two, one, two, three, one]
    ones = [jnp.ones_like(norm)] * 3
    norms = list(split3(norm))
    return rows + (norms + ones if own else ones + norms)


SCALE = 1.0 / (screening * math.log(2.0))


def weigh(square):
    inverse = lax.rsqrt(square)
    decay = jnp.exp2(-(square * inverse))
    return decay * ((inverse * inverse) * (inverse + math.log(2.0)))


def own_place(count):
    bead = lax.axis_index("bead")
    half = lax.div(bead, 2)
    return jnp.where(lax.rem(bead, 2) == 0, half, count - 1 - half)


def offsets_of(lists_ref, skip, origin, margin):
    first = lax.axis_index("space") * lists_ref.shape[1] + origin

    def offset_at(block, m):
        return jnp.clip(lists_ref[m, skip + block] - (first + block), -margin, margin)

    return offset_at


def charges(types):
    charge = jnp.zeros(types.shape, f32)
    for kind in range(4):
        charge = jnp.where(types == kind, CHARGES[kind], charge)
    return charge


def odd_tiles(lines):
    return lines + 8 * (1 - lines // 8 % 2)


def whole_quads(beads):
    return -(-beads // QUAD) * QUAD


def add_forces(group, blocks, margin, listed, offset_at, charge_ref, coord_ref, scratch, charge_from=0):
    rows_ref, sums_ref, far_ref, heavy_ref, near_ref, total_ref, force_ref, *buffers = scratch
    weight_refs = buffers
    beads = coord_ref.shape[1]
    pairs = beads // 2
    frame = min(FRAME, blocks)
    width = frame + 2 * margin
    middle = margin + (frame - 1) / 2.0
    at_once = max(1, 8 // beads)
    lines = at_once * beads
    apart = odd_tiles(lines)
    units = blocks * pairs

    def charge_at(block):
        return charge_ref[:, pl.ds(pl.multiple_of((charge_from + block) * BLOCK, BLOCK), BLOCK)]

    def put(ref, slot, k, value):
        ref[slot, k * apart:k * apart + lines, :] = value

    def centred(block, place):
        spans = [pl.ds(pl.multiple_of((block + i) * BLOCK, BLOCK), BLOCK) for i in range(at_once)]
        coords = [
            (jnp.concatenate([coord_ref[c, :, lanes] for lanes in spans], axis=0) - 1.0) * SCALE for c in range(3)
        ]
        shift = jnp.concatenate(
            [jnp.full((beads, BLOCK), SCALE, f32) * ((place + i).astype(f32) - middle) for i in range(at_once)], axis=0
        )
        coords[0] = coords[0] + shift
        norm = coords[0] * coords[0] + coords[1] * coords[1] + coords[2] * coords[2]
        charge = jnp.concatenate(
            [jnp.broadcast_to(charge_at(block + i), (beads, BLOCK)) for i in range(at_once)], axis=0
        )
        return coords, norm, charge

    def steps(count, one):
        slots = max(n for n in range(1, SLOTS + 1) if count % n == 0)

        def some(turn, carry):
            for slot in range(slots):
                one(turn * slots + slot, slot)
            return carry

        lax.fori_loop(0, count // slots, some, 0)

    nothing = jnp.zeros((lines, BLOCK), f32)
    for slot in range(SLOTS):
        for k in range(PAIR_ROWS, PAIR_PAD):
            put(rows_ref, slot, k, nothing)
        for k in range(12, SUM_ROWS):
            put(sums_ref, slot, k, nothing)
    blank = jnp.zeros((PAIR_PAD, BLOCK), bf16)
    passes = width // at_once

    def one_table(step, slot):
        at_frame = step // passes
        place = (step - at_frame * passes) * at_once
        coords, norm, charge = centred(at_frame * frame + place, place)
        for k, row in enumerate(pair_rows(coords, norm, False)):
            put(rows_ref, slot, k, row)
        for c, v in enumerate([charge] + [charge * x for x in coords]):
            for level, part in enumerate(split3(v)):
                put(sums_ref, slot, level * 4 + c, part)
        for i in range(at_once):
            at = at_frame * width + place + i
            for quad in range(beads // QUAD):
                low = i * beads + quad * QUAD
                four = jnp.concatenate(
                    [rows_ref[slot, pl.ds(low + j, PAIR_PAD, stride=apart), :] for j in range(QUAD)], axis=0
                )
                far_ref[at, quad] = jnp.transpose(four.astype(bf16))
                for half in range(2):
                    heavy_ref[at, 2 * quad + half] = jnp.concatenate(
                        [
                            sums_ref[slot, pl.ds(low + 2 * half + j, SUM_ROWS, stride=apart), :]
                            for j in range(2)
                        ],
                        axis=0,
                    ).astype(bf16)

    def one_own(step, slot):
        block = step * at_once
        place = block - block // frame * frame + margin
        coords, norm, _ = centred(block + margin, place)
        for k, row in enumerate(pair_rows(coords, norm + softening * SCALE * SCALE, True)):
            put(rows_ref, slot, k, row)
        for i in range(at_once):
            for bead in range(beads):
                near_ref[(block + i) * beads + bead] = rows_ref[
                    slot, pl.ds(i * beads + bead, PAIR_PAD, stride=apart), :
                ].astype(bf16)

    steps(blocks // frame * passes, one_table)
    steps(blocks // at_once, one_own)

    def places(unit):
        block = unit // pairs
        at_frame = block // frame
        base = at_frame * width + block - at_frame * frame + margin
        return [base + offset_at(block, m) for m in range(listed)], unit - block * pairs

    def parts(square):
        weight = weigh(square)
        high = weight.astype(bf16)
        return high, (weight - high.astype(f32)).astype(bf16)

    def squares(ats, pair, near, m):
        return jnp.dot(far_ref[ats[m], pair // (QUAD // 2)], near, preferred_element_type=f32)

    def own_columns(unit, half):
        columns = [
            jnp.concatenate([near_ref[2 * unit + j] if k == 2 * half + j else blank for k in range(QUAD)], axis=0)
            for j in range(2)
        ]
        return jnp.concatenate(columns, axis=1)

    def sums(ats, pair, weight_ref):
        tables = [heavy_ref[at, pair] for at in ats]
        return jnp.dot(
            jnp.concatenate([part for table in tables for part in (table, table)], axis=1),
            weight_ref[...], preferred_element_type=f32,
        )

    def keep(total, slot):
        for i in range(2):
            cols = slice(i * BLOCK, (i + 1) * BLOCK)
            row = i * SUM_ROWS
            spot = pl.ds(pl.multiple_of((2 * slot + i) * 8, 8), 8)
            total_ref[spot, :] = total[row:row + 8, cols] + total[row + 8:row + 16, cols]

    def body(step, carry):
        before_ats, before_pair = places(jnp.maximum(step * group - 1, 0))
        for turn in range(group):
            unit = step * group + turn
            now, other = turn % 2, (turn + 1) % 2
            ats, pair = places(unit)
            near = own_columns(unit, turn % 2)
            keep(sums(before_ats, before_pair, weight_refs[other]), jnp.where(unit == 0, units, unit - 1))
            for m in range(listed):
                spot = slice(2 * m * BLOCK, 2 * (m + 1) * BLOCK)
                weight_refs[now][spot, :] = jnp.concatenate(parts(squares(ats, pair, near, m)), axis=0)
            before_ats, before_pair = ats, pair
        return carry

    group = math.gcd(units, group)
    lax.fori_loop(0, units // group, body, 0)
    last_ats, last_pair = places(units - 1)
    keep(sums(last_ats, last_pair, weight_refs[(group - 1) % 2]), units - 1)

    def one_block(block, slot):
        at_frame = block // frame
        place = block - at_frame * frame + margin
        lanes = pl.ds(pl.multiple_of((block + margin) * BLOCK, BLOCK), BLOCK)
        coords = [(coord_ref[c, :, lanes] - 1.0) * SCALE for c in range(3)]
        coords[0] = coords[0] + SCALE * (place.astype(f32) - middle)
        charge = jnp.broadcast_to(SCALE * SCALE * charge_at(block + margin), coords[0].shape)

        def summed(c):
            return sum(total_ref[pl.ds(block * beads * 8 + c + i, beads, stride=8), :] for i in (0, 4))

        near = summed(0)
        own = pl.ds(pl.multiple_of(block * BLOCK, BLOCK), BLOCK)
        for c in range(3):
            force_ref[c, :, own] = charge * (coords[c] * near - summed(c + 1))

    steps(blocks, one_block)


def force_scratch(local, blocks, margin, listed):
    beads = whole_quads(local)
    frame = min(FRAME, blocks)
    tables = (frame + 2 * margin) * (blocks // frame)
    lines = max(8, beads)
    units = blocks * beads // 2
    return [
        pltpu.VMEM((3, beads, (blocks + 2 * margin) * BLOCK), f32),
        pltpu.VMEM((SLOTS, PAIR_PAD * odd_tiles(lines), BLOCK), f32),
        pltpu.VMEM((SLOTS, SUM_ROWS * odd_tiles(lines), BLOCK), f32),
        pltpu.VMEM((tables, beads // QUAD, BLOCK, QUAD * PAIR_PAD), bf16),
        pltpu.VMEM((tables, beads // 2, 2 * SUM_ROWS, BLOCK), bf16),
        pltpu.VMEM((2 * units, PAIR_PAD, BLOCK), bf16),
        pltpu.VMEM(((units + 1) * 16, BLOCK), f32),
        pltpu.VMEM((3, beads, blocks * BLOCK), f32),
        pltpu.VMEM((2 * listed * BLOCK, 2 * BLOCK), bf16),
        pltpu.VMEM((2 * listed * BLOCK, 2 * BLOCK), bf16),
    ]


def call(kernel, args, smem_count, shapes, scratch, work, in_specs=None):
    vmem = pl.BlockSpec(memory_space=pltpu.VMEM)
    smem = pl.BlockSpec(memory_space=pltpu.SMEM)
    return pl.pallas_call(
        kernel,
        out_shape=[jax.ShapeDtypeStruct(shape, f32) for shape in shapes],
        grid=() if in_specs is None else (1,),
        in_specs=in_specs or [smem] * smem_count + [vmem] * (len(args) - smem_count),
        out_specs=[vmem] * len(shapes),
        scratch_shapes=scratch,
        compiler_params=pltpu.CompilerParams(vmem_limit_bytes=(40 if in_specs is None else 62) * 1024 * 1024),
        cost_estimate=pl.CostEstimate(
            flops=20 * work + 1024, bytes_accessed=4 * 1024 * 1024, transcendentals=2 * work
        ),
    )(*args)


def row_of(c, block, blocks, local):
    return (c * blocks + block) * local


def unpack_beads(source, base, blocks, local, target, offset):
    for c in range(3):
        for block in range(blocks):
            row = row_of(base + c, block, blocks, local)
            lane = offset + block * BLOCK
            for group in range(source.shape[0]):
                target[c, group * local:(group + 1) * local, lane:lane + BLOCK] = source[group, row:row + local, :]


def pack_beads(value, c, blocks, local, target):
    for block in range(blocks):
        row = row_of(c, block, blocks, local)
        for group in range(target.shape[0]):
            target[group, row:row + local, :] = value[
                group * local:(group + 1) * local, block * BLOCK:(block + 1) * BLOCK
            ]


FORCE = 6


def clear(coord_ref, local):
    if coord_ref.shape[1] != local:
        coord_ref[...] = jnp.zeros(coord_ref.shape, f32)


def prepare_kernel(
    blocks, x_ref, edge_ref, noise_ref, types_ref, lists_ref, rest_ref, message_ref, charge_ref, mass_ref
):
    steps, _, local, atoms = noise_ref.shape
    edge = message_ref.shape[2]
    types = types_ref[...]
    charge = charges(types)
    mass = jnp.zeros(types.shape, f32)
    for kind in range(4):
        mass = jnp.where(types == kind, MASSES[kind], mass)
    charge_ref[...] = charge
    mass_ref[...] = mass
    for c in range(3):
        message_ref[c] = x_ref[c, :, :edge]
        message_ref[3 + c] = x_ref[c, :, edge:2 * edge]
        message_ref[6 + c] = edge_ref[c]
    for i, row in enumerate([charge[:, :edge], charge[:, edge:2 * edge], mass[:, :edge]]):
        message_ref[9 + i] = jnp.broadcast_to(row, (local, edge))
    message_ref[12] = jnp.zeros((local, edge), f32)
    for m in range(lists_ref.shape[0]):
        at = m * (edge // 8)
        message_ref[12, 0:1, at:at + edge // BLOCK] = lists_ref[m:m + 1, :edge // BLOCK].astype(f32)
    for c in range(3 + 3 * steps):
        for block in range(atoms // BLOCK):
            lanes = slice(block * BLOCK, (block + 1) * BLOCK)
            value = x_ref[c, :, lanes] if c < 3 else noise_ref[c // 3 - 1, c % 3, :, lanes]
            row = row_of(c, block % blocks, blocks, local)
            rest_ref[block // blocks, row:row + local, :] = value


def front_kernel(
    each, margin, listed, lists_ref, types_ref, x_ref, p_ref, pout_ref, charge_ref, coord_ref, *scratch
):
    _, local, _ = x_ref.shape
    blocks = pout_ref.shape[0] * each
    charge_ref[...] = charges(types_ref[...])
    clear(coord_ref, local)
    for c in range(3):
        coord_ref[c, :local, :] = x_ref[c, :, :(blocks + 2 * margin) * BLOCK]
    offset_at = offsets_of(lists_ref, margin, margin, margin)
    add_forces(16, blocks, margin, listed, offset_at, charge_ref, coord_ref, scratch)
    force_ref = scratch[FORCE]
    for c in range(3):
        for block in range(blocks):
            lanes = slice(block * BLOCK, (block + 1) * BLOCK)
            moment = p_ref[c, :, (block + margin) * BLOCK:(block + margin + 1) * BLOCK]
            row = row_of(c, block % each, each, local)
            pout_ref[block // each, row:row + local, :] = moment + half_step * force_ref[c, :local, lanes]


def back_kernel(
    each, margin, listed, lists_ref, charge_ref, x_ref, message_ref, p_ref, front_ref, pout_ref, coord_ref, *scratch
):
    _, local, atoms = x_ref.shape
    edge = margin * BLOCK
    done = front_ref.shape[0]
    first = done * each
    blocks = (pout_ref.shape[0] - done) * each
    own = atoms - first * BLOCK
    clear(coord_ref, local)
    for c in range(3):
        coord_ref[c, :local, :own] = x_ref[c, :, first * BLOCK:]
        for part in range(2):
            coord_ref[c, :local, own + part * edge:own + (part + 1) * edge] = message_ref[3 * part + c]
    offset_at = offsets_of(lists_ref, first, first + margin, margin)
    add_forces(16, blocks, margin, listed, offset_at, charge_ref, coord_ref, scratch, first)
    force_ref = scratch[FORCE]
    pout_ref[:done] = front_ref[...]
    for c in range(3):
        for block in range(blocks):
            lanes = slice(block * BLOCK, (block + 1) * BLOCK)
            at = (first + block) * BLOCK + edge
            if at < atoms:
                moment = p_ref[c, :, at:at + BLOCK]
            else:
                moment = message_ref[6 + c, :, at - atoms:at - atoms + BLOCK]
            row = row_of(c, block % each, each, local)
            pout_ref[done + block // each, row:row + local, :] = moment + half_step * force_ref[c, :local, lanes]


def from_packed(ref, c, block, each, local):
    row = row_of(c, block % each, each, local)
    return ref[block // each, row:row + local, :]


def upper_kernel(each, margin, listed, lists_ref, charge_ref, both_ref, pout_ref, coord_ref, *scratch):
    _, local, atoms = pout_ref.shape
    blocks = atoms // BLOCK
    domain = both_ref.shape[0] * each
    skipped = domain - blocks - 2 * margin
    clear(coord_ref, local)
    for c in range(3):
        for block in range(skipped, domain):
            at = (block - skipped) * BLOCK
            coord_ref[c, :local, at:at + BLOCK] = from_packed(both_ref, c, block, each, local)
    offset_at = offsets_of(lists_ref, domain - blocks, domain - blocks, margin)
    add_forces(16, blocks, margin, listed, offset_at, charge_ref, coord_ref, scratch, skipped + margin)
    force_ref = scratch[FORCE]
    for c in range(3):
        for block in range(blocks):
            lanes = slice(block * BLOCK, (block + 1) * BLOCK)
            moment = from_packed(both_ref, 3 + c, domain - blocks + block - margin, each, local)
            pout_ref[c, :, lanes] = moment + half_step * force_ref[c, :local, lanes]


def lower_kernel(
    each, margin, listed, lists_ref, charge_ref, both_ref, message_ref, upper_ref, xout_ref, pout_ref, coord_ref,
    *scratch,
):
    _, local, atoms = xout_ref.shape
    edge = margin * BLOCK
    lower = atoms - upper_ref.shape[2]
    blocks = lower // BLOCK
    clear(coord_ref, local)
    for c in range(3):
        for part in range(2):
            coord_ref[c, :local, part * edge:(part + 1) * edge] = message_ref[3 * part + c]
        for block in range(blocks):
            at = 2 * edge + block * BLOCK
            coord_ref[c, :local, at:at + BLOCK] = from_packed(both_ref, c, block, each, local)
        xout_ref[c, :, :edge] = message_ref[3 + c]
        for block in range(margin, atoms // BLOCK):
            lanes = slice(block * BLOCK, (block + 1) * BLOCK)
            xout_ref[c, :, lanes] = from_packed(both_ref, c, block - margin, each, local)
        pout_ref[c, :, lower:] = upper_ref[c]
    offset_at = offsets_of(lists_ref, 0, 0, margin)
    add_forces(16, blocks, margin, listed, offset_at, charge_ref, coord_ref, scratch)
    force_ref = scratch[FORCE]
    for c in range(3):
        for block in range(blocks):
            lanes = slice(block * BLOCK, (block + 1) * BLOCK)
            if block < margin:
                moment = message_ref[6 + c, :, lanes]
            else:
                moment = from_packed(both_ref, 3 + c, block - margin, each, local)
            pout_ref[c, :, lanes] = moment + half_step * force_ref[c, :local, lanes]


def thermostat(coords, moments, noises, mass_ref, matrix_ref, matrix_t_ref, table_ref, store):
    beads, width = moments[0].shape
    cosine, ratio, stiffness, damping, kick = [
        jnp.concatenate([table_ref[i]] * (width // BLOCK), axis=1) for i in range(5)
    ]
    first = pl.multiple_of(own_place(mass_ref.shape[1] // width) * width, BLOCK)
    mass = jnp.broadcast_to(mass_ref[:, pl.ds(first, width)], (beads, width))
    spread = kick * jnp.sqrt(thermal * mass)
    drift = ratio / mass
    stiff = stiffness * mass

    def multiply(matrix, values):
        joined = jnp.concatenate(values, axis=1)
        one, two, three = [part.astype(bf16) for part in split3(joined)]
        rows = jnp.concatenate([one, two, one, two, three, one], axis=0)
        out = jnp.dot(matrix, rows, preferred_element_type=f32)
        return [out[:, i * width:(i + 1) * width] for i in range(len(values))]

    mode = multiply(matrix_t_ref[...], coords + moments)
    next_x, next_p = [], []
    for c in range(3):
        mode_x = mode[c]
        mode_p = damping * mode[3 + c] + spread * noises[c]
        next_x.append(cosine * mode_x + drift * mode_p)
        next_p.append(cosine * mode_p - stiff * mode_x)
    beads_now = multiply(matrix_ref[...], next_x + next_p)
    for c in range(3):
        store(c, beads_now[c], beads_now[3 + c])


def modes_kernel(
    blocks, noise_base, rest_ref, p_ref, mass_ref, matrix_ref, matrix_t_ref, table_ref,
    xout_ref, pout_ref, coord_ref, moment_ref, noise_ref,
):
    local = p_ref.shape[1] // (3 * blocks)
    unpack_beads(rest_ref, 0, blocks, local, coord_ref, 0)
    unpack_beads(p_ref, 0, blocks, local, moment_ref, 0)
    unpack_beads(rest_ref, noise_base, blocks, local, noise_ref, 0)

    def store(c, x, p):
        pack_beads(x, c, blocks, local, xout_ref)
        pack_beads(p, c, blocks, local, pout_ref)

    thermostat(
        *[[ref[c] for c in range(3)] for ref in (coord_ref, moment_ref, noise_ref)],
        mass_ref, matrix_ref, matrix_t_ref, table_ref, store,
    )


def middle_kernel(hops, blocks, listed, noise_base, joined, lists_ref, charge_ref, *refs):
    parts = 2 * hops + 1
    x_refs = refs[:parts]
    p_ref, noise_ref, mass_ref, matrix_ref, matrix_t_ref, table_ref = refs[parts:parts + 6]
    outs = refs[parts + 6:parts + (7 if joined else 8)]
    coord_ref, *scratch = refs[parts + len(outs) + 6:]
    beads = coord_ref.shape[1]
    local = beads // p_ref.shape[0]
    width = blocks * BLOCK
    for part in range(parts):
        unpack_beads(x_refs[part], 0, blocks, local, coord_ref, part * width)
    margin = hops * blocks
    first = own_place(p_ref.shape[0]) * blocks
    offset_at = offsets_of(lists_ref, first, first + margin, margin)
    add_forces(16, blocks, margin, listed, offset_at, charge_ref, coord_ref, scratch, first)
    force_ref = scratch[FORCE]
    unpack_beads(p_ref, 0, blocks, local, coord_ref, 0)
    unpack_beads(noise_ref, noise_base, blocks, local, coord_ref, (parts - 1) * width)

    def share(c, part):
        return coord_ref[c, :, part * width:(part + 1) * width]

    def store(c, x, p):
        pack_beads(x, c, blocks, local, outs[0])
        if joined:
            pack_beads(p, 3 + c, blocks, local, outs[0])
        else:
            pack_beads(p, c, blocks, local, outs[1])

    thermostat(
        [share(c, hops) for c in range(3)],
        [share(c, 0) + 2.0 * half_step * force_ref[c] for c in range(3)],
        [share(c, parts - 1) for c in range(3)],
        mass_ref, matrix_ref, matrix_t_ref, table_ref, store,
    )


def fold(count):
    return [i // 2 if i % 2 == 0 else count - 1 - i // 2 for i in range(count)]


def exchange(pieces):
    order = fold(pieces.shape[0])
    group = [order.index(at) for at in range(len(order))]
    return lax.all_to_all(pieces, "bead", split_axis=0, concat_axis=0, axis_index_groups=[group], tiled=True)


def passed(values, step):
    count = lax.axis_size("space")
    return lax.ppermute(values, "space", [(i, (i + step) % count) for i in range(count)])


def round_ring(values, hop):
    count = lax.axis_size("bead")
    domains = lax.axis_size("space")
    order = fold(count)
    device = {}
    for bead in range(count):
        for domain in range(domains):
            device[domain * count + order[bead]] = bead * domains + domain
    total = count * domains
    return lax.ppermute(values, ("bead", "space"), [(device[(at + hop) % total], device[at]) for at in range(total)])


def window(values, hops):
    return [round_ring(values, hop) if hop else values for hop in range(-hops, hops + 1)]


def body(positions, momenta, atom_types, neighbours, thermal_noise):
    count = lax.axis_size("bead")
    _, local, atoms = positions.shape
    beads = local * count
    domain = atoms // BLOCK
    blocks = domain // count
    share = blocks * BLOCK
    hops = -(-HALO // blocks)
    margin = hops * blocks
    edge = margin * BLOCK
    steps = thermal_noise.shape[0]
    listed = neighbours.shape[1]
    order = fold(count)
    lists = neighbours.T
    types = atom_types[None, :]

    packed = (count, 3 * blocks * local, BLOCK)
    whole = [positions.shape, (3, local, edge), thermal_noise.shape, types.shape, lists.shape]
    rest, message, charge, mass = call(
        functools.partial(prepare_kernel, blocks),
        (positions, momenta, thermal_noise, types, lists), 0,
        [(count, (1 + steps) * packed[1], BLOCK), (13, local, edge), (1, atoms), (1, atoms)], [], 0,
        [pl.BlockSpec(shape, lambda i, rank=len(shape): (0,) * rank) for shape in whole],
    )
    message = passed(message, -1)
    rest = exchange(rest)
    side = message[9:, 0]
    first_charge = jnp.concatenate([charge, side[:1], side[1:2]], axis=1)
    moved_mass = jnp.concatenate([mass[:, edge:], side[2:3]], axis=1)
    domains = lax.axis_size("space")
    foreign = side[3].reshape(8, edge // 8)[:listed, :margin].astype(jnp.int32)
    foreign = foreign + jnp.where(lax.axis_index("space") == domains - 1, domains * domain, 0)
    moved_lists = jnp.concatenate([lists[:, margin:], foreign], axis=1)

    matrix, tables = mode_constants(beads)
    at = np.concatenate([order.index(g) * local + np.arange(local) for g in range(count)])
    matrix = matrix[at][:, at]
    fixed = (moved_mass, split_rows(matrix), split_rows(matrix.T), jnp.asarray(tables[:, at]))

    pairs = beads * blocks * listed * BLOCK * BLOCK
    half = domain // 2
    most = domain - half
    (moment,) = call(
        functools.partial(front_kernel, blocks, margin, listed), (lists, types, positions, momenta), 1,
        [(most // blocks,) + packed[1:]],
        [pltpu.VMEM(types.shape, f32)] + force_scratch(local, most, margin, listed), pairs * most // domain,
    )
    moment, rest = lax.optimization_barrier((moment, rest))
    rest = round_ring(rest, hops)
    (moment,) = call(
        functools.partial(back_kernel, blocks, margin, listed),
        (moved_lists, first_charge, positions, message, momenta, moment), 1,
        [packed], force_scratch(local, domain - most, margin, listed), pairs * (domain - most) // domain,
    )
    moment, rest = lax.optimization_barrier((moment, rest))
    coords, moment = call(
        functools.partial(modes_kernel, blocks, 3), (rest, exchange(moment)) + fixed, 0, [packed] * 2,
        [pltpu.VMEM((3, beads, share), f32)] * 3, 0,
    )
    for step in range(1, steps):
        joined = step == steps - 1
        out = call(
            functools.partial(middle_kernel, hops, blocks, listed, 3 * step + 3, joined),
            (moved_lists, first_charge) + tuple(window(coords, hops)) + (moment, rest) + fixed, 1,
            [(count, 6 * blocks * local, BLOCK)] if joined else [packed] * 2,
            force_scratch(beads, blocks, margin, listed), pairs,
        )
        if not joined:
            coords, moment = out
    both = exchange(out[0])

    def ends(low, c):
        pieces = both[low:low + hops, c * packed[1]:(c + 1) * packed[1]]
        return pieces.reshape(hops, 3, blocks, local, BLOCK).transpose(1, 3, 0, 2, 4).reshape(3, local, edge)

    message = passed(jnp.concatenate([
        ends(count - 2 * hops, 0), ends(count - hops, 0), ends(count - hops, 1),
        jnp.broadcast_to(charge[:, None, atoms - edge:], (1, local, edge)),
    ], axis=0), 1)
    (upper,) = call(
        functools.partial(upper_kernel, blocks, margin, listed),
        (lists, first_charge, both), 1,
        [(3, local, most * BLOCK)], force_scratch(local, most, margin, listed), pairs * most // domain,
    )
    last_charge = jnp.concatenate([message[9, :1], first_charge[:, :half * BLOCK + edge]], axis=1)
    return tuple(call(
        functools.partial(lower_kernel, blocks, margin, listed),
        (lists, last_charge, both, message, upper), 1,
        [(3, local, atoms)] * 2, force_scratch(local, domain - most, margin, listed), pairs * (domain - most) // domain,
    ))


def solution(mesh):
    placed = (
        P(None, "bead", "space"),
        P(None, "bead", "space"),
        P("space"),
        P("space", None),
        P(None, None, "bead", "space"),
    )
    return jax.shard_map(
        body,
        mesh=mesh,
        in_specs=placed,
        out_specs=(P(None, "bead", "space"), P(None, "bead", "space")),
        check_vma=False,
    )
```

```python
import functools
import math

import jax
import jax.numpy as jnp
import numpy as np
from jax import lax
from jax.experimental import pallas as pl
from jax.experimental.pallas import tpu as pltpu
from jax.sharding import PartitionSpec as P

BLOCK = 128
HALO = 4

half_step = 0.025
time_step = 0.05
chain_freq = 12.0
thermal = 0.375
centroid_friction = 1.0
screening = 4.0
softening = 0.09
CHARGES = (1.0, -1.0, 0.6, -1.4)
MASSES = (1.0, 2.0, 3.0, 4.0)

PAIR_ROWS = 24
PAIR_PAD = 32
SUM_ROWS = 16
QUAD = 4
SLOTS = 8
FRAME = 16
f32 = jnp.float32
bf16 = jnp.bfloat16


def mode_constants(bead_total):
    j = np.arange(bead_total)[:, None]
    k = np.arange(bead_total)[None, :]
    half = bead_total // 2
    phase = 2.0 * np.pi * ((j * k) % bead_total) / bead_total
    plain = 1.0 / math.sqrt(bead_total)
    paired = math.sqrt(2.0 / bead_total)
    matrix = np.where(
        k == 0,
        plain,
        np.where(
            k < half,
            paired * np.cos(phase),
            np.where(k == half, plain * np.cos(phase), paired * np.sin(phase)),
        ),
    )
    modes = np.arange(bead_total)
    frequency = 2.0 * chain_freq * np.sin(np.pi * modes / bead_total)
    angle = frequency * time_step
    ratio = np.where(modes == 0, time_step, np.sin(angle) / np.where(modes == 0, 1.0, frequency))
    friction = np.where(modes == 0, centroid_friction, 2.0 * frequency)
    damping = np.exp(-friction * time_step)
    kick = np.sqrt(1.0 - damping * damping)
    tables = np.stack([np.cos(angle), ratio, frequency * np.sin(angle), damping, kick])
    tables = np.broadcast_to(tables[:, :, None], tables.shape + (BLOCK,))
    return matrix.astype(np.float32), np.ascontiguousarray(tables).astype(np.float32)


def split_rows(matrix):
    parts = []
    for _ in range(3):
        parts.append(matrix.astype(jnp.bfloat16))
        matrix = matrix - parts[-1].astype(np.float32)
    one, two, three = parts
    return jnp.asarray(np.concatenate([one, one, two, two, one, three], axis=1))


def split3(v):
    one = v.astype(bf16).astype(f32)
    rest = v - one
    two = rest.astype(bf16).astype(f32)
    three = (rest - two).astype(bf16).astype(f32)
    return one, two, three


def pair_rows(coords, norm, own):
    rows = []
    for v in coords:
        one, two, three = split3(v)
        if own:
            one, two, three = -2.0 * one, -2.0 * two, -2.0 * three
            rows += [one, one, two, two, one, three]
        else:
            rows += [one, two, one, two, three, one]
    ones = [jnp.ones_like(norm)] * 3
    norms = list(split3(norm))
    return rows + (norms + ones if own else ones + norms)


SCALE = 1.0 / (screening * math.log(2.0))


def weigh(square):
    inverse = lax.rsqrt(square)
    decay = jnp.exp2(-(square * inverse))
    return decay * ((inverse * inverse) * (inverse + math.log(2.0)))


def own_place(count):
    bead = lax.axis_index("bead")
    half = lax.div(bead, 2)
    return jnp.where(lax.rem(bead, 2) == 0, half, count - 1 - half)


def offsets_of(lists_ref, skip, origin, margin):
    first = lax.axis_index("space") * lists_ref.shape[1] + origin

    def offset_at(block, m):
        return jnp.clip(lists_ref[m, skip + block] - (first + block), -margin, margin)

    return offset_at


def charges(types):
    charge = jnp.zeros(types.shape, f32)
    for kind in range(4):
        charge = jnp.where(types == kind, CHARGES[kind], charge)
    return charge


def odd_tiles(lines):
    return lines + 8 * (1 - lines // 8 % 2)


def whole_quads(beads):
    return -(-beads // QUAD) * QUAD


def add_forces(group, blocks, margin, listed, offset_at, charge_ref, coord_ref, scratch, charge_from=0):
    rows_ref, sums_ref, far_ref, heavy_ref, near_ref, total_ref, force_ref, *buffers = scratch
    weight_refs = buffers
    beads = coord_ref.shape[1]
    pairs = beads // 2
    frame = min(FRAME, blocks)
    width = frame + 2 * margin
    middle = margin + (frame - 1) / 2.0
    at_once = max(1, 8 // beads)
    lines = at_once * beads
    apart = odd_tiles(lines)
    units = blocks * pairs

    def charge_at(block):
        return charge_ref[:, pl.ds(pl.multiple_of((charge_from + block) * BLOCK, BLOCK), BLOCK)]

    def put(ref, slot, k, value):
        ref[slot, k * apart:k * apart + lines, :] = value

    def centred(block, place):
        spans = [pl.ds(pl.multiple_of((block + i) * BLOCK, BLOCK), BLOCK) for i in range(at_once)]
        coords = [
            (jnp.concatenate([coord_ref[c, :, lanes] for lanes in spans], axis=0) - 1.0) * SCALE for c in range(3)
        ]
        shift = jnp.concatenate(
            [jnp.full((beads, BLOCK), SCALE, f32) * ((place + i).astype(f32) - middle) for i in range(at_once)], axis=0
        )
        coords[0] = coords[0] + shift
        norm = coords[0] * coords[0] + coords[1] * coords[1] + coords[2] * coords[2]
        charge = jnp.concatenate(
            [jnp.broadcast_to(charge_at(block + i), (beads, BLOCK)) for i in range(at_once)], axis=0
        )
        return coords, norm, charge

    def steps(count, one):
        slots = max(n for n in range(1, SLOTS + 1) if count % n == 0)

        def some(turn, carry):
            for slot in range(slots):
                one(turn * slots + slot, slot)
            return carry

        lax.fori_loop(0, count // slots, some, 0)

    nothing = jnp.zeros((lines, BLOCK), f32)
    for slot in range(SLOTS):
        for k in range(PAIR_ROWS, PAIR_PAD):
            put(rows_ref, slot, k, nothing)
        for k in range(12, SUM_ROWS):
            put(sums_ref, slot, k, nothing)
    blank = jnp.zeros((PAIR_PAD, BLOCK), bf16)
    passes = width // at_once
    square = (BLOCK, BLOCK)
    unit_matrix = (
        lax.broadcasted_iota(jnp.int32, square, 0) == lax.broadcasted_iota(jnp.int32, square, 1)
    ).astype(f32).astype(bf16)

    def one_table(step, slot):
        at_frame = step // passes
        place = (step - at_frame * passes) * at_once
        coords, norm, charge = centred(at_frame * frame + place, place)
        for k, row in enumerate(pair_rows(coords, norm, False)):
            put(rows_ref, slot, k, row)
        for c, v in enumerate([charge] + [charge * x for x in coords]):
            for level, part in enumerate(split3(v)):
                put(sums_ref, slot, level * 4 + c, part)
        for i in range(at_once):
            at = at_frame * width + place + i
            for quad in range(beads // QUAD):
                low = i * beads + quad * QUAD
                four = jnp.concatenate(
                    [rows_ref[slot, pl.ds(low + j, PAIR_PAD, stride=apart), :] for j in range(QUAD)], axis=0
                )
                far_ref[at, quad] = lax.dot_general(
                    unit_matrix, four.astype(bf16), (((1,), (1,)), ((), ())), preferred_element_type=f32
                ).astype(bf16)
                for half in range(2):
                    heavy_ref[at, 2 * quad + half] = jnp.concatenate(
                        [
                            sums_ref[slot, pl.ds(low + 2 * half + j, SUM_ROWS, stride=apart), :]
                            for j in range(2)
                        ],
                        axis=0,
                    ).astype(bf16)

    def one_own(step, slot):
        block = step * at_once
        place = block - block // frame * frame + margin
        coords, norm, _ = centred(block + margin, place)
        for k, row in enumerate(pair_rows(coords, norm + softening * SCALE * SCALE, True)):
            put(rows_ref, slot, k, row)
        for i in range(at_once):
            for bead in range(beads):
                near_ref[(block + i) * beads + bead] = rows_ref[
                    slot, pl.ds(i * beads + bead, PAIR_PAD, stride=apart), :
                ].astype(bf16)

    steps(blocks // frame * passes, one_table)
    steps(blocks // at_once, one_own)

    def places(unit):
        block = unit // pairs
        at_frame = block // frame
        base = at_frame * width + block - at_frame * frame + margin
        return [base + offset_at(block, m) for m in range(listed)], unit - block * pairs

    def parts(square):
        weight = weigh(square)
        high = weight.astype(bf16)
        return high, (weight - high.astype(f32)).astype(bf16)

    def squares(ats, pair, near, m):
        return jnp.dot(far_ref[ats[m], pair // (QUAD // 2)], near, preferred_element_type=f32)

    def own_columns(unit, half):
        columns = [
            jnp.concatenate([near_ref[2 * unit + j] if k == 2 * half + j else blank for k in range(QUAD)], axis=0)
            for j in range(2)
        ]
        return jnp.concatenate(columns, axis=1)

    def weighted(at, pair, both):
        table = heavy_ref[at, pair]
        return jnp.dot(jnp.concatenate([table, table], axis=1), both, preferred_element_type=f32)

    def keep(total, slot):
        for i in range(2):
            cols = slice(i * BLOCK, (i + 1) * BLOCK)
            row = i * SUM_ROWS
            spot = pl.ds(pl.multiple_of((2 * slot + i) * 8, 8), 8)
            total_ref[spot, :] = total[row:row + 8, cols] + total[row + 8:row + 16, cols]

    def body(step, carry):
        before_ats, before_pair = places(jnp.maximum(step * group - 1, 0))
        for turn in range(group):
            unit = step * group + turn
            now, other = turn % 2, (turn + 1) % 2
            ats, pair = places(unit)
            near = own_columns(unit, turn % 2)
            total = jnp.zeros((2 * SUM_ROWS, 2 * BLOCK), f32)
            for m in range(listed):
                spot = slice(2 * m * BLOCK, 2 * (m + 1) * BLOCK)
                weight_refs[now][spot, :] = jnp.concatenate(parts(squares(ats, pair, near, m)), axis=0)
                total = total + weighted(before_ats[m], before_pair, weight_refs[other][spot, :])
            keep(total, jnp.where(unit == 0, units, unit - 1))
            before_ats, before_pair = ats, pair
        return carry

    group = math.gcd(units, group)
    lax.fori_loop(0, units // group, body, 0)
    last_ats, last_pair = places(units - 1)
    keep(
        sum(
            weighted(last_ats[m], last_pair, weight_refs[(group - 1) % 2][2 * m * BLOCK:2 * (m + 1) * BLOCK, :])
            for m in range(listed)
        ),
        units - 1,
    )

    def one_block(block, slot):
        at_frame = block // frame
        place = block - at_frame * frame + margin
        lanes = pl.ds(pl.multiple_of((block + margin) * BLOCK, BLOCK), BLOCK)
        coords = [(coord_ref[c, :, lanes] - 1.0) * SCALE for c in range(3)]
        coords[0] = coords[0] + SCALE * (place.astype(f32) - middle)
        charge = jnp.broadcast_to(SCALE * SCALE * charge_at(block + margin), coords[0].shape)

        def summed(c):
            return sum(total_ref[pl.ds(block * beads * 8 + c + i, beads, stride=8), :] for i in (0, 4))

        near = summed(0)
        own = pl.ds(pl.multiple_of(block * BLOCK, BLOCK), BLOCK)
        for c in range(3):
            force_ref[c, :, own] = charge * (coords[c] * near - summed(c + 1))

    steps(blocks, one_block)


def force_scratch(local, blocks, margin, listed):
    beads = whole_quads(local)
    frame = min(FRAME, blocks)
    tables = (frame + 2 * margin) * (blocks // frame)
    lines = max(8, beads)
    units = blocks * beads // 2
    return [
        pltpu.VMEM((3, beads, (blocks + 2 * margin) * BLOCK), f32),
        pltpu.VMEM((SLOTS, PAIR_PAD * odd_tiles(lines), BLOCK), f32),
        pltpu.VMEM((SLOTS, SUM_ROWS * odd_tiles(lines), BLOCK), f32),
        pltpu.VMEM((tables, beads // QUAD, BLOCK, QUAD * PAIR_PAD), bf16),
        pltpu.VMEM((tables, beads // 2, 2 * SUM_ROWS, BLOCK), bf16),
        pltpu.VMEM((2 * units, PAIR_PAD, BLOCK), bf16),
        pltpu.VMEM(((units + 1) * 16, BLOCK), f32),
        pltpu.VMEM((3, beads, blocks * BLOCK), f32),
        pltpu.VMEM((2 * listed * BLOCK, 2 * BLOCK), bf16),
        pltpu.VMEM((2 * listed * BLOCK, 2 * BLOCK), bf16),
    ]


def call(kernel, args, smem_count, shapes, scratch, work, in_specs=None):
    vmem = pl.BlockSpec(memory_space=pltpu.VMEM)
    smem = pl.BlockSpec(memory_space=pltpu.SMEM)
    return pl.pallas_call(
        kernel,
        out_shape=[jax.ShapeDtypeStruct(shape, f32) for shape in shapes],
        grid=() if in_specs is None else (1,),
        in_specs=in_specs or [smem] * smem_count + [vmem] * (len(args) - smem_count),
        out_specs=[vmem] * len(shapes),
        scratch_shapes=scratch,
        compiler_params=pltpu.CompilerParams(vmem_limit_bytes=(40 if in_specs is None else 62) * 1024 * 1024),
        cost_estimate=pl.CostEstimate(
            flops=20 * work + 1024, bytes_accessed=4 * 1024 * 1024, transcendentals=2 * work
        ),
    )(*args)


def row_of(c, block, blocks, local):
    return (c * blocks + block) * local


def unpack_beads(source, base, blocks, local, target, offset):
    for c in range(3):
        for block in range(blocks):
            row = row_of(base + c, block, blocks, local)
            lane = offset + block * BLOCK
            for group in range(source.shape[0]):
                target[c, group * local:(group + 1) * local, lane:lane + BLOCK] = source[group, row:row + local, :]


def pack_beads(value, c, blocks, local, target):
    for block in range(blocks):
        row = row_of(c, block, blocks, local)
        for group in range(target.shape[0]):
            target[group, row:row + local, :] = value[
                group * local:(group + 1) * local, block * BLOCK:(block + 1) * BLOCK
            ]


FORCE = 6


def clear(coord_ref, local):
    if coord_ref.shape[1] != local:
        coord_ref[...] = jnp.zeros(coord_ref.shape, f32)


def prepare_kernel(
    blocks, x_ref, edge_ref, noise_ref, types_ref, lists_ref, rest_ref, message_ref, charge_ref, mass_ref
):
    steps, _, local, atoms = noise_ref.shape
    edge = message_ref.shape[2]
    types = types_ref[...]
    charge = charges(types)
    mass = jnp.zeros(types.shape, f32)
    for kind in range(4):
        mass = jnp.where(types == kind, MASSES[kind], mass)
    charge_ref[...] = charge
    mass_ref[...] = mass
    for c in range(3):
        message_ref[c] = x_ref[c, :, :edge]
        message_ref[3 + c] = x_ref[c, :, edge:2 * edge]
        message_ref[6 + c] = edge_ref[c]
    for i, row in enumerate([charge[:, :edge], charge[:, edge:2 * edge], mass[:, :edge]]):
        message_ref[9 + i] = jnp.broadcast_to(row, (local, edge))
    message_ref[12] = jnp.zeros((local, edge), f32)
    for m in range(lists_ref.shape[0]):
        at = m * (edge // 8)
        message_ref[12, 0:1, at:at + edge // BLOCK] = lists_ref[m:m + 1, :edge // BLOCK].astype(f32)
    for c in range(3 + 3 * steps):
        for block in range(atoms // BLOCK):
            lanes = slice(block * BLOCK, (block + 1) * BLOCK)
            value = x_ref[c, :, lanes] if c < 3 else noise_ref[c // 3 - 1, c % 3, :, lanes]
            row = row_of(c, block % blocks, blocks, local)
            rest_ref[block // blocks, row:row + local, :] = value


def front_kernel(
    each, margin, listed, lists_ref, types_ref, x_ref, p_ref, pout_ref, charge_ref, coord_ref, *scratch
):
    _, local, _ = x_ref.shape
    blocks = pout_ref.shape[0] * each
    charge_ref[...] = charges(types_ref[...])
    clear(coord_ref, local)
    for c in range(3):
        coord_ref[c, :local, :] = x_ref[c, :, :(blocks + 2 * margin) * BLOCK]
    offset_at = offsets_of(lists_ref, margin, margin, margin)
    add_forces(16, blocks, margin, listed, offset_at, charge_ref, coord_ref, scratch)
    force_ref = scratch[FORCE]
    for c in range(3):
        for block in range(blocks):
            lanes = slice(block * BLOCK, (block + 1) * BLOCK)
            moment = p_ref[c, :, (block + margin) * BLOCK:(block + margin + 1) * BLOCK]
            row = row_of(c, block % each, each, local)
            pout_ref[block // each, row:row + local, :] = moment + half_step * force_ref[c, :local, lanes]


def back_kernel(
    each, margin, listed, lists_ref, charge_ref, x_ref, message_ref, p_ref, front_ref, pout_ref, coord_ref, *scratch
):
    _, local, atoms = x_ref.shape
    edge = margin * BLOCK
    done = front_ref.shape[0]
    first = done * each
    blocks = (pout_ref.shape[0] - done) * each
    own = atoms - first * BLOCK
    clear(coord_ref, local)
    for c in range(3):
        coord_ref[c, :local, :own] = x_ref[c, :, first * BLOCK:]
        for part in range(2):
            coord_ref[c, :local, own + part * edge:own + (part + 1) * edge] = message_ref[3 * part + c]
    offset_at = offsets_of(lists_ref, first, first + margin, margin)
    add_forces(16, blocks, margin, listed, offset_at, charge_ref, coord_ref, scratch, first)
    force_ref = scratch[FORCE]
    pout_ref[:done] = front_ref[...]
    for c in range(3):
        for block in range(blocks):
            lanes = slice(block * BLOCK, (block + 1) * BLOCK)
            at = (first + block) * BLOCK + edge
            if at < atoms:
                moment = p_ref[c, :, at:at + BLOCK]
            else:
                moment = message_ref[6 + c, :, at - atoms:at - atoms + BLOCK]
            row = row_of(c, block % each, each, local)
            pout_ref[done + block // each, row:row + local, :] = moment + half_step * force_ref[c, :local, lanes]


def from_packed(ref, c, block, each, local):
    row = row_of(c, block % each, each, local)
    return ref[block // each, row:row + local, :]


def upper_kernel(each, margin, listed, lists_ref, charge_ref, both_ref, pout_ref, coord_ref, *scratch):
    _, local, atoms = pout_ref.shape
    blocks = atoms // BLOCK
    domain = both_ref.shape[0] * each
    skipped = domain - blocks - 2 * margin
    clear(coord_ref, local)
    for c in range(3):
        for block in range(skipped, domain):
            at = (block - skipped) * BLOCK
            coord_ref[c, :local, at:at + BLOCK] = from_packed(both_ref, c, block, each, local)
    offset_at = offsets_of(lists_ref, domain - blocks, domain - blocks, margin)
    add_forces(16, blocks, margin, listed, offset_at, charge_ref, coord_ref, scratch, skipped + margin)
    force_ref = scratch[FORCE]
    for c in range(3):
        for block in range(blocks):
            lanes = slice(block * BLOCK, (block + 1) * BLOCK)
            moment = from_packed(both_ref, 3 + c, domain - blocks + block - margin, each, local)
            pout_ref[c, :, lanes] = moment + half_step * force_ref[c, :local, lanes]


def lower_kernel(
    each, margin, listed, lists_ref, charge_ref, both_ref, message_ref, upper_ref, xout_ref, pout_ref, coord_ref,
    *scratch,
):
    _, local, atoms = xout_ref.shape
    edge = margin * BLOCK
    lower = atoms - upper_ref.shape[2]
    blocks = lower // BLOCK
    clear(coord_ref, local)
    for c in range(3):
        for part in range(2):
            coord_ref[c, :local, part * edge:(part + 1) * edge] = message_ref[3 * part + c]
        for block in range(blocks):
            at = 2 * edge + block * BLOCK
            coord_ref[c, :local, at:at + BLOCK] = from_packed(both_ref, c, block, each, local)
        xout_ref[c, :, :edge] = message_ref[3 + c]
        for block in range(margin, atoms // BLOCK):
            lanes = slice(block * BLOCK, (block + 1) * BLOCK)
            xout_ref[c, :, lanes] = from_packed(both_ref, c, block - margin, each, local)
        pout_ref[c, :, lower:] = upper_ref[c]
    offset_at = offsets_of(lists_ref, 0, 0, margin)
    add_forces(16, blocks, margin, listed, offset_at, charge_ref, coord_ref, scratch)
    force_ref = scratch[FORCE]
    for c in range(3):
        for block in range(blocks):
            lanes = slice(block * BLOCK, (block + 1) * BLOCK)
            if block < margin:
                moment = message_ref[6 + c, :, lanes]
            else:
                moment = from_packed(both_ref, 3 + c, block - margin, each, local)
            pout_ref[c, :, lanes] = moment + half_step * force_ref[c, :local, lanes]


def thermostat(coords, moments, noises, mass_ref, matrix_ref, matrix_t_ref, table_ref, store):
    beads, width = moments[0].shape
    cosine, ratio, stiffness, damping, kick = [
        jnp.concatenate([table_ref[i]] * (width // BLOCK), axis=1) for i in range(5)
    ]
    first = pl.multiple_of(own_place(mass_ref.shape[1] // width) * width, BLOCK)
    mass = jnp.broadcast_to(mass_ref[:, pl.ds(first, width)], (beads, width))
    spread = kick * jnp.sqrt(thermal * mass)
    drift = ratio / mass
    stiff = stiffness * mass

    def multiply(matrix, values):
        joined = jnp.concatenate(values, axis=1)
        one, two, three = [part.astype(bf16) for part in split3(joined)]
        rows = jnp.concatenate([one, two, one, two, three, one], axis=0)
        out = jnp.dot(matrix, rows, preferred_element_type=f32)
        return [out[:, i * width:(i + 1) * width] for i in range(len(values))]

    mode = multiply(matrix_t_ref[...], coords + moments)
    next_x, next_p = [], []
    for c in range(3):
        mode_x = mode[c]
        mode_p = damping * mode[3 + c] + spread * noises[c]
        next_x.append(cosine * mode_x + drift * mode_p)
        next_p.append(cosine * mode_p - stiff * mode_x)
    beads_now = multiply(matrix_ref[...], next_x + next_p)
    for c in range(3):
        store(c, beads_now[c], beads_now[3 + c])


def modes_kernel(
    blocks, noise_base, rest_ref, p_ref, mass_ref, matrix_ref, matrix_t_ref, table_ref,
    xout_ref, pout_ref, coord_ref, moment_ref, noise_ref,
):
    local = p_ref.shape[1] // (3 * blocks)
    unpack_beads(rest_ref, 0, blocks, local, coord_ref, 0)
    unpack_beads(p_ref, 0, blocks, local, moment_ref, 0)
    unpack_beads(rest_ref, noise_base, blocks, local, noise_ref, 0)

    def store(c, x, p):
        pack_beads(x, c, blocks, local, xout_ref)
        pack_beads(p, c, blocks, local, pout_ref)

    thermostat(
        *[[ref[c] for c in range(3)] for ref in (coord_ref, moment_ref, noise_ref)],
        mass_ref, matrix_ref, matrix_t_ref, table_ref, store,
    )


def middle_kernel(hops, blocks, listed, noise_base, joined, lists_ref, charge_ref, *refs):
    parts = 2 * hops + 1
    x_refs = refs[:parts]
    p_ref, noise_ref, mass_ref, matrix_ref, matrix_t_ref, table_ref = refs[parts:parts + 6]
    outs = refs[parts + 6:parts + (7 if joined else 8)]
    coord_ref, *scratch = refs[parts + len(outs) + 6:]
    beads = coord_ref.shape[1]
    local = beads // p_ref.shape[0]
    width = blocks * BLOCK
    for part in range(parts):
        unpack_beads(x_refs[part], 0, blocks, local, coord_ref, part * width)
    margin = hops * blocks
    first = own_place(p_ref.shape[0]) * blocks
    offset_at = offsets_of(lists_ref, first, first + margin, margin)
    add_forces(16, blocks, margin, listed, offset_at, charge_ref, coord_ref, scratch, first)
    force_ref = scratch[FORCE]
    unpack_beads(p_ref, 0, blocks, local, coord_ref, 0)
    unpack_beads(noise_ref, noise_base, blocks, local, coord_ref, (parts - 1) * width)

    def share(c, part):
        return coord_ref[c, :, part * width:(part + 1) * width]

    def store(c, x, p):
        pack_beads(x, c, blocks, local, outs[0])
        if joined:
            pack_beads(p, 3 + c, blocks, local, outs[0])
        else:
            pack_beads(p, c, blocks, local, outs[1])

    thermostat(
        [share(c, hops) for c in range(3)],
        [share(c, 0) + 2.0 * half_step * force_ref[c] for c in range(3)],
        [share(c, parts - 1) for c in range(3)],
        mass_ref, matrix_ref, matrix_t_ref, table_ref, store,
    )


def fold(count):
    return [i // 2 if i % 2 == 0 else count - 1 - i // 2 for i in range(count)]


def exchange(pieces):
    order = fold(pieces.shape[0])
    group = [order.index(at) for at in range(len(order))]
    return lax.all_to_all(pieces, "bead", split_axis=0, concat_axis=0, axis_index_groups=[group], tiled=True)


def passed(values, step):
    count = lax.axis_size("space")
    return lax.ppermute(values, "space", [(i, (i + step) % count) for i in range(count)])


def round_ring(values, hop):
    count = lax.axis_size("bead")
    domains = lax.axis_size("space")
    order = fold(count)
    device = {}
    for bead in range(count):
        for domain in range(domains):
            device[domain * count + order[bead]] = bead * domains + domain
    total = count * domains
    return lax.ppermute(values, ("bead", "space"), [(device[(at + hop) % total], device[at]) for at in range(total)])


def window(values, hops):
    return [round_ring(values, hop) if hop else values for hop in range(-hops, hops + 1)]


def body(positions, momenta, atom_types, neighbours, thermal_noise):
    count = lax.axis_size("bead")
    _, local, atoms = positions.shape
    beads = local * count
    domain = atoms // BLOCK
    blocks = domain // count
    share = blocks * BLOCK
    hops = -(-HALO // blocks)
    margin = hops * blocks
    edge = margin * BLOCK
    steps = thermal_noise.shape[0]
    listed = neighbours.shape[1]
    order = fold(count)
    lists = neighbours.T
    types = atom_types[None, :]

    packed = (count, 3 * blocks * local, BLOCK)
    whole = [positions.shape, (3, local, edge), thermal_noise.shape, types.shape, lists.shape]
    rest, message, charge, mass = call(
        functools.partial(prepare_kernel, blocks),
        (positions, momenta, thermal_noise, types, lists), 0,
        [(count, (1 + steps) * packed[1], BLOCK), (13, local, edge), (1, atoms), (1, atoms)], [], 0,
        [pl.BlockSpec(shape, lambda i, rank=len(shape): (0,) * rank) for shape in whole],
    )
    message = passed(message, -1)
    rest = exchange(rest)
    side = message[9:, 0]
    first_charge = jnp.concatenate([charge, side[:1], side[1:2]], axis=1)
    moved_mass = jnp.concatenate([mass[:, edge:], side[2:3]], axis=1)
    domains = lax.axis_size("space")
    foreign = side[3].reshape(8, edge // 8)[:listed, :margin].astype(jnp.int32)
    foreign = foreign + jnp.where(lax.axis_index("space") == domains - 1, domains * domain, 0)
    moved_lists = jnp.concatenate([lists[:, margin:], foreign], axis=1)

    matrix, tables = mode_constants(beads)
    at = np.concatenate([order.index(g) * local + np.arange(local) for g in range(count)])
    matrix = matrix[at][:, at]
    fixed = (moved_mass, split_rows(matrix), split_rows(matrix.T), jnp.asarray(tables[:, at]))

    pairs = beads * blocks * listed * BLOCK * BLOCK
    half = domain // 2
    most = domain - half
    (moment,) = call(
        functools.partial(front_kernel, blocks, margin, listed), (lists, types, positions, momenta), 1,
        [(most // blocks,) + packed[1:]],
        [pltpu.VMEM(types.shape, f32)] + force_scratch(local, most, margin, listed), pairs * most // domain,
    )
    moment, rest = lax.optimization_barrier((moment, rest))
    rest = round_ring(rest, hops)
    (moment,) = call(
        functools.partial(back_kernel, blocks, margin, listed),
        (moved_lists, first_charge, positions, message, momenta, moment), 1,
        [packed], force_scratch(local, domain - most, margin, listed), pairs * (domain - most) // domain,
    )
    moment, rest = lax.optimization_barrier((moment, rest))
    coords, moment = call(
        functools.partial(modes_kernel, blocks, 3), (rest, exchange(moment)) + fixed, 0, [packed] * 2,
        [pltpu.VMEM((3, beads, share), f32)] * 3, 0,
    )
    for step in range(1, steps):
        joined = step == steps - 1
        out = call(
            functools.partial(middle_kernel, hops, blocks, listed, 3 * step + 3, joined),
            (moved_lists, first_charge) + tuple(window(coords, hops)) + (moment, rest) + fixed, 1,
            [(count, 6 * blocks * local, BLOCK)] if joined else [packed] * 2,
            force_scratch(beads, blocks, margin, listed), pairs,
        )
        if not joined:
            coords, moment = out
    both = exchange(out[0])

    def ends(low, c):
        pieces = both[low:low + hops, c * packed[1]:(c + 1) * packed[1]]
        return pieces.reshape(hops, 3, blocks, local, BLOCK).transpose(1, 3, 0, 2, 4).reshape(3, local, edge)

    message = passed(jnp.concatenate([
        ends(count - 2 * hops, 0), ends(count - hops, 0), ends(count - hops, 1),
        jnp.broadcast_to(charge[:, None, atoms - edge:], (1, local, edge)),
    ], axis=0), 1)
    (upper,) = call(
        functools.partial(upper_kernel, blocks, margin, listed),
        (lists, first_charge, both), 1,
        [(3, local, most * BLOCK)], force_scratch(local, most, margin, listed), pairs * most // domain,
    )
    last_charge = jnp.concatenate([message[9, :1], first_charge[:, :half * BLOCK + edge]], axis=1)
    return tuple(call(
        functools.partial(lower_kernel, blocks, margin, listed),
        (lists, last_charge, both, message, upper), 1,
        [(3, local, atoms)] * 2, force_scratch(local, domain - most, margin, listed), pairs * (domain - most) // domain,
    ))


def solution(mesh):
    placed = (
        P(None, "bead", "space"),
        P(None, "bead", "space"),
        P("space"),
        P("space", None),
        P(None, None, "bead", "space"),
    )
    return jax.shard_map(
        body,
        mesh=mesh,
        in_specs=placed,
        out_specs=(P(None, "bead", "space"), P(None, "bead", "space")),
        check_vma=False,
    )
```

```python
import functools
import math

import jax
import jax.numpy as jnp
import numpy as np
from jax import lax
from jax.experimental import pallas as pl
from jax.experimental.pallas import tpu as pltpu
from jax.sharding import PartitionSpec as P

BLOCK = 128
HALO = 4

half_step = 0.025
time_step = 0.05
chain_freq = 12.0
thermal = 0.375
centroid_friction = 1.0
screening = 4.0
softening = 0.09
CHARGES = (1.0, -1.0, 0.6, -1.4)
MASSES = (1.0, 2.0, 3.0, 4.0)

PAIR_ROWS = 24
PAIR_PAD = 32
SUM_ROWS = 16
QUAD = 4
SLOTS = 8
FRAME = 16
f32 = jnp.float32
bf16 = jnp.bfloat16


def mode_constants(bead_total):
    j = np.arange(bead_total)[:, None]
    k = np.arange(bead_total)[None, :]
    half = bead_total // 2
    phase = 2.0 * np.pi * ((j * k) % bead_total) / bead_total
    plain = 1.0 / math.sqrt(bead_total)
    paired = math.sqrt(2.0 / bead_total)
    matrix = np.where(
        k == 0,
        plain,
        np.where(
            k < half,
            paired * np.cos(phase),
            np.where(k == half, plain * np.cos(phase), paired * np.sin(phase)),
        ),
    )
    modes = np.arange(bead_total)
    frequency = 2.0 * chain_freq * np.sin(np.pi * modes / bead_total)
    angle = frequency * time_step
    ratio = np.where(modes == 0, time_step, np.sin(angle) / np.where(modes == 0, 1.0, frequency))
    friction = np.where(modes == 0, centroid_friction, 2.0 * frequency)
    damping = np.exp(-friction * time_step)
    kick = np.sqrt(1.0 - damping * damping)
    tables = np.stack([np.cos(angle), ratio, frequency * np.sin(angle), damping, kick])
    tables = np.broadcast_to(tables[:, :, None], tables.shape + (BLOCK,))
    return matrix.astype(np.float32), np.ascontiguousarray(tables).astype(np.float32)


def split_rows(matrix):
    parts = []
    for _ in range(3):
        parts.append(matrix.astype(jnp.bfloat16))
        matrix = matrix - parts[-1].astype(np.float32)
    one, two, three = parts
    return jnp.asarray(np.concatenate([one, one, two, two, one, three], axis=1))


def split3(v):
    one = v.astype(bf16).astype(f32)
    rest = v - one
    two = rest.astype(bf16).astype(f32)
    three = (rest - two).astype(bf16).astype(f32)
    return one, two, three


def pair_rows(coords, norm, own):
    rows = []
    for v in coords:
        one, two, three = split3(v)
        if own:
            one, two, three = -2.0 * one, -2.0 * two, -2.0 * three
            rows += [one, one, two, two, one, three]
        else:
            rows += [one, two, one, two, three, one]
    ones = [jnp.ones_like(norm)] * 3
    norms = list(split3(norm))
    return rows + (norms + ones if own else ones + norms)


SCALE = 1.0 / (screening * math.log(2.0))


def weigh(square):
    inverse = lax.rsqrt(square)
    decay = jnp.exp2(-(square * inverse))
    return decay * ((inverse * inverse) * (inverse + math.log(2.0)))


def own_place(count):
    bead = lax.axis_index("bead")
    half = lax.div(bead, 2)
    return jnp.where(lax.rem(bead, 2) == 0, half, count - 1 - half)


def offsets_of(lists_ref, skip, origin, margin):
    first = lax.axis_index("space") * lists_ref.shape[1] + origin

    def offset_at(block, m):
        return jnp.clip(lists_ref[m, skip + block] - (first + block), -margin, margin)

    return offset_at


def charges(types):
    charge = jnp.zeros(types.shape, f32)
    for kind in range(4):
        charge = jnp.where(types == kind, CHARGES[kind], charge)
    return charge


def odd_tiles(lines):
    return lines + 8 * (1 - lines // 8 % 2)


def whole_quads(beads):
    return -(-beads // QUAD) * QUAD


def add_forces(group, blocks, margin, listed, offset_at, charge_ref, coord_ref, scratch, charge_from=0):
    rows_ref, sums_ref, far_ref, heavy_ref, near_ref, total_ref, force_ref, *buffers = scratch
    weight_refs = buffers
    beads = coord_ref.shape[1]
    pairs = beads // 2
    frame = min(FRAME, blocks)
    width = frame + 2 * margin
    middle = margin + (frame - 1) / 2.0
    at_once = max(1, 8 // beads)
    lines = at_once * beads
    apart = odd_tiles(lines)
    units = blocks * pairs

    def charge_at(block):
        return charge_ref[:, pl.ds(pl.multiple_of((charge_from + block) * BLOCK, BLOCK), BLOCK)]

    def put(ref, slot, k, value):
        ref[slot, k * apart:k * apart + lines, :] = value

    def centred(block, place):
        spans = [pl.ds(pl.multiple_of((block + i) * BLOCK, BLOCK), BLOCK) for i in range(at_once)]
        coords = [
            (jnp.concatenate([coord_ref[c, :, lanes] for lanes in spans], axis=0) - 1.0) * SCALE for c in range(3)
        ]
        shift = jnp.concatenate(
            [jnp.full((beads, BLOCK), SCALE, f32) * ((place + i).astype(f32) - middle) for i in range(at_once)], axis=0
        )
        coords[0] = coords[0] + shift
        norm = coords[0] * coords[0] + coords[1] * coords[1] + coords[2] * coords[2]
        charge = jnp.concatenate(
            [jnp.broadcast_to(charge_at(block + i), (beads, BLOCK)) for i in range(at_once)], axis=0
        )
        return coords, norm, charge

    def steps(count, one):
        slots = max(n for n in range(1, SLOTS + 1) if count % n == 0)

        def some(turn, carry):
            for slot in range(slots):
                one(turn * slots + slot, slot)
            return carry

        lax.fori_loop(0, count // slots, some, 0)

    nothing = jnp.zeros((lines, BLOCK), f32)
    for slot in range(SLOTS):
        for k in range(PAIR_ROWS, PAIR_PAD):
            put(rows_ref, slot, k, nothing)
        for k in range(12, SUM_ROWS):
            put(sums_ref, slot, k, nothing)
    blank = jnp.zeros((PAIR_PAD, BLOCK), bf16)
    passes = width // at_once

    def one_table(step, slot):
        at_frame = step // passes
        place = (step - at_frame * passes) * at_once
        coords, norm, charge = centred(at_frame * frame + place, place)
        for k, row in enumerate(pair_rows(coords, norm, False)):
            put(rows_ref, slot, k, row)
        for c, v in enumerate([charge] + [charge * x for x in coords]):
            for level, part in enumerate(split3(v)):
                put(sums_ref, slot, level * 4 + c, part)
        for i in range(at_once):
            at = at_frame * width + place + i
            for quad in range(beads // QUAD):
                low = i * beads + quad * QUAD
                four = jnp.concatenate(
                    [rows_ref[slot, pl.ds(low + j, PAIR_PAD, stride=apart), :] for j in range(QUAD)], axis=0
                )
                far_ref[at, quad] = jnp.transpose(four.astype(bf16))
                for half in range(2):
                    heavy_ref[at, 2 * quad + half] = jnp.concatenate(
                        [
                            sums_ref[slot, pl.ds(low + 2 * half + j, SUM_ROWS, stride=apart), :]
                            for j in range(2)
                        ],
                        axis=0,
                    ).astype(bf16)

    def one_own(step, slot):
        block = step * at_once
        place = block - block // frame * frame + margin
        coords, norm, _ = centred(block + margin, place)
        for k, row in enumerate(pair_rows(coords, norm + softening * SCALE * SCALE, True)):
            put(rows_ref, slot, k, row)
        for i in range(at_once):
            for bead in range(beads):
                near_ref[(block + i) * beads + bead] = rows_ref[
                    slot, pl.ds(i * beads + bead, PAIR_PAD, stride=apart), :
                ].astype(bf16)

    steps(blocks // frame * passes, one_table)
    steps(blocks // at_once, one_own)

    def places(unit):
        block = unit // pairs
        at_frame = block // frame
        base = at_frame * width + block - at_frame * frame + margin
        return [base + offset_at(block, m) for m in range(listed)], unit - block * pairs

    def parts(square):
        weight = weigh(square)
        high = weight.astype(bf16)
        return high, (weight - high.astype(f32)).astype(bf16)

    def squares(ats, pair, near, m):
        return jnp.dot(far_ref[ats[m], pair // (QUAD // 2)], near, preferred_element_type=f32)

    def own_columns(unit, half):
        columns = [
            jnp.concatenate([near_ref[2 * unit + j] if k == 2 * half + j else blank for k in range(QUAD)], axis=0)
            for j in range(2)
        ]
        return jnp.concatenate(columns, axis=1)

    def weighted(at, pair, both):
        table = heavy_ref[at, pair]
        return jnp.dot(jnp.concatenate([table, table], axis=1), both, preferred_element_type=f32)

    def keep(total, slot):
        for i in range(2):
            cols = slice(i * BLOCK, (i + 1) * BLOCK)
            row = i * SUM_ROWS
            spot = pl.ds(pl.multiple_of((2 * slot + i) * 8, 8), 8)
            total_ref[spot, :] = total[row:row + 8, cols] + total[row + 8:row + 16, cols]

    def body(step, carry):
        before_ats, before_pair = places(jnp.maximum(step * group - 1, 0))
        for turn in range(group):
            unit = step * group + turn
            now, other = turn % 2, (turn + 1) % 2
            ats, pair = places(unit)
            near = own_columns(unit, turn % 2)
            total = jnp.zeros((2 * SUM_ROWS, 2 * BLOCK), f32)
            for m in range(listed):
                spot = slice(2 * m * BLOCK, 2 * (m + 1) * BLOCK)
                weight_refs[now][spot, :] = jnp.concatenate(parts(squares(ats, pair, near, m)), axis=0)
                total = total + weighted(before_ats[m], before_pair, weight_refs[other][spot, :])
            keep(total, jnp.where(unit == 0, units, unit - 1))
            before_ats, before_pair = ats, pair
        return carry

    group = math.gcd(units, group)
    lax.fori_loop(0, units // group, body, 0)
    last_ats, last_pair = places(units - 1)
    keep(
        sum(
            weighted(last_ats[m], last_pair, weight_refs[(group - 1) % 2][2 * m * BLOCK:2 * (m + 1) * BLOCK, :])
            for m in range(listed)
        ),
        units - 1,
    )

    def one_block(block, slot):
        at_frame = block // frame
        place = block - at_frame * frame + margin
        lanes = pl.ds(pl.multiple_of((block + margin) * BLOCK, BLOCK), BLOCK)
        coords = [(coord_ref[c, :, lanes] - 1.0) * SCALE for c in range(3)]
        coords[0] = coords[0] + SCALE * (place.astype(f32) - middle)
        charge = jnp.broadcast_to(SCALE * SCALE * charge_at(block + margin), coords[0].shape)

        def summed(c):
            return sum(total_ref[pl.ds(block * beads * 8 + c + i, beads, stride=8), :] for i in (0, 4))

        near = summed(0)
        own = pl.ds(pl.multiple_of(block * BLOCK, BLOCK), BLOCK)
        for c in range(3):
            force_ref[c, :, own] = charge * (coords[c] * near - summed(c + 1))

    steps(blocks, one_block)


def force_scratch(local, blocks, margin, listed):
    beads = whole_quads(local)
    frame = min(FRAME, blocks)
    tables = (frame + 2 * margin) * (blocks // frame)
    lines = max(8, beads)
    units = blocks * beads // 2
    return [
        pltpu.VMEM((3, beads, (blocks + 2 * margin) * BLOCK), f32),
        pltpu.VMEM((SLOTS, PAIR_PAD * odd_tiles(lines), BLOCK), f32),
        pltpu.VMEM((SLOTS, SUM_ROWS * odd_tiles(lines), BLOCK), f32),
        pltpu.VMEM((tables, beads // QUAD, BLOCK, QUAD * PAIR_PAD), bf16),
        pltpu.VMEM((tables, beads // 2, 2 * SUM_ROWS, BLOCK), bf16),
        pltpu.VMEM((2 * units, PAIR_PAD, BLOCK), bf16),
        pltpu.VMEM(((units + 1) * 16, BLOCK), f32),
        pltpu.VMEM((3, beads, blocks * BLOCK), f32),
        pltpu.VMEM((2 * listed * BLOCK, 2 * BLOCK), bf16),
        pltpu.VMEM((2 * listed * BLOCK, 2 * BLOCK), bf16),
    ]


def call(kernel, args, smem_count, shapes, scratch, work, in_specs=None):
    vmem = pl.BlockSpec(memory_space=pltpu.VMEM)
    smem = pl.BlockSpec(memory_space=pltpu.SMEM)
    return pl.pallas_call(
        kernel,
        out_shape=[jax.ShapeDtypeStruct(shape, f32) for shape in shapes],
        grid=() if in_specs is None else (1,),
        in_specs=in_specs or [smem] * smem_count + [vmem] * (len(args) - smem_count),
        out_specs=[vmem] * len(shapes),
        scratch_shapes=scratch,
        compiler_params=pltpu.CompilerParams(vmem_limit_bytes=(40 if in_specs is None else 62) * 1024 * 1024),
        cost_estimate=pl.CostEstimate(
            flops=20 * work + 1024, bytes_accessed=4 * 1024 * 1024, transcendentals=2 * work
        ),
    )(*args)


def row_of(c, block, blocks, local):
    return (c * blocks + block) * local


def unpack_beads(source, base, blocks, local, target, offset):
    for c in range(3):
        for block in range(blocks):
            row = row_of(base + c, block, blocks, local)
            lane = offset + block * BLOCK
            for group in range(source.shape[0]):
                target[c, group * local:(group + 1) * local, lane:lane + BLOCK] = source[group, row:row + local, :]


def pack_beads(value, c, blocks, local, target):
    for block in range(blocks):
        row = row_of(c, block, blocks, local)
        for group in range(target.shape[0]):
            target[group, row:row + local, :] = value[
                group * local:(group + 1) * local, block * BLOCK:(block + 1) * BLOCK
            ]


FORCE = 6


def clear(coord_ref, local):
    if coord_ref.shape[1] != local:
        coord_ref[...] = jnp.zeros(coord_ref.shape, f32)


def prepare_kernel(
    blocks, x_ref, edge_ref, noise_ref, types_ref, lists_ref, rest_ref, message_ref, charge_ref, mass_ref
):
    steps, _, local, atoms = noise_ref.shape
    edge = message_ref.shape[2]
    types = types_ref[...]
    charge = charges(types)
    mass = jnp.zeros(types.shape, f32)
    for kind in range(4):
        mass = jnp.where(types == kind, MASSES[kind], mass)
    charge_ref[...] = charge
    mass_ref[...] = mass
    for c in range(3):
        message_ref[c] = x_ref[c, :, :edge]
        message_ref[3 + c] = x_ref[c, :, edge:2 * edge]
        message_ref[6 + c] = edge_ref[c]
    for i, row in enumerate([charge[:, :edge], charge[:, edge:2 * edge], mass[:, :edge]]):
        message_ref[9 + i] = jnp.broadcast_to(row, (local, edge))
    message_ref[12] = jnp.zeros((local, edge), f32)
    for m in range(lists_ref.shape[0]):
        at = m * (edge // 8)
        message_ref[12, 0:1, at:at + edge // BLOCK] = lists_ref[m:m + 1, :edge // BLOCK].astype(f32)
    for c in range(3 + 3 * steps):
        for block in range(atoms // BLOCK):
            lanes = slice(block * BLOCK, (block + 1) * BLOCK)
            value = x_ref[c, :, lanes] if c < 3 else noise_ref[c // 3 - 1, c % 3, :, lanes]
            row = row_of(c, block % blocks, blocks, local)
            rest_ref[block // blocks, row:row + local, :] = value


def front_kernel(
    each, margin, listed, lists_ref, types_ref, x_ref, p_ref, pout_ref, charge_ref, coord_ref, *scratch
):
    _, local, _ = x_ref.shape
    blocks = pout_ref.shape[0] * each
    charge_ref[...] = charges(types_ref[...])
    clear(coord_ref, local)
    for c in range(3):
        coord_ref[c, :local, :] = x_ref[c, :, :(blocks + 2 * margin) * BLOCK]
    offset_at = offsets_of(lists_ref, margin, margin, margin)
    add_forces(16, blocks, margin, listed, offset_at, charge_ref, coord_ref, scratch)
    force_ref = scratch[FORCE]
    for c in range(3):
        for block in range(blocks):
            lanes = slice(block * BLOCK, (block + 1) * BLOCK)
            moment = p_ref[c, :, (block + margin) * BLOCK:(block + margin + 1) * BLOCK]
            row = row_of(c, block % each, each, local)
            pout_ref[block // each, row:row + local, :] = moment + half_step * force_ref[c, :local, lanes]


def back_kernel(
    each, margin, listed, lists_ref, charge_ref, x_ref, message_ref, p_ref, front_ref, pout_ref, coord_ref, *scratch
):
    _, local, atoms = x_ref.shape
    edge = margin * BLOCK
    done = front_ref.shape[0]
    first = done * each
    blocks = (pout_ref.shape[0] - done) * each
    own = atoms - first * BLOCK
    clear(coord_ref, local)
    for c in range(3):
        coord_ref[c, :local, :own] = x_ref[c, :, first * BLOCK:]
        for part in range(2):
            coord_ref[c, :local, own + part * edge:own + (part + 1) * edge] = message_ref[3 * part + c]
    offset_at = offsets_of(lists_ref, first, first + margin, margin)
    add_forces(16, blocks, margin, listed, offset_at, charge_ref, coord_ref, scratch, first)
    force_ref = scratch[FORCE]
    pout_ref[:done] = front_ref[...]
    for c in range(3):
        for block in range(blocks):
            lanes = slice(block * BLOCK, (block + 1) * BLOCK)
            at = (first + block) * BLOCK + edge
            if at < atoms:
                moment = p_ref[c, :, at:at + BLOCK]
            else:
                moment = message_ref[6 + c, :, at - atoms:at - atoms + BLOCK]
            row = row_of(c, block % each, each, local)
            pout_ref[done + block // each, row:row + local, :] = moment + half_step * force_ref[c, :local, lanes]


def from_packed(ref, c, block, each, local):
    row = row_of(c, block % each, each, local)
    return ref[block // each, row:row + local, :]


def upper_kernel(each, margin, listed, lists_ref, charge_ref, both_ref, pout_ref, coord_ref, *scratch):
    _, local, atoms = pout_ref.shape
    blocks = atoms // BLOCK
    domain = both_ref.shape[0] * each
    skipped = domain - blocks - 2 * margin
    clear(coord_ref, local)
    for c in range(3):
        for block in range(skipped, domain):
            at = (block - skipped) * BLOCK
            coord_ref[c, :local, at:at + BLOCK] = from_packed(both_ref, c, block, each, local)
    offset_at = offsets_of(lists_ref, domain - blocks, domain - blocks, margin)
    add_forces(16, blocks, margin, listed, offset_at, charge_ref, coord_ref, scratch, skipped + margin)
    force_ref = scratch[FORCE]
    for c in range(3):
        for block in range(blocks):
            lanes = slice(block * BLOCK, (block + 1) * BLOCK)
            moment = from_packed(both_ref, 3 + c, domain - blocks + block - margin, each, local)
            pout_ref[c, :, lanes] = moment + half_step * force_ref[c, :local, lanes]


def lower_kernel(
    each, margin, listed, lists_ref, charge_ref, both_ref, message_ref, upper_ref, xout_ref, pout_ref, coord_ref,
    *scratch,
):
    _, local, atoms = xout_ref.shape
    edge = margin * BLOCK
    lower = atoms - upper_ref.shape[2]
    blocks = lower // BLOCK
    clear(coord_ref, local)
    for c in range(3):
        for part in range(2):
            coord_ref[c, :local, part * edge:(part + 1) * edge] = message_ref[3 * part + c]
        for block in range(blocks):
            at = 2 * edge + block * BLOCK
            coord_ref[c, :local, at:at + BLOCK] = from_packed(both_ref, c, block, each, local)
        xout_ref[c, :, :edge] = message_ref[3 + c]
        for block in range(margin, atoms // BLOCK):
            lanes = slice(block * BLOCK, (block + 1) * BLOCK)
            xout_ref[c, :, lanes] = from_packed(both_ref, c, block - margin, each, local)
        pout_ref[c, :, lower:] = upper_ref[c]
    offset_at = offsets_of(lists_ref, 0, 0, margin)
    add_forces(16, blocks, margin, listed, offset_at, charge_ref, coord_ref, scratch)
    force_ref = scratch[FORCE]
    for c in range(3):
        for block in range(blocks):
            lanes = slice(block * BLOCK, (block + 1) * BLOCK)
            if block < margin:
                moment = message_ref[6 + c, :, lanes]
            else:
                moment = from_packed(both_ref, 3 + c, block - margin, each, local)
            pout_ref[c, :, lanes] = moment + half_step * force_ref[c, :local, lanes]


def thermostat(coords, moments, noises, mass_ref, matrix_ref, matrix_t_ref, table_ref, store):
    beads, width = moments[0].shape
    cosine, ratio, stiffness, damping, kick = [
        jnp.concatenate([table_ref[i]] * (width // BLOCK), axis=1) for i in range(5)
    ]
    first = pl.multiple_of(own_place(mass_ref.shape[1] // width) * width, BLOCK)
    mass = jnp.broadcast_to(mass_ref[:, pl.ds(first, width)], (beads, width))
    spread = kick * jnp.sqrt(thermal * mass)
    drift = ratio / mass
    stiff = stiffness * mass

    def multiply(matrix, values):
        joined = jnp.concatenate(values, axis=1)
        one, two, three = [part.astype(bf16) for part in split3(joined)]
        rows = jnp.concatenate([one, two, one, two, three, one], axis=0)
        out = jnp.dot(matrix, rows, preferred_element_type=f32)
        return [out[:, i * width:(i + 1) * width] for i in range(len(values))]

    mode = multiply(matrix_t_ref[...], coords + moments)
    next_x, next_p = [], []
    for c in range(3):
        mode_x = mode[c]
        mode_p = damping * mode[3 + c] + spread * noises[c]
        next_x.append(cosine * mode_x + drift * mode_p)
        next_p.append(cosine * mode_p - stiff * mode_x)
    beads_now = multiply(matrix_ref[...], next_x + next_p)
    for c in range(3):
        store(c, beads_now[c], beads_now[3 + c])


def modes_kernel(
    blocks, noise_base, rest_ref, p_ref, mass_ref, matrix_ref, matrix_t_ref, table_ref,
    xout_ref, pout_ref, coord_ref, moment_ref, noise_ref,
):
    local = p_ref.shape[1] // (3 * blocks)
    unpack_beads(rest_ref, 0, blocks, local, coord_ref, 0)
    unpack_beads(p_ref, 0, blocks, local, moment_ref, 0)
    unpack_beads(rest_ref, noise_base, blocks, local, noise_ref, 0)

    def store(c, x, p):
        pack_beads(x, c, blocks, local, xout_ref)
        pack_beads(p, c, blocks, local, pout_ref)

    thermostat(
        *[[ref[c] for c in range(3)] for ref in (coord_ref, moment_ref, noise_ref)],
        mass_ref, matrix_ref, matrix_t_ref, table_ref, store,
    )


def middle_kernel(hops, blocks, listed, noise_base, joined, lists_ref, charge_ref, *refs):
    parts = 2 * hops + 1
    x_refs = refs[:parts]
    p_ref, noise_ref, mass_ref, matrix_ref, matrix_t_ref, table_ref = refs[parts:parts + 6]
    outs = refs[parts + 6:parts + (7 if joined else 8)]
    coord_ref, *scratch = refs[parts + len(outs) + 6:]
    beads = coord_ref.shape[1]
    local = beads // p_ref.shape[0]
    width = blocks * BLOCK
    for part in range(parts):
        unpack_beads(x_refs[part], 0, blocks, local, coord_ref, part * width)
    margin = hops * blocks
    first = own_place(p_ref.shape[0]) * blocks
    offset_at = offsets_of(lists_ref, first, first + margin, margin)
    add_forces(16, blocks, margin, listed, offset_at, charge_ref, coord_ref, scratch, first)
    force_ref = scratch[FORCE]
    unpack_beads(p_ref, 0, blocks, local, coord_ref, 0)
    unpack_beads(noise_ref, noise_base, blocks, local, coord_ref, (parts - 1) * width)

    def share(c, part):
        return coord_ref[c, :, part * width:(part + 1) * width]

    def store(c, x, p):
        pack_beads(x, c, blocks, local, outs[0])
        if joined:
            pack_beads(p, 3 + c, blocks, local, outs[0])
        else:
            pack_beads(p, c, blocks, local, outs[1])

    thermostat(
        [share(c, hops) for c in range(3)],
        [share(c, 0) + 2.0 * half_step * force_ref[c] for c in range(3)],
        [share(c, parts - 1) for c in range(3)],
        mass_ref, matrix_ref, matrix_t_ref, table_ref, store,
    )


def fold(count):
    return [i // 2 if i % 2 == 0 else count - 1 - i // 2 for i in range(count)]


def exchange(pieces):
    order = fold(pieces.shape[0])
    group = [order.index(at) for at in range(len(order))]
    return lax.all_to_all(pieces, "bead", split_axis=0, concat_axis=0, axis_index_groups=[group], tiled=True)


def passed(values, step):
    count = lax.axis_size("space")
    return lax.ppermute(values, "space", [(i, (i + step) % count) for i in range(count)])


def round_ring(values, hop):
    count = lax.axis_size("bead")
    domains = lax.axis_size("space")
    order = fold(count)
    device = {}
    for bead in range(count):
        for domain in range(domains):
            device[domain * count + order[bead]] = bead * domains + domain
    total = count * domains
    return lax.ppermute(values, ("bead", "space"), [(device[(at + hop) % total], device[at]) for at in range(total)])


def window(values, hops):
    return [round_ring(values, hop) if hop else values for hop in range(-hops, hops + 1)]


def body(positions, momenta, atom_types, neighbours, thermal_noise):
    count = lax.axis_size("bead")
    _, local, atoms = positions.shape
    beads = local * count
    domain = atoms // BLOCK
    blocks = domain // count
    share = blocks * BLOCK
    hops = -(-HALO // blocks)
    margin = hops * blocks
    edge = margin * BLOCK
    steps = thermal_noise.shape[0]
    listed = neighbours.shape[1]
    order = fold(count)
    lists = neighbours.T
    types = atom_types[None, :]

    packed = (count, 3 * blocks * local, BLOCK)
    whole = [positions.shape, (3, local, edge), thermal_noise.shape, types.shape, lists.shape]
    rest, message, charge, mass = call(
        functools.partial(prepare_kernel, blocks),
        (positions, momenta, thermal_noise, types, lists), 0,
        [(count, (1 + steps) * packed[1], BLOCK), (13, local, edge), (1, atoms), (1, atoms)], [], 0,
        [pl.BlockSpec(shape, lambda i, rank=len(shape): (0,) * rank) for shape in whole],
    )
    message = passed(message, -1)
    rest = exchange(rest)
    side = message[9:, 0]
    first_charge = jnp.concatenate([charge, side[:1], side[1:2]], axis=1)
    moved_mass = jnp.concatenate([mass[:, edge:], side[2:3]], axis=1)
    domains = lax.axis_size("space")
    foreign = side[3].reshape(8, edge // 8)[:listed, :margin].astype(jnp.int32)
    foreign = foreign + jnp.where(lax.axis_index("space") == domains - 1, domains * domain, 0)
    moved_lists = jnp.concatenate([lists[:, margin:], foreign], axis=1)

    matrix, tables = mode_constants(beads)
    at = np.concatenate([order.index(g) * local + np.arange(local) for g in range(count)])
    matrix = matrix[at][:, at]
    fixed = (moved_mass, split_rows(matrix), split_rows(matrix.T), jnp.asarray(tables[:, at]))

    pairs = beads * blocks * listed * BLOCK * BLOCK
    half = domain // 2
    most = domain - half
    (moment,) = call(
        functools.partial(front_kernel, blocks, margin, listed), (lists, types, positions, momenta), 1,
        [(most // blocks,) + packed[1:]],
        [pltpu.VMEM(types.shape, f32)] + force_scratch(local, most, margin, listed), pairs * most // domain,
    )
    moment, rest = lax.optimization_barrier((moment, rest))
    rest = round_ring(rest, hops)
    (moment,) = call(
        functools.partial(back_kernel, blocks, margin, listed),
        (moved_lists, first_charge, positions, message, momenta, moment), 1,
        [packed], force_scratch(local, domain - most, margin, listed), pairs * (domain - most) // domain,
    )
    moment, rest = lax.optimization_barrier((moment, rest))
    coords, moment = call(
        functools.partial(modes_kernel, blocks, 3), (rest, exchange(moment)) + fixed, 0, [packed] * 2,
        [pltpu.VMEM((3, beads, share), f32)] * 3, 0,
    )
    for step in range(1, steps):
        joined = step == steps - 1
        out = call(
            functools.partial(middle_kernel, hops, blocks, listed, 3 * step + 3, joined),
            (moved_lists, first_charge) + tuple(window(coords, hops)) + (moment, rest) + fixed, 1,
            [(count, 6 * blocks * local, BLOCK)] if joined else [packed] * 2,
            force_scratch(beads, blocks, margin, listed), pairs,
        )
        if not joined:
            coords, moment = out
    both = exchange(out[0])

    def ends(low, c):
        pieces = both[low:low + hops, c * packed[1]:(c + 1) * packed[1]]
        return pieces.reshape(hops, 3, blocks, local, BLOCK).transpose(1, 3, 0, 2, 4).reshape(3, local, edge)

    message = passed(jnp.concatenate([
        ends(count - 2 * hops, 0), ends(count - hops, 0), ends(count - hops, 1),
        jnp.broadcast_to(charge[:, None, atoms - edge:], (1, local, edge)),
    ], axis=0), 1)
    (upper,) = call(
        functools.partial(upper_kernel, blocks, margin, listed),
        (lists, first_charge, both), 1,
        [(3, local, most * BLOCK)], force_scratch(local, most, margin, listed), pairs * most // domain,
    )
    last_charge = jnp.concatenate([message[9, :1], first_charge[:, :half * BLOCK + edge]], axis=1)
    return tuple(call(
        functools.partial(lower_kernel, blocks, margin, listed),
        (lists, last_charge, both, message, upper), 1,
        [(3, local, atoms)] * 2, force_scratch(local, domain - most, margin, listed), pairs * (domain - most) // domain,
    ))


def solution(mesh):
    placed = (
        P(None, "bead", "space"),
        P(None, "bead", "space"),
        P("space"),
        P("space", None),
        P(None, None, "bead", "space"),
    )
    return jax.shard_map(
        body,
        mesh=mesh,
        in_specs=placed,
        out_specs=(P(None, "bead", "space"), P(None, "bead", "space")),
        check_vma=False,
    )
```
